128 devices in a mesh: section: 2 (over core), fsdp: 2 (over x_lo), expert: 32 (over y, x_hi, z).
Axes of the slice: x: 4 (x_hi: 2, x_lo: 2; x = x_hi * 2 + x_lo), y: 4, z: 4, core: 2. Of those that a mesh axis runs over, the one named last changes fastest.
Arguments:
- inputs: bfloat16 [2, 6144, 1536], P(None, ('fsdp', 'expert')), may hold values from -6 to 6
- cotangent: bfloat16 [2, 6144, 1536], P(None, ('fsdp', 'expert')), may hold values from -6 to 6
- segments: int32 [2, 6144], P(None, ('fsdp', 'expert')), may hold values from 0 to 95, never falling along the last dimension, each value on 1 to 96 neighbouring positions
- expert_ids: int32 [2, 2, 6144, 4], P('section', None, ('fsdp', 'expert')), may hold values from 0 to 31, all different within a row; in each aligned block of 96 rows (0 to 95, 96 to 191, ..., all dimensions but the last counted through in order) at most 15 rows name the same one
- gate_logits: float32 [2, 2, 6144, 4], P('section', None, ('fsdp', 'expert')), may hold values from -3 to 3
- w_query: bfloat16 [2, 1536, 1536], P('section', 'fsdp'), may hold values from -0.15625 to 0.15625
- key_projection: bfloat16 [2, 1536, 256], P('section', 'fsdp'), may hold values from -0.15625 to 0.15625
- value_projection: bfloat16 [2, 1536, 256], P('section', 'fsdp'), may hold values from -0.15625 to 0.15625
- w_out: bfloat16 [2, 1536, 1536], P('section', 'fsdp'), may hold values from -0.875 to 0.875
- gain_attn: bfloat16 [2, 1536], P('section', 'fsdp'), may hold values from 0.5 to 1.5
- gain_moe: bfloat16 [2, 1536], P('section', 'fsdp'), may hold values from 0.5 to 1.5
- w_gate: bfloat16 [2, 32, 1536, 768], P('section', 'expert', 'fsdp'), may hold values from -0.15625 to 0.15625
- w_up: bfloat16 [2, 32, 1536, 768], P('section', 'expert', 'fsdp'), may hold values from -0.15625 to 0.15625
- w_down: bfloat16 [2, 32, 768, 1536], P('section', 'expert', 'fsdp'), may hold values from -0.625 to 0.625
Outputs:
- acts: bfloat16 [2, 2, 6144, 1536], P('section', None, ('fsdp', 'expert'))
- in_grads: bfloat16 [2, 2, 6144, 1536], P('section', None, ('fsdp', 'expert'))
- grad_query: float32 [2, 1536, 1536], P('section', 'fsdp')
- grad_key: float32 [2, 1536, 256], P('section', 'fsdp')
- grad_value: float32 [2, 1536, 256], P('section', 'fsdp')
- grad_out: float32 [2, 1536, 1536], P('section', 'fsdp')
- grad_gain_attn: float32 [2, 1536], P('section', 'fsdp')
- grad_gain_moe: float32 [2, 1536], P('section', 'fsdp')
- grad_gate: float32 [2, 32, 1536, 768], P('section', 'expert', 'fsdp')
- grad_up: float32 [2, 32, 1536, 768], P('section', 'expert', 'fsdp')
- grad_down: float32 [2, 32, 768, 1536], P('section', 'expert', 'fsdp')
The draws below stay inside these ranges and needn't reach their ends.
Inputs may be any that keep to these rules, and one draw needn't show every extreme that they name: `segments`: segment ids never fall along a row; a document has 1 to 96 tokens, and one has exactly 96. `expert_ids`: each token names 4 different experts; among the 96 tokens of one device in one micro-batch and section no expert is named more than 15 times, a bound that some block reaches.
All inputs are finite; a program needn't handle non-finite values.
Results may differ from the reference program's by a relative error of at most 0.034.
Values may be sent and summed in bfloat16 or wider, within the bound.
A program may use at most 256 MiB of HBM per device.

```python
import math
import jax
import jax.numpy as jnp
import numpy as np
from jax import lax

MODEL_WIDTH = 1536
QUERY_HEADS = 12
KEY_VALUE_HEADS = 2
HEAD_SIZE = 128
EH = 768
TOP = 4
MB = 2
SEQ = 96
EXPERTS = 32
ROWS = 6144
CAP = 15
DOCS = 96
N_FSDP = 2
N_EXPERT = 32


def block_levels(stream_key, extent, pieces, smallest, largest):
    gain = 1.0
    for position, parts in pieces:
        draws = jax.random.uniform(jax.random.fold_in(jax.random.fold_in(stream_key, 6), position), (parts,), jnp.float32, smallest / len(pieces), largest / len(pieces))
        gain = gain * jnp.repeat(jnp.exp(draws), extent[position] // parts).reshape((-1,) + (1,) * (len(extent) - 1 - position))
    return gain


def length_profile(count, total, limit, skew):
    weights = [(1 << 20) // math.isqrt(grade ** skew) + 1 for grade in range(2, count + 1)]
    spare, counts = total - limit - (count - 1), [1] * (count - 1)
    while spare > 0:
        movable = [i for i in range(count - 1) if counts[i] < limit]
        pool, remaining = sum([weights[i] for i in movable]), spare
        for i in movable:
            addition = min(limit - counts[i], max(1, remaining * weights[i] // pool), spare)
            counts[i] = counts[i] + addition
            spare = spare - addition
    return np.array([limit] + counts)


def uneven_parts(stream_key, number_of, total, bound, skew):
    if number_of == 2:
        one = jax.random.randint(stream_key, (), max(1, total - bound), min(bound, total - 1) + 1)
        return jnp.stack([one, total - one])
    sizes = jnp.asarray(length_profile(number_of, total, bound, skew), jnp.int32)
    pairs = (number_of - 1) // 2
    giver, taker = sizes[1:1 + 2 * pairs:2], sizes[2:2 + 2 * pairs:2]
    room = jnp.minimum(giver - 1, bound - taker)
    moved = jax.random.randint(jax.random.fold_in(stream_key, 1), (pairs,), 0, 1 << 20) % (room + 1)
    sizes = sizes.at[1:1 + 2 * pairs:2].set(giver - moved).at[2:2 + 2 * pairs:2].set(taker + moved)
    return sizes[jax.random.permutation(jax.random.fold_in(stream_key, 2), number_of)]


def deal_out(stream_key, own, number, rows, count, top, reach, slope):
    sequence = jax.random.permutation(stream_key, count)
    packed, usual = shares(count, rows * top, reach, slope, True), shares(count, rows * top, reach, slope, False)
    places = jnp.arange(count)

    def named(sizes, offset_by):
        used = int((sizes > 0).sum())
        fixed = max(1, used // 4)
        passed = fixed + (places - fixed + offset_by * (used - fixed)) % max(1, count - fixed)
        return jnp.zeros((count,), jnp.int32).at[sequence[jnp.where(places < fixed, places, passed)]].set(jnp.asarray(sizes, jnp.int32))

    sizes = jnp.where(number % 4 == 0, named(packed, number // 4), named(usual, number - number // 4 - 1))
    mixed = jax.random.permutation(jax.random.fold_in(own, 3), count)
    source_of, sink = mixed[0:count // 2 * 2:2], mixed[1:count // 2 * 2:2]
    room = jnp.minimum(sizes[source_of] - 1, reach - sizes[sink]) // 2
    room = jnp.where((source_of == sequence[0]) | (sink == sequence[0]) | (sizes[sink] == 0), 0, jnp.maximum(room, 0))
    passed = jax.random.randint(jax.random.fold_in(own, 4), (count // 2,), 0, 1 << 20) % (room + 1)
    sizes = sizes.at[source_of].add(-passed).at[sink].add(passed)
    items = jnp.searchsorted(jnp.cumsum(sizes), jnp.arange(rows * top), side="right").astype(jnp.int32)
    listing = items.reshape(top, rows).T
    listing = listing[jax.random.permutation(jax.random.fold_in(own, 1), rows)]
    offset_by = jax.random.randint(jax.random.fold_in(own, 2), (rows, 1), 0, top)
    return jnp.take_along_axis(listing, (jnp.arange(top)[None, :] + offset_by) % top, axis=1)


def shares(amount, total, reach, lean, full):
    weights = [(1 << 20) // math.isqrt(rank ** lean) + 1 for rank in range(1, amount + 1)]
    largest = reach if full else min(reach, max(-(-total // amount), total * weights[0] // sum(weights)))
    least = 1 if total - largest >= amount - 1 else 0
    given, rest = [largest] + [least] * (amount - 1), total - largest - least * (amount - 1)
    while rest > 0:
        candidates = [i for i in range(1, amount) if given[i] < largest] or [i for i in range(1, amount) if given[i] < reach]
        whole, budget = sum([weights[i] for i in candidates]), rest
        for i in candidates:
            addition = min(reach - given[i], max(1, budget * weights[i] // whole), rest)
            given[i] = given[i] + addition
            rest = rest - addition
    return np.array(given)


def scatter_about(own_key, dims, scale, reach, pieces=(), kind=jnp.bfloat16):
    drawn = scale * jax.random.normal(own_key, dims, jnp.float32)
    if pieces:
        drawn = drawn * block_levels(own_key, dims, pieces, -0.22, 0.18)
    return jnp.clip(drawn, -reach, reach).astype(kind)


def setup_inputs(seed: int = 0) -> dict:
    streams_of = jax.random.split(jax.random.key(seed), 15)
    inputs = scatter_about(streams_of[0], (MB, ROWS, MODEL_WIDTH), 1.0, 6.0, ((1, 64),))
    cotangent = scatter_about(streams_of[1], (MB, ROWS, MODEL_WIDTH), 1.0, 6.0, ((1, 64),))
    segments = jax.vmap(lambda own: jnp.searchsorted(jnp.cumsum(uneven_parts(own, DOCS, ROWS, SEQ, 2)), jnp.arange(ROWS), side="right"))(jax.random.split(streams_of[2], MB)).reshape((MB, ROWS)).astype(jnp.int32)
    expert_ids_keys = jax.random.split(jax.random.fold_in(streams_of[3], 1), 2 * MB * ROWS // SEQ)
    expert_ids_turns = jax.random.permutation(jax.random.fold_in(streams_of[3], 3), 2 * MB * ROWS // SEQ)
    expert_ids = jax.vmap(lambda own, number: deal_out(jax.random.fold_in(streams_of[3], 2), own, number, SEQ, EXPERTS, TOP, CAP, 2))(expert_ids_keys, expert_ids_turns).reshape((2, MB, ROWS, TOP))
    gate_logits = scatter_about(streams_of[4], (2, MB, ROWS, TOP), 0.5, 3.0, ((0, 2), (2, 64)), jnp.float32)
    w_query = scatter_about(streams_of[5], (2, MODEL_WIDTH, QUERY_HEADS * HEAD_SIZE), MODEL_WIDTH ** -0.5, 0.15625, ((0, 2), (1, 2)))
    key_projection = scatter_about(streams_of[6], (2, MODEL_WIDTH, KEY_VALUE_HEADS * HEAD_SIZE), MODEL_WIDTH ** -0.5, 0.15625, ((0, 2), (1, 2)))
    value_projection = scatter_about(streams_of[7], (2, MODEL_WIDTH, KEY_VALUE_HEADS * HEAD_SIZE), MODEL_WIDTH ** -0.5, 0.15625, ((0, 2), (1, 2)))
    w_out = scatter_about(streams_of[8], (2, QUERY_HEADS * HEAD_SIZE, MODEL_WIDTH), (QUERY_HEADS * HEAD_SIZE // 32) ** -0.5, 0.875, ((0, 2), (1, 2)))
    gain_attn = jnp.clip(1.0 + 0.1 * jax.random.normal(streams_of[9], (2, MODEL_WIDTH), jnp.float32), 0.5, 1.5).astype(jnp.bfloat16)
    gain_moe = jnp.clip(1.0 + 0.1 * jax.random.normal(streams_of[10], (2, MODEL_WIDTH), jnp.float32), 0.5, 1.5).astype(jnp.bfloat16)
    w_gate = scatter_about(streams_of[11], (2, EXPERTS, MODEL_WIDTH, EH), MODEL_WIDTH ** -0.5, 0.15625, ((0, 2), (1, 32), (2, 2)))
    w_up = scatter_about(streams_of[12], (2, EXPERTS, MODEL_WIDTH, EH), MODEL_WIDTH ** -0.5, 0.15625, ((0, 2), (1, 32), (2, 2)))
    w_down = scatter_about(streams_of[13], (2, EXPERTS, EH, MODEL_WIDTH), (EH // 8) ** -0.5, 0.625, ((0, 2), (1, 32), (2, 2)))
    return dict(inputs=inputs, cotangent=cotangent, segments=segments, expert_ids=expert_ids, gate_logits=gate_logits, w_query=w_query, key_projection=key_projection, value_projection=value_projection, w_out=w_out, gain_attn=gain_attn, gain_moe=gain_moe, w_gate=w_gate, w_up=w_up, w_down=w_down)


epsilon = 1e-06
rope_base = 1000000.0
highest = lax.Precision.HIGHEST

@jax.custom_vjp
def lower_half(v):
    return lax.optimization_barrier(v.astype(jnp.bfloat16)).astype(jnp.float32)

@jax.custom_vjp
def low_back(v):
    return v

def low_keep(v):
    return (lower_half(v), None)

def low_pass(kept, grad):
    return (grad,)

def back_keep(v):
    return (v, None)

def back_low(kept, grad):
    return (lower_half(grad),)
lower_half.defvjp(low_keep, low_pass)
low_back.defvjp(back_keep, back_low)

def rms_scale(operand, gain_row):
    inverse = lax.rsqrt(lax.optimization_barrier(jnp.mean(operand * operand, axis=-1, keepdims=True)) + epsilon)
    return operand * inverse * gain_row

def rotary_rotation(operand, rotary_angles):
    half_dim = operand.shape[-1] // 2
    cosine = jnp.cos(rotary_angles)[..., None, :]
    sine_part = jnp.sin(rotary_angles)[..., None, :]
    front_half = operand[..., :half_dim]
    second = operand[..., half_dim:]
    return jnp.concatenate([front_half * cosine - second * sine_part, second * cosine + front_half * sine_part], axis=-1)

def layout(segment_rows):
    sequence_length = segment_rows.shape[-1]
    same_doc = segment_rows[:, :, None] == segment_rows[:, None, :]
    row_index = lax.broadcasted_iota(jnp.int32, (sequence_length, sequence_length), 0)
    col_index = lax.broadcasted_iota(jnp.int32, (sequence_length, sequence_length), 1)
    places = lax.optimization_barrier(jnp.sum((same_doc & (col_index < row_index)[None]).astype(jnp.int32), axis=-1))
    frequency = rope_base ** (-(jnp.arange(HEAD_SIZE // 2, dtype=jnp.float32) * 2.0 / HEAD_SIZE))
    rotary_angles = places.astype(jnp.float32)[..., None] * frequency
    return (rotary_angles, same_doc & (col_index <= row_index)[None])

def attend(section_input, segment_rows, w_query, key_projection, value_projection, w_out, gain_attn):
    group_number, sequence_length, width_model = section_input.shape
    rotary_angles, allowed = layout(segment_rows)
    group_portion = QUERY_HEADS // KEY_VALUE_HEADS
    norm_one = lower_half(rms_scale(section_input, gain_attn))
    query_rows = low_back(jnp.einsum('gsd,de->gse', norm_one, w_query, precision=highest))
    query_rows = lower_half(rotary_rotation(query_rows.reshape(group_number, sequence_length, QUERY_HEADS, HEAD_SIZE), rotary_angles))
    query_rows = query_rows.reshape(group_number, sequence_length, KEY_VALUE_HEADS, group_portion, HEAD_SIZE)
    key_head_rows = low_back(jnp.einsum('gsd,de->gse', norm_one, key_projection, precision=highest))
    key_head_rows = lower_half(rotary_rotation(key_head_rows.reshape(group_number, sequence_length, KEY_VALUE_HEADS, HEAD_SIZE), rotary_angles))
    value_head_rows = lower_half(low_back(jnp.einsum('gsd,de->gse', norm_one, value_projection, precision=highest)))
    value_head_rows = value_head_rows.reshape(group_number, sequence_length, KEY_VALUE_HEADS, HEAD_SIZE)
    raw_scores = jnp.einsum('gqhnd,gkhd->ghnqk', query_rows, key_head_rows, precision=highest)
    scores = jnp.where(allowed[:, None, None], low_back(raw_scores) * HEAD_SIZE ** (-0.5), -1e+30)
    top_score = lax.optimization_barrier(jnp.max(scores, axis=-1, keepdims=True))
    exp_scores = jnp.exp(scores - top_score)
    attn_probs = lower_half(exp_scores / lax.optimization_barrier(jnp.sum(exp_scores, axis=-1, keepdims=True)))
    attn_mixed = jnp.einsum('ghnqk,gkhd->gqhnd', attn_probs, value_head_rows, precision=highest)
    attn_mixed = lower_half(low_back(attn_mixed.reshape(group_number, sequence_length, QUERY_HEADS * HEAD_SIZE)))
    return section_input + low_back(jnp.einsum('gsa,ad->gsd', attn_mixed, w_out, precision=highest))

def expert_apply(slot_rows, gate_one, up_one, down_one):
    gate_pre = low_back(jnp.dot(slot_rows, gate_one, precision=highest))
    up_pre = low_back(jnp.dot(slot_rows, up_one, precision=highest))
    hidden = lower_half(jax.nn.gelu(gate_pre) * up_pre)
    return low_back(lower_half(jnp.dot(hidden, down_one, precision=highest)))

def layer_apply(section_input, segment_rows, chosen, logits, weights):
    w_query, key_projection, value_projection, w_out, gain_attn, gain_moe, w_gate, w_up, w_down = weights
    devices = N_FSDP * N_EXPERT
    grouped = section_input.reshape(N_FSDP, N_EXPERT, SEQ, MODEL_WIDTH)
    seg_grouped = segment_rows.reshape(N_FSDP, N_EXPERT, SEQ)

    def attend_group(blocks):
        return attend(blocks[0], blocks[1], w_query, key_projection, value_projection, w_out, gain_attn)
    hidden_one = lax.map(jax.checkpoint(attend_group), (grouped, seg_grouped)).reshape(ROWS, MODEL_WIDTH)
    norm_two = lower_half(rms_scale(hidden_one, gain_moe))
    entry_expert = chosen.reshape(devices, SEQ * TOP)
    one_hot = (entry_expert[:, :, None] == jnp.arange(EXPERTS, dtype=jnp.int32)).astype(jnp.int32)
    entry_slot = lax.optimization_barrier(jnp.sum((jnp.cumsum(one_hot, axis=1) - one_hot) * one_hot, axis=2))
    device_base = jnp.arange(devices, dtype=jnp.int32)[:, None] * CAP
    buffer_place = (entry_expert * (devices * CAP) + device_base + entry_slot).reshape(-1).astype(jnp.int32)
    copies = jnp.repeat(norm_two, TOP, axis=0)
    buffer = jnp.zeros((EXPERTS * devices * CAP, MODEL_WIDTH), jnp.float32).at[buffer_place].set(copies)
    buffer = low_back(buffer).reshape(EXPERTS, devices * CAP, MODEL_WIDTH)

    def expert_group(blocks):
        return expert_apply(blocks[0], blocks[1], blocks[2], blocks[3])
    outputs = lax.map(jax.checkpoint(expert_group), (buffer, w_gate, w_up, w_down))
    picked = outputs.reshape(EXPERTS * devices * CAP, MODEL_WIDTH)[buffer_place].reshape(ROWS, TOP, MODEL_WIDTH)
    gate_weights = jax.nn.softmax(logits, axis=-1)
    return hidden_one + lax.optimization_barrier(jnp.sum(gate_weights[:, :, None] * picked, axis=1))

def reference(inputs, cotangent, segments, expert_ids, gate_logits, w_query, key_projection, value_projection, w_out, gain_attn, gain_moe, w_gate, w_up, w_down):
    stacks = (w_query, key_projection, value_projection, w_out, gain_attn, gain_moe, w_gate, w_up, w_down)
    params_zero = tuple((weight[0].astype(jnp.float32) for weight in stacks))
    params_one = tuple((weight[1].astype(jnp.float32) for weight in stacks))
    totals_zero = tuple((jnp.zeros_like(weight) for weight in params_zero))
    totals_one = tuple((jnp.zeros_like(weight) for weight in params_one))
    act_zero, act_one, grad_zero, grad_one = ([], [], [], [])
    for micro_batch in range(MB):

        def section_zero(section_input, weights):
            return layer_apply(section_input, segments[micro_batch], expert_ids[0, micro_batch], gate_logits[0, micro_batch], weights)

        def section_one(section_input, weights):
            return layer_apply(section_input, segments[micro_batch], expert_ids[1, micro_batch], gate_logits[1, micro_batch], weights)
        first_out, back_zero = jax.vjp(section_zero, inputs[micro_batch].astype(jnp.float32), params_zero)
        middle = lax.optimization_barrier(first_out.astype(jnp.bfloat16))
        last_out, back_one = jax.vjp(section_one, middle.astype(jnp.float32), params_one)
        d_middle, d_one = back_one(cotangent[micro_batch].astype(jnp.float32))
        d_middle = lax.optimization_barrier(d_middle.astype(jnp.bfloat16))
        d_start, d_zero = back_zero(d_middle.astype(jnp.float32))
        totals_zero = tuple((total_sum + grad_part for total_sum, grad_part in zip(totals_zero, d_zero)))
        totals_one = tuple((total_sum + grad_part for total_sum, grad_part in zip(totals_one, d_one)))
        act_zero.append(middle)
        act_one.append(last_out.astype(jnp.bfloat16))
        grad_zero.append(d_start.astype(jnp.bfloat16))
        grad_one.append(d_middle)
    acts = jnp.stack([jnp.stack(act_zero), jnp.stack(act_one)])
    in_grads = jnp.stack([jnp.stack(grad_zero), jnp.stack(grad_one)])
    merged = tuple((jnp.stack([first_part, second_part]) for first_part, second_part in zip(totals_zero, totals_one)))
    return (acts, in_grads, merged[0], merged[1], merged[2], merged[3], merged[4], merged[5], merged[6], merged[7], merged[8])
```

```python
import functools

import jax
import jax.numpy as jnp
from jax import lax
from jax.experimental import pallas as pl
from jax.experimental.pallas import tpu as pltpu
from jax.sharding import PartitionSpec as P

MESH = pl.DeviceIdType.MESH
BF = jnp.bfloat16
F32 = jnp.float32

HEAD = 128
EPS = 1e-06
ROPE_BASE = 1000000.0
GELU_C = 0.7978845608
GELU_A = 0.044715

MB = 2
SEQ = 96
WIDTH = 1536
HALF = 768
EXPERTS = 32
SLOTS = 16
ROWS = EXPERTS * SLOTS
HIDDEN = 768
HEADS = 6
QKV = 1024


def dot(a, b):
    return jnp.dot(a, b, preferred_element_type=F32)


def dot_nt(a, b):
    return lax.dot_general(a, b, (((1,), (1,)), ((), ())), preferred_element_type=F32)


def dot_tn(a, b):
    return lax.dot_general(a, b, (((0,), (0,)), ((), ())), preferred_element_type=F32)


def aligned(start, size, unit):
    return pl.ds(pl.multiple_of(start, unit), size)


def inverse_rms(rows):
    return lax.rsqrt(jnp.mean(rows * rows, axis=-1, keepdims=True) + EPS)


def rms_back(rows, inverse, gain, grad):
    scaled = gain * grad
    return inverse * scaled - rows * (inverse * inverse * inverse) * jnp.mean(
        scaled * rows, axis=-1, keepdims=True
    )


def rotate(head, cos, sin):
    return head * cos + pltpu.roll(head, HEAD // 2, 1) * sin


def section_kernel(
    x_in,
    ct_in,
    wq_in,
    wk_in,
    wv_in,
    wo_in,
    wg_in,
    wu_in,
    wd_in,
    gain_one,
    gain_two,
    ids_t,
    logits_t,
    cos_t,
    sin_t,
    mask_t,
    acts_out,
    ingrad_out,
    gains_out,
    n2rows_out,
    dyrows_out,
    hid_out,
    dgate_out,
    dup_out,
    n1_out,
    dqkv_out,
    att_out,
    da_out,
    wqkv,
    wo,
    wg,
    wu,
    wd,
    xpair,
    n1s,
    qkvs,
    att,
    hid_one,
    part_own,
    part_send,
    part_recv,
    sel,
    cg_hi,
    cg_lo,
    dsend,
    bsend,
    n2recv,
    yrecv,
    dyrecv,
    dn2recv,
    gs,
    us,
    hid,
    acts_s,
    g_buf,
    dh_s,
    da_pair,
    dqkv_all,
    dn1_send,
    dn1_recv,
    ingrad_s,
    gains_acc,
    lw_sem,
    ws_sem,
    wr_sem,
    as_sem,
    ar_sem,
    ps_sem,
    pr_sem,
    xs_sem,
    xr_sem,
    gs_sem,
    gr_sem,
    out_sem,
    go_sem,
):
    sec = lax.axis_index("section")
    f = lax.axis_index("fsdp")
    e = lax.axis_index("expert")
    other = 1 - f
    own_rows = aligned(f * SEQ, SEQ, 16)
    other_rows = aligned(other * SEQ, SEQ, 16)
    own_half = aligned(f * HALF, HALF, 128)
    other_half = aligned(other * HALF, HALF, 128)
    my_slots = aligned(e * SLOTS, SLOTS, 16)
    partner = {"fsdp": other}
    first, second = sec == 0, sec == 1

    barrier = pltpu.get_barrier_semaphore()

    @pl.loop(1, EXPERTS)
    def _(d):
        pl.semaphore_signal(
            barrier, inc=1, device_id={"expert": lax.rem(e + d, EXPERTS)}, device_id_type=MESH
        )

    for place in ({"fsdp": other}, {"section": 1 - sec}, {"section": 1 - sec, "fsdp": other}):
        pl.semaphore_signal(barrier, inc=1, device_id=place, device_id_type=MESH)

    local = [
        (wq_in.at[:, own_half], wqkv.at[own_half, pl.ds(0, HALF)]),
        (wk_in.at[:, aligned(f * HEAD, HEAD, 128)], wqkv.at[own_half, pl.ds(HALF, HEAD)]),
        (wv_in.at[:, aligned(f * HEAD, HEAD, 128)], wqkv.at[own_half, pl.ds(HALF + HEAD, HEAD)]),
        (wo_in, wo),
        (wg_in, wg.at[own_half]),
        (wu_in, wu.at[own_half]),
        (wd_in, wd.at[aligned(f * (HIDDEN // 2), HIDDEN // 2, 16)]),
    ]
    local = [pltpu.make_async_copy(a, b, lw_sem.at[i]) for i, (a, b) in enumerate(local)]
    for copy in local:
        copy.start()
    x_local = pltpu.make_async_copy(x_in, xpair.at[:, own_rows], lw_sem.at[7])
    ct_local = pltpu.make_async_copy(ct_in, g_buf, lw_sem.at[8])
    pl.when(first)(x_local.start)
    pl.when(second)(ct_local.start)

    def remote(src, dst, i):
        return pltpu.make_async_remote_copy(
            src_ref=src,
            dst_ref=dst,
            send_sem=ws_sem.at[i],
            recv_sem=wr_sem.at[i],
            device_id=partner,
            device_id_type=MESH,
        )

    w_attn = [
        remote(wq_in.at[:, other_half], wqkv.at[own_half, pl.ds(0, HALF)], 0),
        remote(
            wk_in.at[:, aligned(other * HEAD, HEAD, 128)],
            wqkv.at[own_half, pl.ds(HALF, HEAD)],
            1,
        ),
        remote(
            wv_in.at[:, aligned(other * HEAD, HEAD, 128)],
            wqkv.at[own_half, pl.ds(HALF + HEAD, HEAD)],
            2,
        ),
    ]
    w_moe = [
        remote(wg_in, wg.at[own_half], 3),
        remote(wu_in, wu.at[own_half], 4),
        remote(wd_in, wd.at[aligned(f * (HIDDEN // 2), HIDDEN // 2, 16)], 5),
    ]
    x_remote = remote(x_in, xpair.at[:, own_rows], 6)

    pl.semaphore_wait(barrier, EXPERTS - 1 + 3)

    @pl.when(first)
    def _():
        x_remote.start()
        for copy in w_attn + w_moe:
            copy.start()

    gains_acc[...] = jnp.zeros_like(gains_acc)

    @pl.loop(0, MB)
    def _(m):
        ids = ids_t[m]
        logits = logits_t[m]
        raised = jnp.exp(logits - jnp.max(logits, axis=0, keepdims=True))
        gates = raised / jnp.sum(raised, axis=0, keepdims=True)
        expert = lax.broadcasted_iota(jnp.int32, (EXPERTS, SEQ), 0)
        named = jnp.zeros((EXPERTS, SEQ), F32)
        weight = jnp.zeros((EXPERTS, SEQ), F32)
        for k in range(4):
            hit = expert == ids[k : k + 1, :]
            named = jnp.where(hit, 1.0, named)
            weight = jnp.where(hit, gates[k : k + 1, :], weight)
        earlier = lax.broadcasted_iota(jnp.int32, (SEQ, SEQ), 0) < lax.broadcasted_iota(
            jnp.int32, (SEQ, SEQ), 1
        )
        slot = dot(named.astype(BF), jnp.where(earlier, 1.0, 0.0).astype(BF))
        slot = jnp.where(named > 0.0, slot, -1.0)
        place = lax.broadcasted_iota(jnp.int32, (EXPERTS, SLOTS, SEQ), 1).astype(F32)
        chosen = jnp.where(
            jnp.broadcast_to(slot[:, None, :], (EXPERTS, SLOTS, SEQ)) == place, 1.0, 0.0
        )
        scaled = chosen * jnp.broadcast_to(weight[:, None, :], (EXPERTS, SLOTS, SEQ))
        scaled = scaled.reshape(ROWS, SEQ)
        high = scaled.astype(BF)
        sel[m] = chosen.reshape(ROWS, SEQ).astype(BF)
        cg_hi[m] = high
        cg_lo[m] = (scaled - high.astype(F32)).astype(BF)

    def exchange(kind, m, src, dst):
        @pl.loop(1, EXPERTS)
        def _(d):
            p = lax.rem(e + d, EXPERTS)
            pltpu.make_async_remote_copy(
                src_ref=src.at[m, aligned(p * SLOTS, SLOTS, 16)],
                dst_ref=dst.at[m, my_slots],
                send_sem=as_sem.at[kind, m],
                recv_sem=ar_sem.at[kind, m],
                device_id={"expert": p},
                device_id_type=MESH,
            ).start()

        dst[m, my_slots] = src[m, my_slots]

    def received(kind, m, dst):
        whole = dst.at[m, pl.ds(0, ROWS - SLOTS)]
        pltpu.make_async_copy(whole, whole, ar_sem.at[kind, m]).wait()

    def sent(kind, m, src):
        whole = src.at[m, pl.ds(0, ROWS - SLOTS)]
        pltpu.make_async_copy(whole, whole, as_sem.at[kind, m]).wait()

    def to_partner(kind, m, src, dst):
        return pltpu.make_async_remote_copy(
            src_ref=src,
            dst_ref=dst,
            send_sem=ps_sem.at[kind, m],
            recv_sem=pr_sem.at[kind, m],
            device_id=partner,
            device_id_type=MESH,
        )

    def acts_copy(m, cross):
        return pltpu.make_async_remote_copy(
            src_ref=acts_s.at[m],
            dst_ref=xpair.at[m, own_rows],
            send_sem=xs_sem.at[cross, m],
            recv_sem=xr_sem.at[f, m],
            device_id={"section": 1, "fsdp": other} if cross else {"section": 1},
            device_id_type=MESH,
        )

    def acts_arrived(m):
        for at, rows in ((f, own_rows), (other, other_rows)):
            place = xpair.at[m, rows]
            pltpu.make_async_copy(place, place, xr_sem.at[at, m]).wait()

    def grad_copy(m):
        return pltpu.make_async_remote_copy(
            src_ref=ingrad_s.at[m],
            dst_ref=g_buf.at[m],
            send_sem=gs_sem.at[m],
            recv_sem=gr_sem.at[m],
            device_id={"section": 0},
            device_id_type=MESH,
        )

    def out_copy(i, src, dst, m):
        return pltpu.make_async_copy(src, dst, out_sem.at[i, m])

    def send_dy(m):
        gate = jnp.sum(cg_hi[m].astype(F32) + cg_lo[m].astype(F32), axis=1, keepdims=True)

        @pl.loop(0, WIDTH // 512)
        def _(j):
            cols = aligned(j * 512, 512, 128)
            bsend[m, :, cols] = (dot(sel[m], g_buf[m, :, cols]) * gate).astype(BF)

        exchange(2, m, bsend, dyrecv)

    @pl.when(second)
    def _():
        ct_local.wait()
        pl.semaphore_wait(go_sem, 1)
        for copy in w_attn:
            copy.start()
        pl.loop(0, MB)(send_dy)
        for copy in w_moe:
            copy.start()

    @pl.when(first)
    def _():
        x_local.wait()
        x_remote.wait_recv()

    for copy in local[:4]:
        copy.wait()
    for copy in w_attn:
        copy.wait_recv()

    def heads_of(ref, m, rows):
        return jnp.concatenate(
            [ref[m, rows, pl.ds(h * HEAD, HEAD)] for h in range(HEADS)], axis=0
        )

    def softmax_of(m, s, queries, keys):
        scores = dot_nt(queries, keys) * HEAD ** (-0.5)
        allowed = jnp.concatenate([mask_t[m, s]] * HEADS, axis=0)
        scores = jnp.where(allowed > 0.0, scores, -1e30)
        raised = jnp.exp(scores - jnp.max(scores, axis=-1, keepdims=True))
        return raised / jnp.sum(raised, axis=-1, keepdims=True)

    def attend(m):
        rows = xpair[m].astype(F32)
        n1s[m] = (rows * inverse_rms(rows) * gain_one[...]).astype(BF)
        cos, sin = cos_t[m], sin_t[m]
        for j in range(4):
            block = dot(n1s[m], wqkv[:, pl.ds(j * 256, 256)])
            qkvs[m, :, pl.ds(j * 256, HEAD)] = rotate(block[:, :HEAD], cos, sin).astype(BF)
            late = block[:, HEAD:]
            if j < 3:
                late = rotate(late, cos, sin)
            qkvs[m, :, pl.ds(j * 256 + HEAD, HEAD)] = late.astype(BF)

        @pl.loop(0, 2)
        def _(s):
            at = aligned(s * SEQ, SEQ, 16)
            queries = heads_of(qkvs, m, at)
            keys = qkvs[m, at, pl.ds(HALF, HEAD)]
            values = qkvs[m, at, pl.ds(HALF + HEAD, HEAD)]
            probs = softmax_of(m, s, queries, keys).astype(BF)
            mixed = dot(probs, values).astype(BF)
            for h in range(HEADS):
                att[m, at, pl.ds(h * HEAD, HEAD)] = mixed[h * SEQ : (h + 1) * SEQ]

        @pl.loop(0, WIDTH // 512)
        def _(j):
            cols = aligned(j * 512, 512, 128)
            block = dot(att[m], wo[:, cols])
            top, low = block[:SEQ], block[SEQ:]
            mine = f == 0
            hid_one[m, :, cols] = jnp.where(mine, top, low)
            part_send[m, :, cols] = jnp.where(mine, low, top).astype(BF)

        to_partner(0, m, part_send.at[m], part_recv.at[m]).start()

    def dispatch(m):
        to_partner(0, m, part_send.at[m], part_recv.at[m]).wait_recv()
        rows = xpair[m, own_rows].astype(F32) + (hid_one[m] + part_recv[m].astype(F32))
        hid_one[m] = rows
        n2 = (rows * inverse_rms(rows) * gain_two[...]).astype(BF)
        dsend[m] = dot(sel[m], n2).astype(BF)
        exchange(0, m, dsend, n2recv)

    def forward(m):
        pl.when(second)(lambda: acts_arrived(m))
        attend(m)
        dispatch(m)

    pl.loop(0, MB)(forward)

    for copy in local[4:]:
        copy.wait()
    for copy in w_moe:
        copy.wait_recv()

    @pl.when(first)
    def _():
        for copy in w_attn + w_moe:
            copy.wait_send()
        pl.semaphore_signal(go_sem, inc=1, device_id={"section": 1}, device_id_type=MESH)

    def experts(m):
        received(0, m, n2recv)
        out_copy(0, n2recv.at[m], n2rows_out.at[m], m).start()

        @pl.loop(0, HIDDEN // 256)
        def _(j):
            cols = aligned(j * 256, 256, 128)
            gate = dot(n2recv[m], wg[:, cols])
            up = dot(n2recv[m], wu[:, cols])
            bend = jnp.tanh(GELU_C * (gate + GELU_A * gate * gate * gate))
            gs[m, :, cols] = gate.astype(BF)
            us[m, :, cols] = up.astype(BF)
            hid[m, :, cols] = (0.5 * gate * (1.0 + bend) * up).astype(BF)

        out_copy(1, hid.at[m], hid_out.at[m], m).start()
        pl.when(second)(lambda: sent(2, m, bsend))

        @pl.loop(0, WIDTH // 512)
        def _(j):
            cols = aligned(j * 512, 512, 128)
            bsend[m, :, cols] = dot(hid[m], wd[:, cols]).astype(BF)

        exchange(1, m, bsend, yrecv)

    pl.loop(0, MB)(experts)

    def combine(m):
        received(1, m, yrecv)

        @pl.loop(0, WIDTH // 512)
        def _(j):
            cols = aligned(j * 512, 512, 128)
            block = yrecv[m, :, cols]
            mixed = dot_tn(cg_hi[m], block) + dot_tn(cg_lo[m], block)
            acts_s[m, :, cols] = (hid_one[m, :, cols] + mixed).astype(BF)

        out_copy(2, acts_s.at[m], acts_out.at[m], m).start()

    @pl.when(first)
    def _():
        @pl.loop(0, MB)
        def _(m):
            combine(m)
            for cross in (0, 1):
                acts_copy(m, cross).start()

        @pl.loop(0, MB)
        def _(m):
            sent(1, m, bsend)
            place = g_buf.at[m]
            pltpu.make_async_copy(place, place, gr_sem.at[m]).wait()
            send_dy(m)

    def experts_back(m):
        received(2, m, dyrecv)
        out_copy(3, dyrecv.at[m], dyrows_out.at[m], m).start()

        @pl.loop(0, HIDDEN // 256)
        def _(j):
            cols = aligned(j * 256, 256, 128)
            dhid = dot_nt(dyrecv[m], wd[cols, :])
            gate = gs[m, :, cols].astype(F32)
            up = us[m, :, cols].astype(F32)
            square = gate * gate
            bend = jnp.tanh(GELU_C * (gate + GELU_A * square * gate))
            half = 0.5 * (1.0 + bend)
            slope = half + 0.5 * gate * (1.0 - bend * bend) * (
                GELU_C * (1.0 + 3.0 * GELU_A * square)
            )
            gs[m, :, cols] = (dhid * up * slope).astype(BF)
            us[m, :, cols] = (dhid * (gate * half)).astype(BF)

        out_copy(4, gs.at[m], dgate_out.at[m], m).start()
        out_copy(5, us.at[m], dup_out.at[m], m).start()
        pl.when(first)(lambda: sent(2, m, bsend))
        pl.when(second)(lambda: sent(1, m, bsend))

        @pl.loop(0, WIDTH // 512)
        def _(j):
            cols = aligned(j * 512, 512, 128)
            block = dot_nt(gs[m], wg[cols, :]) + dot_nt(us[m], wu[cols, :])
            bsend[m, :, cols] = block.astype(BF)

        exchange(3, m, bsend, dn2recv)

    pl.loop(0, MB)(experts_back)

    def attend_back(m):
        received(3, m, dn2recv)
        rows = hid_one[m]
        inverse = inverse_rms(rows)

        @pl.loop(0, WIDTH // 512)
        def _(j):
            cols = aligned(j * 512, 512, 128)
            dh_s[m, :, cols] = dot_tn(sel[m], dn2recv[m, :, cols])

        grad = dh_s[m]
        gains_acc[1:2] += jnp.sum(grad * rows * inverse, axis=0, keepdims=True)
        total = g_buf[m].astype(F32) + rms_back(rows, inverse, gain_two[...], grad)
        dh_s[m] = total
        da_pair[m, own_rows] = total.astype(BF)
        da_copy = to_partner(1, m, da_pair.at[m, own_rows], da_pair.at[m, own_rows])
        da_copy.start()
        da_copy.wait_recv()
        out_copy(6, da_pair.at[m], da_out.at[m], m).start()

        @pl.loop(0, 2)
        def _(s):
            at = aligned(s * SEQ, SEQ, 16)
            dmix = dot_nt(da_pair[m, at], wo[...]).astype(BF)
            dmix = jnp.concatenate(
                [dmix[:, h * HEAD : (h + 1) * HEAD] for h in range(HEADS)], axis=0
            )
            queries = heads_of(qkvs, m, at)
            keys = qkvs[m, at, pl.ds(HALF, HEAD)]
            values = qkvs[m, at, pl.ds(HALF + HEAD, HEAD)]
            probs = softmax_of(m, s, queries, keys)
            dprobs = dot_nt(dmix, values)
            dvalues = dot_tn(probs.astype(BF), dmix)
            dscores = probs * (dprobs - jnp.sum(dprobs * probs, axis=-1, keepdims=True))
            dscores = (dscores * HEAD ** (-0.5)).astype(BF)
            cos = cos_t[m, at]
            sin = -sin_t[m, at]
            dkeys = rotate(dot_tn(dscores, queries), cos, sin)
            dqueries = dot(dscores, keys)
            for h in range(HEADS):
                part = rotate(dqueries[h * SEQ : (h + 1) * SEQ], cos, sin)
                dqkv_all[m, f, at, pl.ds(h * HEAD, HEAD)] = part.astype(BF)
            dqkv_all[m, f, at, pl.ds(HALF, HEAD)] = dkeys.astype(BF)
            dqkv_all[m, f, at, pl.ds(HALF + HEAD, HEAD)] = dvalues.astype(BF)

        dqkv_copy = to_partner(3, m, dqkv_all.at[m, f], dqkv_all.at[m, f])
        dqkv_copy.start()

        @pl.loop(0, WIDTH // 512)
        def _(j):
            cols = aligned(j * 512, 512, 128)
            block = dot_nt(dqkv_all[m, f], wqkv[cols, :])
            top, low = block[:SEQ], block[SEQ:]
            mine = f == 0
            part_own[:, cols] = jnp.where(mine, top, low)
            dn1_send[m, :, cols] = jnp.where(mine, low, top).astype(BF)

        dn1_copy = to_partner(2, m, dn1_send.at[m], dn1_recv.at[m])
        dn1_copy.start()
        dn1_copy.wait_recv()
        grad = part_own[...] + dn1_recv[m].astype(F32)
        rows = xpair[m, own_rows].astype(F32)
        inverse = inverse_rms(rows)
        gains_acc[0:1] += jnp.sum(grad * rows * inverse, axis=0, keepdims=True)
        ingrad_s[m] = (dh_s[m] + rms_back(rows, inverse, gain_one[...], grad)).astype(BF)
        out_copy(7, ingrad_s.at[m], ingrad_out.at[m], m).start()
        pl.when(second)(grad_copy(m).start)

    pl.loop(0, MB)(attend_back)

    pl.when(second)(lambda: pl.loop(0, MB)(combine))

    @pl.loop(0, MB)
    def _(m):
        to_partner(3, m, dqkv_all.at[m, f], dqkv_all.at[m, f]).wait_recv()
        out_copy(8, n1s.at[m, :, own_half], n1_out.at[m], m).start()
        out_copy(9, dqkv_all.at[m], dqkv_out.at[m], m).start()
        out_copy(10, att.at[m], att_out.at[m], m).start()
        sent(0, m, dsend)
        sent(3, m, bsend)
        to_partner(0, m, part_send.at[m], part_recv.at[m]).wait_send()
        to_partner(1, m, da_pair.at[m, own_rows], da_pair.at[m, own_rows]).wait_send()
        to_partner(2, m, dn1_send.at[m], dn1_recv.at[m]).wait_send()
        to_partner(3, m, dqkv_all.at[m, f], dqkv_all.at[m, f]).wait_send()

    gains_out[...] = gains_acc[...]

    @pl.when(first)
    def _():
        x_remote.wait_send()

        @pl.loop(0, MB)
        def _(m):
            for cross in (0, 1):
                acts_copy(m, cross).wait_send()

    @pl.when(second)
    def _():
        for copy in w_attn + w_moe:
            copy.wait_send()

        @pl.loop(0, MB)
        def _(m):
            grad_copy(m).wait_send()

    @pl.loop(0, MB)
    def _(m):
        pairs = (
            (n2recv, n2rows_out),
            (hid, hid_out),
            (acts_s, acts_out),
            (dyrecv, dyrows_out),
            (gs, dgate_out),
            (us, dup_out),
            (da_pair, da_out),
            (ingrad_s, ingrad_out),
            (None, n1_out),
            (dqkv_all, dqkv_out),
            (att, att_out),
        )
        for i, (src, dst) in enumerate(pairs):
            src = n1s.at[m, :, own_half] if src is None else src.at[m]
            out_copy(i, src, dst.at[m], m).wait()


def run_sections(*operands):
    def out(*shape, dtype=BF):
        return jax.ShapeDtypeStruct(shape, dtype)

    vmem = pl.BlockSpec(memory_space=pltpu.VMEM)
    anywhere = pl.BlockSpec(memory_space=pl.ANY)
    dma = pltpu.SemaphoreType.DMA
    return pl.pallas_call(
        section_kernel,
        name="sections",
        out_shape=(
            out(MB, SEQ, WIDTH),
            out(MB, SEQ, WIDTH),
            out(8, WIDTH, dtype=F32),
            out(MB, ROWS, WIDTH),
            out(MB, ROWS, WIDTH),
            out(MB, ROWS, HIDDEN),
            out(MB, ROWS, HIDDEN),
            out(MB, ROWS, HIDDEN),
            out(MB, 2 * SEQ, HALF),
            out(MB, 2, 2 * SEQ, QKV),
            out(MB, 2 * SEQ, HALF),
            out(MB, 2 * SEQ, WIDTH),
        ),
        in_specs=[anywhere] * 9 + [vmem] * 7,
        out_specs=[anywhere] * 2 + [vmem] + [anywhere] * 9,
        scratch_shapes=[
            pltpu.VMEM((WIDTH, QKV), BF),
            pltpu.VMEM((HALF, WIDTH), BF),
            pltpu.VMEM((WIDTH, HIDDEN), BF),
            pltpu.VMEM((WIDTH, HIDDEN), BF),
            pltpu.VMEM((HIDDEN, WIDTH), BF),
            pltpu.VMEM((MB, 2 * SEQ, WIDTH), BF),
            pltpu.VMEM((MB, 2 * SEQ, WIDTH), BF),
            pltpu.VMEM((MB, 2 * SEQ, QKV), BF),
            pltpu.VMEM((MB, 2 * SEQ, HALF), BF),
            pltpu.VMEM((MB, SEQ, WIDTH), F32),
            pltpu.VMEM((SEQ, WIDTH), F32),
            pltpu.VMEM((MB, SEQ, WIDTH), BF),
            pltpu.VMEM((MB, SEQ, WIDTH), BF),
            pltpu.VMEM((MB, ROWS, SEQ), BF),
            pltpu.VMEM((MB, ROWS, SEQ), BF),
            pltpu.VMEM((MB, ROWS, SEQ), BF),
            pltpu.VMEM((MB, ROWS, WIDTH), BF),
            pltpu.VMEM((MB, ROWS, WIDTH), BF),
            pltpu.VMEM((MB, ROWS, WIDTH), BF),
            pltpu.VMEM((MB, ROWS, WIDTH), BF),
            pltpu.VMEM((MB, ROWS, WIDTH), BF),
            pltpu.VMEM((MB, ROWS, WIDTH), BF),
            pltpu.VMEM((MB, ROWS, HIDDEN), BF),
            pltpu.VMEM((MB, ROWS, HIDDEN), BF),
            pltpu.VMEM((MB, ROWS, HIDDEN), BF),
            pltpu.VMEM((MB, SEQ, WIDTH), BF),
            pltpu.VMEM((MB, SEQ, WIDTH), BF),
            pltpu.VMEM((MB, SEQ, WIDTH), F32),
            pltpu.VMEM((MB, 2 * SEQ, WIDTH), BF),
            pltpu.VMEM((MB, 2, 2 * SEQ, QKV), BF),
            pltpu.VMEM((MB, SEQ, WIDTH), BF),
            pltpu.VMEM((MB, SEQ, WIDTH), BF),
            pltpu.VMEM((MB, SEQ, WIDTH), BF),
            pltpu.VMEM((8, WIDTH), F32),
            dma((9,)),
            dma((7,)),
            dma((7,)),
            dma((4, MB)),
            dma((4, MB)),
            dma((4, MB)),
            dma((4, MB)),
            dma((2, MB)),
            dma((2, MB)),
            dma((MB,)),
            dma((MB,)),
            dma((11, MB)),
            pltpu.SemaphoreType.REGULAR,
        ],
        compiler_params=pltpu.CompilerParams(
            collective_id=0, has_side_effects=True, vmem_limit_bytes=62 * 2**20
        ),
    )(*operands)


CHUNK_ROWS = 48
CHUNK_COLS = 1792


def reduce_kernel(v_in, small_in, sum_out, small_out, parts, small, reduced, rs_sem, rr_sem, gs_sem, gr_sem, ss_sem, sr_sem, l_sem):
    e = lax.axis_index("expert")
    barrier = pltpu.get_barrier_semaphore()

    @pl.loop(1, EXPERTS)
    def _(d):
        pl.semaphore_signal(
            barrier, inc=1, device_id={"expert": lax.rem(e + d, EXPERTS)}, device_id_type=MESH
        )

    pl.semaphore_wait(barrier, EXPERTS - 1)

    def remote(src, dst, send, recv, p):
        return pltpu.make_async_remote_copy(
            src_ref=src,
            dst_ref=dst,
            send_sem=send,
            recv_sem=recv,
            device_id={"expert": p},
            device_id_type=MESH,
        )

    def all_but_one(ref, sem):
        part = ref.at[pl.ds(0, EXPERTS - 1)]
        pltpu.make_async_copy(part, part, sem).wait()

    own = pltpu.make_async_copy(v_in.at[e], parts.at[e], l_sem.at[0])
    own.start()

    @pl.loop(1, EXPERTS)
    def _(d):
        p = lax.rem(e + d, EXPERTS)
        remote(v_in.at[p], parts.at[e], rs_sem, rr_sem, p).start()

    @pl.loop(1, EXPERTS)
    def _(d):
        p = lax.rem(e + d, EXPERTS)
        remote(small_in, small.at[e], ss_sem, sr_sem, p).start()

    small[e] = small_in[...]
    own.wait()
    all_but_one(parts, rr_sem)
    for i in range(CHUNK_ROWS // 16):
        rows = pl.ds(i * 16, 16)
        total = lax.fori_loop(
            1,
            EXPERTS,
            lambda k, acc: acc + parts[k, rows].astype(F32),
            parts[0, rows].astype(F32),
        )
        reduced[rows] = total.astype(BF)

    own = pltpu.make_async_copy(reduced, sum_out.at[e], l_sem.at[1])
    own.start()

    @pl.loop(1, EXPERTS)
    def _(d):
        p = lax.rem(e + d, EXPERTS)
        remote(reduced, sum_out.at[e], gs_sem, gr_sem, p).start()

    all_but_one(small, sr_sem)
    small_out[...] = lax.fori_loop(
        1, EXPERTS, lambda k, acc: acc + small[k], small[0]
    )
    own.wait()
    all_but_one(parts, rs_sem)
    all_but_one(small, ss_sem)
    all_but_one(sum_out, gr_sem)
    all_but_one(sum_out, gs_sem)


def reduce_attention(v, small):
    vmem = pl.BlockSpec(memory_space=pltpu.VMEM)
    anywhere = pl.BlockSpec(memory_space=pl.ANY)
    dma = pltpu.SemaphoreType.DMA
    return pl.pallas_call(
        reduce_kernel,
        name="reduce_attention",
        out_shape=(
            jax.ShapeDtypeStruct(v.shape, BF),
            jax.ShapeDtypeStruct(small.shape, F32),
        ),
        in_specs=[anywhere, vmem],
        out_specs=[anywhere, vmem],
        scratch_shapes=[
            pltpu.VMEM((EXPERTS, CHUNK_ROWS, CHUNK_COLS), BF),
            pltpu.VMEM((EXPERTS,) + small.shape, F32),
            pltpu.VMEM((CHUNK_ROWS, CHUNK_COLS), BF),
            dma,
            dma,
            dma,
            dma,
            dma,
            dma,
            dma((2,)),
        ],
        compiler_params=pltpu.CompilerParams(
            collective_id=1, has_side_effects=True, vmem_limit_bytes=40 * 2**20
        ),
    )(v, small)


def swap(block):
    return lax.ppermute(block, "fsdp", [(0, 1), (1, 0)])


def local(
    inputs,
    cotangent,
    segments,
    expert_ids,
    gate_logits,
    w_query,
    key_projection,
    value_projection,
    w_out,
    gain_attn,
    gain_moe,
    w_gate,
    w_up,
    w_down,
):
    f = lax.axis_index("fsdp")
    pair_segments = jnp.swapaxes(lax.all_gather(segments, "fsdp"), 0, 1)
    gains = lax.all_gather(jnp.stack([gain_attn[0], gain_moe[0]]), "fsdp", axis=1, tiled=True)
    gains = gains.astype(F32)
    same = pair_segments[..., :, None] == pair_segments[..., None, :]
    row = lax.broadcasted_iota(jnp.int32, (SEQ, SEQ), 0)
    col = lax.broadcasted_iota(jnp.int32, (SEQ, SEQ), 1)
    places = jnp.sum((same & (col < row)).astype(F32), axis=-1)
    frequency = ROPE_BASE ** (-(jnp.arange(HEAD // 2, dtype=F32) * 2.0 / HEAD))
    angles = places[..., None] * frequency
    cosine, sine = jnp.cos(angles), jnp.sin(angles)
    cos_t = jnp.concatenate([cosine, cosine], axis=-1).reshape(MB, 2 * SEQ, HEAD)
    sin_t = jnp.concatenate([-sine, sine], axis=-1).reshape(MB, 2 * SEQ, HEAD)
    mask_t = (same & (col <= row)).astype(F32)
    (
        acts,
        in_grads,
        gain_parts,
        n2rows,
        dyrows,
        hid,
        dgate,
        dup,
        n1,
        dqkv,
        att,
        da,
    ) = run_sections(
        inputs,
        cotangent,
        w_query[0],
        key_projection[0],
        value_projection[0],
        w_out[0],
        w_gate[0, 0],
        w_up[0, 0],
        w_down[0, 0],
        gains[0:1],
        gains[1:2],
        jnp.swapaxes(expert_ids[0], 1, 2),
        jnp.swapaxes(gate_logits[0], 1, 2),
        cos_t,
        sin_t,
        mask_t,
    )
    n2rows = n2rows.reshape(MB * ROWS, WIDTH)
    dyrows = dyrows.reshape(MB * ROWS, WIDTH)
    hid = hid.reshape(MB * ROWS, HIDDEN)
    dgate = dgate.reshape(MB * ROWS, HIDDEN)
    dup = dup.reshape(MB * ROWS, HIDDEN)

    def pair_sum(left, right, size):
        theirs = lax.dynamic_slice_in_dim(left, (1 - f) * size, size, 1)
        mine = lax.dynamic_slice_in_dim(left, f * size, size, 1)
        arrived = swap(dot_tn(theirs, right).astype(BF))
        return dot_tn(mine, right) + arrived.astype(F32)

    grad_gate = pair_sum(n2rows, dgate, HALF)
    grad_up = pair_sum(n2rows, dup, HALF)
    grad_down = pair_sum(hid, dyrows, HIDDEN // 2)

    n1 = n1.reshape(MB * 2 * SEQ, HALF)
    dqkv = jnp.swapaxes(dqkv, 1, 2).reshape(MB * 2 * SEQ, 2, QKV)
    dq = dqkv[:, :, :HALF].reshape(MB * 2 * SEQ, WIDTH)
    dk = dqkv[:, :, HALF : HALF + HEAD].reshape(MB * 2 * SEQ, 2 * HEAD)
    dv = dqkv[:, :, HALF + HEAD :].reshape(MB * 2 * SEQ, 2 * HEAD)
    v_first = dot_tn(n1, jnp.concatenate([dq, dk], axis=1)).astype(BF)
    gv = dot_tn(n1, dv).astype(BF)
    go = dot_tn(att.reshape(MB * 2 * SEQ, HALF), da.reshape(MB * 2 * SEQ, WIDTH)).astype(BF)
    v_all = jnp.concatenate([v_first, jnp.concatenate([gv, go], axis=1)], axis=0)
    theirs = lax.dynamic_slice_in_dim(gain_parts[:2], (1 - f) * HALF, HALF, 1)
    mine = lax.dynamic_slice_in_dim(gain_parts[:2], f * HALF, HALF, 1)
    small = (mine + swap(theirs)).reshape(12, HEAD)
    small = jnp.concatenate([small, jnp.zeros((4, HEAD), F32)], axis=0)
    total, small = reduce_attention(v_all.reshape(EXPERTS, CHUNK_ROWS, CHUNK_COLS), small)
    total = total.reshape(2 * HALF, CHUNK_COLS).astype(F32)
    small = small[:12].reshape(2, HALF)
    return (
        acts[None],
        in_grads[None],
        total[None, :HALF, :WIDTH],
        total[None, :HALF, WIDTH:],
        total[None, HALF:, : 2 * HEAD],
        total[None, HALF:, 2 * HEAD :],
        small[0][None],
        small[1][None],
        grad_gate[None, None],
        grad_up[None, None],
        grad_down[None, None],
    )


def solution(mesh):
    return jax.shard_map(
        local,
        mesh=mesh,
        in_specs=(
            P(None, ("fsdp", "expert"), None),
            P(None, ("fsdp", "expert"), None),
            P(None, ("fsdp", "expert")),
            P("section", None, ("fsdp", "expert"), None),
            P("section", None, ("fsdp", "expert"), None),
            P("section", "fsdp", None),
            P("section", "fsdp", None),
            P("section", "fsdp", None),
            P("section", "fsdp", None),
            P("section", "fsdp"),
            P("section", "fsdp"),
            P("section", "expert", "fsdp", None),
            P("section", "expert", "fsdp", None),
            P("section", "expert", "fsdp", None),
        ),
        out_specs=(
            P("section", None, ("fsdp", "expert"), None),
            P("section", None, ("fsdp", "expert"), None),
            P("section", "fsdp", None),
            P("section", "fsdp", None),
            P("section", "fsdp", None),
            P("section", "fsdp", None),
            P("section", "fsdp"),
            P("section", "fsdp"),
            P("section", "expert", "fsdp", None),
            P("section", "expert", "fsdp", None),
            P("section", "expert", "fsdp", None),
        ),
        check_vma=False,
    )
```

```python
import functools

import jax
import jax.numpy as jnp
from jax import lax
from jax.experimental import pallas as pl
from jax.experimental.pallas import tpu as pltpu
from jax.sharding import PartitionSpec as P

MESH = pl.DeviceIdType.MESH
BF = jnp.bfloat16
F32 = jnp.float32

HEAD = 128
EPS = 1e-06
ROPE_BASE = 1000000.0
GELU_C = 0.7978845608
GELU_A = 0.044715

MB = 2
SEQ = 96
WIDTH = 1536
HALF = 768
EXPERTS = 32
SLOTS = 16
ROWS = EXPERTS * SLOTS
HIDDEN = 768
HEADS = 6
QKV = 1024


def dot(a, b):
    return jnp.dot(a, b, preferred_element_type=F32)


def dot_nt(a, b):
    return lax.dot_general(a, b, (((1,), (1,)), ((), ())), preferred_element_type=F32)


def dot_tn(a, b):
    return lax.dot_general(a, b, (((0,), (0,)), ((), ())), preferred_element_type=F32)


def aligned(start, size, unit):
    return pl.ds(pl.multiple_of(start, unit), size)


def inverse_rms(rows):
    return lax.rsqrt(jnp.mean(rows * rows, axis=-1, keepdims=True) + EPS)


def rms_back(rows, inverse, gain, grad):
    scaled = gain * grad
    return inverse * scaled - rows * (inverse * inverse * inverse) * jnp.mean(
        scaled * rows, axis=-1, keepdims=True
    )


def rotate(head, cos, sin):
    return head * cos + pltpu.roll(head, HEAD // 2, 1) * sin


def section_kernel(
    x_in,
    ct_in,
    wq_in,
    wk_in,
    wv_in,
    wo_in,
    wg_in,
    wu_in,
    wd_in,
    gain_one,
    gain_two,
    ids_t,
    logits_t,
    cos_t,
    sin_t,
    mask_t,
    acts_out,
    ingrad_out,
    gains_out,
    n2rows_out,
    dyrows_out,
    hid_out,
    dgate_out,
    dup_out,
    n1_out,
    dqkv_out,
    att_out,
    da_out,
    wqkv,
    wo,
    wg,
    wu,
    wd,
    xpair,
    n1s,
    qkvs,
    att,
    hid_one,
    part_own,
    part_send,
    part_recv,
    sel,
    cg_hi,
    cg_lo,
    dsend,
    bsend,
    n2recv,
    yrecv,
    dyrecv,
    dn2recv,
    gs,
    us,
    hid,
    acts_s,
    g_buf,
    dh_s,
    da_pair,
    dqkv_all,
    dn1_send,
    dn1_recv,
    ingrad_s,
    gains_acc,
    lw_sem,
    ws_sem,
    wr_sem,
    as_sem,
    ar_sem,
    ps_sem,
    pr_sem,
    xs_sem,
    xr_sem,
    gs_sem,
    gr_sem,
    out_sem,
    go_sem,
):
    sec = lax.axis_index("section")
    f = lax.axis_index("fsdp")
    e = lax.axis_index("expert")
    other = 1 - f
    own_rows = aligned(f * SEQ, SEQ, 16)
    other_rows = aligned(other * SEQ, SEQ, 16)
    own_half = aligned(f * HALF, HALF, 128)
    other_half = aligned(other * HALF, HALF, 128)
    my_slots = aligned(e * SLOTS, SLOTS, 16)
    partner = {"fsdp": other}
    first, second = sec == 0, sec == 1

    barrier = pltpu.get_barrier_semaphore()

    @pl.loop(1, EXPERTS)
    def _(d):
        pl.semaphore_signal(
            barrier, inc=1, device_id={"expert": lax.rem(e + d, EXPERTS)}, device_id_type=MESH
        )

    for place in ({"fsdp": other}, {"section": 1 - sec}, {"section": 1 - sec, "fsdp": other}):
        pl.semaphore_signal(barrier, inc=1, device_id=place, device_id_type=MESH)

    local = [
        (wq_in.at[:, own_half], wqkv.at[own_half, pl.ds(0, HALF)]),
        (wk_in.at[:, aligned(f * HEAD, HEAD, 128)], wqkv.at[own_half, pl.ds(HALF, HEAD)]),
        (wv_in.at[:, aligned(f * HEAD, HEAD, 128)], wqkv.at[own_half, pl.ds(HALF + HEAD, HEAD)]),
        (wo_in, wo),
        (wg_in, wg.at[own_half]),
        (wu_in, wu.at[own_half]),
        (wd_in, wd.at[aligned(f * (HIDDEN // 2), HIDDEN // 2, 16)]),
    ]
    local = [pltpu.make_async_copy(a, b, lw_sem.at[i]) for i, (a, b) in enumerate(local)]
    for copy in local:
        copy.start()
    x_local = pltpu.make_async_copy(x_in, xpair.at[:, own_rows], lw_sem.at[7])
    ct_local = pltpu.make_async_copy(ct_in, g_buf, lw_sem.at[8])
    pl.when(first)(x_local.start)
    pl.when(second)(ct_local.start)

    def remote(src, dst, i):
        return pltpu.make_async_remote_copy(
            src_ref=src,
            dst_ref=dst,
            send_sem=ws_sem.at[i],
            recv_sem=wr_sem.at[i],
            device_id=partner,
            device_id_type=MESH,
        )

    w_attn = [
        remote(wq_in.at[:, other_half], wqkv.at[own_half, pl.ds(0, HALF)], 0),
        remote(
            wk_in.at[:, aligned(other * HEAD, HEAD, 128)],
            wqkv.at[own_half, pl.ds(HALF, HEAD)],
            1,
        ),
        remote(
            wv_in.at[:, aligned(other * HEAD, HEAD, 128)],
            wqkv.at[own_half, pl.ds(HALF + HEAD, HEAD)],
            2,
        ),
    ]
    w_moe = [
        remote(wg_in, wg.at[own_half], 3),
        remote(wu_in, wu.at[own_half], 4),
        remote(wd_in, wd.at[aligned(f * (HIDDEN // 2), HIDDEN // 2, 16)], 5),
    ]
    x_remote = remote(x_in, xpair.at[:, own_rows], 6)

    pl.semaphore_wait(barrier, EXPERTS - 1 + 3)

    @pl.when(first)
    def _():
        x_remote.start()
        for copy in w_attn + w_moe:
            copy.start()

    gains_acc[...] = jnp.zeros_like(gains_acc)

    @pl.loop(0, MB)
    def _(m):
        ids = ids_t[m]
        logits = logits_t[m]
        raised = jnp.exp(logits - jnp.max(logits, axis=0, keepdims=True))
        gates = raised / jnp.sum(raised, axis=0, keepdims=True)
        expert = lax.broadcasted_iota(jnp.int32, (EXPERTS, SEQ), 0)
        named = jnp.zeros((EXPERTS, SEQ), F32)
        weight = jnp.zeros((EXPERTS, SEQ), F32)
        for k in range(4):
            hit = expert == ids[k : k + 1, :]
            named = jnp.where(hit, 1.0, named)
            weight = jnp.where(hit, gates[k : k + 1, :], weight)
        earlier = lax.broadcasted_iota(jnp.int32, (SEQ, SEQ), 0) < lax.broadcasted_iota(
            jnp.int32, (SEQ, SEQ), 1
        )
        slot = dot(named.astype(BF), jnp.where(earlier, 1.0, 0.0).astype(BF))
        slot = jnp.where(named > 0.0, slot, -1.0)
        place = lax.broadcasted_iota(jnp.int32, (EXPERTS, SLOTS, SEQ), 1).astype(F32)
        chosen = jnp.where(
            jnp.broadcast_to(slot[:, None, :], (EXPERTS, SLOTS, SEQ)) == place, 1.0, 0.0
        )
        scaled = chosen * jnp.broadcast_to(weight[:, None, :], (EXPERTS, SLOTS, SEQ))
        scaled = scaled.reshape(ROWS, SEQ)
        high = scaled.astype(BF)
        sel[m] = chosen.reshape(ROWS, SEQ).astype(BF)
        cg_hi[m] = high
        cg_lo[m] = (scaled - high.astype(F32)).astype(BF)

    def exchange(kind, m, src, dst):
        @pl.loop(1, EXPERTS)
        def _(d):
            p = lax.rem(e + d, EXPERTS)
            pltpu.make_async_remote_copy(
                src_ref=src.at[m, aligned(p * SLOTS, SLOTS, 16)],
                dst_ref=dst.at[m, my_slots],
                send_sem=as_sem.at[kind, m],
                recv_sem=ar_sem.at[kind, m],
                device_id={"expert": p},
                device_id_type=MESH,
            ).start()

        dst[m, my_slots] = src[m, my_slots]

    def received(kind, m, dst):
        whole = dst.at[m, pl.ds(0, ROWS - SLOTS)]
        pltpu.make_async_copy(whole, whole, ar_sem.at[kind, m]).wait()

    def sent(kind, m, src):
        whole = src.at[m, pl.ds(0, ROWS - SLOTS)]
        pltpu.make_async_copy(whole, whole, as_sem.at[kind, m]).wait()

    def to_partner(kind, m, src, dst):
        return pltpu.make_async_remote_copy(
            src_ref=src,
            dst_ref=dst,
            send_sem=ps_sem.at[kind, m],
            recv_sem=pr_sem.at[kind, m],
            device_id=partner,
            device_id_type=MESH,
        )

    def acts_copy(m, cross):
        return pltpu.make_async_remote_copy(
            src_ref=acts_s.at[m],
            dst_ref=xpair.at[m, own_rows],
            send_sem=xs_sem.at[cross, m],
            recv_sem=xr_sem.at[f, m],
            device_id={"section": 1, "fsdp": other} if cross else {"section": 1},
            device_id_type=MESH,
        )

    def acts_arrived(m):
        for at, rows in ((f, own_rows), (other, other_rows)):
            place = xpair.at[m, rows]
            pltpu.make_async_copy(place, place, xr_sem.at[at, m]).wait()

    def grad_copy(m):
        return pltpu.make_async_remote_copy(
            src_ref=ingrad_s.at[m],
            dst_ref=g_buf.at[m],
            send_sem=gs_sem.at[m],
            recv_sem=gr_sem.at[m],
            device_id={"section": 0},
            device_id_type=MESH,
        )

    def out_copy(i, src, dst, m):
        return pltpu.make_async_copy(src, dst, out_sem.at[i, m])

    def send_dy(m):
        gate = jnp.sum(cg_hi[m].astype(F32) + cg_lo[m].astype(F32), axis=1, keepdims=True)

        @pl.loop(0, WIDTH // 512)
        def _(j):
            cols = aligned(j * 512, 512, 128)
            bsend[m, :, cols] = (dot(sel[m], g_buf[m, :, cols]) * gate).astype(BF)

        exchange(2, m, bsend, dyrecv)

    @pl.when(second)
    def _():
        ct_local.wait()
        pl.semaphore_wait(go_sem, 1)
        for copy in w_attn:
            copy.start()
        pl.loop(0, MB)(send_dy)
        for copy in w_moe:
            copy.start()

    @pl.when(first)
    def _():
        x_local.wait()
        x_remote.wait_recv()

    for copy in local[:4]:
        copy.wait()
    for copy in w_attn:
        copy.wait_recv()

    def heads_of(ref, m, rows):
        return jnp.concatenate(
            [ref[m, rows, pl.ds(h * HEAD, HEAD)] for h in range(HEADS)], axis=0
        )

    def softmax_of(m, s, queries, keys):
        scores = dot_nt(queries, keys) * HEAD ** (-0.5)
        allowed = jnp.concatenate([mask_t[m, s]] * HEADS, axis=0)
        scores = jnp.where(allowed > 0.0, scores, -1e30)
        raised = jnp.exp(scores - jnp.max(scores, axis=-1, keepdims=True))
        return raised / jnp.sum(raised, axis=-1, keepdims=True)

    def attend(m):
        rows = xpair[m].astype(F32)
        n1s[m] = (rows * inverse_rms(rows) * gain_one[...]).astype(BF)
        cos, sin = cos_t[m], sin_t[m]
        for j in range(4):
            block = dot(n1s[m], wqkv[:, pl.ds(j * 256, 256)])
            qkvs[m, :, pl.ds(j * 256, HEAD)] = rotate(block[:, :HEAD], cos, sin).astype(BF)
            late = block[:, HEAD:]
            if j < 3:
                late = rotate(late, cos, sin)
            qkvs[m, :, pl.ds(j * 256 + HEAD, HEAD)] = late.astype(BF)

        @pl.loop(0, 2)
        def _(s):
            at = aligned(s * SEQ, SEQ, 16)
            queries = heads_of(qkvs, m, at)
            keys = qkvs[m, at, pl.ds(HALF, HEAD)]
            values = qkvs[m, at, pl.ds(HALF + HEAD, HEAD)]
            probs = softmax_of(m, s, queries, keys).astype(BF)
            mixed = dot(probs, values).astype(BF)
            for h in range(HEADS):
                att[m, at, pl.ds(h * HEAD, HEAD)] = mixed[h * SEQ : (h + 1) * SEQ]

        @pl.loop(0, WIDTH // 512)
        def _(j):
            cols = aligned(j * 512, 512, 128)
            block = dot(att[m], wo[:, cols])
            top, low = block[:SEQ], block[SEQ:]
            mine = f == 0
            hid_one[m, :, cols] = jnp.where(mine, top, low)
            part_send[m, :, cols] = jnp.where(mine, low, top).astype(BF)

        to_partner(0, m, part_send.at[m], part_recv.at[m]).start()

    def dispatch(m):
        to_partner(0, m, part_send.at[m], part_recv.at[m]).wait_recv()
        rows = xpair[m, own_rows].astype(F32) + (hid_one[m] + part_recv[m].astype(F32))
        hid_one[m] = rows
        n2 = (rows * inverse_rms(rows) * gain_two[...]).astype(BF)
        dsend[m] = dot(sel[m], n2).astype(BF)
        exchange(0, m, dsend, n2recv)

    def forward(m):
        pl.when(second)(lambda: acts_arrived(m))
        attend(m)
        dispatch(m)

    pl.loop(0, MB)(forward)

    for copy in local[4:]:
        copy.wait()
    for copy in w_moe:
        copy.wait_recv()

    @pl.when(first)
    def _():
        for copy in w_attn + w_moe:
            copy.wait_send()
        pl.semaphore_signal(go_sem, inc=1, device_id={"section": 1}, device_id_type=MESH)

    def experts(m):
        received(0, m, n2recv)
        out_copy(0, n2recv.at[m], n2rows_out.at[m], m).start()

        @pl.loop(0, HIDDEN // 256)
        def _(j):
            cols = aligned(j * 256, 256, 128)
            gate = dot(n2recv[m], wg[:, cols])
            up = dot(n2recv[m], wu[:, cols])
            bend = jnp.tanh(GELU_C * (gate + GELU_A * gate * gate * gate))
            gs[m, :, cols] = gate.astype(BF)
            us[m, :, cols] = up.astype(BF)
            hid[m, :, cols] = (0.5 * gate * (1.0 + bend) * up).astype(BF)

        out_copy(1, hid.at[m], hid_out.at[m], m).start()
        pl.when(second)(lambda: sent(2, m, bsend))

        @pl.loop(0, WIDTH // 512)
        def _(j):
            cols = aligned(j * 512, 512, 128)
            bsend[m, :, cols] = dot(hid[m], wd[:, cols]).astype(BF)

        exchange(1, m, bsend, yrecv)

    pl.loop(0, MB)(experts)

    def combine(m):
        received(1, m, yrecv)

        @pl.loop(0, WIDTH // 512)
        def _(j):
            cols = aligned(j * 512, 512, 128)
            block = yrecv[m, :, cols]
            mixed = dot_tn(cg_hi[m], block) + dot_tn(cg_lo[m], block)
            acts_s[m, :, cols] = (hid_one[m, :, cols] + mixed).astype(BF)

        out_copy(2, acts_s.at[m], acts_out.at[m], m).start()

    @pl.when(first)
    def _():
        @pl.loop(0, MB)
        def _(m):
            combine(m)
            for cross in (0, 1):
                acts_copy(m, cross).start()

        @pl.loop(0, MB)
        def _(m):
            sent(1, m, bsend)
            place = g_buf.at[m]
            pltpu.make_async_copy(place, place, gr_sem.at[m]).wait()
            send_dy(m)

    def experts_back(m):
        received(2, m, dyrecv)
        out_copy(3, dyrecv.at[m], dyrows_out.at[m], m).start()

        @pl.loop(0, HIDDEN // 256)
        def _(j):
            cols = aligned(j * 256, 256, 128)
            dhid = dot_nt(dyrecv[m], wd[cols, :])
            gate = gs[m, :, cols].astype(F32)
            up = us[m, :, cols].astype(F32)
            square = gate * gate
            bend = jnp.tanh(GELU_C * (gate + GELU_A * square * gate))
            half = 0.5 * (1.0 + bend)
            slope = half + 0.5 * gate * (1.0 - bend * bend) * (
                GELU_C * (1.0 + 3.0 * GELU_A * square)
            )
            gs[m, :, cols] = (dhid * up * slope).astype(BF)
            us[m, :, cols] = (dhid * (gate * half)).astype(BF)

        out_copy(4, gs.at[m], dgate_out.at[m], m).start()
        out_copy(5, us.at[m], dup_out.at[m], m).start()
        pl.when(first)(lambda: sent(2, m, bsend))
        pl.when(second)(lambda: sent(1, m, bsend))

        @pl.loop(0, WIDTH // 512)
        def _(j):
            cols = aligned(j * 512, 512, 128)
            block = dot_nt(gs[m], wg[cols, :]) + dot_nt(us[m], wu[cols, :])
            bsend[m, :, cols] = block.astype(BF)

        exchange(3, m, bsend, dn2recv)

    pl.loop(0, MB)(experts_back)

    def attend_back(m):
        received(3, m, dn2recv)
        rows = hid_one[m]
        inverse = inverse_rms(rows)

        @pl.loop(0, WIDTH // 512)
        def _(j):
            cols = aligned(j * 512, 512, 128)
            dh_s[m, :, cols] = dot_tn(sel[m], dn2recv[m, :, cols])

        grad = dh_s[m]
        gains_acc[1:2] += jnp.sum(grad * rows * inverse, axis=0, keepdims=True)
        total = g_buf[m].astype(F32) + rms_back(rows, inverse, gain_two[...], grad)
        dh_s[m] = total
        da_pair[m, own_rows] = total.astype(BF)
        da_copy = to_partner(1, m, da_pair.at[m, own_rows], da_pair.at[m, own_rows])
        da_copy.start()
        da_copy.wait_recv()
        out_copy(6, da_pair.at[m], da_out.at[m], m).start()

        @pl.loop(0, 2)
        def _(s):
            at = aligned(s * SEQ, SEQ, 16)
            dmix = dot_nt(da_pair[m, at], wo[...]).astype(BF)
            dmix = jnp.concatenate(
                [dmix[:, h * HEAD : (h + 1) * HEAD] for h in range(HEADS)], axis=0
            )
            queries = heads_of(qkvs, m, at)
            keys = qkvs[m, at, pl.ds(HALF, HEAD)]
            values = qkvs[m, at, pl.ds(HALF + HEAD, HEAD)]
            probs = softmax_of(m, s, queries, keys)
            dprobs = dot_nt(dmix, values)
            dvalues = dot_tn(probs.astype(BF), dmix)
            dscores = probs * (dprobs - jnp.sum(dprobs * probs, axis=-1, keepdims=True))
            dscores = (dscores * HEAD ** (-0.5)).astype(BF)
            cos = cos_t[m, at]
            sin = -sin_t[m, at]
            dkeys = rotate(dot_tn(dscores, queries), cos, sin)
            dqueries = dot(dscores, keys)
            for h in range(HEADS):
                part = rotate(dqueries[h * SEQ : (h + 1) * SEQ], cos, sin)
                dqkv_all[m, f, at, pl.ds(h * HEAD, HEAD)] = part.astype(BF)
            dqkv_all[m, f, at, pl.ds(HALF, HEAD)] = dkeys.astype(BF)
            dqkv_all[m, f, at, pl.ds(HALF + HEAD, HEAD)] = dvalues.astype(BF)

        dqkv_copy = to_partner(3, m, dqkv_all.at[m, f], dqkv_all.at[m, f])
        dqkv_copy.start()

        @pl.loop(0, WIDTH // 512)
        def _(j):
            cols = aligned(j * 512, 512, 128)
            block = dot_nt(dqkv_all[m, f], wqkv[cols, :])
            top, low = block[:SEQ], block[SEQ:]
            mine = f == 0
            part_own[:, cols] = jnp.where(mine, top, low)
            dn1_send[m, :, cols] = jnp.where(mine, low, top).astype(BF)

        dn1_copy = to_partner(2, m, dn1_send.at[m], dn1_recv.at[m])
        dn1_copy.start()
        dn1_copy.wait_recv()
        grad = part_own[...] + dn1_recv[m].astype(F32)
        rows = xpair[m, own_rows].astype(F32)
        inverse = inverse_rms(rows)
        gains_acc[0:1] += jnp.sum(grad * rows * inverse, axis=0, keepdims=True)
        ingrad_s[m] = (dh_s[m] + rms_back(rows, inverse, gain_one[...], grad)).astype(BF)
        out_copy(7, ingrad_s.at[m], ingrad_out.at[m], m).start()
        pl.when(second)(grad_copy(m).start)

    pl.loop(0, MB)(attend_back)

    pl.when(second)(lambda: pl.loop(0, MB)(combine))

    @pl.loop(0, MB)
    def _(m):
        to_partner(3, m, dqkv_all.at[m, f], dqkv_all.at[m, f]).wait_recv()
        out_copy(8, n1s.at[m, :, own_half], n1_out.at[m], m).start()
        out_copy(9, dqkv_all.at[m], dqkv_out.at[m], m).start()
        out_copy(10, att.at[m], att_out.at[m], m).start()
        sent(0, m, dsend)
        sent(3, m, bsend)
        to_partner(0, m, part_send.at[m], part_recv.at[m]).wait_send()
        to_partner(1, m, da_pair.at[m, own_rows], da_pair.at[m, own_rows]).wait_send()
        to_partner(2, m, dn1_send.at[m], dn1_recv.at[m]).wait_send()
        to_partner(3, m, dqkv_all.at[m, f], dqkv_all.at[m, f]).wait_send()

    gains_out[...] = gains_acc[...]

    @pl.when(first)
    def _():
        x_remote.wait_send()

        @pl.loop(0, MB)
        def _(m):
            for cross in (0, 1):
                acts_copy(m, cross).wait_send()

    @pl.when(second)
    def _():
        for copy in w_attn + w_moe:
            copy.wait_send()

        @pl.loop(0, MB)
        def _(m):
            grad_copy(m).wait_send()

    @pl.loop(0, MB)
    def _(m):
        pairs = (
            (n2recv, n2rows_out),
            (hid, hid_out),
            (acts_s, acts_out),
            (dyrecv, dyrows_out),
            (gs, dgate_out),
            (us, dup_out),
            (da_pair, da_out),
            (ingrad_s, ingrad_out),
            (None, n1_out),
            (dqkv_all, dqkv_out),
            (att, att_out),
        )
        for i, (src, dst) in enumerate(pairs):
            src = n1s.at[m, :, own_half] if src is None else src.at[m]
            out_copy(i, src, dst.at[m], m).wait()


def run_sections(*operands):
    def out(*shape, dtype=BF):
        return jax.ShapeDtypeStruct(shape, dtype)

    vmem = pl.BlockSpec(memory_space=pltpu.VMEM)
    anywhere = pl.BlockSpec(memory_space=pl.ANY)
    dma = pltpu.SemaphoreType.DMA
    return pl.pallas_call(
        section_kernel,
        name="sections",
        out_shape=(
            out(MB, SEQ, WIDTH),
            out(MB, SEQ, WIDTH),
            out(8, WIDTH, dtype=F32),
            out(MB, ROWS, WIDTH),
            out(MB, ROWS, WIDTH),
            out(MB, ROWS, HIDDEN),
            out(MB, ROWS, HIDDEN),
            out(MB, ROWS, HIDDEN),
            out(MB, 2 * SEQ, HALF),
            out(MB, 2, 2 * SEQ, QKV),
            out(MB, 2 * SEQ, HALF),
            out(MB, 2 * SEQ, WIDTH),
        ),
        in_specs=[anywhere] * 9 + [vmem] * 7,
        out_specs=[anywhere] * 2 + [vmem] + [anywhere] * 9,
        scratch_shapes=[
            pltpu.VMEM((WIDTH, QKV), BF),
            pltpu.VMEM((HALF, WIDTH), BF),
            pltpu.VMEM((WIDTH, HIDDEN), BF),
            pltpu.VMEM((WIDTH, HIDDEN), BF),
            pltpu.VMEM((HIDDEN, WIDTH), BF),
            pltpu.VMEM((MB, 2 * SEQ, WIDTH), BF),
            pltpu.VMEM((MB, 2 * SEQ, WIDTH), BF),
            pltpu.VMEM((MB, 2 * SEQ, QKV), BF),
            pltpu.VMEM((MB, 2 * SEQ, HALF), BF),
            pltpu.VMEM((MB, SEQ, WIDTH), F32),
            pltpu.VMEM((SEQ, WIDTH), F32),
            pltpu.VMEM((MB, SEQ, WIDTH), BF),
            pltpu.VMEM((MB, SEQ, WIDTH), BF),
            pltpu.VMEM((MB, ROWS, SEQ), BF),
            pltpu.VMEM((MB, ROWS, SEQ), BF),
            pltpu.VMEM((MB, ROWS, SEQ), BF),
            pltpu.VMEM((MB, ROWS, WIDTH), BF),
            pltpu.VMEM((MB, ROWS, WIDTH), BF),
            pltpu.VMEM((MB, ROWS, WIDTH), BF),
            pltpu.VMEM((MB, ROWS, WIDTH), BF),
            pltpu.VMEM((MB, ROWS, WIDTH), BF),
            pltpu.VMEM((MB, ROWS, WIDTH), BF),
            pltpu.VMEM((MB, ROWS, HIDDEN), BF),
            pltpu.VMEM((MB, ROWS, HIDDEN), BF),
            pltpu.VMEM((MB, ROWS, HIDDEN), BF),
            pltpu.VMEM((MB, SEQ, WIDTH), BF),
            pltpu.VMEM((MB, SEQ, WIDTH), BF),
            pltpu.VMEM((MB, SEQ, WIDTH), F32),
            pltpu.VMEM((MB, 2 * SEQ, WIDTH), BF),
            pltpu.VMEM((MB, 2, 2 * SEQ, QKV), BF),
            pltpu.VMEM((MB, SEQ, WIDTH), BF),
            pltpu.VMEM((MB, SEQ, WIDTH), BF),
            pltpu.VMEM((MB, SEQ, WIDTH), BF),
            pltpu.VMEM((8, WIDTH), F32),
            dma((9,)),
            dma((7,)),
            dma((7,)),
            dma((4, MB)),
            dma((4, MB)),
            dma((4, MB)),
            dma((4, MB)),
            dma((2, MB)),
            dma((2, MB)),
            dma((MB,)),
            dma((MB,)),
            dma((11, MB)),
            pltpu.SemaphoreType.REGULAR,
        ],
        compiler_params=pltpu.CompilerParams(
            collective_id=0, has_side_effects=True, vmem_limit_bytes=62 * 2**20
        ),
    )(*operands)


BAND = 192
SLICE = 48
WIDE = 1792
NARROW = 896


def grads_kernel(
    n2_in,
    dy_in,
    hid_in,
    dgate_in,
    dup_in,
    n1_in,
    dqkv_in,
    att_in,
    da_in,
    gains_in,
    q_out,
    k_out,
    v_out,
    o_out,
    gate_out,
    up_out,
    down_out,
    gains_out,
    n2,
    dy,
    hid,
    dgate,
    dup,
    n1,
    dqkv,
    att,
    da,
    v_a,
    v_b,
    r1_a,
    r1_b,
    s1_a,
    s1_b,
    r2_a,
    r2_b,
    s2_a,
    s2_b,
    r3_a,
    r3_b,
    g_a,
    g_b,
    their_gate,
    their_up,
    their_down,
    part_gate,
    part_up,
    part_down,
    own_gate,
    own_up,
    own_down,
    small,
    small_recv,
    load_sem,
    send_sem,
    recv_sem,
    pair_send,
    pair_recv,
    small_send,
    small_recv_sem,
    out_sem,
):
    f = lax.axis_index("fsdp")
    e = lax.axis_index("expert")
    y, x, z = e // 8, lax.rem(e // 4, 2), lax.rem(e, 4)
    other = 1 - f
    own_half = aligned(f * HALF, HALF, 128)
    other_half = aligned(other * HALF, HALF, 128)
    own_quarter = aligned(f * (HIDDEN // 2), HIDDEN // 2, 128)
    other_quarter = aligned(other * (HIDDEN // 2), HIDDEN // 2, 128)

    def along_y(d):
        return {"expert": lax.rem(y + d, 4) * 8 + x * 4 + z}

    def along_z(d):
        return {"expert": y * 8 + x * 4 + lax.rem(z + d, 4)}

    twin = {"expert": y * 8 + (1 - x) * 4 + z}
    partner = {"fsdp": other}

    barrier = pltpu.get_barrier_semaphore()
    neighbours = [along_y(d) for d in (1, 2, 3)] + [along_z(d) for d in (1, 2, 3)]
    neighbours += [twin, partner]
    for place in neighbours:
        pl.semaphore_signal(barrier, inc=1, device_id=place, device_id_type=MESH)

    loads = [
        (att_in, att),
        (da_in, da),
        (n1_in, n1),
        (dqkv_in, dqkv),
        (n2_in, n2),
        (dgate_in, dgate),
        (dup_in, dup),
        (hid_in, hid),
        (dy_in, dy),
    ]
    loads = [pltpu.make_async_copy(a, b, load_sem.at[i]) for i, (a, b) in enumerate(loads)]
    for copy in loads:
        copy.start()

    def remote(src, dst, send, recv, place):
        return pltpu.make_async_remote_copy(
            src_ref=src,
            dst_ref=dst,
            send_sem=send,
            recv_sem=recv,
            device_id=place,
            device_id_type=MESH,
        )

    def wait_for(ref, sem):
        pltpu.make_async_copy(ref, ref, sem).wait()

    for copy in loads[:2]:
        copy.wait()

    @pl.loop(0, WIDTH // 512)
    def _(j):
        cols = aligned(j * 512, 512, 128)
        v_b[:, cols] = dot_tn(att[...], da[:, cols]).astype(BF)

    for copy in loads[2:4]:
        copy.wait()

    def over_micro(cols):
        block = jnp.concatenate([dqkv[m, :, :, cols] for m in range(MB)], axis=1)
        return [dot_tn(n1[...], block[g]).astype(BF) for g in range(2)]

    for g, block in enumerate(over_micro(pl.ds(HALF + HEAD, HEAD))):
        v_b[:, pl.ds(WIDTH + g * HEAD, HEAD)] = block
    pl.semaphore_wait(barrier, len(neighbours))

    lanes = (
        (0, v_a, r1_a, s1_a, r2_a, s2_a, r3_a, g_a, along_y, y, along_z, z),
        (1, v_b, r1_b, s1_b, r2_b, s2_b, r3_b, g_b, along_z, z, along_y, y),
    )

    def spread_one(lane):
        i, v, r1, _, _, _, _, _, axis, at, _, _ = lane
        for d in (1, 2, 3):
            rows = aligned(lax.rem(at + d, 4) * BAND, BAND, 16)
            remote(v.at[rows], r1.at[at], send_sem.at[i, 0], recv_sem.at[i, 0], axis(d)).start()

    spread_one(lanes[1])
    for j in range(3):
        for g, block in enumerate(over_micro(pl.ds(j * 256, 256))):
            v_a[:, pl.ds(g * HALF + j * 256, 256)] = block
    for g, block in enumerate(over_micro(pl.ds(HALF, HEAD))):
        v_a[:, pl.ds(WIDTH + g * HEAD, HEAD)] = block
    spread_one(lanes[0])

    small[...] = gains_in[...]
    small_pair = remote(
        small.at[:, other_half],
        small_recv.at[0],
        small_send.at[0],
        small_recv_sem.at[0],
        partner,
    )
    small_pair.start()

    for copy in loads[4:6]:
        copy.wait()
    their_gate[...] = dot_tn(n2[:, other_half], dgate[...]).astype(BF)
    pair = [remote(their_gate, part_gate, pair_send.at[0], pair_recv.at[0], partner)]
    pair[0].start()
    loads[6].wait()
    their_up[...] = dot_tn(n2[:, other_half], dup[...]).astype(BF)
    pair.append(remote(their_up, part_up, pair_send.at[1], pair_recv.at[1], partner))
    pair[1].start()
    for copy in loads[7:]:
        copy.wait()
    their_down[...] = dot_tn(hid[:, other_quarter], dy[...]).astype(BF)
    pair.append(remote(their_down, part_down, pair_send.at[2], pair_recv.at[2], partner))
    pair[2].start()
    own_gate[...] = dot_tn(n2[:, own_half], dgate[...])
    own_up[...] = dot_tn(n2[:, own_half], dup[...])
    own_down[...] = dot_tn(hid[:, own_quarter], dy[...])

    def spread_small(i, axis):
        for d in (1, 2, 3):
            remote(
                small.at[:, pl.ds(0, HALF)],
                small_recv.at[1 + 3 * i + d - 1],
                small_send.at[1 + 3 * i + d - 1],
                small_recv_sem.at[1 + 3 * i + d - 1],
                axis(d),
            ).start()

    def join_small(i, axis):
        for d in (1, 2, 3):
            remote(
                small.at[:, pl.ds(0, HALF)],
                small_recv.at[1 + 3 * i + d - 1],
                small_send.at[1 + 3 * i + d - 1],
                small_recv_sem.at[1 + 3 * i + d - 1],
                axis(d),
            ).wait()
        total = small[:, pl.ds(0, HALF)]
        for d in (1, 2, 3):
            total = total + small_recv[1 + 3 * i + d - 1]
        small[:, pl.ds(0, HALF)] = total

    small_pair.wait()
    small[:, pl.ds(0, HALF)] = small[:, own_half] + small_recv[0]
    spread_small(0, along_y)

    def join_one(lane):
        i, v, r1, s1, r2, _, _, _, _, at, axis, to = lane
        wait_for(r1.at[pl.ds(0, 3)], recv_sem.at[i, 0])
        total = v[aligned(at * BAND, BAND, 16)].astype(F32)
        for d in (1, 2, 3):
            total = total + r1[lax.rem(at + d, 4)].astype(F32)
        s1[...] = total.astype(BF)
        for d in (1, 2, 3):
            rows = aligned(lax.rem(to + d, 4) * SLICE, SLICE, 16)
            remote(s1.at[rows], r2.at[to], send_sem.at[i, 1], recv_sem.at[i, 1], axis(d)).start()

    join_one(lanes[1])
    join_one(lanes[0])
    join_small(0, along_y)
    spread_small(1, along_z)

    mine = aligned(x * NARROW, NARROW, 128)
    theirs = aligned((1 - x) * NARROW, NARROW, 128)

    def join_two(lane):
        i, _, _, s1, r2, s2, r3, _, _, _, _, to = lane
        wait_for(r2.at[pl.ds(0, 3)], recv_sem.at[i, 1])
        total = s1[aligned(to * SLICE, SLICE, 16)].astype(F32)
        for d in (1, 2, 3):
            total = total + r2[lax.rem(to + d, 4)].astype(F32)
        s2[...] = total.astype(BF)
        remote(s2.at[:, theirs], r3, send_sem.at[i, 2], recv_sem.at[i, 2], twin).start()

    join_two(lanes[1])
    join_two(lanes[0])
    join_small(1, along_z)
    small_twin = remote(
        small.at[:, pl.ds(0, HALF)],
        small_recv.at[7],
        small_send.at[7],
        small_recv_sem.at[7],
        twin,
    )
    small_twin.start()

    def place_of(lane):
        _, _, _, _, _, _, _, _, _, at, _, to = lane
        return aligned(at * BAND + to * SLICE, SLICE, 16)

    def join_three(lane):
        i, _, _, _, _, s2, r3, g, _, _, _, _ = lane
        wait_for(r3, recv_sem.at[i, 2])
        total = s2[:, mine].astype(F32) + r3[...].astype(F32)
        g[place_of(lane), mine] = total.astype(BF)
        part = g.at[place_of(lane), mine]
        remote(part, part, send_sem.at[i, 3], recv_sem.at[i, 3], twin).start()

    def gather_two(lane):
        i, _, _, _, _, _, _, g, _, _, axis, _ = lane
        wait_for(g.at[place_of(lane), theirs], recv_sem.at[i, 3])
        part = g.at[place_of(lane)]
        for d in (1, 2, 3):
            remote(part, part, send_sem.at[i, 4], recv_sem.at[i, 4], axis(d)).start()

    def gather_one(lane):
        i, _, _, _, _, _, _, g, axis, at, _, _ = lane
        wait_for(g.at[pl.ds(0, 3 * SLICE)], recv_sem.at[i, 4])
        part = g.at[aligned(at * BAND, BAND, 16)]
        for d in (1, 2, 3):
            remote(part, part, send_sem.at[i, 5], recv_sem.at[i, 5], axis(d)).start()

    for step in (join_three, gather_two, gather_one):
        step(lanes[1])
        step(lanes[0])

    small_twin.wait()
    gains_out[...] = small[:, pl.ds(0, HALF)] + small_recv[7]

    def out_copy(i, src, dst):
        copy = pltpu.make_async_copy(src, dst, out_sem.at[i])
        copy.start()
        return copy

    outs = []
    for i, (arrived, part, own, dst) in enumerate(
        (
            (pair[0], part_gate, own_gate, gate_out),
            (pair[1], part_up, own_up, up_out),
            (pair[2], part_down, own_down, down_out),
        )
    ):
        arrived.wait_recv()
        part[...] = (own[...] + part[...].astype(F32)).astype(BF)
        outs.append(out_copy(i, part, dst))

    wait_for(g_b.at[pl.ds(0, 3 * BAND)], recv_sem.at[1, 5])
    outs.append(out_copy(3, g_b.at[:, pl.ds(0, WIDTH)], o_out))
    outs.append(out_copy(4, g_b.at[:, pl.ds(WIDTH, 256)], v_out))
    wait_for(g_a.at[pl.ds(0, 3 * BAND)], recv_sem.at[0, 5])
    outs.append(out_copy(5, g_a.at[:, pl.ds(0, WIDTH)], q_out))
    outs.append(out_copy(6, g_a.at[:, pl.ds(WIDTH, 256)], k_out))

    for lane in lanes:
        i, v, _, s1, _, s2, _, g = lane[:8]
        wait_for(v.at[pl.ds(0, 3 * BAND)], send_sem.at[i, 0])
        wait_for(s1.at[pl.ds(0, 3 * SLICE)], send_sem.at[i, 1])
        wait_for(s2.at[:, theirs], send_sem.at[i, 2])
        wait_for(g.at[place_of(lane), mine], send_sem.at[i, 3])
        wait_for(g.at[pl.ds(0, 3 * SLICE)], send_sem.at[i, 4])
        wait_for(g.at[pl.ds(0, 3 * BAND)], send_sem.at[i, 5])
    for copy in pair:
        copy.wait_send()
    for copy in outs:
        copy.wait()


def reduce_grads(*operands):
    def out(*shape):
        return jax.ShapeDtypeStruct(shape, BF)

    vmem = pl.BlockSpec(memory_space=pltpu.VMEM)
    anywhere = pl.BlockSpec(memory_space=pl.ANY)
    dma = pltpu.SemaphoreType.DMA
    lane = [
        pltpu.VMEM((HALF, WIDE), BF),
        pltpu.VMEM((4, BAND, WIDE), BF),
        pltpu.VMEM((BAND, WIDE), BF),
        pltpu.VMEM((4, SLICE, WIDE), BF),
        pltpu.VMEM((SLICE, WIDE), BF),
        pltpu.VMEM((SLICE, NARROW), BF),
        pltpu.VMEM((HALF, WIDE), BF),
    ]
    expert = [
        pltpu.VMEM((HALF, HIDDEN), BF),
        pltpu.VMEM((HALF, HIDDEN), BF),
        pltpu.VMEM((HIDDEN // 2, WIDTH), BF),
    ]
    return pl.pallas_call(
        grads_kernel,
        name="grads",
        out_shape=(
            out(HALF, WIDTH),
            out(HALF, 256),
            out(HALF, 256),
            out(HALF, WIDTH),
            out(HALF, HIDDEN),
            out(HALF, HIDDEN),
            out(HIDDEN // 2, WIDTH),
            jax.ShapeDtypeStruct((8, HALF), F32),
        ),
        in_specs=[anywhere] * 9 + [vmem],
        out_specs=[anywhere] * 7 + [vmem],
        scratch_shapes=[
            pltpu.VMEM((MB * ROWS, WIDTH), BF),
            pltpu.VMEM((MB * ROWS, WIDTH), BF),
            pltpu.VMEM((MB * ROWS, HIDDEN), BF),
            pltpu.VMEM((MB * ROWS, HIDDEN), BF),
            pltpu.VMEM((MB * ROWS, HIDDEN), BF),
            pltpu.VMEM((MB * 2 * SEQ, HALF), BF),
            pltpu.VMEM((MB, 2, 2 * SEQ, QKV), BF),
            pltpu.VMEM((MB * 2 * SEQ, HALF), BF),
            pltpu.VMEM((MB * 2 * SEQ, WIDTH), BF),
        ]
        + [part for shape in lane for part in (shape, shape)]
        + expert
        + expert
        + [
            pltpu.VMEM((HALF, HIDDEN), F32),
            pltpu.VMEM((HALF, HIDDEN), F32),
            pltpu.VMEM((HIDDEN // 2, WIDTH), F32),
            pltpu.VMEM((8, WIDTH), F32),
            pltpu.VMEM((8, 8, HALF), F32),
            dma((9,)),
            dma((2, 6)),
            dma((2, 6)),
            dma((3,)),
            dma((3,)),
            dma((8,)),
            dma((8,)),
            dma((7,)),
        ],
        compiler_params=pltpu.CompilerParams(
            collective_id=1, has_side_effects=True, vmem_limit_bytes=62 * 2**20
        ),
    )(*operands)


def local(
    inputs,
    cotangent,
    segments,
    expert_ids,
    gate_logits,
    w_query,
    key_projection,
    value_projection,
    w_out,
    gain_attn,
    gain_moe,
    w_gate,
    w_up,
    w_down,
):
    pair_segments = jnp.swapaxes(lax.all_gather(segments, "fsdp"), 0, 1)
    gains = lax.all_gather(jnp.stack([gain_attn[0], gain_moe[0]]), "fsdp", axis=1, tiled=True)
    gains = gains.astype(F32)
    same = pair_segments[..., :, None] == pair_segments[..., None, :]
    row = lax.broadcasted_iota(jnp.int32, (SEQ, SEQ), 0)
    col = lax.broadcasted_iota(jnp.int32, (SEQ, SEQ), 1)
    places = jnp.sum((same & (col < row)).astype(F32), axis=-1)
    frequency = ROPE_BASE ** (-(jnp.arange(HEAD // 2, dtype=F32) * 2.0 / HEAD))
    angles = places[..., None] * frequency
    cosine, sine = jnp.cos(angles), jnp.sin(angles)
    cos_t = jnp.concatenate([cosine, cosine], axis=-1).reshape(MB, 2 * SEQ, HEAD)
    sin_t = jnp.concatenate([-sine, sine], axis=-1).reshape(MB, 2 * SEQ, HEAD)
    mask_t = (same & (col <= row)).astype(F32)
    (
        acts,
        in_grads,
        gain_parts,
        n2rows,
        dyrows,
        hid,
        dgate,
        dup,
        n1,
        dqkv,
        att,
        da,
    ) = run_sections(
        inputs,
        cotangent,
        w_query[0],
        key_projection[0],
        value_projection[0],
        w_out[0],
        w_gate[0, 0],
        w_up[0, 0],
        w_down[0, 0],
        gains[0:1],
        gains[1:2],
        jnp.swapaxes(expert_ids[0], 1, 2),
        jnp.swapaxes(gate_logits[0], 1, 2),
        cos_t,
        sin_t,
        mask_t,
    )
    gq, gk, gv, go, grad_gate, grad_up, grad_down, gains = reduce_grads(
        n2rows.reshape(MB * ROWS, WIDTH),
        dyrows.reshape(MB * ROWS, WIDTH),
        hid.reshape(MB * ROWS, HIDDEN),
        dgate.reshape(MB * ROWS, HIDDEN),
        dup.reshape(MB * ROWS, HIDDEN),
        n1.reshape(MB * 2 * SEQ, HALF),
        dqkv,
        att.reshape(MB * 2 * SEQ, HALF),
        da.reshape(MB * 2 * SEQ, WIDTH),
        gain_parts,
    )
    return (
        acts[None],
        in_grads[None],
        gq[None].astype(F32),
        gk[None].astype(F32),
        gv[None].astype(F32),
        go[None].astype(F32),
        gains[0:1],
        gains[1:2],
        grad_gate[None, None].astype(F32),
        grad_up[None, None].astype(F32),
        grad_down[None, None].astype(F32),
    )


def solution(mesh):
    return jax.shard_map(
        local,
        mesh=mesh,
        in_specs=(
            P(None, ("fsdp", "expert"), None),
            P(None, ("fsdp", "expert"), None),
            P(None, ("fsdp", "expert")),
            P("section", None, ("fsdp", "expert"), None),
            P("section", None, ("fsdp", "expert"), None),
            P("section", "fsdp", None),
            P("section", "fsdp", None),
            P("section", "fsdp", None),
            P("section", "fsdp", None),
            P("section", "fsdp"),
            P("section", "fsdp"),
            P("section", "expert", "fsdp", None),
            P("section", "expert", "fsdp", None),
            P("section", "expert", "fsdp", None),
        ),
        out_specs=(
            P("section", None, ("fsdp", "expert"), None),
            P("section", None, ("fsdp", "expert"), None),
            P("section", "fsdp", None),
            P("section", "fsdp", None),
            P("section", "fsdp", None),
            P("section", "fsdp", None),
            P("section", "fsdp"),
            P("section", "fsdp"),
            P("section", "expert", "fsdp", None),
            P("section", "expert", "fsdp", None),
            P("section", "expert", "fsdp", None),
        ),
        check_vma=False,
    )
```

```python
import functools

import jax
import jax.numpy as jnp
import numpy as np
from jax import lax
from jax.experimental import pallas as pl
from jax.experimental.pallas import tpu as pltpu
from jax.sharding import PartitionSpec as P

MESH = pl.DeviceIdType.MESH
BF = jnp.bfloat16
F32 = jnp.float32

HEAD = 128
EPS = 1e-06
ROPE_BASE = 1000000.0
GELU_C = 0.7978845608
GELU_A = 0.044715

MB = 2
SEQ = 96
WIDTH = 1536
HALF = 768
EXPERTS = 32
PLANE = 16
SLOTS = 16
ROWS = EXPERTS * SLOTS
HIDDEN = 768
HEADS = 6
QKV = 1024


def dot(a, b):
    return jnp.dot(a, b, preferred_element_type=F32)


def dot_nt(a, b):
    return lax.dot_general(a, b, (((1,), (1,)), ((), ())), preferred_element_type=F32)


def dot_tn(a, b):
    return lax.dot_general(a, b, (((0,), (0,)), ((), ())), preferred_element_type=F32)


def aligned(start, size, unit):
    return pl.ds(pl.multiple_of(start, unit), size)


def inverse_rms(rows):
    return lax.rsqrt(jnp.mean(rows * rows, axis=-1, keepdims=True) + EPS)


def rms_back(rows, inverse, gain, grad):
    scaled = gain * grad
    return inverse * scaled - rows * (inverse * inverse * inverse) * jnp.mean(
        scaled * rows, axis=-1, keepdims=True
    )


def rotate(head, cos, sin):
    return head * cos + pltpu.roll(head, HEAD // 2, 1) * sin


(ATTEND, NORM, TWIN, HIDE, GIVE, FAR, JOIN, GRAD, GRAD_TWIN, BACK, FAR_BACK, MID, ATTEND_BACK, CLOSE, LOAD, REST) = range(16)

FIRST_PLAN = (
    (ATTEND, 0),
    (ATTEND, 1),
    (NORM, 0),
    (TWIN, 0),
    (NORM, 1),
    (TWIN, 1),
    (HIDE, 0),
    (GIVE, 0),
    (HIDE, 1),
    (GIVE, 1),
    (FAR, 0),
    (JOIN, 0),
    (FAR, 1),
    (JOIN, 1),
    (GRAD, 0),
    (GRAD_TWIN, 0),
    (GRAD, 1),
    (GRAD_TWIN, 1),
    (BACK, 0),
    (BACK, 1),
    (FAR_BACK, 0),
    (MID, 0),
    (FAR_BACK, 1),
    (MID, 1),
    (ATTEND_BACK, 0),
    (ATTEND_BACK, 1),
    (CLOSE, 0),
    (CLOSE, 1),
)
SECOND_PLAN = (
    (GRAD, 0),
    (GRAD, 1),
    (LOAD, 0),
    (ATTEND, 0),
    (ATTEND, 1),
    (NORM, 0),
    (TWIN, 0),
    (NORM, 1),
    (TWIN, 1),
    (GRAD_TWIN, 0),
    (GRAD_TWIN, 1),
    (HIDE, 0),
    (BACK, 0),
    (HIDE, 1),
    (BACK, 1),
    (FAR_BACK, 0),
    (MID, 0),
    (FAR_BACK, 1),
    (MID, 1),
    (ATTEND_BACK, 0),
    (ATTEND_BACK, 1),
    (CLOSE, 0),
    (CLOSE, 1),
    (GIVE, 0),
    (GIVE, 1),
    (FAR, 0),
    (JOIN, 0),
    (FAR, 1),
    (JOIN, 1),
)


def section_kernel(
    x_in,
    ct_in,
    wq_in,
    wk_in,
    wv_in,
    wo_in,
    wg_in,
    wu_in,
    wd_in,
    side_in,
    meta_in,
    freq_in,
    acts_out,
    ingrad_out,
    gains_out,
    n2rows_out,
    dyrows_out,
    hid_out,
    dgate_out,
    dup_out,
    n1_out,
    dqkv_out,
    att_out,
    da_out,
    wqkv,
    wo,
    wg,
    wu,
    wd,
    xpair,
    n1s,
    qkvs,
    att,
    hid_one,
    part_own,
    part_send,
    part_recv,
    sel,
    cg_hi,
    cg_lo,
    n2pair,
    gpair,
    dsend,
    bsend,
    n2recv,
    yrecv,
    dyrecv,
    dn2recv,
    gs,
    us,
    hid,
    far_send,
    far_recv,
    acts_s,
    dh_s,
    da_pair,
    dqkv_all,
    dn1_send,
    dn1_recv,
    ingrad_s,
    gains_acc,
    side,
    meta,
    gains,
    cos_t,
    sin_t,
    mask_t,
    lw_sem,
    ws_sem,
    wr_sem,
    as_sem,
    ar_sem,
    ps_sem,
    pr_sem,
    ts_sem,
    tr_sem,
    xs_sem,
    xr_sem,
    gs_sem,
    gr_sem,
    out_sem,
    go_sem,
):
    sec = lax.axis_index("section")
    f = lax.axis_index("fsdp")
    e = lax.axis_index("expert")
    y, x, z = e // 8, lax.rem(e // 4, 2), lax.rem(e, 4)
    q = y * 4 + z
    away = 1 - x
    other = 1 - f
    own_rows = aligned(f * SEQ, SEQ, 16)
    other_rows = aligned(other * SEQ, SEQ, 16)
    own_half = aligned(f * HALF, HALF, 128)
    other_half = aligned(other * HALF, HALF, 128)
    partner = {"fsdp": other}
    twin_place = y * 8 + away * 4 + z
    twin = {"expert": twin_place}
    first, second = sec == 0, sec == 1

    def in_plane(d):
        at = lax.rem(q + d, PLANE)
        return at, {"expert": (at // 4) * 8 + x * 4 + lax.rem(at, 4)}

    barrier = pltpu.get_barrier_semaphore()

    @pl.loop(1, PLANE)
    def _(d):
        pl.semaphore_signal(barrier, inc=1, device_id=in_plane(d)[1], device_id_type=MESH)

    others = (
        twin,
        partner,
        {"section": 1 - sec},
        {"section": 1 - sec, "fsdp": other},
        {"section": 1 - sec, "expert": twin_place},
    )
    for place in others:
        pl.semaphore_signal(barrier, inc=1, device_id=place, device_id_type=MESH)

    local = [
        (wq_in.at[:, own_half], wqkv.at[own_half, pl.ds(0, HALF)]),
        (wk_in.at[:, aligned(f * HEAD, HEAD, 128)], wqkv.at[own_half, pl.ds(HALF, HEAD)]),
        (wv_in.at[:, aligned(f * HEAD, HEAD, 128)], wqkv.at[own_half, pl.ds(HALF + HEAD, HEAD)]),
        (wo_in, wo),
        (wg_in, wg.at[own_half]),
        (wu_in, wu.at[own_half]),
        (wd_in, wd.at[aligned(f * (HIDDEN // 2), HIDDEN // 2, 16)]),
    ]
    local = [pltpu.make_async_copy(a, b, lw_sem.at[i]) for i, (a, b) in enumerate(local)]
    for copy in local:
        copy.start()
    x_local = pltpu.make_async_copy(x_in, xpair.at[:, own_rows], lw_sem.at[7])
    ct_local = pltpu.make_async_copy(ct_in, gpair.at[:, x], lw_sem.at[8])
    pl.when(first)(x_local.start)
    pl.when(second)(ct_local.start)

    def remote(src, dst, send, recv, place):
        return pltpu.make_async_remote_copy(
            src_ref=src,
            dst_ref=dst,
            send_sem=send,
            recv_sem=recv,
            device_id=place,
            device_id_type=MESH,
        )

    def wait_for(ref, sem):
        pltpu.make_async_copy(ref, ref, sem).wait()

    def weight(src, dst, i):
        return remote(src, dst, ws_sem.at[i], wr_sem.at[i], partner)

    w_attn = [
        weight(wq_in.at[:, other_half], wqkv.at[own_half, pl.ds(0, HALF)], 0),
        weight(
            wk_in.at[:, aligned(other * HEAD, HEAD, 128)],
            wqkv.at[own_half, pl.ds(HALF, HEAD)],
            1,
        ),
        weight(
            wv_in.at[:, aligned(other * HEAD, HEAD, 128)],
            wqkv.at[own_half, pl.ds(HALF + HEAD, HEAD)],
            2,
        ),
    ]
    w_moe = [
        weight(wg_in, wg.at[own_half], 3),
        weight(wu_in, wu.at[own_half], 4),
        weight(wd_in, wd.at[aligned(f * (HIDDEN // 2), HIDDEN // 2, 16)], 5),
    ]

    def x_copy(m):
        return weight(x_in.at[m], xpair.at[m, own_rows], 6 + m)

    def ct_copy(m):
        return remote(ct_in.at[m], gpair.at[m, x], ws_sem.at[10 + m], gr_sem.at[x, m], twin)

    side[f] = side_in[...]
    meta[x] = meta_in[...]
    side_copy = weight(side.at[f], side.at[f], 8)
    meta_copy = remote(meta.at[x], meta.at[x], ws_sem.at[9], wr_sem.at[9], twin)
    gains_acc[...] = jnp.zeros_like(gains_acc)

    pl.semaphore_wait(barrier, PLANE - 1 + len(others))
    side_copy.start()
    meta_copy.start()

    @pl.when(first)
    def _():
        x_copy(0).start()
        for copy in w_attn:
            copy.start()
        x_copy(1).start()

    meta_copy.wait_recv()
    earlier = lax.broadcasted_iota(jnp.int32, (SEQ, SEQ), 0) < lax.broadcasted_iota(
        jnp.int32, (SEQ, SEQ), 1
    )
    earlier = jnp.where(earlier, 1.0, 0.0).astype(BF)

    @pl.loop(0, 2 * MB)
    def _(i):
        m, source = lax.rem(i, MB), i // MB
        rows = meta[source, m]
        ids, logits = rows[:4], rows[4:]
        raised = jnp.exp(logits - jnp.max(logits, axis=0, keepdims=True))
        gates = raised / jnp.sum(raised, axis=0, keepdims=True)
        place = lax.broadcasted_iota(jnp.int32, (PLANE, SEQ), 0)
        expert = ((place // 4) * 8 + x * 4 + lax.rem(place, 4)).astype(F32)
        named = jnp.zeros((PLANE, SEQ), F32)
        weights = jnp.zeros((PLANE, SEQ), F32)
        for k in range(4):
            hit = expert == ids[k : k + 1, :]
            named = jnp.where(hit, 1.0, named)
            weights = jnp.where(hit, gates[k : k + 1, :], weights)
        slot = dot(named.astype(BF), earlier)
        slot = jnp.where(named > 0.0, slot, -1.0)
        shape = (PLANE, SLOTS, SEQ)
        count = lax.broadcasted_iota(jnp.int32, shape, 1).astype(F32)
        chosen = jnp.where(jnp.broadcast_to(slot[:, None, :], shape) == count, 1.0, 0.0)
        scaled = chosen * jnp.broadcast_to(weights[:, None, :], shape)
        scaled = scaled.reshape(PLANE * SLOTS, SEQ)
        high = scaled.astype(BF)
        sel[m, source] = chosen.reshape(PLANE * SLOTS, SEQ).astype(BF)
        cg_hi[m, source] = high
        cg_lo[m, source] = (scaled - high.astype(F32)).astype(BF)

    side_copy.wait_recv()
    gains[:, pl.ds(0, HALF)] = side[0, 0:2]
    gains[:, pl.ds(HALF, HALF)] = side[1, 0:2]
    row = lax.broadcasted_iota(jnp.int32, (SEQ, SEQ), 0)
    col = lax.broadcasted_iota(jnp.int32, (SEQ, SEQ), 1)
    lane = lax.broadcasted_iota(jnp.int32, (SEQ, HEAD), 1)
    turn = jnp.where(lane < HEAD // 2, -1.0, 1.0)
    for m in range(MB):
        for s in range(2):
            across = jnp.broadcast_to(side[s, 2 + m : 3 + m, :SEQ], (SEQ, SEQ))
            down = dot_nt(jnp.where(row == col, 1.0, 0.0).astype(BF), across.astype(BF))
            same = jnp.where(down == across, 1.0, 0.0)
            mask_t[m, s] = jnp.where(col <= row, same, 0.0)
            places = jnp.sum(jnp.where(col < row, same, 0.0), axis=1, keepdims=True)
            angles = places * freq_in[...]
            cos_t[m, pl.ds(s * SEQ, SEQ)] = jnp.cos(angles)
            sin_t[m, pl.ds(s * SEQ, SEQ)] = jnp.sin(angles) * turn

    def exchange_half(kind, m, src, dst, source):
        @pl.loop(1, PLANE)
        def _(d):
            at, place = in_plane(d)
            remote(
                src.at[m, at, source],
                dst.at[m, q, source],
                as_sem.at[kind, m],
                ar_sem.at[kind, m],
                place,
            ).start()

        dst[m, q, source] = src[m, q, source]

    def exchange(kind, m, src, dst):
        @pl.loop(1, PLANE)
        def _(d):
            at, place = in_plane(d)
            remote(
                src.at[m, at], dst.at[m, q], as_sem.at[kind, m], ar_sem.at[kind, m], place
            ).start()

        dst[m, q] = src[m, q]

    def received(kind, m, dst):
        wait_for(dst.at[m, pl.ds(0, PLANE - 1)], ar_sem.at[kind, m])

    def sent(kind, m, src):
        wait_for(src.at[m, pl.ds(0, PLANE - 1)], as_sem.at[kind, m])

    def to_partner(kind, m, src, dst):
        return remote(src, dst, ps_sem.at[kind, m], pr_sem.at[kind, m], partner)

    def to_twin(kind, m, src, dst):
        return remote(src, dst, ts_sem.at[kind, m], tr_sem.at[kind, m], twin)

    def n2_copy(m):
        return to_twin(0, m, n2pair.at[m, x], n2pair.at[m, x])

    def far_copy(kind, m):
        return to_twin(kind, m, far_send.at[kind - 1, m], far_recv.at[kind - 1, m])

    def acts_copy(m, cross):
        place = {"section": 1, "fsdp": other} if cross else {"section": 1}
        return remote(
            acts_s.at[m], xpair.at[m, own_rows], xs_sem.at[cross, m], xr_sem.at[f, m], place
        )

    def grad_copy(m, cross):
        place = {"section": 0, "expert": twin_place} if cross else {"section": 0}
        return remote(
            ingrad_s.at[m], gpair.at[m, x], gs_sem.at[cross, m], gr_sem.at[x, m], place
        )

    def out_copy(i, src, dst, m):
        return pltpu.make_async_copy(src, dst, out_sem.at[i, m])

    def flat(ref, m):
        return ref[m].reshape(ROWS, WIDTH)

    def spread(m, source, rows, dst, scale=None):
        @pl.loop(0, WIDTH // 512)
        def _(j):
            cols = aligned(j * 512, 512, 128)
            block = dot(sel[m, source], rows[m, source, :, cols])
            if scale is not None:
                block = block * scale
            dst[m, :, source, :, cols] = block.astype(BF).reshape(PLANE, SLOTS, 512)

    def load_step(m):
        pl.semaphore_wait(go_sem, 1)
        for copy in w_attn:
            copy.start()

    def heads_of(ref, m, rows):
        return jnp.concatenate(
            [ref[m, rows, pl.ds(h * HEAD, HEAD)] for h in range(HEADS)], axis=0
        )

    def softmax_of(m, s, queries, keys):
        scores = dot_nt(queries, keys) * HEAD ** (-0.5)
        allowed = jnp.concatenate([mask_t[m, s]] * HEADS, axis=0)
        scores = jnp.where(allowed > 0.0, scores, -1e30)
        raised = jnp.exp(scores - jnp.max(scores, axis=-1, keepdims=True))
        return raised / jnp.sum(raised, axis=-1, keepdims=True)

    def attend_step(m):
        @pl.when(m == 0)
        def _():
            for copy in local[:4]:
                copy.wait()
            for copy in w_attn:
                copy.wait_recv()
            for copy in w_attn:
                copy.wait_send()
            for copy in w_moe:
                copy.start()
            pl.when(first)(x_local.wait)

            @pl.when(second)
            def _():
                ct_copy(0).start()
                ct_copy(1).start()

        @pl.when(first)
        def _():
            x_copy(m).wait_recv()

        @pl.when(second)
        def _():
            for at, rows in ((f, own_rows), (other, other_rows)):
                wait_for(xpair.at[m, rows], xr_sem.at[at, m])

        rows = xpair[m].astype(F32)
        n1s[m] = (rows * inverse_rms(rows) * gains[0:1]).astype(BF)
        cos, sin = cos_t[m], sin_t[m]
        for j in range(4):
            block = dot(n1s[m], wqkv[:, pl.ds(j * 256, 256)])
            qkvs[m, :, pl.ds(j * 256, HEAD)] = rotate(block[:, :HEAD], cos, sin).astype(BF)
            late = block[:, HEAD:]
            if j < 3:
                late = rotate(late, cos, sin)
            qkvs[m, :, pl.ds(j * 256 + HEAD, HEAD)] = late.astype(BF)

        @pl.loop(0, 2)
        def _(s):
            at = aligned(s * SEQ, SEQ, 16)
            queries = heads_of(qkvs, m, at)
            keys = qkvs[m, at, pl.ds(HALF, HEAD)]
            values = qkvs[m, at, pl.ds(HALF + HEAD, HEAD)]
            probs = softmax_of(m, s, queries, keys).astype(BF)
            mixed = dot(probs, values).astype(BF)
            for h in range(HEADS):
                att[m, at, pl.ds(h * HEAD, HEAD)] = mixed[h * SEQ : (h + 1) * SEQ]

        @pl.loop(0, WIDTH // 512)
        def _(j):
            cols = aligned(j * 512, 512, 128)
            block = dot(att[m], wo[:, cols])
            top, low = block[:SEQ], block[SEQ:]
            mine = f == 0
            hid_one[m, :, cols] = jnp.where(mine, top, low)
            part_send[m, :, cols] = jnp.where(mine, low, top).astype(BF)

        to_partner(0, m, part_send.at[m], part_recv.at[m]).start()

    def norm_step(m):
        to_partner(0, m, part_send.at[m], part_recv.at[m]).wait_recv()
        rows = xpair[m, own_rows].astype(F32) + (hid_one[m] + part_recv[m].astype(F32))
        hid_one[m] = rows
        n2pair[m, x] = (rows * inverse_rms(rows) * gains[1:2]).astype(BF)
        n2_copy(m).start()
        spread(m, x, n2pair, dsend)
        exchange_half(0, m, dsend, n2recv, x)

    def twin_step(m):
        n2_copy(m).wait_recv()
        spread(m, away, n2pair, dsend)
        exchange_half(0, m, dsend, n2recv, away)

    def hide_step(m):
        @pl.when(m == 0)
        def _():
            for copy in local[4:6]:
                copy.wait()
            for copy in w_moe[:2]:
                copy.wait_recv()

        received(0, m, n2recv)
        out_copy(0, n2recv.at[m], n2rows_out.at[m], m).start()

        @pl.loop(0, HIDDEN // 256)
        def _(j):
            cols = aligned(j * 256, 256, 128)
            rows = flat(n2recv, m)
            gate = dot(rows, wg[:, cols])
            up = dot(rows, wu[:, cols])
            bend = jnp.tanh(GELU_C * (gate + GELU_A * gate * gate * gate))
            gs[m, :, cols] = gate.astype(BF)
            us[m, :, cols] = up.astype(BF)
            hid[m, :, cols] = (0.5 * gate * (1.0 + bend) * up).astype(BF)

        out_copy(1, hid.at[m], hid_out.at[m], m).start()

        @pl.when(m == 0)
        def _():
            local[6].wait()
            w_moe[2].wait_recv()
            for copy in w_moe:
                copy.wait_send()

            @pl.when(first)
            def _():
                pl.semaphore_signal(go_sem, inc=1, device_id={"section": 1}, device_id_type=MESH)

    def give_step(m):
        pl.when(second)(lambda: sent(3, m, bsend))

        @pl.loop(0, WIDTH // 512)
        def _(j):
            cols = aligned(j * 512, 512, 128)
            block = dot(hid[m], wd[:, cols]).astype(BF)
            bsend[m, :, :, :, cols] = block.reshape(PLANE, 2, SLOTS, 512)

        exchange(1, m, bsend, yrecv)

    def weighed(m, source, cols):
        block = yrecv[m, :, source, :, cols].reshape(PLANE * SLOTS, 512)
        return dot_tn(cg_hi[m, source], block) + dot_tn(cg_lo[m, source], block)

    def far_step(m):
        received(1, m, yrecv)

        @pl.loop(0, WIDTH // 512)
        def _(j):
            cols = aligned(j * 512, 512, 128)
            far_send[0, m, :, cols] = weighed(m, away, cols).astype(BF)

        far_copy(1, m).start()

        @pl.loop(0, WIDTH // 512)
        def _(j):
            cols = aligned(j * 512, 512, 128)
            part_own[m, :, cols] = hid_one[m, :, cols] + weighed(m, x, cols)

    def join_step(m):
        far_copy(1, m).wait_recv()
        acts_s[m] = (part_own[m] + far_recv[0, m].astype(F32)).astype(BF)

        @pl.when(first)
        def _():
            for cross in (0, 1):
                acts_copy(m, cross).start()

        out_copy(2, acts_s.at[m], acts_out.at[m], m).start()

    def dy_half(m, source):
        gate = cg_hi[m, source].astype(F32) + cg_lo[m, source].astype(F32)
        spread(m, source, gpair, bsend, jnp.sum(gate, axis=1, keepdims=True))
        exchange_half(2, m, bsend, dyrecv, source)

    def grad_step(m):
        @pl.when(first)
        def _():
            sent(1, m, bsend)
            wait_for(gpair.at[m, x], gr_sem.at[x, m])

        @pl.when(jnp.logical_and(second, m == 0))
        def _():
            ct_local.wait()

        dy_half(m, x)

    def grad_twin_step(m):
        wait_for(gpair.at[m, away], gr_sem.at[away, m])
        dy_half(m, away)

    def back_step(m):
        received(2, m, dyrecv)
        out_copy(3, dyrecv.at[m], dyrows_out.at[m], m).start()

        @pl.loop(0, HIDDEN // 256)
        def _(j):
            cols = aligned(j * 256, 256, 128)
            dhid = dot_nt(flat(dyrecv, m), wd[cols, :])
            gate = gs[m, :, cols].astype(F32)
            up = us[m, :, cols].astype(F32)
            square = gate * gate
            bend = jnp.tanh(GELU_C * (gate + GELU_A * square * gate))
            half = 0.5 * (1.0 + bend)
            slope = half + 0.5 * gate * (1.0 - bend * bend) * (
                GELU_C * (1.0 + 3.0 * GELU_A * square)
            )
            gs[m, :, cols] = (dhid * up * slope).astype(BF)
            us[m, :, cols] = (dhid * (gate * half)).astype(BF)

        out_copy(4, gs.at[m], dgate_out.at[m], m).start()
        out_copy(5, us.at[m], dup_out.at[m], m).start()
        sent(2, m, bsend)

        @pl.loop(0, WIDTH // 512)
        def _(j):
            cols = aligned(j * 512, 512, 128)
            block = dot_nt(gs[m], wg[cols, :]) + dot_nt(us[m], wu[cols, :])
            bsend[m, :, :, :, cols] = block.astype(BF).reshape(PLANE, 2, SLOTS, 512)

        exchange(3, m, bsend, dn2recv)

    def gathered(m, source, cols):
        return dot_tn(
            sel[m, source], dn2recv[m, :, source, :, cols].reshape(PLANE * SLOTS, 512)
        )

    def far_back_step(m):
        received(3, m, dn2recv)

        @pl.loop(0, WIDTH // 512)
        def _(j):
            cols = aligned(j * 512, 512, 128)
            far_send[1, m, :, cols] = gathered(m, away, cols).astype(BF)

        far_copy(2, m).start()

        @pl.loop(0, WIDTH // 512)
        def _(j):
            cols = aligned(j * 512, 512, 128)
            dh_s[m, :, cols] = gathered(m, x, cols)

    def mid_step(m):
        far_copy(2, m).wait_recv()
        rows = hid_one[m]
        inverse = inverse_rms(rows)
        grad = dh_s[m] + far_recv[1, m].astype(F32)
        gains_acc[1:2] += jnp.sum(grad * rows * inverse, axis=0, keepdims=True)
        total = gpair[m, x].astype(F32) + rms_back(rows, inverse, gains[1:2], grad)
        dh_s[m] = total
        da_pair[m, own_rows] = total.astype(BF)
        da_copy(m).start()

    def da_copy(m):
        return to_partner(1, m, da_pair.at[m, own_rows], da_pair.at[m, own_rows])

    def dqkv_copy(m):
        return to_partner(3, m, dqkv_all.at[m, f], dqkv_all.at[m, f])

    def dn1_copy(m):
        return to_partner(2, m, dn1_send.at[m], dn1_recv.at[m])

    def attend_back_step(m):
        da_copy(m).wait_recv()
        out_copy(6, da_pair.at[m], da_out.at[m], m).start()

        @pl.loop(0, 2)
        def _(s):
            at = aligned(s * SEQ, SEQ, 16)
            dmix = dot_nt(da_pair[m, at], wo[...]).astype(BF)
            dmix = jnp.concatenate(
                [dmix[:, h * HEAD : (h + 1) * HEAD] for h in range(HEADS)], axis=0
            )
            queries = heads_of(qkvs, m, at)
            keys = qkvs[m, at, pl.ds(HALF, HEAD)]
            values = qkvs[m, at, pl.ds(HALF + HEAD, HEAD)]
            probs = softmax_of(m, s, queries, keys)
            dprobs = dot_nt(dmix, values)
            dvalues = dot_tn(probs.astype(BF), dmix)
            dscores = probs * (dprobs - jnp.sum(dprobs * probs, axis=-1, keepdims=True))
            dscores = (dscores * HEAD ** (-0.5)).astype(BF)
            cos = cos_t[m, at]
            sin = -sin_t[m, at]
            dkeys = rotate(dot_tn(dscores, queries), cos, sin)
            dqueries = dot(dscores, keys)
            for h in range(HEADS):
                part = rotate(dqueries[h * SEQ : (h + 1) * SEQ], cos, sin)
                dqkv_all[m, f, at, pl.ds(h * HEAD, HEAD)] = part.astype(BF)
            dqkv_all[m, f, at, pl.ds(HALF, HEAD)] = dkeys.astype(BF)
            dqkv_all[m, f, at, pl.ds(HALF + HEAD, HEAD)] = dvalues.astype(BF)

        @pl.loop(0, WIDTH // 512)
        def _(j):
            cols = aligned(j * 512, 512, 128)
            block = dot_nt(dqkv_all[m, f], wqkv[cols, :])
            top, low = block[:SEQ], block[SEQ:]
            mine = f == 0
            part_own[m, :, cols] = jnp.where(mine, top, low)
            dn1_send[m, :, cols] = jnp.where(mine, low, top).astype(BF)

        dn1_copy(m).start()
        dqkv_copy(m).start()

    def close_step(m):
        dn1_copy(m).wait_recv()
        grad = part_own[m] + dn1_recv[m].astype(F32)
        rows = xpair[m, own_rows].astype(F32)
        inverse = inverse_rms(rows)
        gains_acc[0:1] += jnp.sum(grad * rows * inverse, axis=0, keepdims=True)
        ingrad_s[m] = (dh_s[m] + rms_back(rows, inverse, gains[0:1], grad)).astype(BF)

        @pl.when(second)
        def _():
            for cross in (0, 1):
                grad_copy(m, cross).start()

        out_copy(7, ingrad_s.at[m], ingrad_out.at[m], m).start()

    steps = {
        ATTEND: attend_step,
        NORM: norm_step,
        TWIN: twin_step,
        HIDE: hide_step,
        GIVE: give_step,
        FAR: far_step,
        JOIN: join_step,
        GRAD: grad_step,
        GRAD_TWIN: grad_twin_step,
        BACK: back_step,
        FAR_BACK: far_back_step,
        MID: mid_step,
        ATTEND_BACK: attend_back_step,
        CLOSE: close_step,
        LOAD: load_step,
    }
    length = max(len(FIRST_PLAN), len(SECOND_PLAN))
    plans = [plan + ((REST, 0),) * (length - len(plan)) for plan in (FIRST_PLAN, SECOND_PLAN)]

    @pl.loop(0, length)
    def _(i):
        code = jnp.int32(REST * MB)
        for at, ((step_a, m_a), (step_b, m_b)) in enumerate(zip(*plans)):
            here = jnp.where(first, step_a * MB + m_a, step_b * MB + m_b)
            code = jnp.where(i == at, here, code)
        m = lax.rem(code, MB)
        for step, work in steps.items():
            pl.when(code // MB == step)(functools.partial(work, m))

    gains_out[...] = gains_acc[...]

    @pl.loop(0, MB)
    def _(m):
        dqkv_copy(m).wait_recv()
        out_copy(8, n1s.at[m, :, own_half], n1_out.at[m], m).start()
        out_copy(9, dqkv_all.at[m], dqkv_out.at[m], m).start()
        out_copy(10, att.at[m], att_out.at[m], m).start()
        sent(0, m, dsend)
        pl.when(first)(lambda: sent(3, m, bsend))
        pl.when(second)(lambda: sent(1, m, bsend))
        to_partner(0, m, part_send.at[m], part_recv.at[m]).wait_send()
        da_copy(m).wait_send()
        dn1_copy(m).wait_send()
        dqkv_copy(m).wait_send()
        n2_copy(m).wait_send()
        far_copy(1, m).wait_send()
        far_copy(2, m).wait_send()

        @pl.when(first)
        def _():
            x_copy(m).wait_send()
            for cross in (0, 1):
                acts_copy(m, cross).wait_send()

        @pl.when(second)
        def _():
            ct_copy(m).wait_send()
            for cross in (0, 1):
                grad_copy(m, cross).wait_send()

    side_copy.wait_send()
    meta_copy.wait_send()

    @pl.loop(0, MB)
    def _(m):
        pairs = (
            (n2recv, n2rows_out),
            (hid, hid_out),
            (acts_s, acts_out),
            (dyrecv, dyrows_out),
            (gs, dgate_out),
            (us, dup_out),
            (da_pair, da_out),
            (ingrad_s, ingrad_out),
            (None, n1_out),
            (dqkv_all, dqkv_out),
            (att, att_out),
        )
        for i, (src, dst) in enumerate(pairs):
            src = n1s.at[m, :, own_half] if src is None else src.at[m]
            out_copy(i, src, dst.at[m], m).wait()


def run_sections(*operands):
    def out(*shape, dtype=BF):
        return jax.ShapeDtypeStruct(shape, dtype)

    vmem = pl.BlockSpec(memory_space=pltpu.VMEM)
    anywhere = pl.BlockSpec(memory_space=pl.ANY)
    dma = pltpu.SemaphoreType.DMA
    blocks = (MB, PLANE, 2, SLOTS, WIDTH)
    return pl.pallas_call(
        section_kernel,
        name="sections",
        out_shape=(
            out(MB, SEQ, WIDTH),
            out(MB, SEQ, WIDTH),
            out(8, WIDTH, dtype=F32),
            out(*blocks),
            out(*blocks),
            out(MB, ROWS, HIDDEN),
            out(MB, ROWS, HIDDEN),
            out(MB, ROWS, HIDDEN),
            out(MB, 2 * SEQ, HALF),
            out(MB, 2, 2 * SEQ, QKV),
            out(MB, 2 * SEQ, HALF),
            out(MB, 2 * SEQ, WIDTH),
        ),
        in_specs=[anywhere] * 9 + [vmem] * 3,
        out_specs=[anywhere] * 2 + [vmem] + [anywhere] * 9,
        scratch_shapes=[
            pltpu.VMEM((WIDTH, QKV), BF),
            pltpu.VMEM((HALF, WIDTH), BF),
            pltpu.VMEM((WIDTH, HIDDEN), BF),
            pltpu.VMEM((WIDTH, HIDDEN), BF),
            pltpu.VMEM((HIDDEN, WIDTH), BF),
            pltpu.VMEM((MB, 2 * SEQ, WIDTH), BF),
            pltpu.VMEM((MB, 2 * SEQ, WIDTH), BF),
            pltpu.VMEM((MB, 2 * SEQ, QKV), BF),
            pltpu.VMEM((MB, 2 * SEQ, HALF), BF),
            pltpu.VMEM((MB, SEQ, WIDTH), F32),
            pltpu.VMEM((MB, SEQ, WIDTH), F32),
            pltpu.VMEM((MB, SEQ, WIDTH), BF),
            pltpu.VMEM((MB, SEQ, WIDTH), BF),
            pltpu.VMEM((MB, 2, PLANE * SLOTS, SEQ), BF),
            pltpu.VMEM((MB, 2, PLANE * SLOTS, SEQ), BF),
            pltpu.VMEM((MB, 2, PLANE * SLOTS, SEQ), BF),
            pltpu.VMEM((MB, 2, SEQ, WIDTH), BF),
            pltpu.VMEM((MB, 2, SEQ, WIDTH), BF),
            pltpu.VMEM(blocks, BF),
            pltpu.VMEM(blocks, BF),
            pltpu.VMEM(blocks, BF),
            pltpu.VMEM(blocks, BF),
            pltpu.VMEM(blocks, BF),
            pltpu.VMEM(blocks, BF),
            pltpu.VMEM((MB, ROWS, HIDDEN), BF),
            pltpu.VMEM((MB, ROWS, HIDDEN), BF),
            pltpu.VMEM((MB, ROWS, HIDDEN), BF),
            pltpu.VMEM((2, MB, SEQ, WIDTH), BF),
            pltpu.VMEM((2, MB, SEQ, WIDTH), BF),
            pltpu.VMEM((MB, SEQ, WIDTH), BF),
            pltpu.VMEM((MB, SEQ, WIDTH), F32),
            pltpu.VMEM((MB, 2 * SEQ, WIDTH), BF),
            pltpu.VMEM((MB, 2, 2 * SEQ, QKV), BF),
            pltpu.VMEM((MB, SEQ, WIDTH), BF),
            pltpu.VMEM((MB, SEQ, WIDTH), BF),
            pltpu.VMEM((MB, SEQ, WIDTH), BF),
            pltpu.VMEM((8, WIDTH), F32),
            pltpu.VMEM((2, 8, HALF), F32),
            pltpu.VMEM((2, MB, 8, SEQ), F32),
            pltpu.VMEM((2, WIDTH), F32),
            pltpu.VMEM((MB, 2 * SEQ, HEAD), F32),
            pltpu.VMEM((MB, 2 * SEQ, HEAD), F32),
            pltpu.VMEM((MB, 2, SEQ, SEQ), F32),
            dma((9,)),
            dma((12,)),
            dma((10,)),
            dma((4, MB)),
            dma((4, MB)),
            dma((4, MB)),
            dma((4, MB)),
            dma((3, MB)),
            dma((3, MB)),
            dma((2, MB)),
            dma((2, MB)),
            dma((2, MB)),
            dma((2, MB)),
            dma((11, MB)),
            pltpu.SemaphoreType.REGULAR,
        ],
        compiler_params=pltpu.CompilerParams(
            collective_id=0, has_side_effects=True, vmem_limit_bytes=62 * 2**20
        ),
    )(*operands)


BAND = 192
SLICE = 48
WIDE = 1792
NARROW = 896


def grads_kernel(
    n2_in,
    dy_in,
    hid_in,
    dgate_in,
    dup_in,
    n1_in,
    dqkv_in,
    att_in,
    da_in,
    gains_in,
    q_out,
    k_out,
    v_out,
    o_out,
    gate_out,
    up_out,
    down_out,
    gains_out,
    n2,
    dy,
    hid,
    dgate,
    dup,
    n1,
    dqkv,
    att,
    da,
    v_a,
    v_b,
    r1_a,
    r1_b,
    s1_a,
    s1_b,
    r2_a,
    r2_b,
    s2_a,
    s2_b,
    r3_a,
    r3_b,
    g_a,
    g_b,
    their_gate,
    their_up,
    their_down,
    part_gate,
    part_up,
    part_down,
    own_gate,
    own_up,
    own_down,
    small,
    small_recv,
    load_sem,
    send_sem,
    recv_sem,
    pair_send,
    pair_recv,
    small_send,
    small_recv_sem,
    out_sem,
):
    f = lax.axis_index("fsdp")
    e = lax.axis_index("expert")
    y, x, z = e // 8, lax.rem(e // 4, 2), lax.rem(e, 4)
    other = 1 - f
    own_half = aligned(f * HALF, HALF, 128)
    other_half = aligned(other * HALF, HALF, 128)
    own_quarter = aligned(f * (HIDDEN // 2), HIDDEN // 2, 128)
    other_quarter = aligned(other * (HIDDEN // 2), HIDDEN // 2, 128)

    def along_y(d):
        return {"expert": lax.rem(y + d, 4) * 8 + x * 4 + z}

    def along_z(d):
        return {"expert": y * 8 + x * 4 + lax.rem(z + d, 4)}

    twin = {"expert": y * 8 + (1 - x) * 4 + z}
    partner = {"fsdp": other}

    barrier = pltpu.get_barrier_semaphore()
    neighbours = [along_y(d) for d in (1, 2, 3)] + [along_z(d) for d in (1, 2, 3)]
    neighbours += [twin, partner]
    for place in neighbours:
        pl.semaphore_signal(barrier, inc=1, device_id=place, device_id_type=MESH)

    loads = [
        (att_in, att),
        (da_in, da),
        (n1_in, n1),
        (dqkv_in, dqkv),
        (n2_in, n2),
        (dgate_in, dgate),
        (dup_in, dup),
        (hid_in, hid),
        (dy_in, dy),
    ]
    loads = [pltpu.make_async_copy(a, b, load_sem.at[i]) for i, (a, b) in enumerate(loads)]
    for copy in loads:
        copy.start()

    def remote(src, dst, send, recv, place):
        return pltpu.make_async_remote_copy(
            src_ref=src,
            dst_ref=dst,
            send_sem=send,
            recv_sem=recv,
            device_id=place,
            device_id_type=MESH,
        )

    def wait_for(ref, sem):
        pltpu.make_async_copy(ref, ref, sem).wait()

    for copy in loads[:2]:
        copy.wait()

    @pl.loop(0, WIDTH // 512)
    def _(j):
        cols = aligned(j * 512, 512, 128)
        v_b[:, cols] = dot_tn(att[...], da[:, cols]).astype(BF)

    for copy in loads[2:4]:
        copy.wait()

    def over_micro(cols):
        block = jnp.concatenate([dqkv[m, :, :, cols] for m in range(MB)], axis=1)
        return [dot_tn(n1[...], block[g]).astype(BF) for g in range(2)]

    for g, block in enumerate(over_micro(pl.ds(HALF + HEAD, HEAD))):
        v_b[:, pl.ds(WIDTH + g * HEAD, HEAD)] = block
    pl.semaphore_wait(barrier, len(neighbours))

    lanes = (
        (0, v_a, r1_a, s1_a, r2_a, s2_a, r3_a, g_a, along_y, y, along_z, z),
        (1, v_b, r1_b, s1_b, r2_b, s2_b, r3_b, g_b, along_z, z, along_y, y),
    )

    def spread_one(lane):
        i, v, r1, _, _, _, _, _, axis, at, _, _ = lane
        for d in (1, 2, 3):
            rows = aligned(lax.rem(at + d, 4) * BAND, BAND, 16)
            remote(v.at[rows], r1.at[at], send_sem.at[i, 0], recv_sem.at[i, 0], axis(d)).start()

    spread_one(lanes[1])
    for j in range(3):
        for g, block in enumerate(over_micro(pl.ds(j * 256, 256))):
            v_a[:, pl.ds(g * HALF + j * 256, 256)] = block
    for g, block in enumerate(over_micro(pl.ds(HALF, HEAD))):
        v_a[:, pl.ds(WIDTH + g * HEAD, HEAD)] = block
    spread_one(lanes[0])

    small[...] = gains_in[...]
    small_pair = remote(
        small.at[:, other_half],
        small_recv.at[0],
        small_send.at[0],
        small_recv_sem.at[0],
        partner,
    )
    small_pair.start()

    for copy in loads[4:6]:
        copy.wait()
    their_gate[...] = dot_tn(n2[:, other_half], dgate[...]).astype(BF)
    pair = [remote(their_gate, part_gate, pair_send.at[0], pair_recv.at[0], partner)]
    pair[0].start()
    loads[6].wait()
    their_up[...] = dot_tn(n2[:, other_half], dup[...]).astype(BF)
    pair.append(remote(their_up, part_up, pair_send.at[1], pair_recv.at[1], partner))
    pair[1].start()
    for copy in loads[7:]:
        copy.wait()
    their_down[...] = dot_tn(hid[:, other_quarter], dy[...]).astype(BF)
    pair.append(remote(their_down, part_down, pair_send.at[2], pair_recv.at[2], partner))
    pair[2].start()
    own_gate[...] = dot_tn(n2[:, own_half], dgate[...])
    own_up[...] = dot_tn(n2[:, own_half], dup[...])
    own_down[...] = dot_tn(hid[:, own_quarter], dy[...])

    def spread_small(i, axis):
        for d in (1, 2, 3):
            remote(
                small.at[:, pl.ds(0, HALF)],
                small_recv.at[1 + 3 * i + d - 1],
                small_send.at[1 + 3 * i + d - 1],
                small_recv_sem.at[1 + 3 * i + d - 1],
                axis(d),
            ).start()

    def join_small(i, axis):
        for d in (1, 2, 3):
            remote(
                small.at[:, pl.ds(0, HALF)],
                small_recv.at[1 + 3 * i + d - 1],
                small_send.at[1 + 3 * i + d - 1],
                small_recv_sem.at[1 + 3 * i + d - 1],
                axis(d),
            ).wait()
        total = small[:, pl.ds(0, HALF)]
        for d in (1, 2, 3):
            total = total + small_recv[1 + 3 * i + d - 1]
        small[:, pl.ds(0, HALF)] = total

    small_pair.wait()
    small[:, pl.ds(0, HALF)] = small[:, own_half] + small_recv[0]
    spread_small(0, along_y)

    def join_one(lane):
        i, v, r1, s1, r2, _, _, _, _, at, axis, to = lane
        wait_for(r1.at[pl.ds(0, 3)], recv_sem.at[i, 0])
        total = v[aligned(at * BAND, BAND, 16)].astype(F32)
        for d in (1, 2, 3):
            total = total + r1[lax.rem(at + d, 4)].astype(F32)
        s1[...] = total.astype(BF)
        for d in (1, 2, 3):
            rows = aligned(lax.rem(to + d, 4) * SLICE, SLICE, 16)
            remote(s1.at[rows], r2.at[to], send_sem.at[i, 1], recv_sem.at[i, 1], axis(d)).start()

    join_one(lanes[1])
    join_one(lanes[0])
    join_small(0, along_y)
    spread_small(1, along_z)

    mine = aligned(x * NARROW, NARROW, 128)
    theirs = aligned((1 - x) * NARROW, NARROW, 128)

    def join_two(lane):
        i, _, _, s1, r2, s2, r3, _, _, _, _, to = lane
        wait_for(r2.at[pl.ds(0, 3)], recv_sem.at[i, 1])
        total = s1[aligned(to * SLICE, SLICE, 16)].astype(F32)
        for d in (1, 2, 3):
            total = total + r2[lax.rem(to + d, 4)].astype(F32)
        s2[...] = total.astype(BF)
        remote(s2.at[:, theirs], r3, send_sem.at[i, 2], recv_sem.at[i, 2], twin).start()

    join_two(lanes[1])
    join_two(lanes[0])
    join_small(1, along_z)
    small_twin = remote(
        small.at[:, pl.ds(0, HALF)],
        small_recv.at[7],
        small_send.at[7],
        small_recv_sem.at[7],
        twin,
    )
    small_twin.start()

    def place_of(lane):
        _, _, _, _, _, _, _, _, _, at, _, to = lane
        return aligned(at * BAND + to * SLICE, SLICE, 16)

    def join_three(lane):
        i, _, _, _, _, s2, r3, g, _, _, _, _ = lane
        wait_for(r3, recv_sem.at[i, 2])
        total = s2[:, mine].astype(F32) + r3[...].astype(F32)
        g[place_of(lane), mine] = total.astype(BF)
        part = g.at[place_of(lane), mine]
        remote(part, part, send_sem.at[i, 3], recv_sem.at[i, 3], twin).start()

    def gather_two(lane):
        i, _, _, _, _, _, _, g, _, _, axis, _ = lane
        wait_for(g.at[place_of(lane), theirs], recv_sem.at[i, 3])
        part = g.at[place_of(lane)]
        for d in (1, 2, 3):
            remote(part, part, send_sem.at[i, 4], recv_sem.at[i, 4], axis(d)).start()

    def gather_one(lane):
        i, _, _, _, _, _, _, g, axis, at, _, _ = lane
        wait_for(g.at[pl.ds(0, 3 * SLICE)], recv_sem.at[i, 4])
        part = g.at[aligned(at * BAND, BAND, 16)]
        for d in (1, 2, 3):
            remote(part, part, send_sem.at[i, 5], recv_sem.at[i, 5], axis(d)).start()

    for step in (join_three, gather_two, gather_one):
        step(lanes[1])
        step(lanes[0])

    small_twin.wait()
    gains_out[...] = small[:, pl.ds(0, HALF)] + small_recv[7]

    def out_copy(i, src, dst):
        copy = pltpu.make_async_copy(src, dst, out_sem.at[i])
        copy.start()
        return copy

    outs = []
    for i, (arrived, part, own, dst) in enumerate(
        (
            (pair[0], part_gate, own_gate, gate_out),
            (pair[1], part_up, own_up, up_out),
            (pair[2], part_down, own_down, down_out),
        )
    ):
        arrived.wait_recv()
        part[...] = (own[...] + part[...].astype(F32)).astype(BF)
        outs.append(out_copy(i, part, dst))

    wait_for(g_b.at[pl.ds(0, 3 * BAND)], recv_sem.at[1, 5])
    outs.append(out_copy(3, g_b.at[:, pl.ds(0, WIDTH)], o_out))
    outs.append(out_copy(4, g_b.at[:, pl.ds(WIDTH, 256)], v_out))
    wait_for(g_a.at[pl.ds(0, 3 * BAND)], recv_sem.at[0, 5])
    outs.append(out_copy(5, g_a.at[:, pl.ds(0, WIDTH)], q_out))
    outs.append(out_copy(6, g_a.at[:, pl.ds(WIDTH, 256)], k_out))

    for lane in lanes:
        i, v, _, s1, _, s2, _, g = lane[:8]
        wait_for(v.at[pl.ds(0, 3 * BAND)], send_sem.at[i, 0])
        wait_for(s1.at[pl.ds(0, 3 * SLICE)], send_sem.at[i, 1])
        wait_for(s2.at[:, theirs], send_sem.at[i, 2])
        wait_for(g.at[place_of(lane), mine], send_sem.at[i, 3])
        wait_for(g.at[pl.ds(0, 3 * SLICE)], send_sem.at[i, 4])
        wait_for(g.at[pl.ds(0, 3 * BAND)], send_sem.at[i, 5])
    for copy in pair:
        copy.wait_send()
    for copy in outs:
        copy.wait()


def reduce_grads(*operands):
    def out(*shape):
        return jax.ShapeDtypeStruct(shape, BF)

    vmem = pl.BlockSpec(memory_space=pltpu.VMEM)
    anywhere = pl.BlockSpec(memory_space=pl.ANY)
    dma = pltpu.SemaphoreType.DMA
    lane = [
        pltpu.VMEM((HALF, WIDE), BF),
        pltpu.VMEM((4, BAND, WIDE), BF),
        pltpu.VMEM((BAND, WIDE), BF),
        pltpu.VMEM((4, SLICE, WIDE), BF),
        pltpu.VMEM((SLICE, WIDE), BF),
        pltpu.VMEM((SLICE, NARROW), BF),
        pltpu.VMEM((HALF, WIDE), BF),
    ]
    expert = [
        pltpu.VMEM((HALF, HIDDEN), BF),
        pltpu.VMEM((HALF, HIDDEN), BF),
        pltpu.VMEM((HIDDEN // 2, WIDTH), BF),
    ]
    return pl.pallas_call(
        grads_kernel,
        name="grads",
        out_shape=(
            out(HALF, WIDTH),
            out(HALF, 256),
            out(HALF, 256),
            out(HALF, WIDTH),
            out(HALF, HIDDEN),
            out(HALF, HIDDEN),
            out(HIDDEN // 2, WIDTH),
            jax.ShapeDtypeStruct((8, HALF), F32),
        ),
        in_specs=[anywhere] * 9 + [vmem],
        out_specs=[anywhere] * 7 + [vmem],
        scratch_shapes=[
            pltpu.VMEM((MB * ROWS, WIDTH), BF),
            pltpu.VMEM((MB * ROWS, WIDTH), BF),
            pltpu.VMEM((MB * ROWS, HIDDEN), BF),
            pltpu.VMEM((MB * ROWS, HIDDEN), BF),
            pltpu.VMEM((MB * ROWS, HIDDEN), BF),
            pltpu.VMEM((MB * 2 * SEQ, HALF), BF),
            pltpu.VMEM((MB, 2, 2 * SEQ, QKV), BF),
            pltpu.VMEM((MB * 2 * SEQ, HALF), BF),
            pltpu.VMEM((MB * 2 * SEQ, WIDTH), BF),
        ]
        + [part for shape in lane for part in (shape, shape)]
        + expert
        + expert
        + [
            pltpu.VMEM((HALF, HIDDEN), F32),
            pltpu.VMEM((HALF, HIDDEN), F32),
            pltpu.VMEM((HIDDEN // 2, WIDTH), F32),
            pltpu.VMEM((8, WIDTH), F32),
            pltpu.VMEM((8, 8, HALF), F32),
            dma((9,)),
            dma((2, 6)),
            dma((2, 6)),
            dma((3,)),
            dma((3,)),
            dma((8,)),
            dma((8,)),
            dma((7,)),
        ],
        compiler_params=pltpu.CompilerParams(
            collective_id=1, has_side_effects=True, vmem_limit_bytes=62 * 2**20
        ),
    )(*operands)


def local(
    inputs,
    cotangent,
    segments,
    expert_ids,
    gate_logits,
    w_query,
    key_projection,
    value_projection,
    w_out,
    gain_attn,
    gain_moe,
    w_gate,
    w_up,
    w_down,
):
    side = jnp.concatenate(
        [
            gain_attn.astype(F32),
            gain_moe.astype(F32),
            jnp.pad(segments.astype(F32), ((0, 0), (0, HALF - SEQ))),
            jnp.zeros((4, HALF), F32),
        ],
        axis=0,
    )
    meta = jnp.concatenate([expert_ids[0].astype(F32), gate_logits[0]], axis=-1)
    meta = jnp.swapaxes(meta, 1, 2)
    steps = np.arange(HEAD) % (HEAD // 2)
    frequency = (ROPE_BASE ** (-steps * 2.0 / HEAD)).astype(np.float32)[None]
    (
        acts,
        in_grads,
        gain_parts,
        n2rows,
        dyrows,
        hid,
        dgate,
        dup,
        n1,
        dqkv,
        att,
        da,
    ) = run_sections(
        inputs,
        cotangent,
        w_query[0],
        key_projection[0],
        value_projection[0],
        w_out[0],
        w_gate[0, 0],
        w_up[0, 0],
        w_down[0, 0],
        side,
        meta,
        jnp.asarray(frequency),
    )
    gq, gk, gv, go, grad_gate, grad_up, grad_down, gains = reduce_grads(
        n2rows.reshape(MB * ROWS, WIDTH),
        dyrows.reshape(MB * ROWS, WIDTH),
        hid.reshape(MB * ROWS, HIDDEN),
        dgate.reshape(MB * ROWS, HIDDEN),
        dup.reshape(MB * ROWS, HIDDEN),
        n1.reshape(MB * 2 * SEQ, HALF),
        dqkv,
        att.reshape(MB * 2 * SEQ, HALF),
        da.reshape(MB * 2 * SEQ, WIDTH),
        gain_parts,
    )
    return (
        acts[None],
        in_grads[None],
        gq[None].astype(F32),
        gk[None].astype(F32),
        gv[None].astype(F32),
        go[None].astype(F32),
        gains[0:1],
        gains[1:2],
        grad_gate[None, None].astype(F32),
        grad_up[None, None].astype(F32),
        grad_down[None, None].astype(F32),
    )


def solution(mesh):
    return jax.shard_map(
        local,
        mesh=mesh,
        in_specs=(
            P(None, ("fsdp", "expert"), None),
            P(None, ("fsdp", "expert"), None),
            P(None, ("fsdp", "expert")),
            P("section", None, ("fsdp", "expert"), None),
            P("section", None, ("fsdp", "expert"), None),
            P("section", "fsdp", None),
            P("section", "fsdp", None),
            P("section", "fsdp", None),
            P("section", "fsdp", None),
            P("section", "fsdp"),
            P("section", "fsdp"),
            P("section", "expert", "fsdp", None),
            P("section", "expert", "fsdp", None),
            P("section", "expert", "fsdp", None),
        ),
        out_specs=(
            P("section", None, ("fsdp", "expert"), None),
            P("section", None, ("fsdp", "expert"), None),
            P("section", "fsdp", None),
            P("section", "fsdp", None),
            P("section", "fsdp", None),
            P("section", "fsdp", None),
            P("section", "fsdp"),
            P("section", "fsdp"),
            P("section", "expert", "fsdp", None),
            P("section", "expert", "fsdp", None),
            P("section", "expert", "fsdp", None),
        ),
        check_vma=False,
    )
```

```python
import functools

import jax
import jax.numpy as jnp
import numpy as np
from jax import lax
from jax.experimental import pallas as pl
from jax.experimental.pallas import tpu as pltpu
from jax.sharding import PartitionSpec as P

MESH = pl.DeviceIdType.MESH
BF = jnp.bfloat16
F32 = jnp.float32

HEAD = 128
EPS = 1e-06
ROPE_BASE = 1000000.0
GELU_C = 0.7978845608
GELU_A = 0.044715

MB = 2
SEQ = 96
WIDTH = 1536
HALF = 768
EXPERTS = 32
PLANE = 16
SLOTS = 16
ROWS = EXPERTS * SLOTS
HIDDEN = 768
HEADS = 6
QKV = 1024


def dot(a, b):
    return jnp.dot(a, b, preferred_element_type=F32)


def dot_nt(a, b):
    return lax.dot_general(a, b, (((1,), (1,)), ((), ())), preferred_element_type=F32)


def dot_tn(a, b):
    return lax.dot_general(a, b, (((0,), (0,)), ((), ())), preferred_element_type=F32)


def aligned(start, size, unit):
    return pl.ds(pl.multiple_of(start, unit), size)


def inverse_rms(rows):
    return lax.rsqrt(jnp.mean(rows * rows, axis=-1, keepdims=True) + EPS)


def rms_back(rows, inverse, gain, grad):
    scaled = gain * grad
    return inverse * scaled - rows * (inverse * inverse * inverse) * jnp.mean(
        scaled * rows, axis=-1, keepdims=True
    )


def rotate(head, cos, sin):
    return head * cos + pltpu.roll(head, HEAD // 2, 1) * sin


(ATTEND, NORM, TWIN, HIDE, GIVE, FAR, JOIN, GRAD, GRAD_TWIN, BACK, FAR_BACK, MID, ATTEND_BACK, CLOSE, LOAD, GRADS_IN, GRADS_OUT, REST) = range(18)

FIRST_PLAN = (
    (ATTEND, 0),
    (ATTEND, 1),
    (NORM, 0),
    (NORM, 1),
    (TWIN, 0),
    (TWIN, 1),
    (HIDE, 0),
    (HIDE, 1),
    (GIVE, 0),
    (GIVE, 1),
    (FAR, 0),
    (JOIN, 0),
    (FAR, 1),
    (JOIN, 1),
    (GRAD, 0),
    (GRAD_TWIN, 0),
    (GRAD, 1),
    (GRAD_TWIN, 1),
    (BACK, 0),
    (BACK, 1),
    (GRADS_IN, 0),
    (FAR_BACK, 0),
    (GRADS_IN, 1),
    (MID, 0),
    (GRADS_OUT, 0),
    (FAR_BACK, 1),
    (ATTEND_BACK, 0),
    (MID, 1),
    (GRADS_OUT, 1),
    (CLOSE, 0),
    (ATTEND_BACK, 1),
    (CLOSE, 1),
)
SECOND_PLAN = (
    (GRAD, 0),
    (GRAD, 1),
    (LOAD, 0),
    (ATTEND, 0),
    (ATTEND, 1),
    (NORM, 0),
    (NORM, 1),
    (TWIN, 0),
    (TWIN, 1),
    (GRAD_TWIN, 0),
    (GRAD_TWIN, 1),
    (HIDE, 0),
    (BACK, 0),
    (HIDE, 1),
    (BACK, 1),
    (GIVE, 0),
    (GIVE, 1),
    (FAR_BACK, 0),
    (GRADS_IN, 0),
    (MID, 0),
    (FAR_BACK, 1),
    (ATTEND_BACK, 0),
    (MID, 1),
    (GRADS_IN, 1),
    (CLOSE, 0),
    (ATTEND_BACK, 1),
    (GRADS_OUT, 0),
    (CLOSE, 1),
    (GRADS_OUT, 1),
    (FAR, 0),
    (FAR, 1),
    (JOIN, 0),
    (JOIN, 1),
)


def section_kernel(
    x_in,
    ct_in,
    wq_in,
    wk_in,
    wv_in,
    wo_in,
    wg_in,
    wu_in,
    wd_in,
    gain_one_in,
    gain_two_in,
    segments_in,
    ids_in,
    logits_in,
    freq_in,
    acts_out,
    ingrad_out,
    gains_out,
    own_gate_out,
    own_up_out,
    own_down_out,
    their_gate_out,
    their_up_out,
    their_down_out,
    n1_out,
    dqkv_out,
    att_out,
    da_out,
    wqkv,
    wo,
    wg,
    wu,
    wd,
    xpair,
    n1s,
    qkvs,
    att,
    hid_one,
    part_own,
    part_send,
    part_recv,
    sel,
    cg_hi,
    cg_lo,
    n2pair,
    gpair,
    dsend,
    bsend,
    n2recv,
    yrecv,
    dyrecv,
    dn2recv,
    gs,
    us,
    hid,
    far_send,
    far_recv,
    acts_s,
    dh_s,
    da_pair,
    dqkv_all,
    dn1_send,
    dn1_recv,
    ingrad_s,
    gains_acc,
    side,
    meta,
    gains,
    cos_t,
    sin_t,
    mask_t,
    lw_sem,
    ws_sem,
    wr_sem,
    as_sem,
    ar_sem,
    ps_sem,
    pr_sem,
    ts_sem,
    tr_sem,
    xs_sem,
    xr_sem,
    gs_sem,
    gr_sem,
    out_sem,
    go_sem,
):
    sec = lax.axis_index("section")
    f = lax.axis_index("fsdp")
    e = lax.axis_index("expert")
    y, x, z = e // 8, lax.rem(e // 4, 2), lax.rem(e, 4)
    q = y * 4 + z
    away = 1 - x
    other = 1 - f
    own_rows = aligned(f * SEQ, SEQ, 16)
    other_rows = aligned(other * SEQ, SEQ, 16)
    own_half = aligned(f * HALF, HALF, 128)
    other_half = aligned(other * HALF, HALF, 128)
    partner = {"fsdp": other}
    twin_place = y * 8 + away * 4 + z
    twin = {"expert": twin_place}
    first, second = sec == 0, sec == 1

    def in_plane(d):
        at = lax.rem(q + d, PLANE)
        return at, {"expert": (at // 4) * 8 + x * 4 + lax.rem(at, 4)}

    barrier = pltpu.get_barrier_semaphore()

    @pl.loop(1, PLANE)
    def _(d):
        pl.semaphore_signal(barrier, inc=1, device_id=in_plane(d)[1], device_id_type=MESH)

    others = (
        twin,
        partner,
        {"section": 1 - sec},
        {"section": 1 - sec, "fsdp": other},
        {"section": 1 - sec, "expert": twin_place},
    )
    for place in others:
        pl.semaphore_signal(barrier, inc=1, device_id=place, device_id_type=MESH)

    local = [
        (wq_in.at[:, own_half], wqkv.at[own_half, pl.ds(0, HALF)]),
        (wk_in.at[:, aligned(f * HEAD, HEAD, 128)], wqkv.at[own_half, pl.ds(HALF, HEAD)]),
        (wv_in.at[:, aligned(f * HEAD, HEAD, 128)], wqkv.at[own_half, pl.ds(HALF + HEAD, HEAD)]),
        (wo_in, wo),
        (wg_in, wg.at[own_half]),
        (wu_in, wu.at[own_half]),
        (wd_in, wd.at[aligned(f * (HIDDEN // 2), HIDDEN // 2, 16)]),
    ]
    local = [pltpu.make_async_copy(a, b, lw_sem.at[i]) for i, (a, b) in enumerate(local)]
    for copy in local:
        copy.start()
    x_local = pltpu.make_async_copy(x_in, xpair.at[:, own_rows], lw_sem.at[7])
    ct_local = pltpu.make_async_copy(ct_in, gpair.at[:, x], lw_sem.at[8])
    pl.when(first)(x_local.start)
    pl.when(second)(ct_local.start)

    def remote(src, dst, send, recv, place):
        return pltpu.make_async_remote_copy(
            src_ref=src,
            dst_ref=dst,
            send_sem=send,
            recv_sem=recv,
            device_id=place,
            device_id_type=MESH,
        )

    def wait_for(ref, sem):
        pltpu.make_async_copy(ref, ref, sem).wait()

    def weight(src, dst, i):
        return remote(src, dst, ws_sem.at[i], wr_sem.at[i], partner)

    w_attn = [
        weight(wq_in.at[:, other_half], wqkv.at[own_half, pl.ds(0, HALF)], 0),
        weight(
            wk_in.at[:, aligned(other * HEAD, HEAD, 128)],
            wqkv.at[own_half, pl.ds(HALF, HEAD)],
            1,
        ),
        weight(
            wv_in.at[:, aligned(other * HEAD, HEAD, 128)],
            wqkv.at[own_half, pl.ds(HALF + HEAD, HEAD)],
            2,
        ),
    ]
    w_moe = [
        weight(wg_in, wg.at[own_half], 3),
        weight(wu_in, wu.at[own_half], 4),
        weight(wd_in, wd.at[aligned(f * (HIDDEN // 2), HIDDEN // 2, 16)], 5),
    ]

    w_pieces = [
        weight(src.at[aligned(i * size, size, 16)], dst.at[aligned(f * 4 * size + i * size, size, 16)], n)
        for n, src, dst, size in (
            (3, wg_in, wg, HALF // 4),
            (4, wu_in, wu, HALF // 4),
            (5, wd_in, wd, HIDDEN // 8),
        )
        for i in range(4)
    ]

    def send_pieces(start, stop):
        for copy in w_pieces[start:stop]:
            copy.start()

    def x_copy(m):
        return weight(x_in.at[m], xpair.at[m, own_rows], 6 + m)

    def ct_copy(m):
        return remote(ct_in.at[m], gpair.at[m, x], ws_sem.at[10 + m], gr_sem.at[x, m], twin)

    side[f, 0:1] = gain_one_in[...].astype(F32)
    side[f, 1:2] = gain_two_in[...].astype(F32)
    side[f, 2:4, :SEQ] = segments_in[...].astype(F32)
    row = lax.broadcasted_iota(jnp.int32, (SEQ, SEQ), 0)
    col = lax.broadcasted_iota(jnp.int32, (SEQ, SEQ), 1)
    unit = jnp.where(row == col, 1.0, 0.0).astype(BF)
    for m in range(MB):
        left = logits_in[m]
        turned = jnp.zeros((4, SEQ), F32)
        for _ in range(3):
            high = left.astype(BF)
            left = left - high.astype(F32)
            turned = turned + dot_tn(high, unit)
        meta[x, m, 0:4] = dot_tn(ids_in[m].astype(F32).astype(BF), unit)
        meta[x, m, 4:8] = turned
    side_copy = weight(side.at[f], side.at[f], 8)
    meta_copy = remote(meta.at[x], meta.at[x], ws_sem.at[9], wr_sem.at[9], twin)
    gains_acc[...] = jnp.zeros_like(gains_acc)

    pl.semaphore_wait(barrier, PLANE - 1 + len(others))
    side_copy.start()
    meta_copy.start()

    @pl.when(first)
    def _():
        x_copy(0).start()
        for copy in w_attn:
            copy.start()
        x_copy(1).start()

    meta_copy.wait_recv()
    earlier = jnp.where(row < col, 1.0, 0.0).astype(BF)

    @pl.loop(0, 2 * MB)
    def _(i):
        m, source = lax.rem(i, MB), i // MB
        rows = meta[source, m]
        ids, logits = rows[:4], rows[4:]
        raised = jnp.exp(logits - jnp.max(logits, axis=0, keepdims=True))
        gates = raised / jnp.sum(raised, axis=0, keepdims=True)
        place = lax.broadcasted_iota(jnp.int32, (PLANE, SEQ), 0)
        expert = ((place // 4) * 8 + x * 4 + lax.rem(place, 4)).astype(F32)
        named = jnp.zeros((PLANE, SEQ), F32)
        weights = jnp.zeros((PLANE, SEQ), F32)
        for k in range(4):
            hit = expert == ids[k : k + 1, :]
            named = jnp.where(hit, 1.0, named)
            weights = jnp.where(hit, gates[k : k + 1, :], weights)
        slot = dot(named.astype(BF), earlier)
        slot = jnp.where(named > 0.0, slot, -1.0)
        shape = (PLANE, SLOTS, SEQ)
        count = lax.broadcasted_iota(jnp.int32, shape, 1).astype(F32)
        chosen = jnp.where(jnp.broadcast_to(slot[:, None, :], shape) == count, 1.0, 0.0)
        scaled = chosen * jnp.broadcast_to(weights[:, None, :], shape)
        scaled = scaled.reshape(PLANE * SLOTS, SEQ)
        high = scaled.astype(BF)
        sel[m, source] = chosen.reshape(PLANE * SLOTS, SEQ).astype(BF)
        cg_hi[m, source] = high
        cg_lo[m, source] = (scaled - high.astype(F32)).astype(BF)

    side_copy.wait_recv()
    gains[:, pl.ds(0, HALF)] = side[0, 0:2]
    gains[:, pl.ds(HALF, HALF)] = side[1, 0:2]
    lane = lax.broadcasted_iota(jnp.int32, (SEQ, HEAD), 1)
    turn = jnp.where(lane < HEAD // 2, -1.0, 1.0)
    for m in range(MB):
        for s in range(2):
            across = jnp.broadcast_to(side[s, 2 + m : 3 + m, :SEQ], (SEQ, SEQ))
            down = dot_nt(unit, across.astype(BF))
            same = jnp.where(down == across, 1.0, 0.0)
            mask_t[m, s] = jnp.where(col <= row, same, 0.0)
            places = jnp.sum(jnp.where(col < row, same, 0.0), axis=1, keepdims=True)
            angles = places * freq_in[...]
            cos_t[m, pl.ds(s * SEQ, SEQ)] = jnp.cos(angles)
            sin_t[m, pl.ds(s * SEQ, SEQ)] = jnp.sin(angles) * turn

    def exchange_half(kind, m, src, dst, source):
        @pl.loop(1, PLANE)
        def _(d):
            at, place = in_plane(d)
            remote(
                src.at[m, at, source],
                dst.at[m, q, source],
                as_sem.at[kind, m],
                ar_sem.at[kind, m],
                place,
            ).start()

        dst[m, q, source] = src[m, q, source]

    def exchange(kind, m, src, dst):
        @pl.loop(1, PLANE)
        def _(d):
            at, place = in_plane(d)
            remote(
                src.at[m, at], dst.at[m, q], as_sem.at[kind, m], ar_sem.at[kind, m], place
            ).start()

        dst[m, q] = src[m, q]

    def received(kind, m, dst):
        wait_for(dst.at[m, pl.ds(0, PLANE - 1)], ar_sem.at[kind, m])

    def sent(kind, m, src):
        wait_for(src.at[m, pl.ds(0, PLANE - 1)], as_sem.at[kind, m])

    def to_partner(kind, m, src, dst):
        return remote(src, dst, ps_sem.at[kind, m], pr_sem.at[kind, m], partner)

    def to_twin(kind, m, src, dst):
        return remote(src, dst, ts_sem.at[kind, m], tr_sem.at[kind, m], twin)

    def n2_copy(m):
        return to_twin(0, m, n2pair.at[m, x], n2pair.at[m, x])

    def far_copy(kind, m):
        return to_twin(kind, m, far_send.at[kind - 1, m], far_recv.at[kind - 1, m])

    def acts_copy(m, cross):
        place = {"section": 1, "fsdp": other} if cross else {"section": 1}
        return remote(
            acts_s.at[m], xpair.at[m, own_rows], xs_sem.at[cross, m], xr_sem.at[f, m], place
        )

    def grad_copy(m, cross):
        place = {"section": 0, "expert": twin_place} if cross else {"section": 0}
        return remote(
            ingrad_s.at[m], gpair.at[m, x], gs_sem.at[cross, m], gr_sem.at[x, m], place
        )

    def out_copy(i, src, dst, m):
        return pltpu.make_async_copy(src, dst, out_sem.at[i, m])

    def flat(ref, m):
        return ref[m].reshape(ROWS, WIDTH)

    def spread(m, source, rows, dst, scale=None):
        @pl.loop(0, WIDTH // 512)
        def _(j):
            cols = aligned(j * 512, 512, 128)
            block = dot(sel[m, source], rows[m, source, :, cols])
            if scale is not None:
                block = block * scale
            dst[m, :, source, :, cols] = block.astype(BF).reshape(PLANE, SLOTS, 512)

    def load_step(m):
        pl.semaphore_wait(go_sem, 1)
        for copy in w_attn:
            copy.start()

    def heads_of(ref, m, rows):
        return jnp.concatenate(
            [ref[m, rows, pl.ds(h * HEAD, HEAD)] for h in range(HEADS)], axis=0
        )

    def softmax_of(m, s, queries, keys):
        scores = dot_nt(queries, keys) * HEAD ** (-0.5)
        allowed = jnp.concatenate([mask_t[m, s]] * HEADS, axis=0)
        scores = jnp.where(allowed > 0.0, scores, -1e30)
        raised = jnp.exp(scores - jnp.max(scores, axis=-1, keepdims=True))
        return raised / jnp.sum(raised, axis=-1, keepdims=True)

    def attend_step(m):
        @pl.when(m == 0)
        def _():
            for copy in local[:4]:
                copy.wait()
            for copy in w_attn:
                copy.wait_recv()
            for copy in w_attn:
                copy.wait_send()
            pl.when(first)(x_local.wait)

            send_pieces(0, 1)

            @pl.when(second)
            def _():
                ct_copy(0).start()
                ct_copy(1).start()
                send_pieces(1, 4)

        @pl.when(first)
        def _():
            x_copy(m).wait_recv()

        @pl.when(second)
        def _():
            for at, rows in ((f, own_rows), (other, other_rows)):
                wait_for(xpair.at[m, rows], xr_sem.at[at, m])

        rows = xpair[m].astype(F32)
        n1s[m] = (rows * inverse_rms(rows) * gains[0:1]).astype(BF)
        cos, sin = cos_t[m], sin_t[m]
        for j in range(4):
            block = dot(n1s[m], wqkv[:, pl.ds(j * 256, 256)])
            qkvs[m, :, pl.ds(j * 256, HEAD)] = rotate(block[:, :HEAD], cos, sin).astype(BF)
            late = block[:, HEAD:]
            if j < 3:
                late = rotate(late, cos, sin)
            qkvs[m, :, pl.ds(j * 256 + HEAD, HEAD)] = late.astype(BF)

        @pl.loop(0, 2)
        def _(s):
            at = aligned(s * SEQ, SEQ, 16)
            queries = heads_of(qkvs, m, at)
            keys = qkvs[m, at, pl.ds(HALF, HEAD)]
            values = qkvs[m, at, pl.ds(HALF + HEAD, HEAD)]
            probs = softmax_of(m, s, queries, keys).astype(BF)
            mixed = dot(probs, values).astype(BF)
            for h in range(HEADS):
                att[m, at, pl.ds(h * HEAD, HEAD)] = mixed[h * SEQ : (h + 1) * SEQ]

        @pl.loop(0, WIDTH // 512)
        def _(j):
            cols = aligned(j * 512, 512, 128)
            block = dot(att[m], wo[:, cols])
            top, low = block[:SEQ], block[SEQ:]
            mine = f == 0
            hid_one[m, :, cols] = jnp.where(mine, top, low)
            part_send[m, :, cols] = jnp.where(mine, low, top).astype(BF)

        to_partner(0, m, part_send.at[m], part_recv.at[m]).start()
        pl.when(jnp.logical_and(first, m == 0))(lambda: send_pieces(1, 2))
        pl.when(jnp.logical_and(first, m == 1))(lambda: send_pieces(2, 4))

    def norm_step(m):
        to_partner(0, m, part_send.at[m], part_recv.at[m]).wait_recv()
        rows = xpair[m, own_rows].astype(F32) + (hid_one[m] + part_recv[m].astype(F32))
        hid_one[m] = rows
        n2pair[m, x] = (rows * inverse_rms(rows) * gains[1:2]).astype(BF)
        n2_copy(m).start()
        pl.when(m == 0)(lambda: send_pieces(4, 5))
        pl.when(m == 1)(lambda: send_pieces(5, 12))
        spread(m, x, n2pair, dsend)
        exchange_half(0, m, dsend, n2recv, x)

    def twin_step(m):
        n2_copy(m).wait_recv()
        spread(m, away, n2pair, dsend)
        exchange_half(0, m, dsend, n2recv, away)

    def hide_step(m):
        @pl.when(m == 0)
        def _():
            for copy in local[4:6]:
                copy.wait()
            for copy in w_moe[:2]:
                copy.wait_recv()

        received(0, m, n2recv)

        @pl.loop(0, HIDDEN // 256)
        def _(j):
            cols = aligned(j * 256, 256, 128)
            rows = flat(n2recv, m)
            gate = dot(rows, wg[:, cols])
            up = dot(rows, wu[:, cols])
            bend = jnp.tanh(GELU_C * (gate + GELU_A * gate * gate * gate))
            gs[m, :, cols] = gate.astype(BF)
            us[m, :, cols] = up.astype(BF)
            hid[m, :, cols] = (0.5 * gate * (1.0 + bend) * up).astype(BF)


    def need_down():
        local[6].wait()
        w_moe[2].wait_recv()
        for copy in w_moe:
            copy.wait_send()

    def give_step(m):
        @pl.when(jnp.logical_and(first, m == 0))
        def _():
            need_down()
            pl.semaphore_signal(go_sem, inc=1, device_id={"section": 1}, device_id_type=MESH)

        sent(0, m, dsend)

        @pl.loop(0, WIDTH // 512)
        def _(j):
            cols = aligned(j * 512, 512, 128)
            block = dot(hid[m], wd[:, cols]).astype(BF)
            dsend[m, :, :, :, cols] = block.reshape(PLANE, 2, SLOTS, 512)

        exchange(1, m, dsend, yrecv)

    def weighed(m, source, cols):
        block = yrecv[m, :, source, :, cols].reshape(PLANE * SLOTS, 512)
        return dot_tn(cg_hi[m, source], block) + dot_tn(cg_lo[m, source], block)

    def far_step(m):
        received(1, m, yrecv)

        @pl.loop(0, WIDTH // 512)
        def _(j):
            cols = aligned(j * 512, 512, 128)
            far_send[0, m, :, cols] = weighed(m, away, cols).astype(BF)

        far_copy(1, m).start()

        @pl.loop(0, WIDTH // 512)
        def _(j):
            cols = aligned(j * 512, 512, 128)
            part_own[m, :, cols] = hid_one[m, :, cols] + weighed(m, x, cols)

    def join_step(m):
        far_copy(1, m).wait_recv()
        acts_s[m] = (part_own[m] + far_recv[0, m].astype(F32)).astype(BF)

        @pl.when(first)
        def _():
            for cross in (0, 1):
                acts_copy(m, cross).start()

        out_copy(3, acts_s.at[m], acts_out.at[m], m).start()

    def dy_half(m, source):
        gate = cg_hi[m, source].astype(F32) + cg_lo[m, source].astype(F32)
        spread(m, source, gpair, bsend, jnp.sum(gate, axis=1, keepdims=True))
        exchange_half(2, m, bsend, dyrecv, source)

    def grad_step(m):
        @pl.when(first)
        def _():
            wait_for(gpair.at[m, x], gr_sem.at[x, m])

        @pl.when(jnp.logical_and(second, m == 0))
        def _():
            ct_local.wait()

        dy_half(m, x)

    def grad_twin_step(m):
        wait_for(gpair.at[m, away], gr_sem.at[away, m])
        dy_half(m, away)

    def back_step(m):
        pl.when(jnp.logical_and(second, m == 0))(need_down)
        received(2, m, dyrecv)

        @pl.loop(0, HIDDEN // 256)
        def _(j):
            cols = aligned(j * 256, 256, 128)
            dhid = dot_nt(flat(dyrecv, m), wd[cols, :])
            gate = gs[m, :, cols].astype(F32)
            up = us[m, :, cols].astype(F32)
            square = gate * gate
            bend = jnp.tanh(GELU_C * (gate + GELU_A * square * gate))
            half = 0.5 * (1.0 + bend)
            slope = half + 0.5 * gate * (1.0 - bend * bend) * (
                GELU_C * (1.0 + 3.0 * GELU_A * square)
            )
            gs[m, :, cols] = (dhid * up * slope).astype(BF)
            us[m, :, cols] = (dhid * (gate * half)).astype(BF)

        sent(2, m, bsend)

        @pl.loop(0, WIDTH // 512)
        def _(j):
            cols = aligned(j * 512, 512, 128)
            block = dot_nt(gs[m], wg[cols, :]) + dot_nt(us[m], wu[cols, :])
            bsend[m, :, :, :, cols] = block.astype(BF).reshape(PLANE, 2, SLOTS, 512)

        exchange(3, m, bsend, dn2recv)

    def gathered(m, source, cols):
        return dot_tn(
            sel[m, source], dn2recv[m, :, source, :, cols].reshape(PLANE * SLOTS, 512)
        )

    def far_back_step(m):
        received(3, m, dn2recv)

        @pl.loop(0, WIDTH // 512)
        def _(j):
            cols = aligned(j * 512, 512, 128)
            far_send[1, m, :, cols] = gathered(m, away, cols).astype(BF)

        far_copy(2, m).start()

        @pl.loop(0, WIDTH // 512)
        def _(j):
            cols = aligned(j * 512, 512, 128)
            dh_s[m, :, cols] = gathered(m, x, cols)

    def mid_step(m):
        far_copy(2, m).wait_recv()
        rows = hid_one[m]
        inverse = inverse_rms(rows)
        grad = dh_s[m] + far_recv[1, m].astype(F32)
        gains_acc[1:2] += jnp.sum(grad * rows * inverse, axis=0, keepdims=True)
        total = gpair[m, x].astype(F32) + rms_back(rows, inverse, gains[1:2], grad)
        dh_s[m] = total
        da_pair[m, own_rows] = total.astype(BF)
        da_copy(m).start()

    def da_copy(m):
        return to_partner(1, m, da_pair.at[m, own_rows], da_pair.at[m, own_rows])

    def dqkv_copy(m):
        return to_partner(3, m, dqkv_all.at[m, f], dqkv_all.at[m, f])

    def dn1_copy(m):
        return to_partner(2, m, dn1_send.at[m], dn1_recv.at[m])

    def attend_back_step(m):
        da_copy(m).wait_recv()
        out_copy(6, da_pair.at[m], da_out.at[m], m).start()

        @pl.loop(0, 2)
        def _(s):
            at = aligned(s * SEQ, SEQ, 16)
            dmix = dot_nt(da_pair[m, at], wo[...]).astype(BF)
            dmix = jnp.concatenate(
                [dmix[:, h * HEAD : (h + 1) * HEAD] for h in range(HEADS)], axis=0
            )
            queries = heads_of(qkvs, m, at)
            keys = qkvs[m, at, pl.ds(HALF, HEAD)]
            values = qkvs[m, at, pl.ds(HALF + HEAD, HEAD)]
            probs = softmax_of(m, s, queries, keys)
            dprobs = dot_nt(dmix, values)
            dvalues = dot_tn(probs.astype(BF), dmix)
            dscores = probs * (dprobs - jnp.sum(dprobs * probs, axis=-1, keepdims=True))
            dscores = (dscores * HEAD ** (-0.5)).astype(BF)
            cos = cos_t[m, at]
            sin = -sin_t[m, at]
            dkeys = rotate(dot_tn(dscores, queries), cos, sin)
            dqueries = dot(dscores, keys)
            for h in range(HEADS):
                part = rotate(dqueries[h * SEQ : (h + 1) * SEQ], cos, sin)
                dqkv_all[m, f, at, pl.ds(h * HEAD, HEAD)] = part.astype(BF)
            dqkv_all[m, f, at, pl.ds(HALF, HEAD)] = dkeys.astype(BF)
            dqkv_all[m, f, at, pl.ds(HALF + HEAD, HEAD)] = dvalues.astype(BF)

        @pl.loop(0, WIDTH // 512)
        def _(j):
            cols = aligned(j * 512, 512, 128)
            block = dot_nt(dqkv_all[m, f], wqkv[cols, :])
            top, low = block[:SEQ], block[SEQ:]
            mine = f == 0
            part_own[m, :, cols] = jnp.where(mine, top, low)
            dn1_send[m, :, cols] = jnp.where(mine, low, top).astype(BF)

        dn1_copy(m).start()

        @pl.when(m == 1)
        def _():
            dqkv_copy(0).start()
            dqkv_copy(1).start()

    def close_step(m):
        dn1_copy(m).wait_recv()
        grad = part_own[m] + dn1_recv[m].astype(F32)
        rows = xpair[m, own_rows].astype(F32)
        inverse = inverse_rms(rows)
        gains_acc[0:1] += jnp.sum(grad * rows * inverse, axis=0, keepdims=True)
        ingrad_s[m] = (dh_s[m] + rms_back(rows, inverse, gains[0:1], grad)).astype(BF)

        @pl.when(second)
        def _():
            for cross in (0, 1):
                grad_copy(m, cross).start()

        out_copy(7, ingrad_s.at[m], ingrad_out.at[m], m).start()

    half_rows = HALF
    quarter_rows = HIDDEN // 2

    def expert_out(i, m):
        src, own, their = (
            (wg, own_gate_out, their_gate_out),
            (wu, own_up_out, their_up_out),
            (wd, own_down_out, their_down_out),
        )[i]
        size = src.shape[0] // 2
        part = src.at[aligned(m * size, size, 16)]
        own = pltpu.make_async_copy(part, own, out_sem.at[i, m])
        their = pltpu.make_async_copy(part, their, out_sem.at[i, m])
        return own, their

    def start_out(i, m):
        own, their = expert_out(i, m)
        pl.when(m == f)(own.start)
        pl.when(m != f)(their.start)

    def grads_in_step(m):
        @pl.loop(0, 3)
        def _(j):
            cols = aligned(m * half_rows + j * 256, 256, 128)
            rows = n2recv[:, :, :, :, cols].reshape(MB * ROWS, 256)
            wg[cols, :] = dot_tn(rows, gs[...].reshape(MB * ROWS, HIDDEN)).astype(BF)
            wu[cols, :] = dot_tn(rows, us[...].reshape(MB * ROWS, HIDDEN)).astype(BF)

        start_out(0, m)
        start_out(1, m)

    def grads_out_step(m):
        cols = aligned(m * quarter_rows, quarter_rows, 128)

        @pl.loop(0, 3)
        def _(j):
            at = aligned(j * 512, 512, 128)
            rows = dyrecv[:, :, :, :, at].reshape(MB * ROWS, 512)
            wd[cols, at] = dot_tn(hid[:, :, cols].reshape(MB * ROWS, quarter_rows), rows).astype(BF)

        start_out(2, m)

    steps = {
        GRADS_IN: grads_in_step,
        GRADS_OUT: grads_out_step,
        ATTEND: attend_step,
        NORM: norm_step,
        TWIN: twin_step,
        HIDE: hide_step,
        GIVE: give_step,
        FAR: far_step,
        JOIN: join_step,
        GRAD: grad_step,
        GRAD_TWIN: grad_twin_step,
        BACK: back_step,
        FAR_BACK: far_back_step,
        MID: mid_step,
        ATTEND_BACK: attend_back_step,
        CLOSE: close_step,
        LOAD: load_step,
    }
    length = max(len(FIRST_PLAN), len(SECOND_PLAN))
    plans = [plan + ((REST, 0),) * (length - len(plan)) for plan in (FIRST_PLAN, SECOND_PLAN)]

    @pl.loop(0, length)
    def _(i):
        code = jnp.int32(REST * MB)
        for at, ((step_a, m_a), (step_b, m_b)) in enumerate(zip(*plans)):
            here = jnp.where(first, step_a * MB + m_a, step_b * MB + m_b)
            code = jnp.where(i == at, here, code)
        m = lax.rem(code, MB)
        for step, work in steps.items():
            pl.when(code // MB == step)(functools.partial(work, m))

    gains_out[...] = gains_acc[...]

    @pl.loop(0, MB)
    def _(m):
        dqkv_copy(m).wait_recv()
        out_copy(8, n1s.at[m, :, own_half], n1_out.at[m], m).start()
        out_copy(9, dqkv_all.at[m], dqkv_out.at[m], m).start()
        out_copy(10, att.at[m], att_out.at[m], m).start()
        sent(1, m, dsend)
        sent(3, m, bsend)
        to_partner(0, m, part_send.at[m], part_recv.at[m]).wait_send()
        da_copy(m).wait_send()
        dn1_copy(m).wait_send()
        dqkv_copy(m).wait_send()
        n2_copy(m).wait_send()
        far_copy(1, m).wait_send()
        far_copy(2, m).wait_send()

        @pl.when(first)
        def _():
            x_copy(m).wait_send()
            for cross in (0, 1):
                acts_copy(m, cross).wait_send()

        @pl.when(second)
        def _():
            ct_copy(m).wait_send()
            for cross in (0, 1):
                grad_copy(m, cross).wait_send()

    side_copy.wait_send()
    meta_copy.wait_send()

    @pl.loop(0, MB)
    def _(m):
        pairs = (
            (3, acts_s.at[m], acts_out.at[m]),
            (6, da_pair.at[m], da_out.at[m]),
            (7, ingrad_s.at[m], ingrad_out.at[m]),
            (8, n1s.at[m, :, own_half], n1_out.at[m]),
            (9, dqkv_all.at[m], dqkv_out.at[m]),
            (10, att.at[m], att_out.at[m]),
        )
        for i, src, dst in pairs:
            out_copy(i, src, dst, m).wait()
        for i in range(3):
            expert_out(i, m)[0].wait()


def run_sections(*operands):
    def out(*shape, dtype=BF):
        return jax.ShapeDtypeStruct(shape, dtype)

    vmem = pl.BlockSpec(memory_space=pltpu.VMEM)
    anywhere = pl.BlockSpec(memory_space=pl.ANY)
    dma = pltpu.SemaphoreType.DMA
    blocks = (MB, PLANE, 2, SLOTS, WIDTH)
    return pl.pallas_call(
        section_kernel,
        name="sections",
        out_shape=(
            out(MB, SEQ, WIDTH),
            out(MB, SEQ, WIDTH),
            out(8, WIDTH, dtype=F32),
            out(HALF, HIDDEN),
            out(HALF, HIDDEN),
            out(HIDDEN // 2, WIDTH),
            out(HALF, HIDDEN),
            out(HALF, HIDDEN),
            out(HIDDEN // 2, WIDTH),
            out(MB, 2 * SEQ, HALF),
            out(MB, 2, 2 * SEQ, QKV),
            out(MB, 2 * SEQ, HALF),
            out(MB, 2 * SEQ, WIDTH),
        ),
        in_specs=[anywhere] * 9 + [vmem] * 6,
        out_specs=[anywhere] * 2 + [vmem] + [anywhere] * 10,
        scratch_shapes=[
            pltpu.VMEM((WIDTH, QKV), BF),
            pltpu.VMEM((HALF, WIDTH), BF),
            pltpu.VMEM((WIDTH, HIDDEN), BF),
            pltpu.VMEM((WIDTH, HIDDEN), BF),
            pltpu.VMEM((HIDDEN, WIDTH), BF),
            pltpu.VMEM((MB, 2 * SEQ, WIDTH), BF),
            pltpu.VMEM((MB, 2 * SEQ, WIDTH), BF),
            pltpu.VMEM((MB, 2 * SEQ, QKV), BF),
            pltpu.VMEM((MB, 2 * SEQ, HALF), BF),
            pltpu.VMEM((MB, SEQ, WIDTH), F32),
            pltpu.VMEM((MB, SEQ, WIDTH), F32),
            pltpu.VMEM((MB, SEQ, WIDTH), BF),
            pltpu.VMEM((MB, SEQ, WIDTH), BF),
            pltpu.VMEM((MB, 2, PLANE * SLOTS, SEQ), BF),
            pltpu.VMEM((MB, 2, PLANE * SLOTS, SEQ), BF),
            pltpu.VMEM((MB, 2, PLANE * SLOTS, SEQ), BF),
            pltpu.VMEM((MB, 2, SEQ, WIDTH), BF),
            pltpu.VMEM((MB, 2, SEQ, WIDTH), BF),
            pltpu.VMEM(blocks, BF),
            pltpu.VMEM(blocks, BF),
            pltpu.VMEM(blocks, BF),
            pltpu.VMEM(blocks, BF),
            pltpu.VMEM(blocks, BF),
            pltpu.VMEM(blocks, BF),
            pltpu.VMEM((MB, ROWS, HIDDEN), BF),
            pltpu.VMEM((MB, ROWS, HIDDEN), BF),
            pltpu.VMEM((MB, ROWS, HIDDEN), BF),
            pltpu.VMEM((2, MB, SEQ, WIDTH), BF),
            pltpu.VMEM((2, MB, SEQ, WIDTH), BF),
            pltpu.VMEM((MB, SEQ, WIDTH), BF),
            pltpu.VMEM((MB, SEQ, WIDTH), F32),
            pltpu.VMEM((MB, 2 * SEQ, WIDTH), BF),
            pltpu.VMEM((MB, 2, 2 * SEQ, QKV), BF),
            pltpu.VMEM((MB, SEQ, WIDTH), BF),
            pltpu.VMEM((MB, SEQ, WIDTH), BF),
            pltpu.VMEM((MB, SEQ, WIDTH), BF),
            pltpu.VMEM((8, WIDTH), F32),
            pltpu.VMEM((2, 8, HALF), F32),
            pltpu.VMEM((2, MB, 8, SEQ), F32),
            pltpu.VMEM((2, WIDTH), F32),
            pltpu.VMEM((MB, 2 * SEQ, HEAD), F32),
            pltpu.VMEM((MB, 2 * SEQ, HEAD), F32),
            pltpu.VMEM((MB, 2, SEQ, SEQ), F32),
            dma((9,)),
            dma((12,)),
            dma((10,)),
            dma((4, MB)),
            dma((4, MB)),
            dma((4, MB)),
            dma((4, MB)),
            dma((3, MB)),
            dma((3, MB)),
            dma((2, MB)),
            dma((2, MB)),
            dma((2, MB)),
            dma((2, MB)),
            dma((11, MB)),
            pltpu.SemaphoreType.REGULAR,
        ],
        compiler_params=pltpu.CompilerParams(
            collective_id=0, has_side_effects=True, vmem_limit_bytes=62 * 2**20
        ),
    )(*operands)


BAND = 192
SLICE = 48
LANES = (("z", 1024), ("y", 1024), ("z", 768), ("y", 768))


def grads_kernel(
    their_gate,
    their_up,
    their_down,
    n1_in,
    dqkv_in,
    att_in,
    da_in,
    gains_in,
    q_out,
    k_out,
    v_out,
    o_out,
    part_gate,
    part_up,
    part_down,
    gains_out,
    n1,
    dqkv,
    att,
    da,
    *rest,
):
    lane_refs, rest = [rest[i * 7 : i * 7 + 7] for i in range(len(LANES))], rest[7 * len(LANES) :]
    (
        small,
        small_recv,
        load_sem,
        send_sem,
        recv_sem,
        pair_send,
        pair_recv,
        small_send,
        small_recv_sem,
        out_sem,
    ) = rest
    f = lax.axis_index("fsdp")
    e = lax.axis_index("expert")
    y, x, z = e // 8, lax.rem(e // 4, 2), lax.rem(e, 4)
    other = 1 - f
    own_half = aligned(f * HALF, HALF, 128)
    other_half = aligned(other * HALF, HALF, 128)

    def along_y(d):
        return {"expert": lax.rem(y + d, 4) * 8 + x * 4 + z}

    def along_z(d):
        return {"expert": y * 8 + x * 4 + lax.rem(z + d, 4)}

    twin = {"expert": y * 8 + (1 - x) * 4 + z}
    partner = {"fsdp": other}

    barrier = pltpu.get_barrier_semaphore()
    neighbours = [along_y(d) for d in (1, 2, 3)] + [along_z(d) for d in (1, 2, 3)]
    neighbours += [twin, partner]
    for place in neighbours:
        pl.semaphore_signal(barrier, inc=1, device_id=place, device_id_type=MESH)

    loads = [
        (att_in, att),
        (da_in, da),
        (n1_in, n1),
        (dqkv_in, dqkv),
    ]
    loads = [pltpu.make_async_copy(a, b, load_sem.at[i]) for i, (a, b) in enumerate(loads)]
    for copy in loads:
        copy.start()

    def remote(src, dst, send, recv, place):
        return pltpu.make_async_remote_copy(
            src_ref=src,
            dst_ref=dst,
            send_sem=send,
            recv_sem=recv,
            device_id=place,
            device_id_type=MESH,
        )

    def wait_for(ref, sem):
        pltpu.make_async_copy(ref, ref, sem).wait()

    class Lane:
        def __init__(self, i):
            self.i = i
            self.v, self.r1, self.s1, self.r2, self.s2, self.r3, self.g = lane_refs[i]
            axes = ((along_y, y), (along_z, z))
            (self.axis, self.at), (self.next, self.to) = axes if LANES[i][0] == "y" else axes[::-1]
            half = LANES[i][1] // 2
            self.mine = aligned(x * half, half, 128)
            self.theirs = aligned((1 - x) * half, half, 128)
            self.place = aligned(self.at * BAND + self.to * SLICE, SLICE, 16)

        def send(self, stage, src, dst, place):
            remote(
                src, dst, send_sem.at[self.i, stage], recv_sem.at[self.i, stage], place
            ).start()

        def arrived(self, stage, ref):
            wait_for(ref, recv_sem.at[self.i, stage])

        def spread(self):
            for d in (1, 2, 3):
                rows = aligned(lax.rem(self.at + d, 4) * BAND, BAND, 16)
                self.send(0, self.v.at[rows], self.r1.at[self.at], self.axis(d))

        def join_one(self):
            self.arrived(0, self.r1.at[pl.ds(0, 3)])
            total = self.v[aligned(self.at * BAND, BAND, 16)].astype(F32)
            for d in (1, 2, 3):
                total = total + self.r1[lax.rem(self.at + d, 4)].astype(F32)
            self.s1[...] = total.astype(BF)
            for d in (1, 2, 3):
                rows = aligned(lax.rem(self.to + d, 4) * SLICE, SLICE, 16)
                self.send(1, self.s1.at[rows], self.r2.at[self.to], self.next(d))

        def join_two(self):
            self.arrived(1, self.r2.at[pl.ds(0, 3)])
            total = self.s1[aligned(self.to * SLICE, SLICE, 16)].astype(F32)
            for d in (1, 2, 3):
                total = total + self.r2[lax.rem(self.to + d, 4)].astype(F32)
            self.s2[...] = total.astype(BF)
            self.send(2, self.s2.at[:, self.theirs], self.r3, twin)

        def join_three(self):
            self.arrived(2, self.r3)
            total = self.s2[:, self.mine].astype(F32) + self.r3[...].astype(F32)
            self.g[self.place, self.mine] = total.astype(BF)
            part = self.g.at[self.place, self.mine]
            self.send(3, part, part, twin)

        def gather_two(self):
            self.arrived(3, self.g.at[self.place, self.theirs])
            part = self.g.at[self.place]
            for d in (1, 2, 3):
                self.send(4, part, part, self.next(d))

        def gather_one(self):
            self.arrived(4, self.g.at[pl.ds(0, 3 * SLICE)])
            part = self.g.at[aligned(self.at * BAND, BAND, 16)]
            for d in (1, 2, 3):
                self.send(5, part, part, self.axis(d))

        def finish(self):
            self.arrived(5, self.g.at[pl.ds(0, 3 * BAND)])

        def drain(self):
            wait_for(self.v.at[pl.ds(0, 3 * BAND)], send_sem.at[self.i, 0])
            wait_for(self.s1.at[pl.ds(0, 3 * SLICE)], send_sem.at[self.i, 1])
            wait_for(self.s2.at[:, self.theirs], send_sem.at[self.i, 2])
            wait_for(self.g.at[self.place, self.mine], send_sem.at[self.i, 3])
            wait_for(self.g.at[pl.ds(0, 3 * SLICE)], send_sem.at[self.i, 4])
            wait_for(self.g.at[pl.ds(0, 3 * BAND)], send_sem.at[self.i, 5])

    out_one, query_one, out_two, query_two = lanes = [Lane(i) for i in range(len(LANES))]

    def over_micro(group, cols):
        block = jnp.concatenate([dqkv[m, group, :, cols] for m in range(MB)], axis=0)
        return dot_tn(n1[...], block).astype(BF)

    for copy in loads[:2]:
        copy.wait()
    for j in range(2):
        cols = pl.ds(j * 512, 512)
        out_one.v[:, cols] = dot_tn(att[...], da[:, cols]).astype(BF)
    pl.semaphore_wait(barrier, len(neighbours))
    out_one.spread()
    for copy in loads[2:4]:
        copy.wait()
    query_one.v[:, pl.ds(0, HALF)] = over_micro(0, pl.ds(0, HALF))
    query_one.v[:, pl.ds(HALF, 256)] = over_micro(1, pl.ds(0, 256))
    query_one.spread()
    small[...] = gains_in[...]
    small_pair = remote(
        small.at[:, other_half],
        small_recv.at[0],
        small_send.at[0],
        small_recv_sem.at[0],
        partner,
    )
    small_pair.start()
    out_two.v[:, pl.ds(0, 512)] = dot_tn(att[...], da[:, pl.ds(1024, 512)]).astype(BF)
    query_two.v[:, pl.ds(0, 512)] = over_micro(1, pl.ds(256, 512))
    for g in range(2):
        query_two.v[:, pl.ds(512 + g * HEAD, HEAD)] = over_micro(g, pl.ds(HALF, HEAD))
        out_two.v[:, pl.ds(512 + g * HEAD, HEAD)] = over_micro(g, pl.ds(HALF + HEAD, HEAD))

    pair = [
        remote(src, dst, pair_send.at[i], pair_recv.at[i], partner)
        for i, (src, dst) in enumerate(
            ((their_gate, part_gate), (their_up, part_up), (their_down, part_down))
        )
    ]
    pieces = [
        remote(src.at[rows], dst.at[rows], pair_send.at[n], pair_recv.at[n], partner)
        for n, src, dst, size in (
            (0, their_gate, part_gate, HALF // 4),
            (1, their_up, part_up, HALF // 4),
            (2, their_down, part_down, HIDDEN // 8),
        )
        for rows in [pl.ds(i * size, size) for i in range(4)]
    ]

    def send_pieces(start, stop):
        for copy in pieces[start:stop]:
            copy.start()

    def spread_small(i, axis):
        for d in (1, 2, 3):
            remote(
                small.at[:, pl.ds(0, HALF)],
                small_recv.at[1 + 3 * i + d - 1],
                small_send.at[1 + 3 * i + d - 1],
                small_recv_sem.at[1 + 3 * i + d - 1],
                axis(d),
            ).start()

    def join_small(i, axis):
        for d in (1, 2, 3):
            remote(
                small.at[:, pl.ds(0, HALF)],
                small_recv.at[1 + 3 * i + d - 1],
                small_send.at[1 + 3 * i + d - 1],
                small_recv_sem.at[1 + 3 * i + d - 1],
                axis(d),
            ).wait()
        total = small[:, pl.ds(0, HALF)]
        for d in (1, 2, 3):
            total = total + small_recv[1 + 3 * i + d - 1]
        small[:, pl.ds(0, HALF)] = total

    small_pair.wait()
    small[:, pl.ds(0, HALF)] = small[:, own_half] + small_recv[0]
    spread_small(0, along_y)

    out_two.spread()
    query_two.spread()
    send_pieces(0, 4)
    join_small(0, along_y)
    spread_small(1, along_z)
    for lane in lanes:
        lane.join_one()
    for lane in lanes:
        lane.join_two()
    join_small(1, along_z)
    small_twin = remote(
        small.at[:, pl.ds(0, HALF)],
        small_recv.at[7],
        small_send.at[7],
        small_recv_sem.at[7],
        twin,
    )
    small_twin.start()
    send_pieces(4, 5)
    for lane in lanes:
        lane.join_three()
    send_pieces(5, 12)
    for lane in lanes:
        lane.gather_two()
    for lane in lanes:
        lane.gather_one()
    small_twin.wait()
    gains_out[...] = small[:, pl.ds(0, HALF)] + small_recv[7]

    outs = []

    def out_copy(src, dst):
        copy = pltpu.make_async_copy(src, dst, out_sem.at[len(outs)])
        copy.start()
        outs.append(copy)

    out_one.finish()
    out_copy(out_one.g, o_out.at[:, pl.ds(0, 1024)])
    query_one.finish()
    out_copy(query_one.g, q_out.at[:, pl.ds(0, 1024)])
    out_two.finish()
    out_copy(out_two.g.at[:, pl.ds(0, 512)], o_out.at[:, pl.ds(1024, 512)])
    out_copy(out_two.g.at[:, pl.ds(512, 256)], v_out)
    query_two.finish()
    out_copy(query_two.g.at[:, pl.ds(0, 512)], q_out.at[:, pl.ds(1024, 512)])
    out_copy(query_two.g.at[:, pl.ds(512, 256)], k_out)

    for lane in lanes:
        lane.drain()
    for copy in pair:
        copy.wait()
    for copy in outs:
        copy.wait()


def reduce_grads(*operands):
    def out(*shape):
        return jax.ShapeDtypeStruct(shape, BF)

    vmem = pl.BlockSpec(memory_space=pltpu.VMEM)
    anywhere = pl.BlockSpec(memory_space=pl.ANY)
    dma = pltpu.SemaphoreType.DMA
    lanes = []
    for _, width in LANES:
        lanes += [
            pltpu.VMEM((HALF, width), BF),
            pltpu.VMEM((4, BAND, width), BF),
            pltpu.VMEM((BAND, width), BF),
            pltpu.VMEM((4, SLICE, width), BF),
            pltpu.VMEM((SLICE, width), BF),
            pltpu.VMEM((SLICE, width // 2), BF),
            pltpu.VMEM((HALF, width), BF),
        ]
    return pl.pallas_call(
        grads_kernel,
        name="grads",
        out_shape=(
            out(HALF, WIDTH),
            out(HALF, 256),
            out(HALF, 256),
            out(HALF, WIDTH),
            out(HALF, HIDDEN),
            out(HALF, HIDDEN),
            out(HIDDEN // 2, WIDTH),
            jax.ShapeDtypeStruct((8, HALF), F32),
        ),
        in_specs=[anywhere] * 7 + [vmem],
        out_specs=[anywhere] * 7 + [vmem],
        scratch_shapes=[
            pltpu.VMEM((MB * 2 * SEQ, HALF), BF),
            pltpu.VMEM((MB, 2, 2 * SEQ, QKV), BF),
            pltpu.VMEM((MB * 2 * SEQ, HALF), BF),
            pltpu.VMEM((MB * 2 * SEQ, WIDTH), BF),
        ]
        + lanes
        + [
            pltpu.VMEM((8, WIDTH), F32),
            pltpu.VMEM((8, 8, HALF), F32),
            dma((4,)),
            dma((len(LANES), 6)),
            dma((len(LANES), 6)),
            dma((3,)),
            dma((3,)),
            dma((8,)),
            dma((8,)),
            dma((9,)),
        ],
        compiler_params=pltpu.CompilerParams(
            collective_id=1, has_side_effects=True, vmem_limit_bytes=62 * 2**20
        ),
    )(*operands)


def finish_kernel(*refs):
    (q, k, v, o, own_g, own_u, own_d, part_g, part_u, part_d, acts, grads, gains), outs = (
        refs[:13],
        refs[13:],
    )
    for src, dst in zip((q, k, v, o), outs):
        dst[...] = src[...].astype(F32)
    for own, part, dst in zip((own_g, own_u, own_d), (part_g, part_u, part_d), outs[4:]):
        dst[...] = own[...].astype(F32) + part[...].astype(F32)
    outs[7][...] = acts[...]
    outs[8][...] = grads[...]
    outs[9][...] = gains[0:1]
    outs[10][...] = gains[1:2]


def finish(*blocks):
    steps = 6

    def spec(rows, cols):
        return pl.BlockSpec((rows // steps, cols), lambda i: (i, 0))

    def whole(rows, cols):
        return pl.BlockSpec((rows, cols), lambda i: (0, 0))

    gains = blocks[-1]
    split = blocks[:-1]
    results = split[:7] + split[10:]
    dtypes = [F32] * 7 + [BF] * 2
    return pl.pallas_call(
        finish_kernel,
        name="finish",
        grid=(steps,),
        out_shape=[jax.ShapeDtypeStruct(b.shape, t) for b, t in zip(results, dtypes)]
        + [jax.ShapeDtypeStruct((1, HALF), F32)] * 2,
        in_specs=[spec(*b.shape) for b in split] + [whole(*gains.shape)],
        out_specs=[spec(*b.shape) for b in results] + [whole(1, HALF)] * 2,
        compiler_params=pltpu.CompilerParams(vmem_limit_bytes=62 * 2**20),
    )(*blocks)


def local(
    inputs,
    cotangent,
    segments,
    expert_ids,
    gate_logits,
    w_query,
    key_projection,
    value_projection,
    w_out,
    gain_attn,
    gain_moe,
    w_gate,
    w_up,
    w_down,
):
    steps = np.arange(HEAD) % (HEAD // 2)
    frequency = (ROPE_BASE ** (-steps * 2.0 / HEAD)).astype(np.float32)[None]
    (
        acts,
        in_grads,
        gain_parts,
        own_gate,
        own_up,
        own_down,
        their_gate,
        their_up,
        their_down,
        n1,
        dqkv,
        att,
        da,
    ) = run_sections(
        inputs,
        cotangent,
        w_query[0],
        key_projection[0],
        value_projection[0],
        w_out[0],
        w_gate[0, 0],
        w_up[0, 0],
        w_down[0, 0],
        gain_attn,
        gain_moe,
        segments,
        expert_ids[0],
        gate_logits[0],
        jnp.asarray(frequency),
    )
    gq, gk, gv, go, part_gate, part_up, part_down, gains = reduce_grads(
        their_gate,
        their_up,
        their_down,
        n1.reshape(MB * 2 * SEQ, HALF),
        dqkv,
        att.reshape(MB * 2 * SEQ, HALF),
        da.reshape(MB * 2 * SEQ, WIDTH),
        gain_parts,
    )
    gq, gk, gv, go, grad_gate, grad_up, grad_down, acts, in_grads, gain_one, gain_two = finish(
        gq,
        gk,
        gv,
        go,
        own_gate,
        own_up,
        own_down,
        part_gate,
        part_up,
        part_down,
        acts.reshape(MB * SEQ, WIDTH),
        in_grads.reshape(MB * SEQ, WIDTH),
        gains,
    )
    return (
        acts.reshape(1, MB, SEQ, WIDTH),
        in_grads.reshape(1, MB, SEQ, WIDTH),
        gq[None],
        gk[None],
        gv[None],
        go[None],
        gain_one,
        gain_two,
        grad_gate[None, None],
        grad_up[None, None],
        grad_down[None, None],
    )


def solution(mesh):
    return jax.shard_map(
        local,
        mesh=mesh,
        in_specs=(
            P(None, ("fsdp", "expert"), None),
            P(None, ("fsdp", "expert"), None),
            P(None, ("fsdp", "expert")),
            P("section", None, ("fsdp", "expert"), None),
            P("section", None, ("fsdp", "expert"), None),
            P("section", "fsdp", None),
            P("section", "fsdp", None),
            P("section", "fsdp", None),
            P("section", "fsdp", None),
            P("section", "fsdp"),
            P("section", "fsdp"),
            P("section", "expert", "fsdp", None),
            P("section", "expert", "fsdp", None),
            P("section", "expert", "fsdp", None),
        ),
        out_specs=(
            P("section", None, ("fsdp", "expert"), None),
            P("section", None, ("fsdp", "expert"), None),
            P("section", "fsdp", None),
            P("section", "fsdp", None),
            P("section", "fsdp", None),
            P("section", "fsdp", None),
            P("section", "fsdp"),
            P("section", "fsdp"),
            P("section", "expert", "fsdp", None),
            P("section", "expert", "fsdp", None),
            P("section", "expert", "fsdp", None),
        ),
        check_vma=False,
    )
```

```python
import functools

import jax
import jax.numpy as jnp
import numpy as np
from jax import lax
from jax.experimental import pallas as pl
from jax.experimental.pallas import tpu as pltpu
from jax.sharding import PartitionSpec as P

MESH = pl.DeviceIdType.MESH
BF = jnp.bfloat16
F32 = jnp.float32

HEAD = 128
EPS = 1e-06
ROPE_BASE = 1000000.0
GELU_C = 0.7978845608
GELU_A = 0.044715

MB = 2
SEQ = 96
WIDTH = 1536
HALF = 768
EXPERTS = 32
PLANE = 16
SLOTS = 16
ROWS = EXPERTS * SLOTS
HIDDEN = 768
HEADS = 6
QKV = 1024


def dot(a, b):
    return jnp.dot(a, b, preferred_element_type=F32)


def dot_nt(a, b):
    return lax.dot_general(a, b, (((1,), (1,)), ((), ())), preferred_element_type=F32)


def dot_tn(a, b):
    return lax.dot_general(a, b, (((0,), (0,)), ((), ())), preferred_element_type=F32)


def aligned(start, size, unit):
    return pl.ds(pl.multiple_of(start, unit), size)


def inverse_rms(rows):
    return lax.rsqrt(jnp.mean(rows * rows, axis=-1, keepdims=True) + EPS)


def rms_back(rows, inverse, gain, grad):
    scaled = gain * grad
    return inverse * scaled - rows * (inverse * inverse * inverse) * jnp.mean(
        scaled * rows, axis=-1, keepdims=True
    )


def rotate(head, cos, sin):
    return head * cos + pltpu.roll(head, HEAD // 2, 1) * sin


(
    ENTER,
    PROJECT,
    ATTEND,
    NORM,
    TWIN,
    HIDE,
    GIVE,
    FAR,
    JOIN,
    GRAD,
    GRAD_TWIN,
    BACK,
    FAR_BACK,
    MID,
    ATTEND_BACK,
    PROJECT_BACK,
    CLOSE,
    LOAD,
    GRADS_IN,
    GRADS_OUT,
    REST,
) = range(21)

FIRST_PLAN = (
    (ENTER, 0, 0),
    (ENTER, 1, 1),
    (PROJECT, 0, 1),
    (PROJECT, 1, 1),
    (ATTEND, 0, 1),
    (ATTEND, 1, 1),
    (NORM, 0, 1),
    (NORM, 1, 6),
    (TWIN, 0, 0),
    (TWIN, 1, 0),
    (HIDE, 0, 0),
    (HIDE, 1, 0),
    (GIVE, 0, 0),
    (GIVE, 1, 0),
    (FAR, 0, 0),
    (JOIN, 0, 0),
    (FAR, 1, 0),
    (JOIN, 1, 0),
    (GRAD, 0, 0),
    (GRAD_TWIN, 0, 0),
    (GRAD, 1, 0),
    (GRAD_TWIN, 1, 0),
    (BACK, 0, 0),
    (BACK, 1, 0),
    (GRADS_IN, 0, 0),
    (FAR_BACK, 0, 0),
    (GRADS_IN, 1, 0),
    (MID, 0, 0),
    (GRADS_OUT, 0, 0),
    (FAR_BACK, 1, 0),
    (ATTEND_BACK, 0, 0),
    (MID, 1, 0),
    (PROJECT_BACK, 0, 0),
    (GRADS_OUT, 1, 0),
    (ATTEND_BACK, 1, 0),
    (CLOSE, 0, 0),
    (PROJECT_BACK, 1, 0),
    (CLOSE, 1, 0),
)
SECOND_PLAN = (
    (GRAD, 0, 0),
    (GRAD, 1, 0),
    (LOAD, 0, 5),
    (ENTER, 0, 0),
    (PROJECT, 0, 1),
    (ENTER, 1, 1),
    (ATTEND, 0, 1),
    (PROJECT, 1, 1),
    (NORM, 0, 1),
    (ATTEND, 1, 1),
    (TWIN, 0, 0),
    (NORM, 1, 1),
    (TWIN, 1, 0),
    (GRAD_TWIN, 0, 0),
    (GRAD_TWIN, 1, 0),
    (HIDE, 0, 0),
    (HIDE, 1, 0),
    (BACK, 0, 0),
    (BACK, 1, 0),
    (GIVE, 0, 0),
    (GIVE, 1, 0),
    (FAR_BACK, 0, 0),
    (GRADS_IN, 0, 0),
    (MID, 0, 0),
    (FAR_BACK, 1, 0),
    (ATTEND_BACK, 0, 0),
    (MID, 1, 0),
    (PROJECT_BACK, 0, 0),
    (GRADS_IN, 1, 0),
    (ATTEND_BACK, 1, 0),
    (CLOSE, 0, 0),
    (GRADS_OUT, 0, 0),
    (PROJECT_BACK, 1, 0),
    (GRADS_OUT, 1, 0),
    (CLOSE, 1, 0),
    (FAR, 0, 0),
    (FAR, 1, 0),
    (JOIN, 0, 0),
    (JOIN, 1, 0),
)


def section_kernel(
    x_in,
    ct_in,
    wq_in,
    wk_in,
    wv_in,
    wo_in,
    wg_in,
    wu_in,
    wd_in,
    gain_one_in,
    gain_two_in,
    segments_in,
    ids_in,
    logits_in,
    freq_in,
    acts_out,
    ingrad_out,
    gains_out,
    own_gate_out,
    own_up_out,
    own_down_out,
    their_gate_out,
    their_up_out,
    their_down_out,
    n1_out,
    dqkv_out,
    att_out,
    da_out,
    wqkv,
    wo,
    wg,
    wu,
    wd,
    x_own,
    n1p,
    n1_send,
    pq_own,
    pq_send,
    pq_recv,
    qkvs,
    att,
    hid_one,
    part_own,
    part_send,
    part_recv,
    sel,
    cg_hi,
    cg_lo,
    n2pair,
    gpair,
    dsend,
    bsend,
    n2recv,
    yrecv,
    dyrecv,
    dn2recv,
    gs,
    us,
    hid,
    far_send,
    far_recv,
    acts_s,
    dh_s,
    da_pair,
    dqkv_all,
    dn1_send,
    dn1_recv,
    ingrad_s,
    gains_acc,
    side,
    meta,
    gains,
    cos_t,
    sin_t,
    mask_t,
    lw_sem,
    ws_sem,
    wr_sem,
    as_sem,
    ar_sem,
    ps_sem,
    pr_sem,
    ts_sem,
    tr_sem,
    xs_sem,
    xr_sem,
    gs_sem,
    gr_sem,
    out_sem,
    go_sem,
):
    sec = lax.axis_index("section")
    f = lax.axis_index("fsdp")
    e = lax.axis_index("expert")
    y, x, z = e // 8, lax.rem(e // 4, 2), lax.rem(e, 4)
    q = y * 4 + z
    away = 1 - x
    other = 1 - f
    own_rows = aligned(f * SEQ, SEQ, 16)
    own_half = aligned(f * HALF, HALF, 128)
    other_half = aligned(other * HALF, HALF, 128)
    partner = {"fsdp": other}
    twin_place = y * 8 + away * 4 + z
    twin = {"expert": twin_place}
    first, second = sec == 0, sec == 1

    def in_plane(d):
        at = lax.rem(q + d, PLANE)
        return at, {"expert": (at // 4) * 8 + x * 4 + lax.rem(at, 4)}

    barrier = pltpu.get_barrier_semaphore()

    @pl.loop(1, PLANE)
    def _(d):
        pl.semaphore_signal(barrier, inc=1, device_id=in_plane(d)[1], device_id_type=MESH)

    others = (
        twin,
        partner,
        {"section": 1 - sec},
        {"section": 1 - sec, "expert": twin_place},
    )
    for place in others:
        pl.semaphore_signal(barrier, inc=1, device_id=place, device_id_type=MESH)

    local = []
    for g in range(2):
        local += [
            (wq_in.at[:, pl.ds(g * HALF, HALF)], wqkv.at[:, pl.ds(g * QKV, HALF)]),
            (wk_in.at[:, pl.ds(g * HEAD, HEAD)], wqkv.at[:, pl.ds(g * QKV + HALF, HEAD)]),
            (wv_in.at[:, pl.ds(g * HEAD, HEAD)], wqkv.at[:, pl.ds(g * QKV + HALF + HEAD, HEAD)]),
        ]
    local += [
        (wo_in, wo),
        (wg_in, wg.at[own_half]),
        (wu_in, wu.at[own_half]),
        (wd_in, wd.at[aligned(f * (HIDDEN // 2), HIDDEN // 2, 16)]),
    ]
    local = [pltpu.make_async_copy(a, b, lw_sem.at[i]) for i, (a, b) in enumerate(local)]
    for copy in local:
        copy.start()
    x_local = pltpu.make_async_copy(x_in, x_own, lw_sem.at[10])
    ct_local = pltpu.make_async_copy(ct_in, gpair.at[:, x], lw_sem.at[11])
    pl.when(first)(x_local.start)
    pl.when(second)(ct_local.start)

    def remote(src, dst, send, recv, place):
        return pltpu.make_async_remote_copy(
            src_ref=src,
            dst_ref=dst,
            send_sem=send,
            recv_sem=recv,
            device_id=place,
            device_id_type=MESH,
        )

    def wait_for(ref, sem):
        pltpu.make_async_copy(ref, ref, sem).wait()

    def weight(src, dst, i):
        return remote(src, dst, ws_sem.at[i], wr_sem.at[i], partner)

    w_moe = [
        weight(wg_in, wg.at[own_half], 3),
        weight(wu_in, wu.at[own_half], 4),
        weight(wd_in, wd.at[aligned(f * (HIDDEN // 2), HIDDEN // 2, 16)], 5),
    ]

    w_pieces = [
        weight(src.at[aligned(i * size, size, 16)], dst.at[aligned(f * 4 * size + i * size, size, 16)], n)
        for n, src, dst, size in (
            (3, wg_in, wg, HALF // 4),
            (4, wu_in, wu, HALF // 4),
            (5, wd_in, wd, HIDDEN // 8),
        )
        for i in range(4)
    ]

    def ct_copy(m):
        return remote(ct_in.at[m], gpair.at[m, x], ws_sem.at[10 + m], gr_sem.at[x, m], twin)

    side[f, 0:1] = gain_one_in[...].astype(F32)
    side[f, 1:2] = gain_two_in[...].astype(F32)
    side[f, 2:4, :SEQ] = segments_in[...].astype(F32)
    for m in range(MB):
        meta[x, m, 0:4] = ids_in[m].astype(F32)
        meta[x, m, 4:8] = logits_in[m]
    row = lax.broadcasted_iota(jnp.int32, (SEQ, SEQ), 0)
    col = lax.broadcasted_iota(jnp.int32, (SEQ, SEQ), 1)
    unit = jnp.where(row == col, 1.0, 0.0).astype(BF)
    side_copy = weight(side.at[f], side.at[f], 8)
    meta_copy = remote(meta.at[x], meta.at[x], ws_sem.at[9], wr_sem.at[9], twin)
    gains_acc[...] = jnp.zeros_like(gains_acc)

    pl.semaphore_wait(barrier, PLANE - 1 + len(others))
    side_copy.start()
    meta_copy.start()

    meta_copy.wait_recv()
    earlier = jnp.where(row < col, 1.0, 0.0).astype(BF)

    @pl.loop(0, 2 * MB)
    def _(i):
        m, source = lax.rem(i, MB), i // MB
        rows = meta[source, m]
        ids, logits = rows[:4], rows[4:]
        raised = jnp.exp(logits - jnp.max(logits, axis=0, keepdims=True))
        gates = raised / jnp.sum(raised, axis=0, keepdims=True)
        place = lax.broadcasted_iota(jnp.int32, (PLANE, SEQ), 0)
        expert = ((place // 4) * 8 + x * 4 + lax.rem(place, 4)).astype(F32)
        named = jnp.zeros((PLANE, SEQ), F32)
        weights = jnp.zeros((PLANE, SEQ), F32)
        for k in range(4):
            hit = expert == ids[k : k + 1, :]
            named = jnp.where(hit, 1.0, named)
            weights = jnp.where(hit, gates[k : k + 1, :], weights)
        slot = dot(named.astype(BF), earlier)
        slot = jnp.where(named > 0.0, slot, -1.0)
        shape = (PLANE, SLOTS, SEQ)
        count = lax.broadcasted_iota(jnp.int32, shape, 1).astype(F32)
        chosen = jnp.where(jnp.broadcast_to(slot[:, None, :], shape) == count, 1.0, 0.0)
        scaled = chosen * jnp.broadcast_to(weights[:, None, :], shape)
        scaled = scaled.reshape(PLANE * SLOTS, SEQ)
        high = scaled.astype(BF)
        sel[m, source] = chosen.reshape(PLANE * SLOTS, SEQ).astype(BF)
        cg_hi[m, source] = high
        cg_lo[m, source] = (scaled - high.astype(F32)).astype(BF)

    side_copy.wait_recv()
    gains[:, pl.ds(0, HALF)] = side[0, 0:2]
    gains[:, pl.ds(HALF, HALF)] = side[1, 0:2]
    lane = lax.broadcasted_iota(jnp.int32, (SEQ, HEAD), 1)
    turn = jnp.where(lane < HEAD // 2, -1.0, 1.0)
    for m in range(MB):
        for s in range(2):
            across = jnp.broadcast_to(side[s, 2 + m : 3 + m, :SEQ], (SEQ, SEQ))
            down = dot_nt(unit, across.astype(BF))
            same = jnp.where(down == across, 1.0, 0.0)
            mask_t[m, s] = jnp.where(col <= row, same, 0.0)
            places = jnp.sum(jnp.where(col < row, same, 0.0), axis=1, keepdims=True)
            angles = places * freq_in[...]
            cos_t[m, pl.ds(s * SEQ, SEQ)] = jnp.cos(angles)
            sin_t[m, pl.ds(s * SEQ, SEQ)] = jnp.sin(angles) * turn

    def exchange_half(kind, m, src, dst, source):
        @pl.loop(1, PLANE)
        def _(d):
            at, place = in_plane(d)
            remote(
                src.at[m, at, source],
                dst.at[m, q, source],
                as_sem.at[kind, m],
                ar_sem.at[kind, m],
                place,
            ).start()

        dst[m, q, source] = src[m, q, source]

    def exchange(kind, m, src, dst):
        @pl.loop(1, PLANE)
        def _(d):
            at, place = in_plane(d)
            remote(
                src.at[m, at], dst.at[m, q], as_sem.at[kind, m], ar_sem.at[kind, m], place
            ).start()

        dst[m, q] = src[m, q]

    def received(kind, m, dst):
        wait_for(dst.at[m, pl.ds(0, PLANE - 1)], ar_sem.at[kind, m])

    def sent(kind, m, src):
        wait_for(src.at[m, pl.ds(0, PLANE - 1)], as_sem.at[kind, m])

    def to_partner(kind, m, src, dst):
        return remote(src, dst, ps_sem.at[kind, m], pr_sem.at[kind, m], partner)

    def to_twin(kind, m, src, dst):
        return remote(src, dst, ts_sem.at[kind, m], tr_sem.at[kind, m], twin)

    def n2_copy(m):
        return to_twin(0, m, n2pair.at[m, x], n2pair.at[m, x])

    def far_copy(kind, m):
        return to_twin(kind, m, far_send.at[kind - 1, m], far_recv.at[kind - 1, m])

    def acts_copy(m):
        return remote(acts_s.at[m], x_own.at[m], xs_sem.at[m], xr_sem.at[m], {"section": 1})

    def n1_copy(m):
        return to_partner(4, m, n1_send.at[m], n1p.at[m, own_rows])

    def pq_copy(m):
        return to_partner(5, m, pq_send.at[m], pq_recv.at[m])

    def grad_copy(m, cross):
        place = {"section": 0, "expert": twin_place} if cross else {"section": 0}
        return remote(
            ingrad_s.at[m], gpair.at[m, x], gs_sem.at[cross, m], gr_sem.at[x, m], place
        )

    def out_copy(i, src, dst, m):
        return pltpu.make_async_copy(src, dst, out_sem.at[i, m])

    def flat(ref, m):
        return ref[m].reshape(ROWS, WIDTH)

    def spread(m, source, rows, dst, scale=None):
        @pl.loop(0, WIDTH // 512)
        def _(j):
            cols = aligned(j * 512, 512, 128)
            block = dot(sel[m, source], rows[m, source, :, cols])
            if scale is not None:
                block = block * scale
            dst[m, :, source, :, cols] = block.astype(BF).reshape(PLANE, SLOTS, 512)

    def load_step(m):
        pl.semaphore_wait(go_sem, 1)
        ct_copy(0).start()
        ct_copy(1).start()

    def heads_of(ref, m, rows):
        return jnp.concatenate(
            [ref[m, rows, pl.ds(h * HEAD, HEAD)] for h in range(HEADS)], axis=0
        )

    def softmax_of(m, s, queries, keys):
        scores = dot_nt(queries, keys) * HEAD ** (-0.5)
        allowed = jnp.concatenate([mask_t[m, s]] * HEADS, axis=0)
        scores = jnp.where(allowed > 0.0, scores, -1e30)
        raised = jnp.exp(scores - jnp.max(scores, axis=-1, keepdims=True))
        return raised / jnp.sum(raised, axis=-1, keepdims=True)

    def enter_step(m):
        pl.when(jnp.logical_and(first, m == 0))(x_local.wait)
        pl.when(second)(lambda: wait_for(x_own.at[m], xr_sem.at[m]))
        rows = x_own[m].astype(F32)
        scale = inverse_rms(rows)
        n1p[m, own_rows] = (x_own[m, :, own_half].astype(F32) * scale * gains[0:1, own_half]).astype(BF)
        n1_send[m] = (
            x_own[m, :, other_half].astype(F32) * scale * gains[0:1, other_half]
        ).astype(BF)
        n1_copy(m).start()

    def project_step(m):
        @pl.when(m == 0)
        def _():
            for copy in local[:6]:
                copy.wait()

        n1_copy(m).wait_recv()

        @pl.loop(0, QKV // 512)
        def _(j):
            cols = aligned(j * 512, 512, 128)
            from_w = aligned(other * QKV + j * 512, 512, 128)
            pq_send[m, :, cols] = dot(n1p[m], wqkv[:, from_w]).astype(BF)

        pq_copy(m).start()

        @pl.loop(0, QKV // 512)
        def _(j):
            cols = aligned(j * 512, 512, 128)
            from_w = aligned(f * QKV + j * 512, 512, 128)
            pq_own[m, :, cols] = dot(n1p[m], wqkv[:, from_w])

    def attend_step(m):
        pl.when(m == 0)(local[6].wait)
        pq_copy(m).wait_recv()
        cos, sin = cos_t[m], sin_t[m]
        for j in range(2 * HEADS - 4):
            cols = pl.ds(j * HEAD, HEAD)
            head = pq_own[m, :, cols] + pq_recv[m, :, cols].astype(F32)
            if j <= HEADS:
                head = rotate(head, cos, sin)
            qkvs[m, :, cols] = head.astype(BF)

        @pl.loop(0, 2)
        def _(s):
            at = aligned(s * SEQ, SEQ, 16)
            queries = heads_of(qkvs, m, at)
            keys = qkvs[m, at, pl.ds(HALF, HEAD)]
            values = qkvs[m, at, pl.ds(HALF + HEAD, HEAD)]
            probs = softmax_of(m, s, queries, keys).astype(BF)
            mixed = dot(probs, values).astype(BF)
            for h in range(HEADS):
                att[m, at, pl.ds(h * HEAD, HEAD)] = mixed[h * SEQ : (h + 1) * SEQ]

        @pl.loop(0, WIDTH // 512)
        def _(j):
            cols = aligned(j * 512, 512, 128)
            block = dot(att[m], wo[:, cols])
            top, low = block[:SEQ], block[SEQ:]
            mine = f == 0
            hid_one[m, :, cols] = jnp.where(mine, top, low)
            part_send[m, :, cols] = jnp.where(mine, low, top).astype(BF)

        to_partner(0, m, part_send.at[m], part_recv.at[m]).start()

    def norm_step(m):
        to_partner(0, m, part_send.at[m], part_recv.at[m]).wait_recv()
        rows = x_own[m].astype(F32) + (hid_one[m] + part_recv[m].astype(F32))
        hid_one[m] = rows
        n2pair[m, x] = (rows * inverse_rms(rows) * gains[1:2]).astype(BF)
        n2_copy(m).start()
        spread(m, x, n2pair, dsend)
        exchange_half(0, m, dsend, n2recv, x)

    def twin_step(m):
        n2_copy(m).wait_recv()
        spread(m, away, n2pair, dsend)
        exchange_half(0, m, dsend, n2recv, away)

    def hide_step(m):
        @pl.when(m == 0)
        def _():
            for copy in local[7:9]:
                copy.wait()
            for copy in w_moe[:2]:
                copy.wait_recv()

        received(0, m, n2recv)

        @pl.loop(0, HIDDEN // 256)
        def _(j):
            cols = aligned(j * 256, 256, 128)
            rows = flat(n2recv, m)
            gate = dot(rows, wg[:, cols])
            up = dot(rows, wu[:, cols])
            bend = jnp.tanh(GELU_C * (gate + GELU_A * gate * gate * gate))
            gs[m, :, cols] = gate.astype(BF)
            us[m, :, cols] = up.astype(BF)
            hid[m, :, cols] = (0.5 * gate * (1.0 + bend) * up).astype(BF)


    def need_down():
        local[9].wait()
        w_moe[2].wait_recv()
        for copy in w_moe:
            copy.wait_send()

    def give_step(m):
        @pl.when(jnp.logical_and(first, m == 0))
        def _():
            need_down()
            pl.semaphore_signal(go_sem, inc=1, device_id={"section": 1}, device_id_type=MESH)

        sent(0, m, dsend)

        @pl.loop(0, WIDTH // 512)
        def _(j):
            cols = aligned(j * 512, 512, 128)
            block = dot(hid[m], wd[:, cols]).astype(BF)
            dsend[m, :, :, :, cols] = block.reshape(PLANE, 2, SLOTS, 512)

        exchange(1, m, dsend, yrecv)

    def weighed(m, source, cols):
        block = yrecv[m, :, source, :, cols].reshape(PLANE * SLOTS, 512)
        return dot_tn(cg_hi[m, source], block) + dot_tn(cg_lo[m, source], block)

    def far_step(m):
        received(1, m, yrecv)

        @pl.loop(0, WIDTH // 512)
        def _(j):
            cols = aligned(j * 512, 512, 128)
            far_send[0, m, :, cols] = weighed(m, away, cols).astype(BF)

        far_copy(1, m).start()

        @pl.loop(0, WIDTH // 512)
        def _(j):
            cols = aligned(j * 512, 512, 128)
            part_own[m, :, cols] = hid_one[m, :, cols] + weighed(m, x, cols)

    def join_step(m):
        far_copy(1, m).wait_recv()
        acts_s[m] = (part_own[m] + far_recv[0, m].astype(F32)).astype(BF)

        @pl.when(first)
        def _():
            acts_copy(m).start()

        out_copy(3, acts_s.at[m], acts_out.at[m], m).start()

    def dy_half(m, source):
        gate = cg_hi[m, source].astype(F32) + cg_lo[m, source].astype(F32)
        spread(m, source, gpair, bsend, jnp.sum(gate, axis=1, keepdims=True))
        exchange_half(2, m, bsend, dyrecv, source)

    def grad_step(m):
        @pl.when(first)
        def _():
            wait_for(gpair.at[m, x], gr_sem.at[x, m])

        @pl.when(jnp.logical_and(second, m == 0))
        def _():
            ct_local.wait()

        dy_half(m, x)

    def grad_twin_step(m):
        wait_for(gpair.at[m, away], gr_sem.at[away, m])
        dy_half(m, away)

    def back_step(m):
        pl.when(jnp.logical_and(second, m == 0))(need_down)
        received(2, m, dyrecv)

        @pl.loop(0, HIDDEN // 256)
        def _(j):
            cols = aligned(j * 256, 256, 128)
            dhid = dot_nt(flat(dyrecv, m), wd[cols, :])
            gate = gs[m, :, cols].astype(F32)
            up = us[m, :, cols].astype(F32)
            square = gate * gate
            bend = jnp.tanh(GELU_C * (gate + GELU_A * square * gate))
            half = 0.5 * (1.0 + bend)
            slope = half + 0.5 * gate * (1.0 - bend * bend) * (
                GELU_C * (1.0 + 3.0 * GELU_A * square)
            )
            gs[m, :, cols] = (dhid * up * slope).astype(BF)
            us[m, :, cols] = (dhid * (gate * half)).astype(BF)

        sent(2, m, bsend)

        @pl.loop(0, WIDTH // 512)
        def _(j):
            cols = aligned(j * 512, 512, 128)
            block = dot_nt(gs[m], wg[cols, :]) + dot_nt(us[m], wu[cols, :])
            bsend[m, :, :, :, cols] = block.astype(BF).reshape(PLANE, 2, SLOTS, 512)

        exchange(3, m, bsend, dn2recv)

    def gathered(m, source, cols):
        return dot_tn(
            sel[m, source], dn2recv[m, :, source, :, cols].reshape(PLANE * SLOTS, 512)
        )

    def far_back_step(m):
        received(3, m, dn2recv)

        @pl.loop(0, WIDTH // 512)
        def _(j):
            cols = aligned(j * 512, 512, 128)
            far_send[1, m, :, cols] = gathered(m, away, cols).astype(BF)

        far_copy(2, m).start()

        @pl.loop(0, WIDTH // 512)
        def _(j):
            cols = aligned(j * 512, 512, 128)
            dh_s[m, :, cols] = gathered(m, x, cols)

    def mid_step(m):
        far_copy(2, m).wait_recv()
        rows = hid_one[m]
        inverse = inverse_rms(rows)
        grad = dh_s[m] + far_recv[1, m].astype(F32)
        gains_acc[1:2] += jnp.sum(grad * rows * inverse, axis=0, keepdims=True)
        total = gpair[m, x].astype(F32) + rms_back(rows, inverse, gains[1:2], grad)
        dh_s[m] = total
        da_pair[m, own_rows] = total.astype(BF)
        da_copy(m).start()

    def da_copy(m):
        return to_partner(1, m, da_pair.at[m, own_rows], da_pair.at[m, own_rows])

    def dqkv_copy(m):
        return to_partner(3, m, dqkv_all.at[m, f], dqkv_all.at[m, f])

    def dn1_copy(m):
        return to_partner(2, m, dn1_send.at[m], dn1_recv.at[m])

    def attend_back_step(m):
        da_copy(m).wait_recv()
        out_copy(6, da_pair.at[m], da_out.at[m], m).start()

        @pl.loop(0, 2)
        def _(s):
            at = aligned(s * SEQ, SEQ, 16)
            dmix = dot_nt(da_pair[m, at], wo[...]).astype(BF)
            dmix = jnp.concatenate(
                [dmix[:, h * HEAD : (h + 1) * HEAD] for h in range(HEADS)], axis=0
            )
            queries = heads_of(qkvs, m, at)
            keys = qkvs[m, at, pl.ds(HALF, HEAD)]
            values = qkvs[m, at, pl.ds(HALF + HEAD, HEAD)]
            probs = softmax_of(m, s, queries, keys)
            dprobs = dot_nt(dmix, values)
            dvalues = dot_tn(probs.astype(BF), dmix)
            dscores = probs * (dprobs - jnp.sum(dprobs * probs, axis=-1, keepdims=True))
            dscores = (dscores * HEAD ** (-0.5)).astype(BF)
            cos = cos_t[m, at]
            sin = -sin_t[m, at]
            dkeys = rotate(dot_tn(dscores, queries), cos, sin)
            dqueries = dot(dscores, keys)
            for h in range(HEADS):
                part = rotate(dqueries[h * SEQ : (h + 1) * SEQ], cos, sin)
                dqkv_all[m, f, at, pl.ds(h * HEAD, HEAD)] = part.astype(BF)
            dqkv_all[m, f, at, pl.ds(HALF, HEAD)] = dkeys.astype(BF)
            dqkv_all[m, f, at, pl.ds(HALF + HEAD, HEAD)] = dvalues.astype(BF)
            part = dqkv_all.at[m, f, at]
            to_partner(3, m, part, part).start()

    def project_back_step(m):
        dqkv_copy(m).wait_recv()

        @pl.loop(0, HALF // 256)
        def _(j):
            cols = aligned(j * 256, 256, 128)
            block = dot_nt(dqkv_all[m, 0], wqkv[cols, pl.ds(0, QKV)])
            block = block + dot_nt(dqkv_all[m, 1], wqkv[cols, pl.ds(QKV, QKV)])
            top, low = block[:SEQ], block[SEQ:]
            mine = f == 0
            part_own[m, :, aligned(f * HALF + j * 256, 256, 128)] = jnp.where(mine, top, low)
            dn1_send[m, :, cols] = jnp.where(mine, low, top).astype(BF)

        dn1_copy(m).start()

    def close_step(m):
        dn1_copy(m).wait_recv()
        part_own[m, :, other_half] = dn1_recv[m].astype(F32)
        grad = part_own[m]
        rows = x_own[m].astype(F32)
        inverse = inverse_rms(rows)
        gains_acc[0:1] += jnp.sum(grad * rows * inverse, axis=0, keepdims=True)
        ingrad_s[m] = (dh_s[m] + rms_back(rows, inverse, gains[0:1], grad)).astype(BF)

        @pl.when(second)
        def _():
            for cross in (0, 1):
                grad_copy(m, cross).start()

        out_copy(7, ingrad_s.at[m], ingrad_out.at[m], m).start()

    half_rows = HALF
    quarter_rows = HIDDEN // 2

    def expert_out(i, m):
        src, own, their = (
            (wg, own_gate_out, their_gate_out),
            (wu, own_up_out, their_up_out),
            (wd, own_down_out, their_down_out),
        )[i]
        size = src.shape[0] // 2
        part = src.at[aligned(m * size, size, 16)]
        own = pltpu.make_async_copy(part, own, out_sem.at[i, m])
        their = pltpu.make_async_copy(part, their, out_sem.at[i, m])
        return own, their

    def start_out(i, m):
        own, their = expert_out(i, m)
        pl.when(m == f)(own.start)
        pl.when(m != f)(their.start)

    def grads_in_step(m):
        @pl.loop(0, 3)
        def _(j):
            cols = aligned(m * half_rows + j * 256, 256, 128)
            rows = n2recv[:, :, :, :, cols].reshape(MB * ROWS, 256)
            wg[cols, :] = dot_tn(rows, gs[...].reshape(MB * ROWS, HIDDEN)).astype(BF)
            wu[cols, :] = dot_tn(rows, us[...].reshape(MB * ROWS, HIDDEN)).astype(BF)

        start_out(0, m)
        start_out(1, m)

    def grads_out_step(m):
        cols = aligned(m * quarter_rows, quarter_rows, 128)

        @pl.loop(0, 3)
        def _(j):
            at = aligned(j * 512, 512, 128)
            rows = dyrecv[:, :, :, :, at].reshape(MB * ROWS, 512)
            wd[cols, at] = dot_tn(hid[:, :, cols].reshape(MB * ROWS, quarter_rows), rows).astype(BF)

        start_out(2, m)

    steps = {
        GRADS_IN: grads_in_step,
        GRADS_OUT: grads_out_step,
        ENTER: enter_step,
        PROJECT: project_step,
        PROJECT_BACK: project_back_step,
        ATTEND: attend_step,
        NORM: norm_step,
        TWIN: twin_step,
        HIDE: hide_step,
        GIVE: give_step,
        FAR: far_step,
        JOIN: join_step,
        GRAD: grad_step,
        GRAD_TWIN: grad_twin_step,
        BACK: back_step,
        FAR_BACK: far_back_step,
        MID: mid_step,
        ATTEND_BACK: attend_back_step,
        CLOSE: close_step,
        LOAD: load_step,
    }
    length = max(len(FIRST_PLAN), len(SECOND_PLAN))
    plans = [plan + ((REST, 0, 0),) * (length - len(plan)) for plan in (FIRST_PLAN, SECOND_PLAN)]

    @pl.loop(0, length)
    def _(i):
        code = jnp.int32(REST * MB)
        for at, ((step_a, m_a, _), (step_b, m_b, _)) in enumerate(zip(*plans)):
            here = jnp.where(first, step_a * MB + m_a, step_b * MB + m_b)
            code = jnp.where(i == at, here, code)
        m = lax.rem(code, MB)
        for step, work in steps.items():
            pl.when(code // MB == step)(functools.partial(work, m))
        for mine, plan in zip((first, second), plans):
            start = 0
            for at, (_, _, count) in enumerate(plan):
                if count:
                    part = w_pieces[start : start + count]

                    @pl.when(jnp.logical_and(mine, i == at))
                    def _():
                        for copy in part:
                            copy.start()

                start += count

    gains_out[...] = gains_acc[...]

    @pl.loop(0, MB)
    def _(m):
        out_copy(8, n1p.at[m], n1_out.at[m], m).start()
        out_copy(9, dqkv_all.at[m], dqkv_out.at[m], m).start()
        out_copy(10, att.at[m], att_out.at[m], m).start()
        sent(1, m, dsend)
        sent(3, m, bsend)
        to_partner(0, m, part_send.at[m], part_recv.at[m]).wait_send()
        da_copy(m).wait_send()
        dn1_copy(m).wait_send()
        dqkv_copy(m).wait_send()
        n1_copy(m).wait_send()
        pq_copy(m).wait_send()
        n2_copy(m).wait_send()
        far_copy(1, m).wait_send()
        far_copy(2, m).wait_send()

        @pl.when(first)
        def _():
            acts_copy(m).wait_send()

        @pl.when(second)
        def _():
            ct_copy(m).wait_send()
            for cross in (0, 1):
                grad_copy(m, cross).wait_send()

    side_copy.wait_send()
    meta_copy.wait_send()

    @pl.loop(0, MB)
    def _(m):
        pairs = (
            (3, acts_s.at[m], acts_out.at[m]),
            (6, da_pair.at[m], da_out.at[m]),
            (7, ingrad_s.at[m], ingrad_out.at[m]),
            (8, n1p.at[m], n1_out.at[m]),
            (9, dqkv_all.at[m], dqkv_out.at[m]),
            (10, att.at[m], att_out.at[m]),
        )
        for i, src, dst in pairs:
            out_copy(i, src, dst, m).wait()
        for i in range(3):
            expert_out(i, m)[0].wait()


def run_sections(*operands):
    def out(*shape, dtype=BF):
        return jax.ShapeDtypeStruct(shape, dtype)

    vmem = pl.BlockSpec(memory_space=pltpu.VMEM)
    anywhere = pl.BlockSpec(memory_space=pl.ANY)
    dma = pltpu.SemaphoreType.DMA
    blocks = (MB, PLANE, 2, SLOTS, WIDTH)
    return pl.pallas_call(
        section_kernel,
        name="sections",
        out_shape=(
            out(MB, SEQ, WIDTH),
            out(MB, SEQ, WIDTH),
            out(8, WIDTH, dtype=F32),
            out(HALF, HIDDEN),
            out(HALF, HIDDEN),
            out(HIDDEN // 2, WIDTH),
            out(HALF, HIDDEN),
            out(HALF, HIDDEN),
            out(HIDDEN // 2, WIDTH),
            out(MB, 2 * SEQ, HALF),
            out(MB, 2, 2 * SEQ, QKV),
            out(MB, 2 * SEQ, HALF),
            out(MB, 2 * SEQ, WIDTH),
        ),
        in_specs=[anywhere] * 9 + [vmem] * 6,
        out_specs=[anywhere] * 2 + [vmem] + [anywhere] * 10,
        scratch_shapes=[
            pltpu.VMEM((HALF, 2 * QKV), BF),
            pltpu.VMEM((HALF, WIDTH), BF),
            pltpu.VMEM((WIDTH, HIDDEN), BF),
            pltpu.VMEM((WIDTH, HIDDEN), BF),
            pltpu.VMEM((HIDDEN, WIDTH), BF),
            pltpu.VMEM((MB, SEQ, WIDTH), BF),
            pltpu.VMEM((MB, 2 * SEQ, HALF), BF),
            pltpu.VMEM((MB, SEQ, HALF), BF),
            pltpu.VMEM((MB, 2 * SEQ, QKV), F32),
            pltpu.VMEM((MB, 2 * SEQ, QKV), BF),
            pltpu.VMEM((MB, 2 * SEQ, QKV), BF),
            pltpu.VMEM((MB, 2 * SEQ, QKV), BF),
            pltpu.VMEM((MB, 2 * SEQ, HALF), BF),
            pltpu.VMEM((MB, SEQ, WIDTH), F32),
            pltpu.VMEM((MB, SEQ, WIDTH), F32),
            pltpu.VMEM((MB, SEQ, WIDTH), BF),
            pltpu.VMEM((MB, SEQ, WIDTH), BF),
            pltpu.VMEM((MB, 2, PLANE * SLOTS, SEQ), BF),
            pltpu.VMEM((MB, 2, PLANE * SLOTS, SEQ), BF),
            pltpu.VMEM((MB, 2, PLANE * SLOTS, SEQ), BF),
            pltpu.VMEM((MB, 2, SEQ, WIDTH), BF),
            pltpu.VMEM((MB, 2, SEQ, WIDTH), BF),
            pltpu.VMEM(blocks, BF),
            pltpu.VMEM(blocks, BF),
            pltpu.VMEM(blocks, BF),
            pltpu.VMEM(blocks, BF),
            pltpu.VMEM(blocks, BF),
            pltpu.VMEM(blocks, BF),
            pltpu.VMEM((MB, ROWS, HIDDEN), BF),
            pltpu.VMEM((MB, ROWS, HIDDEN), BF),
            pltpu.VMEM((MB, ROWS, HIDDEN), BF),
            pltpu.VMEM((2, MB, SEQ, WIDTH), BF),
            pltpu.VMEM((2, MB, SEQ, WIDTH), BF),
            pltpu.VMEM((MB, SEQ, WIDTH), BF),
            pltpu.VMEM((MB, SEQ, WIDTH), F32),
            pltpu.VMEM((MB, 2 * SEQ, WIDTH), BF),
            pltpu.VMEM((MB, 2, 2 * SEQ, QKV), BF),
            pltpu.VMEM((MB, SEQ, HALF), BF),
            pltpu.VMEM((MB, SEQ, HALF), BF),
            pltpu.VMEM((MB, SEQ, WIDTH), BF),
            pltpu.VMEM((8, WIDTH), F32),
            pltpu.VMEM((2, 8, HALF), F32),
            pltpu.VMEM((2, MB, 8, SEQ), F32),
            pltpu.VMEM((2, WIDTH), F32),
            pltpu.VMEM((MB, 2 * SEQ, HEAD), F32),
            pltpu.VMEM((MB, 2 * SEQ, HEAD), F32),
            pltpu.VMEM((MB, 2, SEQ, SEQ), F32),
            dma((12,)),
            dma((12,)),
            dma((10,)),
            dma((4, MB)),
            dma((4, MB)),
            dma((6, MB)),
            dma((6, MB)),
            dma((3, MB)),
            dma((3, MB)),
            dma((MB,)),
            dma((MB,)),
            dma((2, MB)),
            dma((2, MB)),
            dma((11, MB)),
            pltpu.SemaphoreType.REGULAR,
        ],
        compiler_params=pltpu.CompilerParams(
            collective_id=0, has_side_effects=True, vmem_limit_bytes=62 * 2**20
        ),
    )(*operands)


BAND = 192
SLICE = 48
LANES = (("z", 1024), ("y", 1024), ("z", 768), ("y", 768))


def grads_kernel(
    their_gate,
    their_up,
    their_down,
    n1_in,
    dqkv_in,
    att_in,
    da_in,
    gains_in,
    q_out,
    k_out,
    v_out,
    o_out,
    part_gate,
    part_up,
    part_down,
    gains_out,
    n1,
    dqkv,
    att,
    da,
    *rest,
):
    lane_refs, rest = [rest[i * 7 : i * 7 + 7] for i in range(len(LANES))], rest[7 * len(LANES) :]
    (
        small,
        small_recv,
        load_sem,
        send_sem,
        recv_sem,
        pair_send,
        pair_recv,
        small_send,
        small_recv_sem,
        out_sem,
    ) = rest
    f = lax.axis_index("fsdp")
    e = lax.axis_index("expert")
    y, x, z = e // 8, lax.rem(e // 4, 2), lax.rem(e, 4)
    other = 1 - f
    own_half = aligned(f * HALF, HALF, 128)
    other_half = aligned(other * HALF, HALF, 128)

    def along_y(d):
        return {"expert": lax.rem(y + d, 4) * 8 + x * 4 + z}

    def along_z(d):
        return {"expert": y * 8 + x * 4 + lax.rem(z + d, 4)}

    twin = {"expert": y * 8 + (1 - x) * 4 + z}
    partner = {"fsdp": other}

    barrier = pltpu.get_barrier_semaphore()
    neighbours = [along_y(d) for d in (1, 2, 3)] + [along_z(d) for d in (1, 2, 3)]
    neighbours += [twin, partner]
    for place in neighbours:
        pl.semaphore_signal(barrier, inc=1, device_id=place, device_id_type=MESH)

    loads = [
        (att_in, att),
        (da_in, da),
        (n1_in, n1),
        (dqkv_in, dqkv),
    ]
    loads = [pltpu.make_async_copy(a, b, load_sem.at[i]) for i, (a, b) in enumerate(loads)]
    for copy in loads:
        copy.start()

    def remote(src, dst, send, recv, place):
        return pltpu.make_async_remote_copy(
            src_ref=src,
            dst_ref=dst,
            send_sem=send,
            recv_sem=recv,
            device_id=place,
            device_id_type=MESH,
        )

    def wait_for(ref, sem):
        pltpu.make_async_copy(ref, ref, sem).wait()

    class Lane:
        def __init__(self, i):
            self.i = i
            self.v, self.r1, self.s1, self.r2, self.s2, self.r3, self.g = lane_refs[i]
            axes = ((along_y, y), (along_z, z))
            (self.axis, self.at), (self.next, self.to) = axes if LANES[i][0] == "y" else axes[::-1]
            half = LANES[i][1] // 2
            self.mine = aligned(x * half, half, 128)
            self.theirs = aligned((1 - x) * half, half, 128)
            self.place = aligned(self.at * BAND + self.to * SLICE, SLICE, 16)

        def send(self, stage, src, dst, place):
            remote(
                src, dst, send_sem.at[self.i, stage], recv_sem.at[self.i, stage], place
            ).start()

        def arrived(self, stage, ref):
            wait_for(ref, recv_sem.at[self.i, stage])

        def spread(self):
            for d in (1, 2, 3):
                rows = aligned(lax.rem(self.at + d, 4) * BAND, BAND, 16)
                self.send(0, self.v.at[rows], self.r1.at[self.at], self.axis(d))

        def join_one(self):
            self.arrived(0, self.r1.at[pl.ds(0, 3)])
            total = self.v[aligned(self.at * BAND, BAND, 16)].astype(F32)
            for d in (1, 2, 3):
                total = total + self.r1[lax.rem(self.at + d, 4)].astype(F32)
            self.s1[...] = total.astype(BF)
            for d in (1, 2, 3):
                rows = aligned(lax.rem(self.to + d, 4) * SLICE, SLICE, 16)
                self.send(1, self.s1.at[rows], self.r2.at[self.to], self.next(d))

        def join_two(self):
            self.arrived(1, self.r2.at[pl.ds(0, 3)])
            total = self.s1[aligned(self.to * SLICE, SLICE, 16)].astype(F32)
            for d in (1, 2, 3):
                total = total + self.r2[lax.rem(self.to + d, 4)].astype(F32)
            self.s2[...] = total.astype(BF)
            self.send(2, self.s2.at[:, self.theirs], self.r3, twin)

        def join_three(self):
            self.arrived(2, self.r3)
            total = self.s2[:, self.mine].astype(F32) + self.r3[...].astype(F32)
            self.g[self.place, self.mine] = total.astype(BF)
            part = self.g.at[self.place, self.mine]
            self.send(3, part, part, twin)

        def gather_two(self):
            self.arrived(3, self.g.at[self.place, self.theirs])
            part = self.g.at[self.place]
            for d in (1, 2, 3):
                self.send(4, part, part, self.next(d))

        def gather_one(self):
            self.arrived(4, self.g.at[pl.ds(0, 3 * SLICE)])
            part = self.g.at[aligned(self.at * BAND, BAND, 16)]
            for d in (1, 2, 3):
                self.send(5, part, part, self.axis(d))

        def finish(self):
            self.arrived(5, self.g.at[pl.ds(0, 3 * BAND)])

        def drain(self):
            wait_for(self.v.at[pl.ds(0, 3 * BAND)], send_sem.at[self.i, 0])
            wait_for(self.s1.at[pl.ds(0, 3 * SLICE)], send_sem.at[self.i, 1])
            wait_for(self.s2.at[:, self.theirs], send_sem.at[self.i, 2])
            wait_for(self.g.at[self.place, self.mine], send_sem.at[self.i, 3])
            wait_for(self.g.at[pl.ds(0, 3 * SLICE)], send_sem.at[self.i, 4])
            wait_for(self.g.at[pl.ds(0, 3 * BAND)], send_sem.at[self.i, 5])

    out_one, query_one, out_two, query_two = lanes = [Lane(i) for i in range(len(LANES))]

    def over_micro(group, cols):
        block = jnp.concatenate([dqkv[m, group, :, cols] for m in range(MB)], axis=0)
        return dot_tn(n1[...], block).astype(BF)

    for copy in loads[:2]:
        copy.wait()
    for j in range(2):
        cols = pl.ds(j * 512, 512)
        out_one.v[:, cols] = dot_tn(att[...], da[:, cols]).astype(BF)
    pl.semaphore_wait(barrier, len(neighbours))
    out_one.spread()
    for copy in loads[2:4]:
        copy.wait()
    query_one.v[:, pl.ds(0, HALF)] = over_micro(0, pl.ds(0, HALF))
    query_one.v[:, pl.ds(HALF, 256)] = over_micro(1, pl.ds(0, 256))
    query_one.spread()
    small[...] = gains_in[...]
    small_pair = remote(
        small.at[:, other_half],
        small_recv.at[0],
        small_send.at[0],
        small_recv_sem.at[0],
        partner,
    )
    small_pair.start()
    out_two.v[:, pl.ds(0, 512)] = dot_tn(att[...], da[:, pl.ds(1024, 512)]).astype(BF)
    query_two.v[:, pl.ds(0, 512)] = over_micro(1, pl.ds(256, 512))
    for g in range(2):
        query_two.v[:, pl.ds(512 + g * HEAD, HEAD)] = over_micro(g, pl.ds(HALF, HEAD))
        out_two.v[:, pl.ds(512 + g * HEAD, HEAD)] = over_micro(g, pl.ds(HALF + HEAD, HEAD))

    pair = [
        remote(src, dst, pair_send.at[i], pair_recv.at[i], partner)
        for i, (src, dst) in enumerate(
            ((their_gate, part_gate), (their_up, part_up), (their_down, part_down))
        )
    ]
    pieces = [
        remote(src.at[rows], dst.at[rows], pair_send.at[n], pair_recv.at[n], partner)
        for n, src, dst, size in (
            (0, their_gate, part_gate, HALF // 4),
            (1, their_up, part_up, HALF // 4),
            (2, their_down, part_down, HIDDEN // 8),
        )
        for rows in [pl.ds(i * size, size) for i in range(4)]
    ]

    def send_pieces(start, stop):
        for copy in pieces[start:stop]:
            copy.start()

    def spread_small(i, axis):
        for d in (1, 2, 3):
            remote(
                small.at[:, pl.ds(0, HALF)],
                small_recv.at[1 + 3 * i + d - 1],
                small_send.at[1 + 3 * i + d - 1],
                small_recv_sem.at[1 + 3 * i + d - 1],
                axis(d),
            ).start()

    def join_small(i, axis):
        for d in (1, 2, 3):
            remote(
                small.at[:, pl.ds(0, HALF)],
                small_recv.at[1 + 3 * i + d - 1],
                small_send.at[1 + 3 * i + d - 1],
                small_recv_sem.at[1 + 3 * i + d - 1],
                axis(d),
            ).wait()
        total = small[:, pl.ds(0, HALF)]
        for d in (1, 2, 3):
            total = total + small_recv[1 + 3 * i + d - 1]
        small[:, pl.ds(0, HALF)] = total

    small_pair.wait()
    small[:, pl.ds(0, HALF)] = small[:, own_half] + small_recv[0]
    spread_small(0, along_y)

    out_two.spread()
    query_two.spread()
    send_pieces(0, 4)
    join_small(0, along_y)
    spread_small(1, along_z)
    for lane in lanes:
        lane.join_one()
    for lane in lanes:
        lane.join_two()
    join_small(1, along_z)
    small_twin = remote(
        small.at[:, pl.ds(0, HALF)],
        small_recv.at[7],
        small_send.at[7],
        small_recv_sem.at[7],
        twin,
    )
    small_twin.start()
    send_pieces(4, 5)
    for lane in lanes:
        lane.join_three()
    send_pieces(5, 12)
    for lane in lanes:
        lane.gather_two()
    for lane in lanes:
        lane.gather_one()
    small_twin.wait()
    gains_out[...] = small[:, pl.ds(0, HALF)] + small_recv[7]

    outs = []

    def out_copy(src, dst):
        copy = pltpu.make_async_copy(src, dst, out_sem.at[len(outs)])
        copy.start()
        outs.append(copy)

    out_one.finish()
    out_copy(out_one.g, o_out.at[:, pl.ds(0, 1024)])
    query_one.finish()
    out_copy(query_one.g, q_out.at[:, pl.ds(0, 1024)])
    out_two.finish()
    out_copy(out_two.g.at[:, pl.ds(0, 512)], o_out.at[:, pl.ds(1024, 512)])
    out_copy(out_two.g.at[:, pl.ds(512, 256)], v_out)
    query_two.finish()
    out_copy(query_two.g.at[:, pl.ds(0, 512)], q_out.at[:, pl.ds(1024, 512)])
    out_copy(query_two.g.at[:, pl.ds(512, 256)], k_out)

    for lane in lanes:
        lane.drain()
    for copy in pair:
        copy.wait()
    for copy in outs:
        copy.wait()


def reduce_grads(*operands):
    def out(*shape):
        return jax.ShapeDtypeStruct(shape, BF)

    vmem = pl.BlockSpec(memory_space=pltpu.VMEM)
    anywhere = pl.BlockSpec(memory_space=pl.ANY)
    dma = pltpu.SemaphoreType.DMA
    lanes = []
    for _, width in LANES:
        lanes += [
            pltpu.VMEM((HALF, width), BF),
            pltpu.VMEM((4, BAND, width), BF),
            pltpu.VMEM((BAND, width), BF),
            pltpu.VMEM((4, SLICE, width), BF),
            pltpu.VMEM((SLICE, width), BF),
            pltpu.VMEM((SLICE, width // 2), BF),
            pltpu.VMEM((HALF, width), BF),
        ]
    return pl.pallas_call(
        grads_kernel,
        name="grads",
        out_shape=(
            out(HALF, WIDTH),
            out(HALF, 256),
            out(HALF, 256),
            out(HALF, WIDTH),
            out(HALF, HIDDEN),
            out(HALF, HIDDEN),
            out(HIDDEN // 2, WIDTH),
            jax.ShapeDtypeStruct((8, HALF), F32),
        ),
        in_specs=[anywhere] * 7 + [vmem],
        out_specs=[anywhere] * 7 + [vmem],
        scratch_shapes=[
            pltpu.VMEM((MB * 2 * SEQ, HALF), BF),
            pltpu.VMEM((MB, 2, 2 * SEQ, QKV), BF),
            pltpu.VMEM((MB * 2 * SEQ, HALF), BF),
            pltpu.VMEM((MB * 2 * SEQ, WIDTH), BF),
        ]
        + lanes
        + [
            pltpu.VMEM((8, WIDTH), F32),
            pltpu.VMEM((8, 8, HALF), F32),
            dma((4,)),
            dma((len(LANES), 6)),
            dma((len(LANES), 6)),
            dma((3,)),
            dma((3,)),
            dma((8,)),
            dma((8,)),
            dma((9,)),
        ],
        compiler_params=pltpu.CompilerParams(
            collective_id=1, has_side_effects=True, vmem_limit_bytes=62 * 2**20
        ),
    )(*operands)


def finish_kernel(*refs):
    (q, k, v, o, own_g, own_u, own_d, part_g, part_u, part_d, acts, grads, gains), outs = (
        refs[:13],
        refs[13:],
    )
    for src, dst in zip((q, k, v, o), outs):
        dst[...] = src[...].astype(F32)
    for own, part, dst in zip((own_g, own_u, own_d), (part_g, part_u, part_d), outs[4:]):
        dst[...] = own[...].astype(F32) + part[...].astype(F32)
    outs[7][...] = acts[...]
    outs[8][...] = grads[...]
    outs[9][...] = gains[0:1]
    outs[10][...] = gains[1:2]


def finish(*blocks):
    steps = 6

    def spec(rows, cols):
        return pl.BlockSpec((rows // steps, cols), lambda i: (i, 0))

    def whole(rows, cols):
        return pl.BlockSpec((rows, cols), lambda i: (0, 0))

    gains = blocks[-1]
    split = blocks[:-1]
    results = split[:7] + split[10:]
    dtypes = [F32] * 7 + [BF] * 2
    return pl.pallas_call(
        finish_kernel,
        name="finish",
        grid=(steps,),
        out_shape=[jax.ShapeDtypeStruct(b.shape, t) for b, t in zip(results, dtypes)]
        + [jax.ShapeDtypeStruct((1, HALF), F32)] * 2,
        in_specs=[spec(*b.shape) for b in split] + [whole(*gains.shape)],
        out_specs=[spec(*b.shape) for b in results] + [whole(1, HALF)] * 2,
        compiler_params=pltpu.CompilerParams(vmem_limit_bytes=62 * 2**20),
    )(*blocks)


def local(
    inputs,
    cotangent,
    segments,
    expert_ids,
    gate_logits,
    w_query,
    key_projection,
    value_projection,
    w_out,
    gain_attn,
    gain_moe,
    w_gate,
    w_up,
    w_down,
):
    steps = np.arange(HEAD) % (HEAD // 2)
    frequency = (ROPE_BASE ** (-steps * 2.0 / HEAD)).astype(np.float32)[None]
    (
        acts,
        in_grads,
        gain_parts,
        own_gate,
        own_up,
        own_down,
        their_gate,
        their_up,
        their_down,
        n1,
        dqkv,
        att,
        da,
    ) = run_sections(
        inputs,
        cotangent,
        w_query[0],
        key_projection[0],
        value_projection[0],
        w_out[0],
        w_gate[0, 0],
        w_up[0, 0],
        w_down[0, 0],
        gain_attn,
        gain_moe,
        segments,
        jnp.swapaxes(expert_ids[0], 1, 2),
        jnp.swapaxes(gate_logits[0], 1, 2),
        jnp.asarray(frequency),
    )
    gq, gk, gv, go, part_gate, part_up, part_down, gains = reduce_grads(
        their_gate,
        their_up,
        their_down,
        n1.reshape(MB * 2 * SEQ, HALF),
        dqkv,
        att.reshape(MB * 2 * SEQ, HALF),
        da.reshape(MB * 2 * SEQ, WIDTH),
        gain_parts,
    )
    gq, gk, gv, go, grad_gate, grad_up, grad_down, acts, in_grads, gain_one, gain_two = finish(
        gq,
        gk,
        gv,
        go,
        own_gate,
        own_up,
        own_down,
        part_gate,
        part_up,
        part_down,
        acts.reshape(MB * SEQ, WIDTH),
        in_grads.reshape(MB * SEQ, WIDTH),
        gains,
    )
    return (
        acts.reshape(1, MB, SEQ, WIDTH),
        in_grads.reshape(1, MB, SEQ, WIDTH),
        gq[None],
        gk[None],
        gv[None],
        go[None],
        gain_one,
        gain_two,
        grad_gate[None, None],
        grad_up[None, None],
        grad_down[None, None],
    )


def solution(mesh):
    return jax.shard_map(
        local,
        mesh=mesh,
        in_specs=(
            P(None, ("fsdp", "expert"), None),
            P(None, ("fsdp", "expert"), None),
            P(None, ("fsdp", "expert")),
            P("section", None, ("fsdp", "expert"), None),
            P("section", None, ("fsdp", "expert"), None),
            P("section", "fsdp", None),
            P("section", "fsdp", None),
            P("section", "fsdp", None),
            P("section", "fsdp", None),
            P("section", "fsdp"),
            P("section", "fsdp"),
            P("section", "expert", "fsdp", None),
            P("section", "expert", "fsdp", None),
            P("section", "expert", "fsdp", None),
        ),
        out_specs=(
            P("section", None, ("fsdp", "expert"), None),
            P("section", None, ("fsdp", "expert"), None),
            P("section", "fsdp", None),
            P("section", "fsdp", None),
            P("section", "fsdp", None),
            P("section", "fsdp", None),
            P("section", "fsdp"),
            P("section", "fsdp"),
            P("section", "expert", "fsdp", None),
            P("section", "expert", "fsdp", None),
            P("section", "expert", "fsdp", None),
        ),
        check_vma=False,
    )
```

```python
import functools

import jax
import jax.numpy as jnp
import numpy as np
from jax import lax
from jax.experimental import pallas as pl
from jax.experimental.pallas import tpu as pltpu
from jax.sharding import PartitionSpec as P

MESH = pl.DeviceIdType.MESH
BF = jnp.bfloat16
F32 = jnp.float32

HEAD = 128
EPS = 1e-06
ROPE_BASE = 1000000.0
GELU_C = 0.7978845608
GELU_A = 0.044715

MB = 2
SEQ = 96
WIDTH = 1536
HALF = 768
EXPERTS = 32
PLANE = 16
SLOTS = 16
ROWS = EXPERTS * SLOTS
HIDDEN = 768
HEADS = 6
QKV = 1024


def dot(a, b):
    return jnp.dot(a, b, preferred_element_type=F32)


def dot_nt(a, b):
    return lax.dot_general(a, b, (((1,), (1,)), ((), ())), preferred_element_type=F32)


def dot_tn(a, b):
    return lax.dot_general(a, b, (((0,), (0,)), ((), ())), preferred_element_type=F32)


def aligned(start, size, unit):
    return pl.ds(pl.multiple_of(start, unit), size)


def inverse_rms(rows):
    return lax.rsqrt(jnp.mean(rows * rows, axis=-1, keepdims=True) + EPS)


def rms_back(rows, inverse, gain, grad):
    scaled = gain * grad
    return inverse * scaled - rows * (inverse * inverse * inverse) * jnp.mean(
        scaled * rows, axis=-1, keepdims=True
    )


def rotate(head, cos, sin):
    return head * cos + pltpu.roll(head, HEAD // 2, 1) * sin


(
    ENTER,
    PROJECT,
    ATTEND,
    NORM,
    TWIN,
    HIDE,
    GIVE,
    FAR,
    JOIN,
    GRAD,
    GRAD_TWIN,
    BACK,
    FAR_BACK,
    MID,
    ATTEND_BACK,
    PROJECT_BACK,
    CLOSE,
    LOAD,
    IN_A,
    IN_B,
    IN_C,
    OUT_A,
    OUT_B,
    OUT_C,
    REST,
) = range(25)

FIRST_PLAN = (
    (ENTER, 0, 0),
    (ENTER, 1, 1),
    (PROJECT, 0, 1),
    (PROJECT, 1, 1),
    (ATTEND, 0, 1),
    (ATTEND, 1, 1),
    (NORM, 0, 1),
    (NORM, 1, 6),
    (TWIN, 0, 0),
    (TWIN, 1, 0),
    (HIDE, 0, 0),
    (HIDE, 1, 0),
    (GIVE, 0, 0),
    (GIVE, 1, 0),
    (FAR, 0, 0),
    (JOIN, 0, 0),
    (FAR, 1, 0),
    (JOIN, 1, 0),
    (GRAD, 0, 0),
    (GRAD_TWIN, 0, 0),
    (GRAD, 1, 0),
    (GRAD_TWIN, 1, 0),
    (BACK, 0, 0),
    (BACK, 1, 0),
    (IN_A, 0, 0),
    (IN_B, 0, 0),
    (IN_C, 0, 0),
    (FAR_BACK, 0, 0),
    (IN_A, 1, 0),
    (IN_B, 1, 0),
    (MID, 0, 0),
    (IN_C, 1, 0),
    (OUT_A, 0, 0),
    (OUT_B, 0, 0),
    (FAR_BACK, 1, 0),
    (ATTEND_BACK, 0, 0),
    (MID, 1, 0),
    (OUT_C, 0, 0),
    (PROJECT_BACK, 0, 0),
    (OUT_A, 1, 0),
    (ATTEND_BACK, 1, 0),
    (CLOSE, 0, 0),
    (OUT_B, 1, 0),
    (PROJECT_BACK, 1, 0),
    (OUT_C, 1, 0),
    (CLOSE, 1, 0),
)
SECOND_PLAN = (
    (GRAD, 0, 0),
    (GRAD, 1, 0),
    (LOAD, 0, 5),
    (ENTER, 0, 0),
    (PROJECT, 0, 1),
    (ENTER, 1, 1),
    (ATTEND, 0, 1),
    (PROJECT, 1, 1),
    (NORM, 0, 1),
    (ATTEND, 1, 1),
    (TWIN, 0, 0),
    (NORM, 1, 1),
    (TWIN, 1, 0),
    (GRAD_TWIN, 0, 0),
    (GRAD_TWIN, 1, 0),
    (HIDE, 0, 0),
    (HIDE, 1, 0),
    (BACK, 0, 0),
    (BACK, 1, 0),
    (GIVE, 0, 0),
    (GIVE, 1, 0),
    (FAR_BACK, 0, 0),
    (MID, 0, 0),
    (FAR_BACK, 1, 0),
    (ATTEND_BACK, 0, 0),
    (MID, 1, 0),
    (PROJECT_BACK, 0, 0),
    (ATTEND_BACK, 1, 0),
    (CLOSE, 0, 0),
    (PROJECT_BACK, 1, 0),
    (CLOSE, 1, 0),
    (IN_A, 0, 0),
    (IN_B, 0, 0),
    (IN_C, 0, 0),
    (IN_A, 1, 0),
    (IN_B, 1, 0),
    (IN_C, 1, 0),
    (OUT_A, 0, 0),
    (OUT_B, 0, 0),
    (OUT_C, 0, 0),
    (OUT_A, 1, 0),
    (OUT_B, 1, 0),
    (OUT_C, 1, 0),
    (FAR, 0, 0),
    (FAR, 1, 0),
    (JOIN, 0, 0),
    (JOIN, 1, 0),
)


def section_kernel(
    x_in,
    ct_in,
    wq_in,
    wk_in,
    wv_in,
    wo_in,
    wg_in,
    wu_in,
    wd_in,
    gain_one_in,
    gain_two_in,
    segments_in,
    ids_in,
    logits_in,
    freq_in,
    acts_out,
    ingrad_out,
    gains_out,
    own_gate_out,
    own_up_out,
    own_down_out,
    their_gate_out,
    their_up_out,
    their_down_out,
    n1_out,
    dqkv_out,
    att_out,
    da_out,
    wqkv,
    wo,
    wg,
    wu,
    wd,
    x_own,
    n1p,
    n1_send,
    pq_own,
    pq_send,
    pq_recv,
    qkvs,
    att,
    hid_one,
    part_own,
    part_send,
    part_recv,
    sel,
    cg_hi,
    cg_lo,
    n2pair,
    gpair,
    dsend,
    bsend,
    n2recv,
    yrecv,
    dyrecv,
    dn2recv,
    gs,
    us,
    hid,
    far_send,
    far_recv,
    acts_s,
    dh_s,
    da_pair,
    dqkv_all,
    dn1_send,
    dn1_recv,
    ingrad_s,
    gains_acc,
    side,
    meta,
    gains,
    cos_t,
    sin_t,
    mask_t,
    lw_sem,
    ws_sem,
    wr_sem,
    as_sem,
    ar_sem,
    ps_sem,
    pr_sem,
    ts_sem,
    tr_sem,
    xs_sem,
    xr_sem,
    gs_sem,
    gr_sem,
    out_sem,
    go_sem,
):
    sec = lax.axis_index("section")
    f = lax.axis_index("fsdp")
    e = lax.axis_index("expert")
    y, x, z = e // 8, lax.rem(e // 4, 2), lax.rem(e, 4)
    q = y * 4 + z
    away = 1 - x
    other = 1 - f
    own_rows = aligned(f * SEQ, SEQ, 16)
    own_half = aligned(f * HALF, HALF, 128)
    other_half = aligned(other * HALF, HALF, 128)
    partner = {"fsdp": other}
    twin_place = y * 8 + away * 4 + z
    twin = {"expert": twin_place}
    first, second = sec == 0, sec == 1

    def in_plane(d):
        at = lax.rem(q + d, PLANE)
        return at, {"expert": (at // 4) * 8 + x * 4 + lax.rem(at, 4)}

    barrier = pltpu.get_barrier_semaphore()

    @pl.loop(1, PLANE)
    def _(d):
        pl.semaphore_signal(barrier, inc=1, device_id=in_plane(d)[1], device_id_type=MESH)

    others = (
        twin,
        partner,
        {"section": 1 - sec},
        {"section": 1 - sec, "expert": twin_place},
    )
    for place in others:
        pl.semaphore_signal(barrier, inc=1, device_id=place, device_id_type=MESH)

    local = []
    for g in range(2):
        local += [
            (wq_in.at[:, pl.ds(g * HALF, HALF)], wqkv.at[:, pl.ds(g * QKV, HALF)]),
            (wk_in.at[:, pl.ds(g * HEAD, HEAD)], wqkv.at[:, pl.ds(g * QKV + HALF, HEAD)]),
            (wv_in.at[:, pl.ds(g * HEAD, HEAD)], wqkv.at[:, pl.ds(g * QKV + HALF + HEAD, HEAD)]),
        ]
    local += [
        (wo_in, wo),
        (wg_in, wg.at[own_half]),
        (wu_in, wu.at[own_half]),
        (wd_in, wd.at[aligned(f * (HIDDEN // 2), HIDDEN // 2, 16)]),
    ]
    local = [pltpu.make_async_copy(a, b, lw_sem.at[i]) for i, (a, b) in enumerate(local)]
    for copy in local:
        copy.start()
    x_local = pltpu.make_async_copy(x_in, x_own, lw_sem.at[10])
    ct_local = pltpu.make_async_copy(ct_in, gpair.at[:, x], lw_sem.at[11])
    pl.when(first)(x_local.start)
    pl.when(second)(ct_local.start)

    def remote(src, dst, send, recv, place):
        return pltpu.make_async_remote_copy(
            src_ref=src,
            dst_ref=dst,
            send_sem=send,
            recv_sem=recv,
            device_id=place,
            device_id_type=MESH,
        )

    def wait_for(ref, sem):
        pltpu.make_async_copy(ref, ref, sem).wait()

    def weight(src, dst, i):
        return remote(src, dst, ws_sem.at[i], wr_sem.at[i], partner)

    w_moe = [
        weight(wg_in, wg.at[own_half], 3),
        weight(wu_in, wu.at[own_half], 4),
        weight(wd_in, wd.at[aligned(f * (HIDDEN // 2), HIDDEN // 2, 16)], 5),
    ]

    w_pieces = [
        weight(src.at[aligned(i * size, size, 16)], dst.at[aligned(f * 4 * size + i * size, size, 16)], n)
        for n, src, dst, size in (
            (3, wg_in, wg, HALF // 4),
            (4, wu_in, wu, HALF // 4),
            (5, wd_in, wd, HIDDEN // 8),
        )
        for i in range(4)
    ]

    def ct_copy(m):
        return remote(ct_in.at[m], gpair.at[m, x], ws_sem.at[10 + m], gr_sem.at[x, m], twin)

    side[f, 0:1] = gain_one_in[...].astype(F32)
    side[f, 1:2] = gain_two_in[...].astype(F32)
    side[f, 2:4, :SEQ] = segments_in[...].astype(F32)
    for m in range(MB):
        meta[x, m, 0:4] = ids_in[m].astype(F32)
        meta[x, m, 4:8] = logits_in[m]
    row = lax.broadcasted_iota(jnp.int32, (SEQ, SEQ), 0)
    col = lax.broadcasted_iota(jnp.int32, (SEQ, SEQ), 1)
    unit = jnp.where(row == col, 1.0, 0.0).astype(BF)
    side_copy = weight(side.at[f], side.at[f], 8)
    meta_copy = remote(meta.at[x], meta.at[x], ws_sem.at[9], wr_sem.at[9], twin)
    gains_acc[...] = jnp.zeros_like(gains_acc)

    pl.semaphore_wait(barrier, PLANE - 1 + len(others))
    side_copy.start()
    meta_copy.start()

    meta_copy.wait_recv()
    earlier = jnp.where(row < col, 1.0, 0.0).astype(BF)

    @pl.loop(0, 2 * MB)
    def _(i):
        m, source = lax.rem(i, MB), i // MB
        rows = meta[source, m]
        ids, logits = rows[:4], rows[4:]
        raised = jnp.exp(logits - jnp.max(logits, axis=0, keepdims=True))
        gates = raised / jnp.sum(raised, axis=0, keepdims=True)
        place = lax.broadcasted_iota(jnp.int32, (PLANE, SEQ), 0)
        expert = ((place // 4) * 8 + x * 4 + lax.rem(place, 4)).astype(F32)
        named = jnp.zeros((PLANE, SEQ), F32)
        weights = jnp.zeros((PLANE, SEQ), F32)
        for k in range(4):
            hit = expert == ids[k : k + 1, :]
            named = jnp.where(hit, 1.0, named)
            weights = jnp.where(hit, gates[k : k + 1, :], weights)
        slot = dot(named.astype(BF), earlier)
        slot = jnp.where(named > 0.0, slot, -1.0)
        shape = (PLANE, SLOTS, SEQ)
        count = lax.broadcasted_iota(jnp.int32, shape, 1).astype(F32)
        chosen = jnp.where(jnp.broadcast_to(slot[:, None, :], shape) == count, 1.0, 0.0)
        scaled = chosen * jnp.broadcast_to(weights[:, None, :], shape)
        scaled = scaled.reshape(PLANE * SLOTS, SEQ)
        high = scaled.astype(BF)
        sel[m, source] = chosen.reshape(PLANE * SLOTS, SEQ).astype(BF)
        cg_hi[m, source] = high
        cg_lo[m, source] = (scaled - high.astype(F32)).astype(BF)

    side_copy.wait_recv()
    gains[:, pl.ds(0, HALF)] = side[0, 0:2]
    gains[:, pl.ds(HALF, HALF)] = side[1, 0:2]
    lane = lax.broadcasted_iota(jnp.int32, (SEQ, HEAD), 1)
    turn = jnp.where(lane < HEAD // 2, -1.0, 1.0)
    for m in range(MB):
        for s in range(2):
            across = jnp.broadcast_to(side[s, 2 + m : 3 + m, :SEQ], (SEQ, SEQ))
            down = dot_nt(unit, across.astype(BF))
            same = jnp.where(down == across, 1.0, 0.0)
            mask_t[m, s] = jnp.where(col <= row, same, 0.0)
            places = jnp.sum(jnp.where(col < row, same, 0.0), axis=1, keepdims=True)
            angles = places * freq_in[...]
            cos_t[m, pl.ds(s * SEQ, SEQ)] = jnp.cos(angles)
            sin_t[m, pl.ds(s * SEQ, SEQ)] = jnp.sin(angles) * turn

    def exchange_half(kind, m, src, dst, source):
        @pl.loop(1, PLANE)
        def _(d):
            at, place = in_plane(d)
            remote(
                src.at[m, at, source],
                dst.at[m, q, source],
                as_sem.at[kind, m],
                ar_sem.at[kind, m],
                place,
            ).start()

        dst[m, q, source] = src[m, q, source]

    def exchange(kind, m, src, dst):
        @pl.loop(1, PLANE)
        def _(d):
            at, place = in_plane(d)
            remote(
                src.at[m, at], dst.at[m, q], as_sem.at[kind, m], ar_sem.at[kind, m], place
            ).start()

        dst[m, q] = src[m, q]

    def received(kind, m, dst):
        wait_for(dst.at[m, pl.ds(0, PLANE - 1)], ar_sem.at[kind, m])

    def sent(kind, m, src):
        wait_for(src.at[m, pl.ds(0, PLANE - 1)], as_sem.at[kind, m])

    def to_partner(kind, m, src, dst):
        return remote(src, dst, ps_sem.at[kind, m], pr_sem.at[kind, m], partner)

    def to_twin(kind, m, src, dst):
        return remote(src, dst, ts_sem.at[kind, m], tr_sem.at[kind, m], twin)

    def n2_copy(m):
        return to_twin(0, m, n2pair.at[m, x], n2pair.at[m, x])

    def far_copy(kind, m):
        return to_twin(kind, m, far_send.at[kind - 1, m], far_recv.at[kind - 1, m])

    def acts_copy(m):
        return remote(acts_s.at[m], x_own.at[m], xs_sem.at[m], xr_sem.at[m], {"section": 1})

    def n1_copy(m):
        return to_partner(4, m, n1_send.at[m], n1p.at[m, own_rows])

    def pq_copy(m):
        return to_partner(5, m, pq_send.at[m], pq_recv.at[m])

    def grad_copy(m, cross):
        place = {"section": 0, "expert": twin_place} if cross else {"section": 0}
        return remote(
            ingrad_s.at[m], gpair.at[m, x], gs_sem.at[cross, m], gr_sem.at[x, m], place
        )

    def out_copy(i, src, dst, m):
        return pltpu.make_async_copy(src, dst, out_sem.at[i, m])

    def flat(ref, m):
        return ref[m].reshape(ROWS, WIDTH)

    def spread(m, source, rows, dst, scale=None):
        @pl.loop(0, WIDTH // 512)
        def _(j):
            cols = aligned(j * 512, 512, 128)
            block = dot(sel[m, source], rows[m, source, :, cols])
            if scale is not None:
                block = block * scale
            dst[m, :, source, :, cols] = block.astype(BF).reshape(PLANE, SLOTS, 512)

    def load_step(m):
        pl.semaphore_wait(go_sem, 1)
        ct_copy(0).start()
        ct_copy(1).start()

    def heads_of(ref, m, rows):
        return jnp.concatenate(
            [ref[m, rows, pl.ds(h * HEAD, HEAD)] for h in range(HEADS)], axis=0
        )

    def softmax_of(m, s, queries, keys):
        scores = dot_nt(queries, keys) * HEAD ** (-0.5)
        allowed = jnp.concatenate([mask_t[m, s]] * HEADS, axis=0)
        scores = jnp.where(allowed > 0.0, scores, -1e30)
        raised = jnp.exp(scores - jnp.max(scores, axis=-1, keepdims=True))
        return raised / jnp.sum(raised, axis=-1, keepdims=True)

    def enter_step(m):
        pl.when(jnp.logical_and(first, m == 0))(x_local.wait)
        pl.when(second)(lambda: wait_for(x_own.at[m], xr_sem.at[m]))
        rows = x_own[m].astype(F32)
        scale = inverse_rms(rows)
        n1p[m, own_rows] = (x_own[m, :, own_half].astype(F32) * scale * gains[0:1, own_half]).astype(BF)
        n1_send[m] = (
            x_own[m, :, other_half].astype(F32) * scale * gains[0:1, other_half]
        ).astype(BF)
        n1_copy(m).start()

    def project_step(m):
        @pl.when(m == 0)
        def _():
            for copy in local[:6]:
                copy.wait()

        n1_copy(m).wait_recv()

        @pl.loop(0, QKV // 512)
        def _(j):
            cols = aligned(j * 512, 512, 128)
            from_w = aligned(other * QKV + j * 512, 512, 128)
            pq_send[m, :, cols] = dot(n1p[m], wqkv[:, from_w]).astype(BF)

        pq_copy(m).start()

        @pl.loop(0, QKV // 512)
        def _(j):
            cols = aligned(j * 512, 512, 128)
            from_w = aligned(f * QKV + j * 512, 512, 128)
            pq_own[m, :, cols] = dot(n1p[m], wqkv[:, from_w])

    def attend_step(m):
        pl.when(m == 0)(local[6].wait)
        pq_copy(m).wait_recv()
        cos, sin = cos_t[m], sin_t[m]
        for j in range(2 * HEADS - 4):
            cols = pl.ds(j * HEAD, HEAD)
            head = pq_own[m, :, cols] + pq_recv[m, :, cols].astype(F32)
            if j <= HEADS:
                head = rotate(head, cos, sin)
            qkvs[m, :, cols] = head.astype(BF)

        @pl.loop(0, 2)
        def _(i):
            s = jnp.where(i == 0, other, f)
            at = aligned(s * SEQ, SEQ, 16)
            queries = heads_of(qkvs, m, at)
            keys = qkvs[m, at, pl.ds(HALF, HEAD)]
            values = qkvs[m, at, pl.ds(HALF + HEAD, HEAD)]
            probs = softmax_of(m, s, queries, keys).astype(BF)
            mixed = dot(probs, values).astype(BF)
            for h in range(HEADS):
                att[m, at, pl.ds(h * HEAD, HEAD)] = mixed[h * SEQ : (h + 1) * SEQ]

            @pl.loop(0, WIDTH // 512)
            def _(j):
                cols = aligned(j * 512, 512, 128)
                block = dot(att[m, at], wo[:, cols])

                @pl.when(i == 0)
                def _():
                    part_send[m, :, cols] = block.astype(BF)

                @pl.when(i == 1)
                def _():
                    hid_one[m, :, cols] = block

            pl.when(i == 0)(to_partner(0, m, part_send.at[m], part_recv.at[m]).start)

    def norm_step(m):
        to_partner(0, m, part_send.at[m], part_recv.at[m]).wait_recv()
        rows = x_own[m].astype(F32) + (hid_one[m] + part_recv[m].astype(F32))
        hid_one[m] = rows
        n2pair[m, x] = (rows * inverse_rms(rows) * gains[1:2]).astype(BF)
        n2_copy(m).start()
        spread(m, x, n2pair, dsend)
        exchange_half(0, m, dsend, n2recv, x)

    def twin_step(m):
        n2_copy(m).wait_recv()
        spread(m, away, n2pair, dsend)
        exchange_half(0, m, dsend, n2recv, away)

    def hide_step(m):
        @pl.when(m == 0)
        def _():
            for copy in local[7:9]:
                copy.wait()
            for copy in w_moe[:2]:
                copy.wait_recv()

        received(0, m, n2recv)

        @pl.loop(0, HIDDEN // 256)
        def _(j):
            cols = aligned(j * 256, 256, 128)
            rows = flat(n2recv, m)
            gate = dot(rows, wg[:, cols])
            up = dot(rows, wu[:, cols])
            bend = jnp.tanh(GELU_C * (gate + GELU_A * gate * gate * gate))
            gs[m, :, cols] = gate.astype(BF)
            us[m, :, cols] = up.astype(BF)
            hid[m, :, cols] = (0.5 * gate * (1.0 + bend) * up).astype(BF)


    def need_down():
        local[9].wait()
        w_moe[2].wait_recv()
        for copy in w_moe:
            copy.wait_send()

    def give_step(m):
        @pl.when(jnp.logical_and(first, m == 0))
        def _():
            need_down()
            pl.semaphore_signal(go_sem, inc=1, device_id={"section": 1}, device_id_type=MESH)

        sent(0, m, dsend)

        @pl.loop(0, WIDTH // 512)
        def _(j):
            cols = aligned(j * 512, 512, 128)
            block = dot(hid[m], wd[:, cols]).astype(BF)
            dsend[m, :, :, :, cols] = block.reshape(PLANE, 2, SLOTS, 512)

        exchange(1, m, dsend, yrecv)

    def weighed(m, source, cols):
        block = yrecv[m, :, source, :, cols].reshape(PLANE * SLOTS, 512)
        return dot_tn(cg_hi[m, source], block) + dot_tn(cg_lo[m, source], block)

    def far_step(m):
        received(1, m, yrecv)

        @pl.loop(0, WIDTH // 512)
        def _(j):
            cols = aligned(j * 512, 512, 128)
            far_send[0, m, :, cols] = weighed(m, away, cols).astype(BF)

        far_copy(1, m).start()

        @pl.loop(0, WIDTH // 512)
        def _(j):
            cols = aligned(j * 512, 512, 128)
            part_own[m, :, cols] = hid_one[m, :, cols] + weighed(m, x, cols)

    def join_step(m):
        far_copy(1, m).wait_recv()
        acts_s[m] = (part_own[m] + far_recv[0, m].astype(F32)).astype(BF)

        @pl.when(first)
        def _():
            acts_copy(m).start()

        out_copy(3, acts_s.at[m], acts_out.at[m], m).start()

    def dy_half(m, source):
        gate = cg_hi[m, source].astype(F32) + cg_lo[m, source].astype(F32)
        spread(m, source, gpair, bsend, jnp.sum(gate, axis=1, keepdims=True))
        exchange_half(2, m, bsend, dyrecv, source)

    def grad_step(m):
        @pl.when(first)
        def _():
            wait_for(gpair.at[m, x], gr_sem.at[x, m])

        @pl.when(jnp.logical_and(second, m == 0))
        def _():
            ct_local.wait()

        dy_half(m, x)

    def grad_twin_step(m):
        wait_for(gpair.at[m, away], gr_sem.at[away, m])
        dy_half(m, away)

    def back_step(m):
        pl.when(jnp.logical_and(second, m == 0))(need_down)
        received(2, m, dyrecv)

        @pl.loop(0, HIDDEN // 256)
        def _(j):
            cols = aligned(j * 256, 256, 128)
            dhid = dot_nt(flat(dyrecv, m), wd[cols, :])
            gate = gs[m, :, cols].astype(F32)
            up = us[m, :, cols].astype(F32)
            square = gate * gate
            bend = jnp.tanh(GELU_C * (gate + GELU_A * square * gate))
            half = 0.5 * (1.0 + bend)
            slope = half + 0.5 * gate * (1.0 - bend * bend) * (
                GELU_C * (1.0 + 3.0 * GELU_A * square)
            )
            gs[m, :, cols] = (dhid * up * slope).astype(BF)
            us[m, :, cols] = (dhid * (gate * half)).astype(BF)

        sent(2, m, bsend)

        @pl.loop(0, WIDTH // 512)
        def _(j):
            cols = aligned(j * 512, 512, 128)
            block = dot_nt(gs[m], wg[cols, :]) + dot_nt(us[m], wu[cols, :])
            bsend[m, :, :, :, cols] = block.astype(BF).reshape(PLANE, 2, SLOTS, 512)

        exchange(3, m, bsend, dn2recv)

    def gathered(m, source, cols):
        return dot_tn(
            sel[m, source], dn2recv[m, :, source, :, cols].reshape(PLANE * SLOTS, 512)
        )

    def far_back_step(m):
        received(3, m, dn2recv)

        @pl.when(jnp.logical_and(first, m == 1))
        def _():
            pl.semaphore_signal(go_sem, inc=1, device_id={"section": 1}, device_id_type=MESH)


        @pl.loop(0, WIDTH // 512)
        def _(j):
            cols = aligned(j * 512, 512, 128)
            far_send[1, m, :, cols] = gathered(m, away, cols).astype(BF)

        far_copy(2, m).start()

        @pl.loop(0, WIDTH // 512)
        def _(j):
            cols = aligned(j * 512, 512, 128)
            dh_s[m, :, cols] = gathered(m, x, cols)

    def mid_step(m):
        far_copy(2, m).wait_recv()
        rows = hid_one[m]
        inverse = inverse_rms(rows)
        grad = dh_s[m] + far_recv[1, m].astype(F32)
        gains_acc[1:2] += jnp.sum(grad * rows * inverse, axis=0, keepdims=True)
        total = gpair[m, x].astype(F32) + rms_back(rows, inverse, gains[1:2], grad)
        dh_s[m] = total
        da_pair[m, own_rows] = total.astype(BF)
        da_copy(m).start()

    def da_copy(m):
        return to_partner(1, m, da_pair.at[m, own_rows], da_pair.at[m, own_rows])

    def dqkv_copy(m):
        return to_partner(3, m, dqkv_all.at[m, f], dqkv_all.at[m, f])

    def dn1_copy(m):
        return to_partner(2, m, dn1_send.at[m], dn1_recv.at[m])

    def attend_back_step(m):
        @pl.loop(0, 2)
        def _(i):
            s = jnp.where(i == 0, f, other)

            @pl.when(i == 1)
            def _():
                da_copy(m).wait_recv()
                out_copy(6, da_pair.at[m], da_out.at[m], m).start()

            at = aligned(s * SEQ, SEQ, 16)
            dmix = dot_nt(da_pair[m, at], wo[...]).astype(BF)
            dmix = jnp.concatenate(
                [dmix[:, h * HEAD : (h + 1) * HEAD] for h in range(HEADS)], axis=0
            )
            queries = heads_of(qkvs, m, at)
            keys = qkvs[m, at, pl.ds(HALF, HEAD)]
            values = qkvs[m, at, pl.ds(HALF + HEAD, HEAD)]
            probs = softmax_of(m, s, queries, keys)
            dprobs = dot_nt(dmix, values)
            dvalues = dot_tn(probs.astype(BF), dmix)
            dscores = probs * (dprobs - jnp.sum(dprobs * probs, axis=-1, keepdims=True))
            dscores = (dscores * HEAD ** (-0.5)).astype(BF)
            cos = cos_t[m, at]
            sin = -sin_t[m, at]
            dkeys = rotate(dot_tn(dscores, queries), cos, sin)
            dqueries = dot(dscores, keys)
            for h in range(HEADS):
                part = rotate(dqueries[h * SEQ : (h + 1) * SEQ], cos, sin)
                dqkv_all[m, f, at, pl.ds(h * HEAD, HEAD)] = part.astype(BF)
            dqkv_all[m, f, at, pl.ds(HALF, HEAD)] = dkeys.astype(BF)
            dqkv_all[m, f, at, pl.ds(HALF + HEAD, HEAD)] = dvalues.astype(BF)
            part = dqkv_all.at[m, f, at]
            to_partner(3, m, part, part).start()

    def project_back_step(m):
        dqkv_copy(m).wait_recv()

        @pl.loop(0, 2)
        def _(i):
            at = aligned(jnp.where(i == 0, other, f) * SEQ, SEQ, 16)

            @pl.loop(0, HALF // 256)
            def _(j):
                cols = aligned(j * 256, 256, 128)
                block = dot_nt(dqkv_all[m, 0, at], wqkv[cols, pl.ds(0, QKV)])
                block = block + dot_nt(dqkv_all[m, 1, at], wqkv[cols, pl.ds(QKV, QKV)])

                @pl.when(i == 0)
                def _():
                    dn1_send[m, :, cols] = block.astype(BF)

                @pl.when(i == 1)
                def _():
                    part_own[m, :, aligned(f * HALF + j * 256, 256, 128)] = block

            pl.when(i == 0)(dn1_copy(m).start)

    def close_step(m):
        dn1_copy(m).wait_recv()
        part_own[m, :, other_half] = dn1_recv[m].astype(F32)
        grad = part_own[m]
        rows = x_own[m].astype(F32)
        inverse = inverse_rms(rows)
        gains_acc[0:1] += jnp.sum(grad * rows * inverse, axis=0, keepdims=True)
        ingrad_s[m] = (dh_s[m] + rms_back(rows, inverse, gains[0:1], grad)).astype(BF)

        @pl.when(second)
        def _():
            for cross in (0, 1):
                grad_copy(m, cross).start()

        out_copy(7, ingrad_s.at[m], ingrad_out.at[m], m).start()

    half_rows = HALF
    quarter_rows = HIDDEN // 2

    def expert_out(i, m):
        src, own, their = (
            (wg, own_gate_out, their_gate_out),
            (wu, own_up_out, their_up_out),
            (wd, own_down_out, their_down_out),
        )[i]
        size = src.shape[0] // 2
        part = src.at[aligned(m * size, size, 16)]
        own = pltpu.make_async_copy(part, own, out_sem.at[i, m])
        their = pltpu.make_async_copy(part, their, out_sem.at[i, m])
        return own, their

    def start_out(i, m):
        own, their = expert_out(i, m)
        pl.when(m == f)(own.start)
        pl.when(m != f)(their.start)

    def grads_in_step(j, m):
        cols = aligned(m * half_rows + j * 256, 256, 128)
        rows = n2recv[:, :, :, :, cols].reshape(MB * ROWS, 256)
        wg[cols, :] = dot_tn(rows, gs[...].reshape(MB * ROWS, HIDDEN)).astype(BF)
        wu[cols, :] = dot_tn(rows, us[...].reshape(MB * ROWS, HIDDEN)).astype(BF)
        if j == 2:
            start_out(0, m)
            start_out(1, m)

    def grads_out_step(j, m):
        cols = aligned(m * quarter_rows, quarter_rows, 128)
        at = pl.ds(j * 512, 512)
        rows = dyrecv[:, :, :, :, at].reshape(MB * ROWS, 512)
        wd[cols, at] = dot_tn(hid[:, :, cols].reshape(MB * ROWS, quarter_rows), rows).astype(BF)
        if j == 2:
            start_out(2, m)

    steps = {
        IN_A: functools.partial(grads_in_step, 0),
        IN_B: functools.partial(grads_in_step, 1),
        IN_C: functools.partial(grads_in_step, 2),
        OUT_A: functools.partial(grads_out_step, 0),
        OUT_B: functools.partial(grads_out_step, 1),
        OUT_C: functools.partial(grads_out_step, 2),
        ENTER: enter_step,
        PROJECT: project_step,
        PROJECT_BACK: project_back_step,
        ATTEND: attend_step,
        NORM: norm_step,
        TWIN: twin_step,
        HIDE: hide_step,
        GIVE: give_step,
        FAR: far_step,
        JOIN: join_step,
        GRAD: grad_step,
        GRAD_TWIN: grad_twin_step,
        BACK: back_step,
        FAR_BACK: far_back_step,
        MID: mid_step,
        ATTEND_BACK: attend_back_step,
        CLOSE: close_step,
        LOAD: load_step,
    }
    length = max(len(FIRST_PLAN), len(SECOND_PLAN))
    plans = [plan + ((REST, 0, 0),) * (length - len(plan)) for plan in (FIRST_PLAN, SECOND_PLAN)]

    @pl.loop(0, length)
    def _(i):
        code = jnp.int32(REST * MB)
        for at, ((step_a, m_a, _), (step_b, m_b, _)) in enumerate(zip(*plans)):
            here = jnp.where(first, step_a * MB + m_a, step_b * MB + m_b)
            code = jnp.where(i == at, here, code)
        m = lax.rem(code, MB)
        for step, work in steps.items():
            pl.when(code // MB == step)(functools.partial(work, m))
        for mine, plan in zip((first, second), plans):
            start = 0
            for at, (_, _, count) in enumerate(plan):
                if count:
                    part = w_pieces[start : start + count]

                    @pl.when(jnp.logical_and(mine, i == at))
                    def _():
                        for copy in part:
                            copy.start()

                start += count

    pl.when(second)(lambda: pl.semaphore_wait(go_sem, 1))

    gains_out[...] = gains_acc[...]

    @pl.loop(0, MB)
    def _(m):
        out_copy(8, n1p.at[m], n1_out.at[m], m).start()
        out_copy(9, dqkv_all.at[m], dqkv_out.at[m], m).start()
        out_copy(10, att.at[m], att_out.at[m], m).start()
        sent(1, m, dsend)
        sent(3, m, bsend)
        to_partner(0, m, part_send.at[m], part_recv.at[m]).wait_send()
        da_copy(m).wait_send()
        dn1_copy(m).wait_send()
        dqkv_copy(m).wait_send()
        n1_copy(m).wait_send()
        pq_copy(m).wait_send()
        n2_copy(m).wait_send()
        far_copy(1, m).wait_send()
        far_copy(2, m).wait_send()

        @pl.when(first)
        def _():
            acts_copy(m).wait_send()

        @pl.when(second)
        def _():
            ct_copy(m).wait_send()
            for cross in (0, 1):
                grad_copy(m, cross).wait_send()

    side_copy.wait_send()
    meta_copy.wait_send()

    @pl.loop(0, MB)
    def _(m):
        pairs = (
            (3, acts_s.at[m], acts_out.at[m]),
            (6, da_pair.at[m], da_out.at[m]),
            (7, ingrad_s.at[m], ingrad_out.at[m]),
            (8, n1p.at[m], n1_out.at[m]),
            (9, dqkv_all.at[m], dqkv_out.at[m]),
            (10, att.at[m], att_out.at[m]),
        )
        for i, src, dst in pairs:
            out_copy(i, src, dst, m).wait()
        for i in range(3):
            expert_out(i, m)[0].wait()


def run_sections(*operands):
    def out(*shape, dtype=BF):
        return jax.ShapeDtypeStruct(shape, dtype)

    vmem = pl.BlockSpec(memory_space=pltpu.VMEM)
    anywhere = pl.BlockSpec(memory_space=pl.ANY)
    dma = pltpu.SemaphoreType.DMA
    blocks = (MB, PLANE, 2, SLOTS, WIDTH)
    return pl.pallas_call(
        section_kernel,
        name="sections",
        out_shape=(
            out(MB, SEQ, WIDTH),
            out(MB, SEQ, WIDTH),
            out(8, WIDTH, dtype=F32),
            out(HALF, HIDDEN),
            out(HALF, HIDDEN),
            out(HIDDEN // 2, WIDTH),
            out(HALF, HIDDEN),
            out(HALF, HIDDEN),
            out(HIDDEN // 2, WIDTH),
            out(MB, 2 * SEQ, HALF),
            out(MB, 2, 2 * SEQ, QKV),
            out(MB, 2 * SEQ, HALF),
            out(MB, 2 * SEQ, WIDTH),
        ),
        in_specs=[anywhere] * 9 + [vmem] * 6,
        out_specs=[anywhere] * 2 + [vmem] + [anywhere] * 10,
        scratch_shapes=[
            pltpu.VMEM((HALF, 2 * QKV), BF),
            pltpu.VMEM((HALF, WIDTH), BF),
            pltpu.VMEM((WIDTH, HIDDEN), BF),
            pltpu.VMEM((WIDTH, HIDDEN), BF),
            pltpu.VMEM((HIDDEN, WIDTH), BF),
            pltpu.VMEM((MB, SEQ, WIDTH), BF),
            pltpu.VMEM((MB, 2 * SEQ, HALF), BF),
            pltpu.VMEM((MB, SEQ, HALF), BF),
            pltpu.VMEM((MB, 2 * SEQ, QKV), F32),
            pltpu.VMEM((MB, 2 * SEQ, QKV), BF),
            pltpu.VMEM((MB, 2 * SEQ, QKV), BF),
            pltpu.VMEM((MB, 2 * SEQ, QKV), BF),
            pltpu.VMEM((MB, 2 * SEQ, HALF), BF),
            pltpu.VMEM((MB, SEQ, WIDTH), F32),
            pltpu.VMEM((MB, SEQ, WIDTH), F32),
            pltpu.VMEM((MB, SEQ, WIDTH), BF),
            pltpu.VMEM((MB, SEQ, WIDTH), BF),
            pltpu.VMEM((MB, 2, PLANE * SLOTS, SEQ), BF),
            pltpu.VMEM((MB, 2, PLANE * SLOTS, SEQ), BF),
            pltpu.VMEM((MB, 2, PLANE * SLOTS, SEQ), BF),
            pltpu.VMEM((MB, 2, SEQ, WIDTH), BF),
            pltpu.VMEM((MB, 2, SEQ, WIDTH), BF),
            pltpu.VMEM(blocks, BF),
            pltpu.VMEM(blocks, BF),
            pltpu.VMEM(blocks, BF),
            pltpu.VMEM(blocks, BF),
            pltpu.VMEM(blocks, BF),
            pltpu.VMEM(blocks, BF),
            pltpu.VMEM((MB, ROWS, HIDDEN), BF),
            pltpu.VMEM((MB, ROWS, HIDDEN), BF),
            pltpu.VMEM((MB, ROWS, HIDDEN), BF),
            pltpu.VMEM((2, MB, SEQ, WIDTH), BF),
            pltpu.VMEM((2, MB, SEQ, WIDTH), BF),
            pltpu.VMEM((MB, SEQ, WIDTH), BF),
            pltpu.VMEM((MB, SEQ, WIDTH), F32),
            pltpu.VMEM((MB, 2 * SEQ, WIDTH), BF),
            pltpu.VMEM((MB, 2, 2 * SEQ, QKV), BF),
            pltpu.VMEM((MB, SEQ, HALF), BF),
            pltpu.VMEM((MB, SEQ, HALF), BF),
            pltpu.VMEM((MB, SEQ, WIDTH), BF),
            pltpu.VMEM((8, WIDTH), F32),
            pltpu.VMEM((2, 8, HALF), F32),
            pltpu.VMEM((2, MB, 8, SEQ), F32),
            pltpu.VMEM((2, WIDTH), F32),
            pltpu.VMEM((MB, 2 * SEQ, HEAD), F32),
            pltpu.VMEM((MB, 2 * SEQ, HEAD), F32),
            pltpu.VMEM((MB, 2, SEQ, SEQ), F32),
            dma((12,)),
            dma((12,)),
            dma((10,)),
            dma((4, MB)),
            dma((4, MB)),
            dma((6, MB)),
            dma((6, MB)),
            dma((3, MB)),
            dma((3, MB)),
            dma((MB,)),
            dma((MB,)),
            dma((2, MB)),
            dma((2, MB)),
            dma((11, MB)),
            pltpu.SemaphoreType.REGULAR,
        ],
        compiler_params=pltpu.CompilerParams(
            collective_id=0, has_side_effects=True, vmem_limit_bytes=62 * 2**20
        ),
    )(*operands)


BAND = 192
SLICE = 48
LANES = (("z", 1024), ("y", 1024), ("z", 768), ("y", 768))


def grads_kernel(
    their_gate,
    their_up,
    their_down,
    n1_in,
    dqkv_in,
    att_in,
    da_in,
    gains_in,
    q_out,
    k_out,
    v_out,
    o_out,
    part_gate,
    part_up,
    part_down,
    gains_out,
    n1,
    dqkv,
    att,
    da,
    *rest,
):
    lane_refs, rest = [rest[i * 9 : i * 9 + 9] for i in range(len(LANES))], rest[9 * len(LANES) :]
    (
        small,
        small_recv,
        load_sem,
        send_sem,
        recv_sem,
        pair_send,
        pair_recv,
        small_send,
        small_recv_sem,
        out_sem,
    ) = rest
    f = lax.axis_index("fsdp")
    e = lax.axis_index("expert")
    y, x, z = e // 8, lax.rem(e // 4, 2), lax.rem(e, 4)
    other = 1 - f
    own_half = aligned(f * HALF, HALF, 128)
    other_half = aligned(other * HALF, HALF, 128)

    def along_y(d):
        return {"expert": lax.rem(y + d, 4) * 8 + x * 4 + z}

    def along_z(d):
        return {"expert": y * 8 + x * 4 + lax.rem(z + d, 4)}

    twin = {"expert": y * 8 + (1 - x) * 4 + z}
    partner = {"fsdp": other}

    barrier = pltpu.get_barrier_semaphore()
    neighbours = [along_y(d) for d in (1, 2, 3)] + [along_z(d) for d in (1, 2, 3)]
    neighbours += [twin, partner]
    for place in neighbours:
        pl.semaphore_signal(barrier, inc=1, device_id=place, device_id_type=MESH)

    loads = [
        (att_in, att),
        (da_in, da),
        (n1_in, n1),
        (dqkv_in, dqkv),
    ]
    loads = [pltpu.make_async_copy(a, b, load_sem.at[i]) for i, (a, b) in enumerate(loads)]
    for copy in loads:
        copy.start()

    def remote(src, dst, send, recv, place):
        return pltpu.make_async_remote_copy(
            src_ref=src,
            dst_ref=dst,
            send_sem=send,
            recv_sem=recv,
            device_id=place,
            device_id_type=MESH,
        )

    def wait_for(ref, sem):
        pltpu.make_async_copy(ref, ref, sem).wait()

    class Lane:
        def __init__(self, i):
            self.i = i
            self.v, self.far, self.merged, self.r1, self.s1, self.r2, self.s2, self.r3, self.g = (
                lane_refs[i]
            )
            axes = ((along_y, y), (along_z, z))
            (axis, at), (self.next, self.to) = axes if LANES[i][0] == "y" else axes[::-1]
            self.right, self.left = axis(1), axis(3)
            self.at = at
            half = LANES[i][1] // 2
            self.mine = aligned(x * half, half, 128)
            self.theirs = aligned((1 - x) * half, half, 128)
            self.place = aligned(at * BAND + self.to * SLICE, SLICE, 16)

        def rows(self, distance, part=None):
            start = lax.rem(self.at + distance, 4) * BAND
            if part is None:
                return aligned(start, BAND, 16)
            return aligned(start + part * (BAND // 2), BAND // 2, 16)

        def send(self, stage, src, dst, place):
            remote(
                src, dst, send_sem.at[self.i, stage], recv_sem.at[self.i, stage], place
            ).start()

        def arrived(self, stage, ref):
            wait_for(ref, recv_sem.at[self.i, stage])

        def spread(self):
            low = pl.ds(BAND // 2, BAND // 2)
            top = pl.ds(0, BAND // 2)
            self.send(0, self.v.at[self.rows(2, 0)], self.far.at[0], self.right)
            self.send(1, self.v.at[self.rows(2, 1)], self.far.at[1], self.left)
            self.send(2, self.v.at[self.rows(1, 1)], self.r1.at[0, low], self.right)
            self.send(3, self.v.at[self.rows(3, 0)], self.r1.at[1, top], self.left)

        def merge(self):
            low = pl.ds(BAND // 2, BAND // 2)
            top = pl.ds(0, BAND // 2)
            self.arrived(0, self.far.at[0])
            total = self.v[self.rows(1, 0)].astype(F32) + self.far[0].astype(F32)
            self.merged[0] = total.astype(BF)
            self.send(2, self.merged.at[0], self.r1.at[0, top], self.right)
            self.arrived(1, self.far.at[1])
            total = self.v[self.rows(3, 1)].astype(F32) + self.far[1].astype(F32)
            self.merged[1] = total.astype(BF)
            self.send(3, self.merged.at[1], self.r1.at[1, low], self.left)

        def join_one(self):
            self.arrived(2, self.r1.at[0])
            self.arrived(3, self.r1.at[1])
            total = self.v[self.rows(0)].astype(F32)
            total = total + self.r1[0].astype(F32) + self.r1[1].astype(F32)
            self.s1[...] = total.astype(BF)
            for d in (1, 2, 3):
                rows = aligned(lax.rem(self.to + d, 4) * SLICE, SLICE, 16)
                self.send(4, self.s1.at[rows], self.r2.at[self.to], self.next(d))

        def join_two(self):
            self.arrived(4, self.r2.at[pl.ds(0, 3)])
            total = self.s1[aligned(self.to * SLICE, SLICE, 16)].astype(F32)
            for d in (1, 2, 3):
                total = total + self.r2[lax.rem(self.to + d, 4)].astype(F32)
            self.s2[...] = total.astype(BF)
            self.send(5, self.s2.at[:, self.theirs], self.r3, twin)

        def join_three(self):
            self.arrived(5, self.r3)
            total = self.s2[:, self.mine].astype(F32) + self.r3[...].astype(F32)
            self.g[self.place, self.mine] = total.astype(BF)
            part = self.g.at[self.place, self.mine]
            self.send(6, part, part, twin)

        def gather_two(self):
            self.arrived(6, self.g.at[self.place, self.theirs])
            part = self.g.at[self.place]
            for d in (1, 2, 3):
                self.send(7, part, part, self.next(d))

        def gather_one(self):
            self.arrived(7, self.g.at[pl.ds(0, 3 * SLICE)])
            top, low = self.g.at[self.rows(0, 0)], self.g.at[self.rows(0, 1)]
            self.send(8, top, top, self.right)
            self.send(9, low, low, self.left)
            self.send(10, low, low, self.right)
            self.send(11, top, top, self.left)

        def pass_on(self):
            top, low = self.g.at[self.rows(3, 0)], self.g.at[self.rows(1, 1)]
            self.arrived(8, top)
            self.send(12, top, top, self.right)
            self.arrived(9, low)
            self.send(13, low, low, self.left)

        def finish(self):
            part = self.g.at[pl.ds(0, BAND // 2)]
            for stage in (10, 11, 12, 13):
                self.arrived(stage, part)

        def drain(self):
            half = self.v.at[pl.ds(0, BAND // 2)]
            band = self.v.at[pl.ds(0, BAND)]
            slices = self.v.at[pl.ds(0, 3 * SLICE)]
            sizes = [half, half, band, band, slices, self.s2.at[:, self.theirs]]
            sizes += [self.g.at[self.place, self.mine], slices] + [half] * 6
            for stage, ref in enumerate(sizes):
                wait_for(ref, send_sem.at[self.i, stage])

    out_one, query_one, out_two, query_two = lanes = [Lane(i) for i in range(len(LANES))]

    def over_micro(group, cols):
        block = jnp.concatenate([dqkv[m, group, :, cols] for m in range(MB)], axis=0)
        return dot_tn(n1[...], block).astype(BF)

    for copy in loads[:2]:
        copy.wait()
    for j in range(2):
        cols = pl.ds(j * 512, 512)
        out_one.v[:, cols] = dot_tn(att[...], da[:, cols]).astype(BF)
    pl.semaphore_wait(barrier, len(neighbours))
    out_one.spread()
    for copy in loads[2:4]:
        copy.wait()
    query_one.v[:, pl.ds(0, HALF)] = over_micro(0, pl.ds(0, HALF))
    query_one.v[:, pl.ds(HALF, 256)] = over_micro(1, pl.ds(0, 256))
    query_one.spread()
    small[...] = gains_in[...]
    small_pair = remote(
        small.at[:, other_half],
        small_recv.at[0],
        small_send.at[0],
        small_recv_sem.at[0],
        partner,
    )
    small_pair.start()
    out_two.v[:, pl.ds(0, 512)] = dot_tn(att[...], da[:, pl.ds(1024, 512)]).astype(BF)
    query_two.v[:, pl.ds(0, 512)] = over_micro(1, pl.ds(256, 512))
    for g in range(2):
        query_two.v[:, pl.ds(512 + g * HEAD, HEAD)] = over_micro(g, pl.ds(HALF, HEAD))
        out_two.v[:, pl.ds(512 + g * HEAD, HEAD)] = over_micro(g, pl.ds(HALF + HEAD, HEAD))

    pair = [
        remote(src, dst, pair_send.at[i], pair_recv.at[i], partner)
        for i, (src, dst) in enumerate(
            ((their_gate, part_gate), (their_up, part_up), (their_down, part_down))
        )
    ]
    pieces = [
        remote(src.at[rows], dst.at[rows], pair_send.at[n], pair_recv.at[n], partner)
        for n, src, dst, size in (
            (0, their_gate, part_gate, HALF // 4),
            (1, their_up, part_up, HALF // 4),
            (2, their_down, part_down, HIDDEN // 8),
        )
        for rows in [pl.ds(i * size, size) for i in range(4)]
    ]

    def send_pieces(start, stop):
        for copy in pieces[start:stop]:
            copy.start()

    def spread_small(i, axis):
        for d in (1, 2, 3):
            remote(
                small.at[:, pl.ds(0, HALF)],
                small_recv.at[1 + 3 * i + d - 1],
                small_send.at[1 + 3 * i + d - 1],
                small_recv_sem.at[1 + 3 * i + d - 1],
                axis(d),
            ).start()

    def join_small(i, axis):
        for d in (1, 2, 3):
            remote(
                small.at[:, pl.ds(0, HALF)],
                small_recv.at[1 + 3 * i + d - 1],
                small_send.at[1 + 3 * i + d - 1],
                small_recv_sem.at[1 + 3 * i + d - 1],
                axis(d),
            ).wait()
        total = small[:, pl.ds(0, HALF)]
        for d in (1, 2, 3):
            total = total + small_recv[1 + 3 * i + d - 1]
        small[:, pl.ds(0, HALF)] = total

    small_pair.wait()
    small[:, pl.ds(0, HALF)] = small[:, own_half] + small_recv[0]
    spread_small(0, along_y)

    out_two.spread()
    query_two.spread()
    send_pieces(0, 4)
    join_small(0, along_y)
    spread_small(1, along_z)
    for lane in lanes:
        lane.merge()
    for lane in lanes:
        lane.join_one()
    for lane in lanes:
        lane.join_two()
    join_small(1, along_z)
    small_twin = remote(
        small.at[:, pl.ds(0, HALF)],
        small_recv.at[7],
        small_send.at[7],
        small_recv_sem.at[7],
        twin,
    )
    small_twin.start()
    send_pieces(4, 5)
    for lane in lanes:
        lane.join_three()
    send_pieces(5, 12)
    for lane in lanes:
        lane.gather_two()
    for lane in lanes:
        lane.gather_one()
    for lane in lanes:
        lane.pass_on()
    small_twin.wait()
    gains_out[...] = small[:, pl.ds(0, HALF)] + small_recv[7]

    outs = []

    def out_copy(src, dst):
        copy = pltpu.make_async_copy(src, dst, out_sem.at[len(outs)])
        copy.start()
        outs.append(copy)

    out_one.finish()
    out_copy(out_one.g, o_out.at[:, pl.ds(0, 1024)])
    query_one.finish()
    out_copy(query_one.g, q_out.at[:, pl.ds(0, 1024)])
    out_two.finish()
    out_copy(out_two.g.at[:, pl.ds(0, 512)], o_out.at[:, pl.ds(1024, 512)])
    out_copy(out_two.g.at[:, pl.ds(512, 256)], v_out)
    query_two.finish()
    out_copy(query_two.g.at[:, pl.ds(0, 512)], q_out.at[:, pl.ds(1024, 512)])
    out_copy(query_two.g.at[:, pl.ds(512, 256)], k_out)

    for lane in lanes:
        lane.drain()
    for copy in pair:
        copy.wait()
    for copy in outs:
        copy.wait()


def reduce_grads(*operands):
    def out(*shape):
        return jax.ShapeDtypeStruct(shape, BF)

    vmem = pl.BlockSpec(memory_space=pltpu.VMEM)
    anywhere = pl.BlockSpec(memory_space=pl.ANY)
    dma = pltpu.SemaphoreType.DMA
    lanes = []
    for _, width in LANES:
        lanes += [
            pltpu.VMEM((HALF, width), BF),
            pltpu.VMEM((2, BAND // 2, width), BF),
            pltpu.VMEM((2, BAND // 2, width), BF),
            pltpu.VMEM((2, BAND, width), BF),
            pltpu.VMEM((BAND, width), BF),
            pltpu.VMEM((4, SLICE, width), BF),
            pltpu.VMEM((SLICE, width), BF),
            pltpu.VMEM((SLICE, width // 2), BF),
            pltpu.VMEM((HALF, width), BF),
        ]
    return pl.pallas_call(
        grads_kernel,
        name="grads",
        out_shape=(
            out(HALF, WIDTH),
            out(HALF, 256),
            out(HALF, 256),
            out(HALF, WIDTH),
            out(HALF, HIDDEN),
            out(HALF, HIDDEN),
            out(HIDDEN // 2, WIDTH),
            jax.ShapeDtypeStruct((8, HALF), F32),
        ),
        in_specs=[anywhere] * 7 + [vmem],
        out_specs=[anywhere] * 7 + [vmem],
        scratch_shapes=[
            pltpu.VMEM((MB * 2 * SEQ, HALF), BF),
            pltpu.VMEM((MB, 2, 2 * SEQ, QKV), BF),
            pltpu.VMEM((MB * 2 * SEQ, HALF), BF),
            pltpu.VMEM((MB * 2 * SEQ, WIDTH), BF),
        ]
        + lanes
        + [
            pltpu.VMEM((8, WIDTH), F32),
            pltpu.VMEM((8, 8, HALF), F32),
            dma((4,)),
            dma((len(LANES), 14)),
            dma((len(LANES), 14)),
            dma((3,)),
            dma((3,)),
            dma((8,)),
            dma((8,)),
            dma((9,)),
        ],
        compiler_params=pltpu.CompilerParams(
            collective_id=1, has_side_effects=True, vmem_limit_bytes=62 * 2**20
        ),
    )(*operands)


def finish_kernel(*refs):
    (q, k, v, o, own_g, own_u, own_d, part_g, part_u, part_d, acts, grads, gains), outs = (
        refs[:13],
        refs[13:],
    )
    for src, dst in zip((q, k, v, o), outs):
        dst[...] = src[...].astype(F32)
    for own, part, dst in zip((own_g, own_u, own_d), (part_g, part_u, part_d), outs[4:]):
        dst[...] = own[...].astype(F32) + part[...].astype(F32)
    outs[7][...] = acts[...]
    outs[8][...] = grads[...]
    outs[9][...] = gains[0:1]
    outs[10][...] = gains[1:2]


def finish(*blocks):
    steps = 4

    def spec(rows, cols):
        return pl.BlockSpec((rows // steps, cols), lambda i: (i, 0))

    def whole(rows, cols):
        return pl.BlockSpec((rows, cols), lambda i: (0, 0))

    gains = blocks[-1]
    split = blocks[:-1]
    results = split[:7] + split[10:]
    dtypes = [F32] * 7 + [BF] * 2
    return pl.pallas_call(
        finish_kernel,
        name="finish",
        grid=(steps,),
        out_shape=[jax.ShapeDtypeStruct(b.shape, t) for b, t in zip(results, dtypes)]
        + [jax.ShapeDtypeStruct((1, HALF), F32)] * 2,
        in_specs=[spec(*b.shape) for b in split] + [whole(*gains.shape)],
        out_specs=[spec(*b.shape) for b in results] + [whole(1, HALF)] * 2,
        compiler_params=pltpu.CompilerParams(vmem_limit_bytes=62 * 2**20),
    )(*blocks)


def local(
    inputs,
    cotangent,
    segments,
    expert_ids,
    gate_logits,
    w_query,
    key_projection,
    value_projection,
    w_out,
    gain_attn,
    gain_moe,
    w_gate,
    w_up,
    w_down,
):
    steps = np.arange(HEAD) % (HEAD // 2)
    frequency = (ROPE_BASE ** (-steps * 2.0 / HEAD)).astype(np.float32)[None]
    (
        acts,
        in_grads,
        gain_parts,
        own_gate,
        own_up,
        own_down,
        their_gate,
        their_up,
        their_down,
        n1,
        dqkv,
        att,
        da,
    ) = run_sections(
        inputs,
        cotangent,
        w_query[0],
        key_projection[0],
        value_projection[0],
        w_out[0],
        w_gate[0, 0],
        w_up[0, 0],
        w_down[0, 0],
        gain_attn,
        gain_moe,
        segments,
        jnp.swapaxes(expert_ids[0], 1, 2),
        jnp.swapaxes(gate_logits[0], 1, 2),
        jnp.asarray(frequency),
    )
    gq, gk, gv, go, part_gate, part_up, part_down, gains = reduce_grads(
        their_gate,
        their_up,
        their_down,
        n1.reshape(MB * 2 * SEQ, HALF),
        dqkv,
        att.reshape(MB * 2 * SEQ, HALF),
        da.reshape(MB * 2 * SEQ, WIDTH),
        gain_parts,
    )
    gq, gk, gv, go, grad_gate, grad_up, grad_down, acts, in_grads, gain_one, gain_two = finish(
        gq,
        gk,
        gv,
        go,
        own_gate,
        own_up,
        own_down,
        part_gate,
        part_up,
        part_down,
        acts.reshape(MB * SEQ, WIDTH),
        in_grads.reshape(MB * SEQ, WIDTH),
        gains,
    )
    return (
        acts.reshape(1, MB, SEQ, WIDTH),
        in_grads.reshape(1, MB, SEQ, WIDTH),
        gq[None],
        gk[None],
        gv[None],
        go[None],
        gain_one,
        gain_two,
        grad_gate[None, None],
        grad_up[None, None],
        grad_down[None, None],
    )


def solution(mesh):
    return jax.shard_map(
        local,
        mesh=mesh,
        in_specs=(
            P(None, ("fsdp", "expert"), None),
            P(None, ("fsdp", "expert"), None),
            P(None, ("fsdp", "expert")),
            P("section", None, ("fsdp", "expert"), None),
            P("section", None, ("fsdp", "expert"), None),
            P("section", "fsdp", None),
            P("section", "fsdp", None),
            P("section", "fsdp", None),
            P("section", "fsdp", None),
            P("section", "fsdp"),
            P("section", "fsdp"),
            P("section", "expert", "fsdp", None),
            P("section", "expert", "fsdp", None),
            P("section", "expert", "fsdp", None),
        ),
        out_specs=(
            P("section", None, ("fsdp", "expert"), None),
            P("section", None, ("fsdp", "expert"), None),
            P("section", "fsdp", None),
            P("section", "fsdp", None),
            P("section", "fsdp", None),
            P("section", "fsdp", None),
            P("section", "fsdp"),
            P("section", "fsdp"),
            P("section", "expert", "fsdp", None),
            P("section", "expert", "fsdp", None),
            P("section", "expert", "fsdp", None),
        ),
        check_vma=False,
    )
```

```python
import functools

import jax
import jax.numpy as jnp
import numpy as np
from jax import lax
from jax.experimental import pallas as pl
from jax.experimental.pallas import tpu as pltpu
from jax.sharding import PartitionSpec as P

MESH = pl.DeviceIdType.MESH
BF = jnp.bfloat16
F32 = jnp.float32

HEAD = 128
EPS = 1e-06
ROPE_BASE = 1000000.0
GELU_C = 0.7978845608
GELU_A = 0.044715

MB = 2
SEQ = 96
WIDTH = 1536
HALF = 768
EXPERTS = 32
PLANE = 16
SLOTS = 16
ROWS = EXPERTS * SLOTS
HIDDEN = 768
HEADS = 6
QKV = 1024


def dot(a, b):
    return jnp.dot(a, b, preferred_element_type=F32)


def dot_nt(a, b):
    return lax.dot_general(a, b, (((1,), (1,)), ((), ())), preferred_element_type=F32)


def dot_tn(a, b):
    return lax.dot_general(a, b, (((0,), (0,)), ((), ())), preferred_element_type=F32)


def aligned(start, size, unit):
    return pl.ds(pl.multiple_of(start, unit), size)


def inverse_rms(rows):
    return lax.rsqrt(jnp.mean(rows * rows, axis=-1, keepdims=True) + EPS)


def rms_back(rows, inverse, gain, grad):
    scaled = gain * grad
    return inverse * scaled - rows * (inverse * inverse * inverse) * jnp.mean(
        scaled * rows, axis=-1, keepdims=True
    )


def rotate(head, cos, sin):
    return head * cos + pltpu.roll(head, HEAD // 2, 1) * sin


(
    ENTER,
    PROJECT,
    ATTEND,
    NORM,
    TWIN,
    HIDE,
    GIVE,
    FAR,
    JOIN,
    GRAD,
    GRAD_TWIN,
    BACK_NEAR,
    BACK_FAR,
    FAR_BACK,
    MID,
    ATTEND_BACK,
    PROJECT_BACK,
    CLOSE,
    LOAD,
    IN_A,
    IN_B,
    IN_C,
    OUT_A,
    OUT_B,
    OUT_C,
    REST,
) = range(26)

FIRST_PLAN = (
    (ENTER, 0, 0),
    (ENTER, 1, 1),
    (PROJECT, 0, 1),
    (PROJECT, 1, 1),
    (ATTEND, 0, 1),
    (ATTEND, 1, 1),
    (NORM, 0, 1),
    (NORM, 1, 6),
    (TWIN, 0, 0),
    (TWIN, 1, 0),
    (HIDE, 0, 0),
    (HIDE, 1, 0),
    (GIVE, 0, 0),
    (GIVE, 1, 0),
    (FAR, 0, 0),
    (JOIN, 0, 0),
    (FAR, 1, 0),
    (JOIN, 1, 0),
    (GRAD, 0, 0),
    (GRAD_TWIN, 0, 0),
    (GRAD, 1, 0),
    (BACK_NEAR, 0, 0),
    (GRAD_TWIN, 1, 0),
    (BACK_FAR, 0, 0),
    (BACK_FAR, 1, 0),
    (BACK_NEAR, 1, 0),
    (FAR_BACK, 0, 0),
    (IN_A, 0, 0),
    (IN_B, 0, 0),
    (IN_C, 0, 0),
    (MID, 0, 0),
    (IN_A, 1, 0),
    (IN_B, 1, 0),
    (FAR_BACK, 1, 0),
    (ATTEND_BACK, 0, 0),
    (MID, 1, 0),
    (IN_C, 1, 0),
    (OUT_A, 0, 0),
    (PROJECT_BACK, 0, 0),
    (OUT_B, 0, 0),
    (ATTEND_BACK, 1, 0),
    (CLOSE, 0, 0),
    (OUT_C, 0, 0),
    (OUT_A, 1, 0),
    (PROJECT_BACK, 1, 0),
    (OUT_B, 1, 0),
    (OUT_C, 1, 0),
    (CLOSE, 1, 0),
)
SECOND_PLAN = (
    (GRAD, 0, 0),
    (GRAD, 1, 0),
    (LOAD, 0, 3),
    (ENTER, 0, 0),
    (PROJECT, 0, 1),
    (ENTER, 1, 0),
    (ATTEND, 0, 1),
    (PROJECT, 1, 0),
    (NORM, 0, 1),
    (ATTEND, 1, 1),
    (TWIN, 0, 0),
    (NORM, 1, 5),
    (TWIN, 1, 0),
    (GRAD_TWIN, 0, 0),
    (GRAD_TWIN, 1, 0),
    (HIDE, 0, 0),
    (HIDE, 1, 0),
    (BACK_FAR, 0, 0),
    (BACK_NEAR, 0, 0),
    (BACK_FAR, 1, 0),
    (BACK_NEAR, 1, 0),
    (GIVE, 0, 0),
    (GIVE, 1, 0),
    (FAR_BACK, 0, 0),
    (MID, 0, 0),
    (FAR_BACK, 1, 0),
    (ATTEND_BACK, 0, 0),
    (MID, 1, 0),
    (PROJECT_BACK, 0, 0),
    (ATTEND_BACK, 1, 0),
    (CLOSE, 0, 0),
    (PROJECT_BACK, 1, 0),
    (CLOSE, 1, 0),
    (IN_A, 0, 0),
    (IN_B, 0, 0),
    (IN_C, 0, 0),
    (IN_A, 1, 0),
    (IN_B, 1, 0),
    (IN_C, 1, 0),
    (OUT_A, 0, 0),
    (OUT_B, 0, 0),
    (OUT_C, 0, 0),
    (OUT_A, 1, 0),
    (OUT_B, 1, 0),
    (OUT_C, 1, 0),
    (FAR, 0, 0),
    (FAR, 1, 0),
    (JOIN, 0, 0),
    (JOIN, 1, 0),
)


def section_kernel(
    x_in,
    ct_in,
    wq_in,
    wk_in,
    wv_in,
    wo_in,
    wg_in,
    wu_in,
    wd_in,
    gain_one_in,
    gain_two_in,
    segments_in,
    ids_in,
    logits_in,
    freq_in,
    acts_out,
    ingrad_out,
    gains_out,
    own_gate_out,
    own_up_out,
    own_down_out,
    their_gate_out,
    their_up_out,
    their_down_out,
    n1_out,
    dqkv_out,
    att_out,
    da_out,
    wqkv,
    wo,
    wg,
    wu,
    wd,
    x_own,
    n1p,
    n1_send,
    pq_own,
    pq_send,
    pq_recv,
    qkvs,
    att,
    hid_one,
    part_own,
    part_send,
    part_recv,
    sel,
    cg_hi,
    cg_lo,
    n2pair,
    gpair,
    dsend,
    bsend,
    n2recv,
    yrecv,
    dyrecv,
    dn2recv,
    gs,
    us,
    hid,
    far_send,
    far_recv,
    acts_s,
    dh_s,
    da_pair,
    dqkv_all,
    dn1_send,
    dn1_recv,
    ingrad_s,
    gains_acc,
    side,
    meta,
    gains,
    cos_t,
    sin_t,
    mask_t,
    lw_sem,
    ws_sem,
    wr_sem,
    as_sem,
    ar_sem,
    ps_sem,
    pr_sem,
    ts_sem,
    tr_sem,
    xs_sem,
    xr_sem,
    gs_sem,
    gr_sem,
    out_sem,
    go_sem,
):
    sec = lax.axis_index("section")
    f = lax.axis_index("fsdp")
    e = lax.axis_index("expert")
    y, x, z = e // 8, lax.rem(e // 4, 2), lax.rem(e, 4)
    q = y * 4 + z
    away = 1 - x
    other = 1 - f
    own_rows = aligned(f * SEQ, SEQ, 16)
    own_half = aligned(f * HALF, HALF, 128)
    other_half = aligned(other * HALF, HALF, 128)
    partner = {"fsdp": other}
    twin_place = y * 8 + away * 4 + z
    twin = {"expert": twin_place}
    first, second = sec == 0, sec == 1

    def in_plane(d):
        at = lax.rem(q + d, PLANE)
        return at, {"expert": (at // 4) * 8 + x * 4 + lax.rem(at, 4)}

    barrier = pltpu.get_barrier_semaphore()

    @pl.loop(1, PLANE)
    def _(d):
        pl.semaphore_signal(barrier, inc=1, device_id=in_plane(d)[1], device_id_type=MESH)

    others = (
        twin,
        partner,
        {"section": 1 - sec},
        {"section": 1 - sec, "expert": twin_place},
    )
    for place in others:
        pl.semaphore_signal(barrier, inc=1, device_id=place, device_id_type=MESH)

    local = []
    for g in range(2):
        local += [
            (wq_in.at[:, pl.ds(g * HALF, HALF)], wqkv.at[:, pl.ds(g * QKV, HALF)]),
            (wk_in.at[:, pl.ds(g * HEAD, HEAD)], wqkv.at[:, pl.ds(g * QKV + HALF, HEAD)]),
            (wv_in.at[:, pl.ds(g * HEAD, HEAD)], wqkv.at[:, pl.ds(g * QKV + HALF + HEAD, HEAD)]),
        ]
    local += [
        (wo_in, wo),
        (wg_in, wg.at[own_half]),
        (wu_in, wu.at[own_half]),
        (wd_in, wd.at[aligned(f * (HIDDEN // 2), HIDDEN // 2, 16)]),
    ]
    local = [pltpu.make_async_copy(a, b, lw_sem.at[i]) for i, (a, b) in enumerate(local)]
    for copy in local:
        copy.start()
    x_local = pltpu.make_async_copy(x_in, x_own, lw_sem.at[10])
    ct_local = pltpu.make_async_copy(ct_in, gpair.at[:, x], lw_sem.at[11])
    pl.when(first)(x_local.start)
    pl.when(second)(ct_local.start)

    def remote(src, dst, send, recv, place):
        return pltpu.make_async_remote_copy(
            src_ref=src,
            dst_ref=dst,
            send_sem=send,
            recv_sem=recv,
            device_id=place,
            device_id_type=MESH,
        )

    def wait_for(ref, sem):
        pltpu.make_async_copy(ref, ref, sem).wait()

    def weight(src, dst, i):
        return remote(src, dst, ws_sem.at[i], wr_sem.at[i], partner)

    w_moe = [
        weight(wg_in, wg.at[own_half], 3),
        weight(wu_in, wu.at[own_half], 4),
        weight(wd_in, wd.at[aligned(f * (HIDDEN // 2), HIDDEN // 2, 16)], 5),
    ]

    w_pieces = [
        weight(src.at[aligned(i * size, size, 16)], dst.at[aligned(f * 4 * size + i * size, size, 16)], n)
        for n, src, dst, size in (
            (3, wg_in, wg, HALF // 4),
            (4, wu_in, wu, HALF // 4),
            (5, wd_in, wd, HIDDEN // 8),
        )
        for i in range(4)
    ]

    def ct_copy(m):
        return remote(ct_in.at[m], gpair.at[m, x], ws_sem.at[10 + m], gr_sem.at[x, m], twin)

    side[f, 0:1] = gain_one_in[...].astype(F32)
    side[f, 1:2] = gain_two_in[...].astype(F32)
    side[f, 2:4, :SEQ] = segments_in[...].astype(F32)
    for m in range(MB):
        meta[x, m, 0:4] = ids_in[m].astype(F32)
        meta[x, m, 4:8] = logits_in[m]
    row = lax.broadcasted_iota(jnp.int32, (SEQ, SEQ), 0)
    col = lax.broadcasted_iota(jnp.int32, (SEQ, SEQ), 1)
    unit = jnp.where(row == col, 1.0, 0.0).astype(BF)
    side_copy = weight(side.at[f], side.at[f], 8)
    meta_copy = remote(meta.at[x], meta.at[x], ws_sem.at[9], wr_sem.at[9], twin)
    gains_acc[...] = jnp.zeros_like(gains_acc)

    pl.semaphore_wait(barrier, PLANE - 1 + len(others))
    side_copy.start()
    meta_copy.start()

    meta_copy.wait_recv()
    earlier = jnp.where(row < col, 1.0, 0.0).astype(BF)

    @pl.loop(0, 2 * MB)
    def _(i):
        m, source = lax.rem(i, MB), i // MB
        rows = meta[source, m]
        ids, logits = rows[:4], rows[4:]
        raised = jnp.exp(logits - jnp.max(logits, axis=0, keepdims=True))
        gates = raised / jnp.sum(raised, axis=0, keepdims=True)
        place = lax.broadcasted_iota(jnp.int32, (PLANE, SEQ), 0)
        expert = ((place // 4) * 8 + x * 4 + lax.rem(place, 4)).astype(F32)
        named = jnp.zeros((PLANE, SEQ), F32)
        weights = jnp.zeros((PLANE, SEQ), F32)
        for k in range(4):
            hit = expert == ids[k : k + 1, :]
            named = jnp.where(hit, 1.0, named)
            weights = jnp.where(hit, gates[k : k + 1, :], weights)
        slot = dot(named.astype(BF), earlier)
        slot = jnp.where(named > 0.0, slot, -1.0)
        shape = (PLANE, SLOTS, SEQ)
        count = lax.broadcasted_iota(jnp.int32, shape, 1).astype(F32)
        chosen = jnp.where(jnp.broadcast_to(slot[:, None, :], shape) == count, 1.0, 0.0)
        scaled = chosen * jnp.broadcast_to(weights[:, None, :], shape)
        scaled = scaled.reshape(PLANE * SLOTS, SEQ)
        high = scaled.astype(BF)
        sel[m, source] = chosen.reshape(PLANE * SLOTS, SEQ).astype(BF)
        cg_hi[m, source] = high
        cg_lo[m, source] = (scaled - high.astype(F32)).astype(BF)

    side_copy.wait_recv()
    gains[:, pl.ds(0, HALF)] = side[0, 0:2]
    gains[:, pl.ds(HALF, HALF)] = side[1, 0:2]
    lane = lax.broadcasted_iota(jnp.int32, (SEQ, HEAD), 1)
    turn = jnp.where(lane < HEAD // 2, -1.0, 1.0)
    for m in range(MB):
        for s in range(2):
            across = jnp.broadcast_to(side[s, 2 + m : 3 + m, :SEQ], (SEQ, SEQ))
            down = dot_nt(unit, across.astype(BF))
            same = jnp.where(down == across, 1.0, 0.0)
            mask_t[m, s] = jnp.where(col <= row, same, 0.0)
            places = jnp.sum(jnp.where(col < row, same, 0.0), axis=1, keepdims=True)
            angles = places * freq_in[...]
            cos_t[m, pl.ds(s * SEQ, SEQ)] = jnp.cos(angles)
            sin_t[m, pl.ds(s * SEQ, SEQ)] = jnp.sin(angles) * turn

    def exchange_half(kind, m, src, dst, source):
        @pl.loop(1, PLANE)
        def _(d):
            at, place = in_plane(d)
            remote(
                src.at[m, at, source],
                dst.at[m, q, source],
                as_sem.at[kind, m, source],
                ar_sem.at[kind, m, source],
                place,
            ).start()

        dst[m, q, source] = src[m, q, source]

    def received(kind, m, dst, source):
        wait_for(dst.at[m, pl.ds(0, PLANE - 1), source], ar_sem.at[kind, m, source])

    def sent(kind, m, src, source):
        wait_for(src.at[m, pl.ds(0, PLANE - 1), source], as_sem.at[kind, m, source])

    def to_partner(kind, m, src, dst):
        return remote(src, dst, ps_sem.at[kind, m], pr_sem.at[kind, m], partner)

    def to_twin(kind, m, src, dst):
        return remote(src, dst, ts_sem.at[kind, m], tr_sem.at[kind, m], twin)

    def n2_copy(m):
        return to_twin(0, m, n2pair.at[m, x], n2pair.at[m, x])

    def far_copy(kind, m):
        return to_twin(kind, m, far_send.at[kind - 1, m], far_recv.at[kind - 1, m])

    def acts_copy(m):
        return remote(acts_s.at[m], x_own.at[m], xs_sem.at[m], xr_sem.at[m], {"section": 1})

    def n1_copy(m):
        return to_partner(4, m, n1_send.at[m], n1p.at[m, own_rows])

    def pq_copy(m):
        return to_partner(5, m, pq_send.at[m], pq_recv.at[m])

    def grad_copy(m, cross):
        place = {"section": 0, "expert": twin_place} if cross else {"section": 0}
        return remote(
            ingrad_s.at[m], gpair.at[m, x], gs_sem.at[cross, m], gr_sem.at[x, m], place
        )

    def out_copy(i, src, dst, m):
        return pltpu.make_async_copy(src, dst, out_sem.at[i, m])

    def flat(ref, m):
        return ref[m].reshape(ROWS, WIDTH)

    def spread(m, source, rows, dst, scale=None):
        @pl.loop(0, WIDTH // 512)
        def _(j):
            cols = aligned(j * 512, 512, 128)
            block = dot(sel[m, source], rows[m, source, :, cols])
            if scale is not None:
                block = block * scale
            dst[m, :, source, :, cols] = block.astype(BF).reshape(PLANE, SLOTS, 512)

    def load_step(m):
        pl.semaphore_wait(go_sem, 1)
        ct_copy(0).start()
        ct_copy(1).start()

    def heads_of(ref, m, rows):
        return jnp.concatenate(
            [ref[m, rows, pl.ds(h * HEAD, HEAD)] for h in range(HEADS)], axis=0
        )

    def softmax_of(m, s, queries, keys):
        scores = dot_nt(queries, keys) * HEAD ** (-0.5)
        allowed = jnp.concatenate([mask_t[m, s]] * HEADS, axis=0)
        scores = jnp.where(allowed > 0.0, scores, -1e30)
        raised = jnp.exp(scores - jnp.max(scores, axis=-1, keepdims=True))
        return raised / jnp.sum(raised, axis=-1, keepdims=True)

    def enter_step(m):
        pl.when(jnp.logical_and(first, m == 0))(x_local.wait)
        pl.when(second)(lambda: wait_for(x_own.at[m], xr_sem.at[m]))
        rows = x_own[m].astype(F32)
        scale = inverse_rms(rows)
        n1p[m, own_rows] = (x_own[m, :, own_half].astype(F32) * scale * gains[0:1, own_half]).astype(BF)
        n1_send[m] = (
            x_own[m, :, other_half].astype(F32) * scale * gains[0:1, other_half]
        ).astype(BF)
        n1_copy(m).start()

    def project_step(m):
        @pl.when(m == 0)
        def _():
            for copy in local[:6]:
                copy.wait()

        n1_copy(m).wait_recv()

        @pl.loop(0, QKV // 512)
        def _(j):
            cols = aligned(j * 512, 512, 128)
            from_w = aligned(other * QKV + j * 512, 512, 128)
            pq_send[m, :, cols] = dot(n1p[m], wqkv[:, from_w]).astype(BF)

        pq_copy(m).start()

        @pl.loop(0, QKV // 512)
        def _(j):
            cols = aligned(j * 512, 512, 128)
            from_w = aligned(f * QKV + j * 512, 512, 128)
            pq_own[m, :, cols] = dot(n1p[m], wqkv[:, from_w])

    def attend_step(m):
        pl.when(m == 0)(local[6].wait)
        pq_copy(m).wait_recv()
        cos, sin = cos_t[m], sin_t[m]
        for j in range(2 * HEADS - 4):
            cols = pl.ds(j * HEAD, HEAD)
            head = pq_own[m, :, cols] + pq_recv[m, :, cols].astype(F32)
            if j <= HEADS:
                head = rotate(head, cos, sin)
            qkvs[m, :, cols] = head.astype(BF)

        @pl.loop(0, 2)
        def _(i):
            s = jnp.where(i == 0, other, f)
            at = aligned(s * SEQ, SEQ, 16)
            queries = heads_of(qkvs, m, at)
            keys = qkvs[m, at, pl.ds(HALF, HEAD)]
            values = qkvs[m, at, pl.ds(HALF + HEAD, HEAD)]
            probs = softmax_of(m, s, queries, keys).astype(BF)
            mixed = dot(probs, values).astype(BF)
            for h in range(HEADS):
                att[m, at, pl.ds(h * HEAD, HEAD)] = mixed[h * SEQ : (h + 1) * SEQ]

            @pl.loop(0, WIDTH // 512)
            def _(j):
                cols = aligned(j * 512, 512, 128)
                block = dot(att[m, at], wo[:, cols])

                @pl.when(i == 0)
                def _():
                    part_send[m, :, cols] = block.astype(BF)

                @pl.when(i == 1)
                def _():
                    hid_one[m, :, cols] = block

            pl.when(i == 0)(to_partner(0, m, part_send.at[m], part_recv.at[m]).start)

    def norm_step(m):
        to_partner(0, m, part_send.at[m], part_recv.at[m]).wait_recv()
        rows = x_own[m].astype(F32) + (hid_one[m] + part_recv[m].astype(F32))
        hid_one[m] = rows
        n2pair[m, x] = (rows * inverse_rms(rows) * gains[1:2]).astype(BF)
        n2_copy(m).start()
        spread(m, x, n2pair, dsend)
        exchange_half(0, m, dsend, n2recv, x)

    def twin_step(m):
        n2_copy(m).wait_recv()
        spread(m, away, n2pair, dsend)
        exchange_half(0, m, dsend, n2recv, away)

    def hide_step(m):
        @pl.when(m == 0)
        def _():
            for copy in local[7:9]:
                copy.wait()
            for copy in w_moe[:2]:
                copy.wait_recv()

        for source in range(2):
            received(0, m, n2recv, source)

        @pl.loop(0, HIDDEN // 256)
        def _(j):
            cols = aligned(j * 256, 256, 128)
            rows = flat(n2recv, m)
            gate = dot(rows, wg[:, cols])
            up = dot(rows, wu[:, cols])
            bend = jnp.tanh(GELU_C * (gate + GELU_A * gate * gate * gate))
            shape = (PLANE, 2, SLOTS, 256)
            gs[m, :, :, :, cols] = gate.astype(BF).reshape(shape)
            us[m, :, :, :, cols] = up.astype(BF).reshape(shape)
            mixed = (0.5 * gate * (1.0 + bend) * up).astype(BF)
            hid[m, :, :, :, cols] = mixed.reshape(shape)


    def need_down():
        local[9].wait()
        w_moe[2].wait_recv()
        for copy in w_moe:
            copy.wait_send()

    def give_step(m):
        @pl.when(jnp.logical_and(first, m == 0))
        def _():
            need_down()
            pl.semaphore_signal(go_sem, inc=1, device_id={"section": 1}, device_id_type=MESH)

        @pl.loop(0, 2)
        def _(i):
            source = jnp.where(i == 0, away, x)
            sent(0, m, dsend, source)
            rows = hid[m, :, source].reshape(PLANE * SLOTS, HIDDEN)

            @pl.loop(0, WIDTH // 512)
            def _(j):
                cols = aligned(j * 512, 512, 128)
                block = dot(rows, wd[:, cols]).astype(BF)
                dsend[m, :, source, :, cols] = block.reshape(PLANE, SLOTS, 512)

            exchange_half(1, m, dsend, yrecv, source)

    def weighed(m, source, cols):
        block = yrecv[m, :, source, :, cols].reshape(PLANE * SLOTS, 512)
        return dot_tn(cg_hi[m, source], block) + dot_tn(cg_lo[m, source], block)

    def far_step(m):
        received(1, m, yrecv, away)

        @pl.loop(0, WIDTH // 512)
        def _(j):
            cols = aligned(j * 512, 512, 128)
            far_send[0, m, :, cols] = weighed(m, away, cols).astype(BF)

        far_copy(1, m).start()
        received(1, m, yrecv, x)

        @pl.loop(0, WIDTH // 512)
        def _(j):
            cols = aligned(j * 512, 512, 128)
            part_own[m, :, cols] = hid_one[m, :, cols] + weighed(m, x, cols)

    def join_step(m):
        far_copy(1, m).wait_recv()
        acts_s[m] = (part_own[m] + far_recv[0, m].astype(F32)).astype(BF)

        @pl.when(first)
        def _():
            acts_copy(m).start()

        out_copy(3, acts_s.at[m], acts_out.at[m], m).start()

    def dy_half(m, source):
        gate = cg_hi[m, source].astype(F32) + cg_lo[m, source].astype(F32)
        spread(m, source, gpair, bsend, jnp.sum(gate, axis=1, keepdims=True))
        exchange_half(2, m, bsend, dyrecv, source)

    def grad_step(m):
        @pl.when(first)
        def _():
            wait_for(gpair.at[m, x], gr_sem.at[x, m])

        @pl.when(jnp.logical_and(second, m == 0))
        def _():
            ct_local.wait()

        dy_half(m, x)

    def grad_twin_step(m):
        wait_for(gpair.at[m, away], gr_sem.at[away, m])
        dy_half(m, away)

    def back_step(source, m):
        pl.when(jnp.logical_and(second, jnp.logical_and(m == 0, source == away)))(need_down)
        received(2, m, dyrecv, source)

        @pl.loop(0, HIDDEN // 256)
        def _(j):
            cols = aligned(j * 256, 256, 128)
            shape = (PLANE, SLOTS, 256)
            dhid = dot_nt(dyrecv[m, :, source].reshape(PLANE * SLOTS, WIDTH), wd[cols, :])
            gate = gs[m, :, source, :, cols].reshape(PLANE * SLOTS, 256).astype(F32)
            up = us[m, :, source, :, cols].reshape(PLANE * SLOTS, 256).astype(F32)
            square = gate * gate
            bend = jnp.tanh(GELU_C * (gate + GELU_A * square * gate))
            half = 0.5 * (1.0 + bend)
            slope = half + 0.5 * gate * (1.0 - bend * bend) * (
                GELU_C * (1.0 + 3.0 * GELU_A * square)
            )
            gs[m, :, source, :, cols] = (dhid * up * slope).astype(BF).reshape(shape)
            us[m, :, source, :, cols] = (dhid * (gate * half)).astype(BF).reshape(shape)

        sent(2, m, bsend, source)

        @pl.loop(0, WIDTH // 512)
        def _(j):
            cols = aligned(j * 512, 512, 128)
            dgate = gs[m, :, source].reshape(PLANE * SLOTS, HIDDEN)
            dup = us[m, :, source].reshape(PLANE * SLOTS, HIDDEN)
            block = dot_nt(dgate, wg[cols, :]) + dot_nt(dup, wu[cols, :])
            bsend[m, :, source, :, cols] = block.astype(BF).reshape(PLANE, SLOTS, 512)

        exchange_half(3, m, bsend, dn2recv, source)

    def gathered(m, source, cols):
        return dot_tn(
            sel[m, source], dn2recv[m, :, source, :, cols].reshape(PLANE * SLOTS, 512)
        )

    def far_back_step(m):
        received(3, m, dn2recv, away)


        @pl.loop(0, WIDTH // 512)
        def _(j):
            cols = aligned(j * 512, 512, 128)
            far_send[1, m, :, cols] = gathered(m, away, cols).astype(BF)

        far_copy(2, m).start()
        received(3, m, dn2recv, x)

        @pl.when(jnp.logical_and(first, m == 1))
        def _():
            pl.semaphore_signal(go_sem, inc=1, device_id={"section": 1}, device_id_type=MESH)

        @pl.loop(0, WIDTH // 512)
        def _(j):
            cols = aligned(j * 512, 512, 128)
            dh_s[m, :, cols] = gathered(m, x, cols)

    def mid_step(m):
        far_copy(2, m).wait_recv()
        rows = hid_one[m]
        inverse = inverse_rms(rows)
        grad = dh_s[m] + far_recv[1, m].astype(F32)
        gains_acc[1:2] += jnp.sum(grad * rows * inverse, axis=0, keepdims=True)
        total = gpair[m, x].astype(F32) + rms_back(rows, inverse, gains[1:2], grad)
        dh_s[m] = total
        da_pair[m, own_rows] = total.astype(BF)
        da_copy(m).start()

    def da_copy(m):
        return to_partner(1, m, da_pair.at[m, own_rows], da_pair.at[m, own_rows])

    def dqkv_copy(m):
        return to_partner(3, m, dqkv_all.at[m, f], dqkv_all.at[m, f])

    def dn1_copy(m):
        return to_partner(2, m, dn1_send.at[m], dn1_recv.at[m])

    def attend_back_step(m):
        @pl.loop(0, 2)
        def _(i):
            s = jnp.where(i == 0, f, other)

            @pl.when(i == 1)
            def _():
                da_copy(m).wait_recv()
                out_copy(6, da_pair.at[m], da_out.at[m], m).start()

            at = aligned(s * SEQ, SEQ, 16)
            dmix = dot_nt(da_pair[m, at], wo[...]).astype(BF)
            dmix = jnp.concatenate(
                [dmix[:, h * HEAD : (h + 1) * HEAD] for h in range(HEADS)], axis=0
            )
            queries = heads_of(qkvs, m, at)
            keys = qkvs[m, at, pl.ds(HALF, HEAD)]
            values = qkvs[m, at, pl.ds(HALF + HEAD, HEAD)]
            probs = softmax_of(m, s, queries, keys)
            dprobs = dot_nt(dmix, values)
            dvalues = dot_tn(probs.astype(BF), dmix)
            dscores = probs * (dprobs - jnp.sum(dprobs * probs, axis=-1, keepdims=True))
            dscores = (dscores * HEAD ** (-0.5)).astype(BF)
            cos = cos_t[m, at]
            sin = -sin_t[m, at]
            dkeys = rotate(dot_tn(dscores, queries), cos, sin)
            dqueries = dot(dscores, keys)
            for h in range(HEADS):
                part = rotate(dqueries[h * SEQ : (h + 1) * SEQ], cos, sin)
                dqkv_all[m, f, at, pl.ds(h * HEAD, HEAD)] = part.astype(BF)
            dqkv_all[m, f, at, pl.ds(HALF, HEAD)] = dkeys.astype(BF)
            dqkv_all[m, f, at, pl.ds(HALF + HEAD, HEAD)] = dvalues.astype(BF)
            part = dqkv_all.at[m, f, at]
            to_partner(3, m, part, part).start()

    def project_back_step(m):
        dqkv_copy(m).wait_recv()

        @pl.loop(0, 2)
        def _(i):
            at = aligned(jnp.where(i == 0, other, f) * SEQ, SEQ, 16)

            @pl.loop(0, HALF // 256)
            def _(j):
                cols = aligned(j * 256, 256, 128)
                block = dot_nt(dqkv_all[m, 0, at], wqkv[cols, pl.ds(0, QKV)])
                block = block + dot_nt(dqkv_all[m, 1, at], wqkv[cols, pl.ds(QKV, QKV)])

                @pl.when(i == 0)
                def _():
                    dn1_send[m, :, cols] = block.astype(BF)

                @pl.when(i == 1)
                def _():
                    part_own[m, :, aligned(f * HALF + j * 256, 256, 128)] = block

            pl.when(i == 0)(dn1_copy(m).start)

    def close_step(m):
        dn1_copy(m).wait_recv()
        part_own[m, :, other_half] = dn1_recv[m].astype(F32)
        grad = part_own[m]
        rows = x_own[m].astype(F32)
        inverse = inverse_rms(rows)
        gains_acc[0:1] += jnp.sum(grad * rows * inverse, axis=0, keepdims=True)
        ingrad_s[m] = (dh_s[m] + rms_back(rows, inverse, gains[0:1], grad)).astype(BF)

        @pl.when(second)
        def _():
            for cross in (0, 1):
                grad_copy(m, cross).start()

        out_copy(7, ingrad_s.at[m], ingrad_out.at[m], m).start()
        out_copy(8, n1p.at[m], n1_out.at[m], m).start()
        out_copy(9, dqkv_all.at[m], dqkv_out.at[m], m).start()
        out_copy(10, att.at[m], att_out.at[m], m).start()

    half_rows = HALF
    quarter_rows = HIDDEN // 2

    def expert_out(i, m):
        src, own, their = (
            (wg, own_gate_out, their_gate_out),
            (wu, own_up_out, their_up_out),
            (wd, own_down_out, their_down_out),
        )[i]
        size = src.shape[0] // 2
        part = src.at[aligned(m * size, size, 16)]
        own = pltpu.make_async_copy(part, own, out_sem.at[i, m])
        their = pltpu.make_async_copy(part, their, out_sem.at[i, m])
        return own, their

    def start_out(i, m):
        own, their = expert_out(i, m)
        pl.when(m == f)(own.start)
        pl.when(m != f)(their.start)

    def grads_in_step(j, m):
        cols = aligned(m * half_rows + j * 256, 256, 128)
        rows = n2recv[:, :, :, :, cols].reshape(MB * ROWS, 256)
        wg[cols, :] = dot_tn(rows, gs[...].reshape(MB * ROWS, HIDDEN)).astype(BF)
        wu[cols, :] = dot_tn(rows, us[...].reshape(MB * ROWS, HIDDEN)).astype(BF)
        if j == 2:
            start_out(0, m)
            start_out(1, m)

    def grads_out_step(j, m):
        cols = aligned(m * quarter_rows, quarter_rows, 128)
        at = pl.ds(j * 512, 512)
        rows = dyrecv[:, :, :, :, at].reshape(MB * ROWS, 512)
        wd[cols, at] = dot_tn(hid[:, :, :, :, cols].reshape(MB * ROWS, quarter_rows), rows).astype(BF)
        if j == 2:
            start_out(2, m)

    steps = {
        IN_A: functools.partial(grads_in_step, 0),
        IN_B: functools.partial(grads_in_step, 1),
        IN_C: functools.partial(grads_in_step, 2),
        OUT_A: functools.partial(grads_out_step, 0),
        OUT_B: functools.partial(grads_out_step, 1),
        OUT_C: functools.partial(grads_out_step, 2),
        ENTER: enter_step,
        PROJECT: project_step,
        PROJECT_BACK: project_back_step,
        ATTEND: attend_step,
        NORM: norm_step,
        TWIN: twin_step,
        HIDE: hide_step,
        GIVE: give_step,
        FAR: far_step,
        JOIN: join_step,
        GRAD: grad_step,
        GRAD_TWIN: grad_twin_step,
        BACK_NEAR: functools.partial(back_step, x),
        BACK_FAR: functools.partial(back_step, away),
        FAR_BACK: far_back_step,
        MID: mid_step,
        ATTEND_BACK: attend_back_step,
        CLOSE: close_step,
        LOAD: load_step,
    }
    length = max(len(FIRST_PLAN), len(SECOND_PLAN))
    plans = [plan + ((REST, 0, 0),) * (length - len(plan)) for plan in (FIRST_PLAN, SECOND_PLAN)]

    @pl.loop(0, length)
    def _(i):
        code = jnp.int32(REST * MB)
        for at, ((step_a, m_a, _), (step_b, m_b, _)) in enumerate(zip(*plans)):
            here = jnp.where(first, step_a * MB + m_a, step_b * MB + m_b)
            code = jnp.where(i == at, here, code)
        m = lax.rem(code, MB)
        for step, work in steps.items():
            pl.when(code // MB == step)(functools.partial(work, m))
        for mine, plan in zip((first, second), plans):
            start = 0
            for at, (_, _, count) in enumerate(plan):
                if count:
                    part = w_pieces[start : start + count]

                    @pl.when(jnp.logical_and(mine, i == at))
                    def _():
                        for copy in part:
                            copy.start()

                start += count

    pl.when(second)(lambda: pl.semaphore_wait(go_sem, 1))

    gains_out[...] = gains_acc[...]

    @pl.loop(0, MB)
    def _(m):
        for source in range(2):
            sent(1, m, dsend, source)
            sent(3, m, bsend, source)
        to_partner(0, m, part_send.at[m], part_recv.at[m]).wait_send()
        da_copy(m).wait_send()
        dn1_copy(m).wait_send()
        dqkv_copy(m).wait_send()
        n1_copy(m).wait_send()
        pq_copy(m).wait_send()
        n2_copy(m).wait_send()
        far_copy(1, m).wait_send()
        far_copy(2, m).wait_send()

        @pl.when(first)
        def _():
            acts_copy(m).wait_send()

        @pl.when(second)
        def _():
            ct_copy(m).wait_send()
            for cross in (0, 1):
                grad_copy(m, cross).wait_send()

    side_copy.wait_send()
    meta_copy.wait_send()

    @pl.loop(0, MB)
    def _(m):
        pairs = (
            (3, acts_s.at[m], acts_out.at[m]),
            (6, da_pair.at[m], da_out.at[m]),
            (7, ingrad_s.at[m], ingrad_out.at[m]),
            (8, n1p.at[m], n1_out.at[m]),
            (9, dqkv_all.at[m], dqkv_out.at[m]),
            (10, att.at[m], att_out.at[m]),
        )
        for i, src, dst in pairs:
            out_copy(i, src, dst, m).wait()
        for i in range(3):
            expert_out(i, m)[0].wait()


def run_sections(*operands):
    def out(*shape, dtype=BF):
        return jax.ShapeDtypeStruct(shape, dtype)

    vmem = pl.BlockSpec(memory_space=pltpu.VMEM)
    anywhere = pl.BlockSpec(memory_space=pl.ANY)
    dma = pltpu.SemaphoreType.DMA
    blocks = (MB, PLANE, 2, SLOTS, WIDTH)
    return pl.pallas_call(
        section_kernel,
        name="sections",
        out_shape=(
            out(MB, SEQ, WIDTH),
            out(MB, SEQ, WIDTH),
            out(8, WIDTH, dtype=F32),
            out(HALF, HIDDEN),
            out(HALF, HIDDEN),
            out(HIDDEN // 2, WIDTH),
            out(HALF, HIDDEN),
            out(HALF, HIDDEN),
            out(HIDDEN // 2, WIDTH),
            out(MB, 2 * SEQ, HALF),
            out(MB, 2, 2 * SEQ, QKV),
            out(MB, 2 * SEQ, HALF),
            out(MB, 2 * SEQ, WIDTH),
        ),
        in_specs=[anywhere] * 9 + [vmem] * 6,
        out_specs=[anywhere] * 2 + [vmem] + [anywhere] * 10,
        scratch_shapes=[
            pltpu.VMEM((HALF, 2 * QKV), BF),
            pltpu.VMEM((HALF, WIDTH), BF),
            pltpu.VMEM((WIDTH, HIDDEN), BF),
            pltpu.VMEM((WIDTH, HIDDEN), BF),
            pltpu.VMEM((HIDDEN, WIDTH), BF),
            pltpu.VMEM((MB, SEQ, WIDTH), BF),
            pltpu.VMEM((MB, 2 * SEQ, HALF), BF),
            pltpu.VMEM((MB, SEQ, HALF), BF),
            pltpu.VMEM((MB, 2 * SEQ, QKV), F32),
            pltpu.VMEM((MB, 2 * SEQ, QKV), BF),
            pltpu.VMEM((MB, 2 * SEQ, QKV), BF),
            pltpu.VMEM((MB, 2 * SEQ, QKV), BF),
            pltpu.VMEM((MB, 2 * SEQ, HALF), BF),
            pltpu.VMEM((MB, SEQ, WIDTH), F32),
            pltpu.VMEM((MB, SEQ, WIDTH), F32),
            pltpu.VMEM((MB, SEQ, WIDTH), BF),
            pltpu.VMEM((MB, SEQ, WIDTH), BF),
            pltpu.VMEM((MB, 2, PLANE * SLOTS, SEQ), BF),
            pltpu.VMEM((MB, 2, PLANE * SLOTS, SEQ), BF),
            pltpu.VMEM((MB, 2, PLANE * SLOTS, SEQ), BF),
            pltpu.VMEM((MB, 2, SEQ, WIDTH), BF),
            pltpu.VMEM((MB, 2, SEQ, WIDTH), BF),
            pltpu.VMEM(blocks, BF),
            pltpu.VMEM(blocks, BF),
            pltpu.VMEM(blocks, BF),
            pltpu.VMEM(blocks, BF),
            pltpu.VMEM(blocks, BF),
            pltpu.VMEM(blocks, BF),
            pltpu.VMEM(blocks[:-1] + (HIDDEN,), BF),
            pltpu.VMEM(blocks[:-1] + (HIDDEN,), BF),
            pltpu.VMEM(blocks[:-1] + (HIDDEN,), BF),
            pltpu.VMEM((2, MB, SEQ, WIDTH), BF),
            pltpu.VMEM((2, MB, SEQ, WIDTH), BF),
            pltpu.VMEM((MB, SEQ, WIDTH), BF),
            pltpu.VMEM((MB, SEQ, WIDTH), F32),
            pltpu.VMEM((MB, 2 * SEQ, WIDTH), BF),
            pltpu.VMEM((MB, 2, 2 * SEQ, QKV), BF),
            pltpu.VMEM((MB, SEQ, HALF), BF),
            pltpu.VMEM((MB, SEQ, HALF), BF),
            pltpu.VMEM((MB, SEQ, WIDTH), BF),
            pltpu.VMEM((8, WIDTH), F32),
            pltpu.VMEM((2, 8, HALF), F32),
            pltpu.VMEM((2, MB, 8, SEQ), F32),
            pltpu.VMEM((2, WIDTH), F32),
            pltpu.VMEM((MB, 2 * SEQ, HEAD), F32),
            pltpu.VMEM((MB, 2 * SEQ, HEAD), F32),
            pltpu.VMEM((MB, 2, SEQ, SEQ), F32),
            dma((12,)),
            dma((12,)),
            dma((10,)),
            dma((4, MB, 2)),
            dma((4, MB, 2)),
            dma((6, MB)),
            dma((6, MB)),
            dma((3, MB)),
            dma((3, MB)),
            dma((MB,)),
            dma((MB,)),
            dma((2, MB)),
            dma((2, MB)),
            dma((11, MB)),
            pltpu.SemaphoreType.REGULAR,
        ],
        compiler_params=pltpu.CompilerParams(
            collective_id=0, has_side_effects=True, vmem_limit_bytes=62 * 2**20
        ),
    )(*operands)


BAND = 192
SLICE = 48
LANES = (("z", 1024), ("y", 1024), ("z", 768), ("y", 768))


def grads_kernel(
    their_gate,
    their_up,
    their_down,
    n1_in,
    dqkv_in,
    att_in,
    da_in,
    gains_in,
    q_out,
    k_out,
    v_out,
    o_out,
    part_gate,
    part_up,
    part_down,
    gains_out,
    n1,
    dqkv,
    att,
    da,
    *rest,
):
    lane_refs, rest = [rest[i * 9 : i * 9 + 9] for i in range(len(LANES))], rest[9 * len(LANES) :]
    (
        small,
        small_recv,
        load_sem,
        send_sem,
        recv_sem,
        pair_send,
        pair_recv,
        small_send,
        small_recv_sem,
        out_sem,
    ) = rest
    f = lax.axis_index("fsdp")
    e = lax.axis_index("expert")
    y, x, z = e // 8, lax.rem(e // 4, 2), lax.rem(e, 4)
    other = 1 - f
    own_half = aligned(f * HALF, HALF, 128)
    other_half = aligned(other * HALF, HALF, 128)

    def along_y(d):
        return {"expert": lax.rem(y + d, 4) * 8 + x * 4 + z}

    def along_z(d):
        return {"expert": y * 8 + x * 4 + lax.rem(z + d, 4)}

    twin = {"expert": y * 8 + (1 - x) * 4 + z}
    partner = {"fsdp": other}

    barrier = pltpu.get_barrier_semaphore()
    neighbours = [along_y(d) for d in (1, 2, 3)] + [along_z(d) for d in (1, 2, 3)]
    neighbours += [twin, partner]
    for place in neighbours:
        pl.semaphore_signal(barrier, inc=1, device_id=place, device_id_type=MESH)

    loads = [
        (att_in, att),
        (da_in, da),
        (n1_in, n1),
        (dqkv_in, dqkv),
    ]
    loads = [pltpu.make_async_copy(a, b, load_sem.at[i]) for i, (a, b) in enumerate(loads)]
    for copy in loads:
        copy.start()

    def remote(src, dst, send, recv, place):
        return pltpu.make_async_remote_copy(
            src_ref=src,
            dst_ref=dst,
            send_sem=send,
            recv_sem=recv,
            device_id=place,
            device_id_type=MESH,
        )

    def wait_for(ref, sem):
        pltpu.make_async_copy(ref, ref, sem).wait()

    class Lane:
        def __init__(self, i):
            self.i = i
            self.v, self.far, self.merged, self.r1, self.s1, self.r2, self.s2, self.r3, self.g = (
                lane_refs[i]
            )
            axes = ((along_y, y), (along_z, z))
            (axis, at), (self.next, self.to) = axes if LANES[i][0] == "y" else axes[::-1]
            self.right, self.left = axis(1), axis(3)
            self.at = at
            half = LANES[i][1] // 2
            self.mine = aligned(x * half, half, 128)
            self.theirs = aligned((1 - x) * half, half, 128)
            self.place = aligned(at * BAND + self.to * SLICE, SLICE, 16)

        def rows(self, distance, part=None):
            start = lax.rem(self.at + distance, 4) * BAND
            if part is None:
                return aligned(start, BAND, 16)
            return aligned(start + part * (BAND // 2), BAND // 2, 16)

        def send(self, stage, src, dst, place):
            remote(
                src, dst, send_sem.at[self.i, stage], recv_sem.at[self.i, stage], place
            ).start()

        def arrived(self, stage, ref):
            wait_for(ref, recv_sem.at[self.i, stage])

        def spread(self):
            low = pl.ds(BAND // 2, BAND // 2)
            top = pl.ds(0, BAND // 2)
            self.send(0, self.v.at[self.rows(2, 0)], self.far.at[0], self.right)
            self.send(1, self.v.at[self.rows(2, 1)], self.far.at[1], self.left)
            self.send(2, self.v.at[self.rows(1, 1)], self.r1.at[0, low], self.right)
            self.send(3, self.v.at[self.rows(3, 0)], self.r1.at[1, top], self.left)

        def merge(self):
            low = pl.ds(BAND // 2, BAND // 2)
            top = pl.ds(0, BAND // 2)
            self.arrived(0, self.far.at[0])
            total = self.v[self.rows(1, 0)].astype(F32) + self.far[0].astype(F32)
            self.merged[0] = total.astype(BF)
            self.send(2, self.merged.at[0], self.r1.at[0, top], self.right)
            self.arrived(1, self.far.at[1])
            total = self.v[self.rows(3, 1)].astype(F32) + self.far[1].astype(F32)
            self.merged[1] = total.astype(BF)
            self.send(3, self.merged.at[1], self.r1.at[1, low], self.left)

        def join_one(self):
            self.arrived(2, self.r1.at[0])
            self.arrived(3, self.r1.at[1])
            total = self.v[self.rows(0)].astype(F32)
            total = total + self.r1[0].astype(F32) + self.r1[1].astype(F32)
            self.s1[...] = total.astype(BF)
            for d in (1, 2, 3):
                rows = aligned(lax.rem(self.to + d, 4) * SLICE, SLICE, 16)
                self.send(4, self.s1.at[rows], self.r2.at[self.to], self.next(d))

        def join_two(self):
            self.arrived(4, self.r2.at[pl.ds(0, 3)])
            total = self.s1[aligned(self.to * SLICE, SLICE, 16)].astype(F32)
            for d in (1, 2, 3):
                total = total + self.r2[lax.rem(self.to + d, 4)].astype(F32)
            self.s2[...] = total.astype(BF)
            self.send(5, self.s2.at[:, self.theirs], self.r3, twin)

        def join_three(self):
            self.arrived(5, self.r3)
            total = self.s2[:, self.mine].astype(F32) + self.r3[...].astype(F32)
            self.g[self.place, self.mine] = total.astype(BF)
            part = self.g.at[self.place, self.mine]
            self.send(6, part, part, twin)

        def gather_two(self):
            self.arrived(6, self.g.at[self.place, self.theirs])
            part = self.g.at[self.place]
            for d in (1, 2, 3):
                self.send(7, part, part, self.next(d))

        def gather_one(self):
            self.arrived(7, self.g.at[pl.ds(0, 3 * SLICE)])
            top, low = self.g.at[self.rows(0, 0)], self.g.at[self.rows(0, 1)]
            self.send(8, top, top, self.right)
            self.send(9, low, low, self.left)
            self.send(10, low, low, self.right)
            self.send(11, top, top, self.left)

        def pass_on(self):
            top, low = self.g.at[self.rows(3, 0)], self.g.at[self.rows(1, 1)]
            self.arrived(8, top)
            self.send(12, top, top, self.right)
            self.arrived(9, low)
            self.send(13, low, low, self.left)

        def finish(self):
            part = self.g.at[pl.ds(0, BAND // 2)]
            for stage in (10, 11, 12, 13):
                self.arrived(stage, part)

        def drain(self):
            half = self.v.at[pl.ds(0, BAND // 2)]
            band = self.v.at[pl.ds(0, BAND)]
            slices = self.v.at[pl.ds(0, 3 * SLICE)]
            sizes = [half, half, band, band, slices, self.s2.at[:, self.theirs]]
            sizes += [self.g.at[self.place, self.mine], slices] + [half] * 6
            for stage, ref in enumerate(sizes):
                wait_for(ref, send_sem.at[self.i, stage])

    out_one, query_one, out_two, query_two = lanes = [Lane(i) for i in range(len(LANES))]

    def over_micro(group, cols):
        block = jnp.concatenate([dqkv[m, group, :, cols] for m in range(MB)], axis=0)
        return dot_tn(n1[...], block).astype(BF)

    for copy in loads[:2]:
        copy.wait()
    for j in range(2):
        cols = pl.ds(j * 512, 512)
        out_one.v[:, cols] = dot_tn(att[...], da[:, cols]).astype(BF)
    pl.semaphore_wait(barrier, len(neighbours))
    out_one.spread()
    for copy in loads[2:4]:
        copy.wait()
    query_one.v[:, pl.ds(0, HALF)] = over_micro(0, pl.ds(0, HALF))
    query_one.v[:, pl.ds(HALF, 256)] = over_micro(1, pl.ds(0, 256))
    query_one.spread()
    small[...] = gains_in[...]
    small_pair = remote(
        small.at[:, other_half],
        small_recv.at[0],
        small_send.at[0],
        small_recv_sem.at[0],
        partner,
    )
    small_pair.start()
    out_two.v[:, pl.ds(0, 512)] = dot_tn(att[...], da[:, pl.ds(1024, 512)]).astype(BF)
    query_two.v[:, pl.ds(0, 512)] = over_micro(1, pl.ds(256, 512))
    for g in range(2):
        query_two.v[:, pl.ds(512 + g * HEAD, HEAD)] = over_micro(g, pl.ds(HALF, HEAD))
        out_two.v[:, pl.ds(512 + g * HEAD, HEAD)] = over_micro(g, pl.ds(HALF + HEAD, HEAD))

    pair = [
        remote(src, dst, pair_send.at[i], pair_recv.at[i], partner)
        for i, (src, dst) in enumerate(
            ((their_gate, part_gate), (their_up, part_up), (their_down, part_down))
        )
    ]
    pieces = [
        remote(src.at[rows], dst.at[rows], pair_send.at[n], pair_recv.at[n], partner)
        for n, src, dst, size in (
            (0, their_gate, part_gate, HALF // 4),
            (1, their_up, part_up, HALF // 4),
            (2, their_down, part_down, HIDDEN // 8),
        )
        for rows in [pl.ds(i * size, size) for i in range(4)]
    ]

    def send_pieces(start, stop):
        for copy in pieces[start:stop]:
            copy.start()

    def spread_small(i, axis):
        for d in (1, 2, 3):
            remote(
                small.at[:, pl.ds(0, HALF)],
                small_recv.at[1 + 3 * i + d - 1],
                small_send.at[1 + 3 * i + d - 1],
                small_recv_sem.at[1 + 3 * i + d - 1],
                axis(d),
            ).start()

    def join_small(i, axis):
        for d in (1, 2, 3):
            remote(
                small.at[:, pl.ds(0, HALF)],
                small_recv.at[1 + 3 * i + d - 1],
                small_send.at[1 + 3 * i + d - 1],
                small_recv_sem.at[1 + 3 * i + d - 1],
                axis(d),
            ).wait()
        total = small[:, pl.ds(0, HALF)]
        for d in (1, 2, 3):
            total = total + small_recv[1 + 3 * i + d - 1]
        small[:, pl.ds(0, HALF)] = total

    small_pair.wait()
    small[:, pl.ds(0, HALF)] = small[:, own_half] + small_recv[0]
    spread_small(0, along_y)

    out_two.spread()
    query_two.spread()
    send_pieces(0, 4)
    join_small(0, along_y)
    spread_small(1, along_z)
    for lane in lanes:
        lane.merge()
    for lane in lanes:
        lane.join_one()
    for lane in lanes:
        lane.join_two()
    join_small(1, along_z)
    small_twin = remote(
        small.at[:, pl.ds(0, HALF)],
        small_recv.at[7],
        small_send.at[7],
        small_recv_sem.at[7],
        twin,
    )
    small_twin.start()
    send_pieces(4, 5)
    for lane in lanes:
        lane.join_three()
    send_pieces(5, 12)
    for lane in lanes:
        lane.gather_two()
    for lane in lanes:
        lane.gather_one()
    for lane in lanes:
        lane.pass_on()
    small_twin.wait()
    gains_out[...] = small[:, pl.ds(0, HALF)] + small_recv[7]

    outs = []

    def out_copy(src, dst):
        copy = pltpu.make_async_copy(src, dst, out_sem.at[len(outs)])
        copy.start()
        outs.append(copy)

    out_one.finish()
    out_copy(out_one.g, o_out.at[:, pl.ds(0, 1024)])
    query_one.finish()
    out_copy(query_one.g, q_out.at[:, pl.ds(0, 1024)])
    out_two.finish()
    out_copy(out_two.g.at[:, pl.ds(0, 512)], o_out.at[:, pl.ds(1024, 512)])
    out_copy(out_two.g.at[:, pl.ds(512, 256)], v_out)
    query_two.finish()
    out_copy(query_two.g.at[:, pl.ds(0, 512)], q_out.at[:, pl.ds(1024, 512)])
    out_copy(query_two.g.at[:, pl.ds(512, 256)], k_out)

    for lane in lanes:
        lane.drain()
    for copy in pair:
        copy.wait()
    for copy in outs:
        copy.wait()


def reduce_grads(*operands):
    def out(*shape):
        return jax.ShapeDtypeStruct(shape, BF)

    vmem = pl.BlockSpec(memory_space=pltpu.VMEM)
    anywhere = pl.BlockSpec(memory_space=pl.ANY)
    dma = pltpu.SemaphoreType.DMA
    lanes = []
    for _, width in LANES:
        lanes += [
            pltpu.VMEM((HALF, width), BF),
            pltpu.VMEM((2, BAND // 2, width), BF),
            pltpu.VMEM((2, BAND // 2, width), BF),
            pltpu.VMEM((2, BAND, width), BF),
            pltpu.VMEM((BAND, width), BF),
            pltpu.VMEM((4, SLICE, width), BF),
            pltpu.VMEM((SLICE, width), BF),
            pltpu.VMEM((SLICE, width // 2), BF),
            pltpu.VMEM((HALF, width), BF),
        ]
    return pl.pallas_call(
        grads_kernel,
        name="grads",
        out_shape=(
            out(HALF, WIDTH),
            out(HALF, 256),
            out(HALF, 256),
            out(HALF, WIDTH),
            out(HALF, HIDDEN),
            out(HALF, HIDDEN),
            out(HIDDEN // 2, WIDTH),
            jax.ShapeDtypeStruct((8, HALF), F32),
        ),
        in_specs=[anywhere] * 7 + [vmem],
        out_specs=[anywhere] * 7 + [vmem],
        scratch_shapes=[
            pltpu.VMEM((MB * 2 * SEQ, HALF), BF),
            pltpu.VMEM((MB, 2, 2 * SEQ, QKV), BF),
            pltpu.VMEM((MB * 2 * SEQ, HALF), BF),
            pltpu.VMEM((MB * 2 * SEQ, WIDTH), BF),
        ]
        + lanes
        + [
            pltpu.VMEM((8, WIDTH), F32),
            pltpu.VMEM((8, 8, HALF), F32),
            dma((4,)),
            dma((len(LANES), 14)),
            dma((len(LANES), 14)),
            dma((3,)),
            dma((3,)),
            dma((8,)),
            dma((8,)),
            dma((9,)),
        ],
        compiler_params=pltpu.CompilerParams(
            collective_id=1, has_side_effects=True, vmem_limit_bytes=62 * 2**20
        ),
    )(*operands)


def finish_kernel(*refs):
    (q, k, v, o, own_g, own_u, own_d, part_g, part_u, part_d, acts, grads, gains), outs = (
        refs[:13],
        refs[13:],
    )
    for src, dst in zip((q, k, v, o), outs):
        dst[...] = src[...].astype(F32)
    for own, part, dst in zip((own_g, own_u, own_d), (part_g, part_u, part_d), outs[4:]):
        dst[...] = own[...].astype(F32) + part[...].astype(F32)
    outs[7][...] = acts[...]
    outs[8][...] = grads[...]
    outs[9][...] = gains[0:1]
    outs[10][...] = gains[1:2]


def finish(*blocks):
    steps = 4

    def spec(rows, cols):
        return pl.BlockSpec((rows // steps, cols), lambda i: (i, 0))

    def whole(rows, cols):
        return pl.BlockSpec((rows, cols), lambda i: (0, 0))

    gains = blocks[-1]
    split = blocks[:-1]
    results = split[:7] + split[10:]
    dtypes = [F32] * 7 + [BF] * 2
    return pl.pallas_call(
        finish_kernel,
        name="finish",
        grid=(steps,),
        out_shape=[jax.ShapeDtypeStruct(b.shape, t) for b, t in zip(results, dtypes)]
        + [jax.ShapeDtypeStruct((1, HALF), F32)] * 2,
        in_specs=[spec(*b.shape) for b in split] + [whole(*gains.shape)],
        out_specs=[spec(*b.shape) for b in results] + [whole(1, HALF)] * 2,
        compiler_params=pltpu.CompilerParams(vmem_limit_bytes=62 * 2**20),
    )(*blocks)


def local(
    inputs,
    cotangent,
    segments,
    expert_ids,
    gate_logits,
    w_query,
    key_projection,
    value_projection,
    w_out,
    gain_attn,
    gain_moe,
    w_gate,
    w_up,
    w_down,
):
    steps = np.arange(HEAD) % (HEAD // 2)
    frequency = (ROPE_BASE ** (-steps * 2.0 / HEAD)).astype(np.float32)[None]
    (
        acts,
        in_grads,
        gain_parts,
        own_gate,
        own_up,
        own_down,
        their_gate,
        their_up,
        their_down,
        n1,
        dqkv,
        att,
        da,
    ) = run_sections(
        inputs,
        cotangent,
        w_query[0],
        key_projection[0],
        value_projection[0],
        w_out[0],
        w_gate[0, 0],
        w_up[0, 0],
        w_down[0, 0],
        gain_attn,
        gain_moe,
        segments,
        jnp.swapaxes(expert_ids[0], 1, 2),
        jnp.swapaxes(gate_logits[0], 1, 2),
        jnp.asarray(frequency),
    )
    gq, gk, gv, go, part_gate, part_up, part_down, gains = reduce_grads(
        their_gate,
        their_up,
        their_down,
        n1.reshape(MB * 2 * SEQ, HALF),
        dqkv,
        att.reshape(MB * 2 * SEQ, HALF),
        da.reshape(MB * 2 * SEQ, WIDTH),
        gain_parts,
    )
    gq, gk, gv, go, grad_gate, grad_up, grad_down, acts, in_grads, gain_one, gain_two = finish(
        gq,
        gk,
        gv,
        go,
        own_gate,
        own_up,
        own_down,
        part_gate,
        part_up,
        part_down,
        acts.reshape(MB * SEQ, WIDTH),
        in_grads.reshape(MB * SEQ, WIDTH),
        gains,
    )
    return (
        acts.reshape(1, MB, SEQ, WIDTH),
        in_grads.reshape(1, MB, SEQ, WIDTH),
        gq[None],
        gk[None],
        gv[None],
        go[None],
        gain_one,
        gain_two,
        grad_gate[None, None],
        grad_up[None, None],
        grad_down[None, None],
    )


def solution(mesh):
    return jax.shard_map(
        local,
        mesh=mesh,
        in_specs=(
            P(None, ("fsdp", "expert"), None),
            P(None, ("fsdp", "expert"), None),
            P(None, ("fsdp", "expert")),
            P("section", None, ("fsdp", "expert"), None),
            P("section", None, ("fsdp", "expert"), None),
            P("section", "fsdp", None),
            P("section", "fsdp", None),
            P("section", "fsdp", None),
            P("section", "fsdp", None),
            P("section", "fsdp"),
            P("section", "fsdp"),
            P("section", "expert", "fsdp", None),
            P("section", "expert", "fsdp", None),
            P("section", "expert", "fsdp", None),
        ),
        out_specs=(
            P("section", None, ("fsdp", "expert"), None),
            P("section", None, ("fsdp", "expert"), None),
            P("section", "fsdp", None),
            P("section", "fsdp", None),
            P("section", "fsdp", None),
            P("section", "fsdp", None),
            P("section", "fsdp"),
            P("section", "fsdp"),
            P("section", "expert", "fsdp", None),
            P("section", "expert", "fsdp", None),
            P("section", "expert", "fsdp", None),
        ),
        check_vma=False,
    )
```

```python
import functools

import jax
import jax.numpy as jnp
import numpy as np
from jax import lax
from jax.experimental import pallas as pl
from jax.experimental.pallas import tpu as pltpu
from jax.sharding import PartitionSpec as P

MESH = pl.DeviceIdType.MESH
BF = jnp.bfloat16
F32 = jnp.float32

HEAD = 128
EPS = 1e-06
ROPE_BASE = 1000000.0
GELU_C = 0.7978845608
GELU_A = 0.044715

MB = 2
SEQ = 96
WIDTH = 1536
HALF = 768
EXPERTS = 32
PLANE = 16
SLOTS = 16
ROWS = EXPERTS * SLOTS
HIDDEN = 768
HEADS = 6
QKV = 1024


def dot(a, b):
    return jnp.dot(a, b, preferred_element_type=F32)


def dot_nt(a, b):
    return lax.dot_general(a, b, (((1,), (1,)), ((), ())), preferred_element_type=F32)


def dot_tn(a, b):
    return lax.dot_general(a, b, (((0,), (0,)), ((), ())), preferred_element_type=F32)


def aligned(start, size, unit):
    return pl.ds(pl.multiple_of(start, unit), size)


def inverse_rms(rows):
    return lax.rsqrt(jnp.mean(rows * rows, axis=-1, keepdims=True) + EPS)


def rms_back(rows, inverse, gain, grad):
    scaled = gain * grad
    return inverse * scaled - rows * (inverse * inverse * inverse) * jnp.mean(
        scaled * rows, axis=-1, keepdims=True
    )


def rotate(head, cos, sin):
    return head * cos + pltpu.roll(head, HEAD // 2, 1) * sin


(
    ENTER,
    PROJECT,
    ATTEND,
    NORM,
    TWIN,
    HIDE,
    GIVE,
    FAR,
    JOIN,
    GRAD,
    GRAD_TWIN,
    BACK_NEAR,
    BACK_FAR,
    FAR_BACK,
    MID,
    ATTEND_BACK,
    PROJECT_BACK,
    CLOSE,
    LOAD,
    IN_A,
    IN_B,
    IN_C,
    OUT_A,
    OUT_B,
    OUT_C,
    REST,
) = range(26)

FIRST_PLAN = (
    (ENTER, 0, 0),
    (ENTER, 1, 1),
    (PROJECT, 0, 0),
    (PROJECT, 1, 1),
    (ATTEND, 0, 1),
    (ATTEND, 1, 0),
    (NORM, 0, 1),
    (NORM, 1, 8),
    (TWIN, 0, 0),
    (TWIN, 1, 0),
    (HIDE, 0, 0),
    (HIDE, 1, 0),
    (GIVE, 0, 0),
    (GIVE, 1, 0),
    (FAR, 0, 0),
    (JOIN, 0, 0),
    (FAR, 1, 0),
    (JOIN, 1, 0),
    (GRAD, 0, 0),
    (GRAD_TWIN, 0, 0),
    (GRAD, 1, 0),
    (BACK_NEAR, 0, 0),
    (GRAD_TWIN, 1, 0),
    (BACK_FAR, 0, 0),
    (BACK_FAR, 1, 0),
    (BACK_NEAR, 1, 0),
    (FAR_BACK, 0, 0),
    (IN_A, 0, 0),
    (IN_B, 0, 0),
    (IN_C, 0, 0),
    (MID, 0, 0),
    (IN_A, 1, 0),
    (IN_B, 1, 0),
    (FAR_BACK, 1, 0),
    (ATTEND_BACK, 0, 0),
    (MID, 1, 0),
    (IN_C, 1, 0),
    (OUT_A, 0, 0),
    (PROJECT_BACK, 0, 0),
    (OUT_B, 0, 0),
    (ATTEND_BACK, 1, 0),
    (CLOSE, 0, 0),
    (OUT_C, 0, 0),
    (OUT_A, 1, 0),
    (PROJECT_BACK, 1, 0),
    (OUT_B, 1, 0),
    (OUT_C, 1, 0),
    (CLOSE, 1, 0),
)
SECOND_PLAN = (
    (GRAD, 0, 0),
    (GRAD, 1, 0),
    (LOAD, 0, 3),
    (ENTER, 0, 0),
    (PROJECT, 0, 1),
    (ENTER, 1, 0),
    (ATTEND, 0, 1),
    (PROJECT, 1, 0),
    (NORM, 0, 1),
    (ATTEND, 1, 1),
    (TWIN, 0, 0),
    (NORM, 1, 5),
    (TWIN, 1, 0),
    (GRAD_TWIN, 0, 0),
    (GRAD_TWIN, 1, 0),
    (HIDE, 0, 0),
    (HIDE, 1, 0),
    (BACK_FAR, 0, 0),
    (BACK_NEAR, 0, 0),
    (BACK_FAR, 1, 0),
    (BACK_NEAR, 1, 0),
    (GIVE, 0, 0),
    (GIVE, 1, 0),
    (FAR_BACK, 0, 0),
    (MID, 0, 0),
    (FAR_BACK, 1, 0),
    (ATTEND_BACK, 0, 0),
    (MID, 1, 0),
    (PROJECT_BACK, 0, 0),
    (ATTEND_BACK, 1, 0),
    (CLOSE, 0, 0),
    (PROJECT_BACK, 1, 0),
    (CLOSE, 1, 0),
    (IN_A, 0, 0),
    (IN_B, 0, 0),
    (IN_C, 0, 0),
    (IN_A, 1, 0),
    (IN_B, 1, 0),
    (IN_C, 1, 0),
    (OUT_A, 0, 0),
    (OUT_B, 0, 0),
    (OUT_C, 0, 0),
    (OUT_A, 1, 0),
    (OUT_B, 1, 0),
    (OUT_C, 1, 0),
    (FAR, 0, 0),
    (FAR, 1, 0),
    (JOIN, 0, 0),
    (JOIN, 1, 0),
)


def section_kernel(
    x_in,
    ct_in,
    wq_in,
    wk_in,
    wv_in,
    wo_in,
    wg_in,
    wu_in,
    wd_in,
    gain_one_in,
    gain_two_in,
    segments_in,
    ids_in,
    logits_in,
    freq_in,
    acts_out,
    ingrad_out,
    gains_out,
    own_gate_out,
    own_up_out,
    own_down_out,
    their_gate_out,
    their_up_out,
    their_down_out,
    n1_out,
    dqkv_out,
    att_out,
    da_out,
    wqkv,
    wo,
    wg,
    wu,
    wd,
    x_own,
    n1p,
    n1_send,
    pq_own,
    pq_send,
    pq_recv,
    qkvs,
    att,
    hid_one,
    part_own,
    part_send,
    part_recv,
    sel,
    cg_hi,
    cg_lo,
    n2pair,
    gpair,
    dsend,
    bsend,
    n2recv,
    yrecv,
    dyrecv,
    dn2recv,
    gs,
    us,
    hid,
    far_send,
    far_recv,
    acts_s,
    dh_s,
    da_pair,
    dqkv_all,
    dn1_send,
    dn1_recv,
    ingrad_s,
    gains_acc,
    side,
    meta,
    gains,
    cos_t,
    sin_t,
    mask_t,
    lw_sem,
    ws_sem,
    wr_sem,
    as_sem,
    ar_sem,
    ps_sem,
    pr_sem,
    ts_sem,
    tr_sem,
    xs_sem,
    xr_sem,
    gs_sem,
    gr_sem,
    out_sem,
    go_sem,
):
    sec = lax.axis_index("section")
    f = lax.axis_index("fsdp")
    e = lax.axis_index("expert")
    y, x, z = e // 8, lax.rem(e // 4, 2), lax.rem(e, 4)
    q = y * 4 + z
    away = 1 - x
    other = 1 - f
    own_rows = aligned(f * SEQ, SEQ, 16)
    own_half = aligned(f * HALF, HALF, 128)
    other_half = aligned(other * HALF, HALF, 128)
    partner = {"fsdp": other}
    twin_place = y * 8 + away * 4 + z
    twin = {"expert": twin_place}
    first, second = sec == 0, sec == 1

    def in_plane(d):
        at = lax.rem(q + d, PLANE)
        return at, {"expert": (at // 4) * 8 + x * 4 + lax.rem(at, 4)}

    barrier = pltpu.get_barrier_semaphore()

    @pl.loop(1, PLANE)
    def _(d):
        pl.semaphore_signal(barrier, inc=1, device_id=in_plane(d)[1], device_id_type=MESH)

    others = (
        twin,
        partner,
        {"section": 1 - sec},
        {"section": 1 - sec, "expert": twin_place},
    )
    for place in others:
        pl.semaphore_signal(barrier, inc=1, device_id=place, device_id_type=MESH)

    local = []
    for g in range(2):
        local += [
            (wq_in.at[:, pl.ds(g * HALF, HALF)], wqkv.at[:, pl.ds(g * QKV, HALF)]),
            (wk_in.at[:, pl.ds(g * HEAD, HEAD)], wqkv.at[:, pl.ds(g * QKV + HALF, HEAD)]),
            (wv_in.at[:, pl.ds(g * HEAD, HEAD)], wqkv.at[:, pl.ds(g * QKV + HALF + HEAD, HEAD)]),
        ]
    local += [
        (wo_in, wo),
        (wg_in, wg.at[own_half]),
        (wu_in, wu.at[own_half]),
        (wd_in, wd.at[aligned(f * (HIDDEN // 2), HIDDEN // 2, 16)]),
    ]
    local = [pltpu.make_async_copy(a, b, lw_sem.at[i]) for i, (a, b) in enumerate(local)]
    for copy in local:
        copy.start()
    x_local = pltpu.make_async_copy(x_in, x_own, lw_sem.at[10])
    ct_local = pltpu.make_async_copy(ct_in, gpair.at[:, x], lw_sem.at[11])
    pl.when(first)(x_local.start)
    pl.when(second)(ct_local.start)

    def remote(src, dst, send, recv, place):
        return pltpu.make_async_remote_copy(
            src_ref=src,
            dst_ref=dst,
            send_sem=send,
            recv_sem=recv,
            device_id=place,
            device_id_type=MESH,
        )

    def wait_for(ref, sem):
        pltpu.make_async_copy(ref, ref, sem).wait()

    def weight(src, dst, i):
        return remote(src, dst, ws_sem.at[i], wr_sem.at[i], partner)

    w_moe = [
        weight(wg_in, wg.at[own_half], 3),
        weight(wu_in, wu.at[own_half], 4),
        weight(wd_in, wd.at[aligned(f * (HIDDEN // 2), HIDDEN // 2, 16)], 5),
    ]

    w_pieces = [
        weight(src.at[aligned(i * size, size, 16)], dst.at[aligned(f * 4 * size + i * size, size, 16)], n)
        for n, src, dst, size in (
            (3, wg_in, wg, HALF // 4),
            (4, wu_in, wu, HALF // 4),
            (5, wd_in, wd, HIDDEN // 8),
        )
        for i in range(4)
    ]

    def ct_copy(m):
        return remote(ct_in.at[m], gpair.at[m, x], ws_sem.at[10 + m], gr_sem.at[x, m], twin)

    side[f, 0:1] = gain_one_in[...].astype(F32)
    side[f, 1:2] = gain_two_in[...].astype(F32)
    side[f, 2:4, :SEQ] = segments_in[...].astype(F32)
    for m in range(MB):
        meta[x, m, 0:4] = ids_in[m].astype(F32)
        meta[x, m, 4:8] = logits_in[m]
    row = lax.broadcasted_iota(jnp.int32, (SEQ, SEQ), 0)
    col = lax.broadcasted_iota(jnp.int32, (SEQ, SEQ), 1)
    unit = jnp.where(row == col, 1.0, 0.0).astype(BF)
    side_copy = weight(side.at[f], side.at[f], 8)
    meta_copy = remote(meta.at[x], meta.at[x], ws_sem.at[9], wr_sem.at[9], twin)
    gains_acc[...] = jnp.zeros_like(gains_acc)

    pl.semaphore_wait(barrier, PLANE - 1 + len(others))
    side_copy.start()
    meta_copy.start()

    meta_copy.wait_recv()
    earlier = jnp.where(row < col, 1.0, 0.0).astype(BF)

    @pl.loop(0, 2 * MB)
    def _(i):
        m, source = lax.rem(i, MB), i // MB
        rows = meta[source, m]
        ids, logits = rows[:4], rows[4:]
        raised = jnp.exp(logits - jnp.max(logits, axis=0, keepdims=True))
        gates = raised / jnp.sum(raised, axis=0, keepdims=True)
        place = lax.broadcasted_iota(jnp.int32, (PLANE, SEQ), 0)
        expert = ((place // 4) * 8 + x * 4 + lax.rem(place, 4)).astype(F32)
        named = jnp.zeros((PLANE, SEQ), F32)
        weights = jnp.zeros((PLANE, SEQ), F32)
        for k in range(4):
            hit = expert == ids[k : k + 1, :]
            named = jnp.where(hit, 1.0, named)
            weights = jnp.where(hit, gates[k : k + 1, :], weights)
        slot = dot(named.astype(BF), earlier)
        slot = jnp.where(named > 0.0, slot, -1.0)
        shape = (PLANE, SLOTS, SEQ)
        count = lax.broadcasted_iota(jnp.int32, shape, 1).astype(F32)
        chosen = jnp.where(jnp.broadcast_to(slot[:, None, :], shape) == count, 1.0, 0.0)
        scaled = chosen * jnp.broadcast_to(weights[:, None, :], shape)
        scaled = scaled.reshape(PLANE * SLOTS, SEQ)
        high = scaled.astype(BF)
        sel[m, source] = chosen.reshape(PLANE * SLOTS, SEQ).astype(BF)
        cg_hi[m, source] = high
        cg_lo[m, source] = (scaled - high.astype(F32)).astype(BF)

    side_copy.wait_recv()
    gains[:, pl.ds(0, HALF)] = side[0, 0:2]
    gains[:, pl.ds(HALF, HALF)] = side[1, 0:2]
    lane = lax.broadcasted_iota(jnp.int32, (SEQ, HEAD), 1)
    turn = jnp.where(lane < HEAD // 2, -1.0, 1.0)
    for m in range(MB):
        for s in range(2):
            across = jnp.broadcast_to(side[s, 2 + m : 3 + m, :SEQ], (SEQ, SEQ))
            down = dot_nt(unit, across.astype(BF))
            same = jnp.where(down == across, 1.0, 0.0)
            mask_t[m, s] = jnp.where(col <= row, same, 0.0)
            places = jnp.sum(jnp.where(col < row, same, 0.0), axis=1, keepdims=True)
            angles = places * freq_in[...]
            cos_t[m, pl.ds(s * SEQ, SEQ)] = jnp.cos(angles)
            sin_t[m, pl.ds(s * SEQ, SEQ)] = jnp.sin(angles) * turn

    def exchange_half(kind, m, src, dst, source):
        @pl.loop(1, PLANE)
        def _(d):
            at, place = in_plane(d)
            remote(
                src.at[m, at, source],
                dst.at[m, q, source],
                as_sem.at[kind, m, source],
                ar_sem.at[kind, m, source],
                place,
            ).start()

        dst[m, q, source] = src[m, q, source]

    def received(kind, m, dst, source):
        wait_for(dst.at[m, pl.ds(0, PLANE - 1), source], ar_sem.at[kind, m, source])

    def sent(kind, m, src, source):
        wait_for(src.at[m, pl.ds(0, PLANE - 1), source], as_sem.at[kind, m, source])

    def to_partner(kind, m, src, dst):
        return remote(src, dst, ps_sem.at[kind, m], pr_sem.at[kind, m], partner)

    def to_twin(kind, m, src, dst):
        return remote(src, dst, ts_sem.at[kind, m], tr_sem.at[kind, m], twin)

    def n2_copy(m):
        return to_twin(0, m, n2pair.at[m, x], n2pair.at[m, x])

    def far_copy(kind, m):
        return to_twin(kind, m, far_send.at[kind - 1, m], far_recv.at[kind - 1, m])

    def acts_copy(m):
        return remote(acts_s.at[m], x_own.at[m], xs_sem.at[m], xr_sem.at[m], {"section": 1})

    def n1_copy(m):
        return to_partner(4, m, n1_send.at[m], n1p.at[m, own_rows])

    def pq_copy(m):
        return to_partner(5, m, pq_send.at[m], pq_recv.at[m])

    def grad_copy(m, cross):
        place = {"section": 0, "expert": twin_place} if cross else {"section": 0}
        return remote(
            ingrad_s.at[m], gpair.at[m, x], gs_sem.at[cross, m], gr_sem.at[x, m], place
        )

    def out_copy(i, src, dst, m):
        return pltpu.make_async_copy(src, dst, out_sem.at[i, m])

    def flat(ref, m):
        return ref[m].reshape(ROWS, WIDTH)

    def spread(m, source, rows, dst, scale=None):
        @pl.loop(0, WIDTH // 512)
        def _(j):
            cols = aligned(j * 512, 512, 128)
            block = dot(sel[m, source], rows[m, source, :, cols])
            if scale is not None:
                block = block * scale
            dst[m, :, source, :, cols] = block.astype(BF).reshape(PLANE, SLOTS, 512)

    def load_step(m):
        pl.semaphore_wait(go_sem, 1)
        ct_copy(0).start()
        ct_copy(1).start()

    def heads_of(ref, m, rows):
        return jnp.concatenate(
            [ref[m, rows, pl.ds(h * HEAD, HEAD)] for h in range(HEADS)], axis=0
        )

    def softmax_of(m, s, queries, keys):
        scores = dot_nt(queries, keys) * HEAD ** (-0.5)
        allowed = jnp.concatenate([mask_t[m, s]] * HEADS, axis=0)
        scores = jnp.where(allowed > 0.0, scores, -1e30)
        raised = jnp.exp(scores - jnp.max(scores, axis=-1, keepdims=True))
        return raised / jnp.sum(raised, axis=-1, keepdims=True)

    def enter_step(m):
        pl.when(jnp.logical_and(first, m == 0))(x_local.wait)
        pl.when(second)(lambda: wait_for(x_own.at[m], xr_sem.at[m]))
        rows = x_own[m].astype(F32)
        scale = inverse_rms(rows)
        n1p[m, own_rows] = (x_own[m, :, own_half].astype(F32) * scale * gains[0:1, own_half]).astype(BF)
        n1_send[m] = (
            x_own[m, :, other_half].astype(F32) * scale * gains[0:1, other_half]
        ).astype(BF)
        n1_copy(m).start()

    def project_step(m):
        @pl.when(m == 0)
        def _():
            for copy in local[:6]:
                copy.wait()

        n1_copy(m).wait_recv()

        @pl.loop(0, QKV // 512)
        def _(j):
            cols = aligned(j * 512, 512, 128)
            from_w = aligned(other * QKV + j * 512, 512, 128)
            pq_send[m, :, cols] = dot(n1p[m], wqkv[:, from_w]).astype(BF)

        pq_copy(m).start()

        @pl.loop(0, QKV // 512)
        def _(j):
            cols = aligned(j * 512, 512, 128)
            from_w = aligned(f * QKV + j * 512, 512, 128)
            pq_own[m, :, cols] = dot(n1p[m], wqkv[:, from_w])

    def attend_step(m):
        pl.when(m == 0)(local[6].wait)
        pq_copy(m).wait_recv()
        cos, sin = cos_t[m], sin_t[m]
        for j in range(2 * HEADS - 4):
            cols = pl.ds(j * HEAD, HEAD)
            head = pq_own[m, :, cols] + pq_recv[m, :, cols].astype(F32)
            if j <= HEADS:
                head = rotate(head, cos, sin)
            qkvs[m, :, cols] = head.astype(BF)

        @pl.loop(0, 2)
        def _(i):
            s = jnp.where(i == 0, other, f)
            at = aligned(s * SEQ, SEQ, 16)
            queries = heads_of(qkvs, m, at)
            keys = qkvs[m, at, pl.ds(HALF, HEAD)]
            values = qkvs[m, at, pl.ds(HALF + HEAD, HEAD)]
            probs = softmax_of(m, s, queries, keys).astype(BF)
            mixed = dot(probs, values).astype(BF)
            for h in range(HEADS):
                att[m, at, pl.ds(h * HEAD, HEAD)] = mixed[h * SEQ : (h + 1) * SEQ]

            @pl.loop(0, WIDTH // 512)
            def _(j):
                cols = aligned(j * 512, 512, 128)
                block = dot(att[m, at], wo[:, cols])

                @pl.when(i == 0)
                def _():
                    part_send[m, :, cols] = block.astype(BF)

                @pl.when(i == 1)
                def _():
                    hid_one[m, :, cols] = block

            pl.when(i == 0)(to_partner(0, m, part_send.at[m], part_recv.at[m]).start)

    def norm_step(m):
        to_partner(0, m, part_send.at[m], part_recv.at[m]).wait_recv()
        rows = x_own[m].astype(F32) + (hid_one[m] + part_recv[m].astype(F32))
        hid_one[m] = rows
        n2pair[m, x] = (rows * inverse_rms(rows) * gains[1:2]).astype(BF)
        n2_copy(m).start()
        spread(m, x, n2pair, dsend)
        exchange_half(0, m, dsend, n2recv, x)

    def twin_step(m):
        n2_copy(m).wait_recv()
        spread(m, away, n2pair, dsend)
        exchange_half(0, m, dsend, n2recv, away)

    def hide_step(m):
        @pl.when(m == 0)
        def _():
            for copy in local[7:9]:
                copy.wait()
            for copy in w_moe[:2]:
                copy.wait_recv()

        for source in range(2):
            received(0, m, n2recv, source)

        @pl.loop(0, HIDDEN // 256)
        def _(j):
            cols = aligned(j * 256, 256, 128)
            rows = flat(n2recv, m)
            gate = dot(rows, wg[:, cols])
            up = dot(rows, wu[:, cols])
            bend = jnp.tanh(GELU_C * (gate + GELU_A * gate * gate * gate))
            shape = (PLANE, 2, SLOTS, 256)
            gs[m, :, :, :, cols] = gate.astype(BF).reshape(shape)
            us[m, :, :, :, cols] = up.astype(BF).reshape(shape)
            mixed = (0.5 * gate * (1.0 + bend) * up).astype(BF)
            hid[m, :, :, :, cols] = mixed.reshape(shape)


    def need_down():
        local[9].wait()
        w_moe[2].wait_recv()
        for copy in w_moe:
            copy.wait_send()

    def give_step(m):
        @pl.when(jnp.logical_and(first, m == 0))
        def _():
            need_down()
            pl.semaphore_signal(go_sem, inc=1, device_id={"section": 1}, device_id_type=MESH)

        @pl.loop(0, 2)
        def _(i):
            source = jnp.where(i == 0, away, x)
            sent(0, m, dsend, source)
            rows = hid[m, :, source].reshape(PLANE * SLOTS, HIDDEN)

            @pl.loop(0, WIDTH // 512)
            def _(j):
                cols = aligned(j * 512, 512, 128)
                block = dot(rows, wd[:, cols]).astype(BF)
                dsend[m, :, source, :, cols] = block.reshape(PLANE, SLOTS, 512)

            exchange_half(1, m, dsend, yrecv, source)

    def weighed(m, source, cols):
        block = yrecv[m, :, source, :, cols].reshape(PLANE * SLOTS, 512)
        return dot_tn(cg_hi[m, source], block) + dot_tn(cg_lo[m, source], block)

    def far_step(m):
        received(1, m, yrecv, away)

        @pl.loop(0, WIDTH // 512)
        def _(j):
            cols = aligned(j * 512, 512, 128)
            far_send[0, m, :, cols] = weighed(m, away, cols).astype(BF)

        far_copy(1, m).start()
        received(1, m, yrecv, x)

        @pl.loop(0, WIDTH // 512)
        def _(j):
            cols = aligned(j * 512, 512, 128)
            part_own[m, :, cols] = hid_one[m, :, cols] + weighed(m, x, cols)

    def join_step(m):
        far_copy(1, m).wait_recv()
        acts_s[m] = (part_own[m] + far_recv[0, m].astype(F32)).astype(BF)

        @pl.when(first)
        def _():
            acts_copy(m).start()

        out_copy(3, acts_s.at[m], acts_out.at[m], m).start()

    def dy_half(m, source):
        gate = cg_hi[m, source].astype(F32) + cg_lo[m, source].astype(F32)
        spread(m, source, gpair, bsend, jnp.sum(gate, axis=1, keepdims=True))
        exchange_half(2, m, bsend, dyrecv, source)

    def grad_step(m):
        @pl.when(first)
        def _():
            wait_for(gpair.at[m, x], gr_sem.at[x, m])

        @pl.when(jnp.logical_and(second, m == 0))
        def _():
            ct_local.wait()

        dy_half(m, x)

    def grad_twin_step(m):
        wait_for(gpair.at[m, away], gr_sem.at[away, m])
        dy_half(m, away)

    def back_step(source, m):
        pl.when(jnp.logical_and(second, jnp.logical_and(m == 0, source == away)))(need_down)
        received(2, m, dyrecv, source)

        @pl.loop(0, HIDDEN // 256)
        def _(j):
            cols = aligned(j * 256, 256, 128)
            shape = (PLANE, SLOTS, 256)
            dhid = dot_nt(dyrecv[m, :, source].reshape(PLANE * SLOTS, WIDTH), wd[cols, :])
            gate = gs[m, :, source, :, cols].reshape(PLANE * SLOTS, 256).astype(F32)
            up = us[m, :, source, :, cols].reshape(PLANE * SLOTS, 256).astype(F32)
            square = gate * gate
            bend = jnp.tanh(GELU_C * (gate + GELU_A * square * gate))
            half = 0.5 * (1.0 + bend)
            slope = half + 0.5 * gate * (1.0 - bend * bend) * (
                GELU_C * (1.0 + 3.0 * GELU_A * square)
            )
            gs[m, :, source, :, cols] = (dhid * up * slope).astype(BF).reshape(shape)
            us[m, :, source, :, cols] = (dhid * (gate * half)).astype(BF).reshape(shape)

        sent(2, m, bsend, source)

        @pl.loop(0, WIDTH // 512)
        def _(j):
            cols = aligned(j * 512, 512, 128)
            dgate = gs[m, :, source].reshape(PLANE * SLOTS, HIDDEN)
            dup = us[m, :, source].reshape(PLANE * SLOTS, HIDDEN)
            block = dot_nt(dgate, wg[cols, :]) + dot_nt(dup, wu[cols, :])
            bsend[m, :, source, :, cols] = block.astype(BF).reshape(PLANE, SLOTS, 512)

        exchange_half(3, m, bsend, dn2recv, source)

    def gathered(m, source, cols):
        return dot_tn(
            sel[m, source], dn2recv[m, :, source, :, cols].reshape(PLANE * SLOTS, 512)
        )

    def far_back_step(m):
        received(3, m, dn2recv, away)


        @pl.loop(0, WIDTH // 512)
        def _(j):
            cols = aligned(j * 512, 512, 128)
            far_send[1, m, :, cols] = gathered(m, away, cols).astype(BF)

        far_copy(2, m).start()
        received(3, m, dn2recv, x)

        @pl.when(jnp.logical_and(first, m == 1))
        def _():
            pl.semaphore_signal(go_sem, inc=1, device_id={"section": 1}, device_id_type=MESH)

        @pl.loop(0, WIDTH // 512)
        def _(j):
            cols = aligned(j * 512, 512, 128)
            dh_s[m, :, cols] = gathered(m, x, cols)

    def mid_step(m):
        far_copy(2, m).wait_recv()
        rows = hid_one[m]
        inverse = inverse_rms(rows)
        grad = dh_s[m] + far_recv[1, m].astype(F32)
        gains_acc[1:2] += jnp.sum(grad * rows * inverse, axis=0, keepdims=True)
        total = gpair[m, x].astype(F32) + rms_back(rows, inverse, gains[1:2], grad)
        dh_s[m] = total
        da_pair[m, own_rows] = total.astype(BF)
        da_copy(m).start()

    def da_copy(m):
        return to_partner(1, m, da_pair.at[m, own_rows], da_pair.at[m, own_rows])

    def dqkv_copy(m):
        return to_partner(3, m, dqkv_all.at[m, f], dqkv_all.at[m, f])

    def dn1_copy(m):
        return to_partner(2, m, dn1_send.at[m], dn1_recv.at[m])

    def attend_back_step(m):
        @pl.loop(0, 2)
        def _(i):
            s = jnp.where(i == 0, f, other)

            @pl.when(i == 1)
            def _():
                da_copy(m).wait_recv()
                out_copy(6, da_pair.at[m], da_out.at[m], m).start()

            at = aligned(s * SEQ, SEQ, 16)
            dmix = dot_nt(da_pair[m, at], wo[...]).astype(BF)
            dmix = jnp.concatenate(
                [dmix[:, h * HEAD : (h + 1) * HEAD] for h in range(HEADS)], axis=0
            )
            queries = heads_of(qkvs, m, at)
            keys = qkvs[m, at, pl.ds(HALF, HEAD)]
            values = qkvs[m, at, pl.ds(HALF + HEAD, HEAD)]
            probs = softmax_of(m, s, queries, keys)
            dprobs = dot_nt(dmix, values)
            dvalues = dot_tn(probs.astype(BF), dmix)
            dscores = probs * (dprobs - jnp.sum(dprobs * probs, axis=-1, keepdims=True))
            dscores = (dscores * HEAD ** (-0.5)).astype(BF)
            cos = cos_t[m, at]
            sin = -sin_t[m, at]
            dkeys = rotate(dot_tn(dscores, queries), cos, sin)
            dqueries = dot(dscores, keys)
            for h in range(HEADS):
                part = rotate(dqueries[h * SEQ : (h + 1) * SEQ], cos, sin)
                dqkv_all[m, f, at, pl.ds(h * HEAD, HEAD)] = part.astype(BF)
            dqkv_all[m, f, at, pl.ds(HALF, HEAD)] = dkeys.astype(BF)
            dqkv_all[m, f, at, pl.ds(HALF + HEAD, HEAD)] = dvalues.astype(BF)
            part = dqkv_all.at[m, f, at]
            to_partner(3, m, part, part).start()

    def project_back_step(m):
        dqkv_copy(m).wait_recv()

        @pl.loop(0, 2)
        def _(i):
            at = aligned(jnp.where(i == 0, other, f) * SEQ, SEQ, 16)

            @pl.loop(0, HALF // 256)
            def _(j):
                cols = aligned(j * 256, 256, 128)
                block = dot_nt(dqkv_all[m, 0, at], wqkv[cols, pl.ds(0, QKV)])
                block = block + dot_nt(dqkv_all[m, 1, at], wqkv[cols, pl.ds(QKV, QKV)])

                @pl.when(i == 0)
                def _():
                    dn1_send[m, :, cols] = block.astype(BF)

                @pl.when(i == 1)
                def _():
                    part_own[m, :, aligned(f * HALF + j * 256, 256, 128)] = block

            pl.when(i == 0)(dn1_copy(m).start)

    def close_step(m):
        dn1_copy(m).wait_recv()
        part_own[m, :, other_half] = dn1_recv[m].astype(F32)
        grad = part_own[m]
        rows = x_own[m].astype(F32)
        inverse = inverse_rms(rows)
        gains_acc[0:1] += jnp.sum(grad * rows * inverse, axis=0, keepdims=True)
        ingrad_s[m] = (dh_s[m] + rms_back(rows, inverse, gains[0:1], grad)).astype(BF)

        @pl.when(second)
        def _():
            for cross in (0, 1):
                grad_copy(m, cross).start()

        out_copy(7, ingrad_s.at[m], ingrad_out.at[m], m).start()
        out_copy(8, n1p.at[m], n1_out.at[m], m).start()
        out_copy(9, dqkv_all.at[m], dqkv_out.at[m], m).start()
        out_copy(10, att.at[m], att_out.at[m], m).start()

    half_rows = HALF
    quarter_rows = HIDDEN // 2

    def expert_out(i, m):
        src, own, their = (
            (wg, own_gate_out, their_gate_out),
            (wu, own_up_out, their_up_out),
            (wd, own_down_out, their_down_out),
        )[i]
        size = src.shape[0] // 2
        part = src.at[aligned(m * size, size, 16)]
        own = pltpu.make_async_copy(part, own, out_sem.at[i, m])
        their = pltpu.make_async_copy(part, their, out_sem.at[i, m])
        return own, their

    def start_out(i, m):
        own, their = expert_out(i, m)
        pl.when(m == f)(own.start)
        pl.when(m != f)(their.start)

    def grads_in_step(j, m):
        cols = aligned(m * half_rows + j * 256, 256, 128)
        rows = n2recv[:, :, :, :, cols].reshape(MB * ROWS, 256)
        wg[cols, :] = dot_tn(rows, gs[...].reshape(MB * ROWS, HIDDEN)).astype(BF)
        wu[cols, :] = dot_tn(rows, us[...].reshape(MB * ROWS, HIDDEN)).astype(BF)
        if j == 2:
            start_out(0, m)
            start_out(1, m)

    def grads_out_step(j, m):
        cols = aligned(m * quarter_rows, quarter_rows, 128)
        at = pl.ds(j * 512, 512)
        rows = dyrecv[:, :, :, :, at].reshape(MB * ROWS, 512)
        wd[cols, at] = dot_tn(hid[:, :, :, :, cols].reshape(MB * ROWS, quarter_rows), rows).astype(BF)
        if j == 2:
            start_out(2, m)

    steps = {
        IN_A: functools.partial(grads_in_step, 0),
        IN_B: functools.partial(grads_in_step, 1),
        IN_C: functools.partial(grads_in_step, 2),
        OUT_A: functools.partial(grads_out_step, 0),
        OUT_B: functools.partial(grads_out_step, 1),
        OUT_C: functools.partial(grads_out_step, 2),
        ENTER: enter_step,
        PROJECT: project_step,
        PROJECT_BACK: project_back_step,
        ATTEND: attend_step,
        NORM: norm_step,
        TWIN: twin_step,
        HIDE: hide_step,
        GIVE: give_step,
        FAR: far_step,
        JOIN: join_step,
        GRAD: grad_step,
        GRAD_TWIN: grad_twin_step,
        BACK_NEAR: functools.partial(back_step, x),
        BACK_FAR: functools.partial(back_step, away),
        FAR_BACK: far_back_step,
        MID: mid_step,
        ATTEND_BACK: attend_back_step,
        CLOSE: close_step,
        LOAD: load_step,
    }
    length = max(len(FIRST_PLAN), len(SECOND_PLAN))
    plans = [plan + ((REST, 0, 0),) * (length - len(plan)) for plan in (FIRST_PLAN, SECOND_PLAN)]

    @pl.loop(0, length)
    def _(i):
        code = jnp.int32(REST * MB)
        for at, ((step_a, m_a, _), (step_b, m_b, _)) in enumerate(zip(*plans)):
            here = jnp.where(first, step_a * MB + m_a, step_b * MB + m_b)
            code = jnp.where(i == at, here, code)
        m = lax.rem(code, MB)
        for step, work in steps.items():
            pl.when(code // MB == step)(functools.partial(work, m))
        for mine, plan in zip((first, second), plans):
            start = 0
            for at, (_, _, count) in enumerate(plan):
                if count:
                    part = w_pieces[start : start + count]

                    @pl.when(jnp.logical_and(mine, i == at))
                    def _():
                        for copy in part:
                            copy.start()

                start += count

    pl.when(second)(lambda: pl.semaphore_wait(go_sem, 1))

    gains_out[...] = gains_acc[...]

    @pl.loop(0, MB)
    def _(m):
        for source in range(2):
            sent(1, m, dsend, source)
            sent(3, m, bsend, source)
        to_partner(0, m, part_send.at[m], part_recv.at[m]).wait_send()
        da_copy(m).wait_send()
        dn1_copy(m).wait_send()
        dqkv_copy(m).wait_send()
        n1_copy(m).wait_send()
        pq_copy(m).wait_send()
        n2_copy(m).wait_send()
        far_copy(1, m).wait_send()
        far_copy(2, m).wait_send()

        @pl.when(first)
        def _():
            acts_copy(m).wait_send()

        @pl.when(second)
        def _():
            ct_copy(m).wait_send()
            for cross in (0, 1):
                grad_copy(m, cross).wait_send()

    side_copy.wait_send()
    meta_copy.wait_send()

    @pl.loop(0, MB)
    def _(m):
        pairs = (
            (3, acts_s.at[m], acts_out.at[m]),
            (6, da_pair.at[m], da_out.at[m]),
            (7, ingrad_s.at[m], ingrad_out.at[m]),
            (8, n1p.at[m], n1_out.at[m]),
            (9, dqkv_all.at[m], dqkv_out.at[m]),
            (10, att.at[m], att_out.at[m]),
        )
        for i, src, dst in pairs:
            out_copy(i, src, dst, m).wait()
        for i in range(3):
            expert_out(i, m)[0].wait()


def run_sections(*operands):
    def out(*shape, dtype=BF):
        return jax.ShapeDtypeStruct(shape, dtype)

    vmem = pl.BlockSpec(memory_space=pltpu.VMEM)
    anywhere = pl.BlockSpec(memory_space=pl.ANY)
    dma = pltpu.SemaphoreType.DMA
    blocks = (MB, PLANE, 2, SLOTS, WIDTH)
    return pl.pallas_call(
        section_kernel,
        name="sections",
        out_shape=(
            out(MB, SEQ, WIDTH),
            out(MB, SEQ, WIDTH),
            out(8, WIDTH, dtype=F32),
            out(HALF, HIDDEN),
            out(HALF, HIDDEN),
            out(HIDDEN // 2, WIDTH),
            out(HALF, HIDDEN),
            out(HALF, HIDDEN),
            out(HIDDEN // 2, WIDTH),
            out(MB, 2 * SEQ, HALF),
            out(MB, 2, 2 * SEQ, QKV),
            out(MB, 2 * SEQ, HALF),
            out(MB, 2 * SEQ, WIDTH),
        ),
        in_specs=[anywhere] * 9 + [vmem] * 6,
        out_specs=[anywhere] * 2 + [vmem] + [anywhere] * 10,
        scratch_shapes=[
            pltpu.VMEM((HALF, 2 * QKV), BF),
            pltpu.VMEM((HALF, WIDTH), BF),
            pltpu.VMEM((WIDTH, HIDDEN), BF),
            pltpu.VMEM((WIDTH, HIDDEN), BF),
            pltpu.VMEM((HIDDEN, WIDTH), BF),
            pltpu.VMEM((MB, SEQ, WIDTH), BF),
            pltpu.VMEM((MB, 2 * SEQ, HALF), BF),
            pltpu.VMEM((MB, SEQ, HALF), BF),
            pltpu.VMEM((MB, 2 * SEQ, QKV), F32),
            pltpu.VMEM((MB, 2 * SEQ, QKV), BF),
            pltpu.VMEM((MB, 2 * SEQ, QKV), BF),
            pltpu.VMEM((MB, 2 * SEQ, QKV), BF),
            pltpu.VMEM((MB, 2 * SEQ, HALF), BF),
            pltpu.VMEM((MB, SEQ, WIDTH), F32),
            pltpu.VMEM((MB, SEQ, WIDTH), F32),
            pltpu.VMEM((MB, SEQ, WIDTH), BF),
            pltpu.VMEM((MB, SEQ, WIDTH), BF),
            pltpu.VMEM((MB, 2, PLANE * SLOTS, SEQ), BF),
            pltpu.VMEM((MB, 2, PLANE * SLOTS, SEQ), BF),
            pltpu.VMEM((MB, 2, PLANE * SLOTS, SEQ), BF),
            pltpu.VMEM((MB, 2, SEQ, WIDTH), BF),
            pltpu.VMEM((MB, 2, SEQ, WIDTH), BF),
            pltpu.VMEM(blocks, BF),
            pltpu.VMEM(blocks, BF),
            pltpu.VMEM(blocks, BF),
            pltpu.VMEM(blocks, BF),
            pltpu.VMEM(blocks, BF),
            pltpu.VMEM(blocks, BF),
            pltpu.VMEM(blocks[:-1] + (HIDDEN,), BF),
            pltpu.VMEM(blocks[:-1] + (HIDDEN,), BF),
            pltpu.VMEM(blocks[:-1] + (HIDDEN,), BF),
            pltpu.VMEM((2, MB, SEQ, WIDTH), BF),
            pltpu.VMEM((2, MB, SEQ, WIDTH), BF),
            pltpu.VMEM((MB, SEQ, WIDTH), BF),
            pltpu.VMEM((MB, SEQ, WIDTH), F32),
            pltpu.VMEM((MB, 2 * SEQ, WIDTH), BF),
            pltpu.VMEM((MB, 2, 2 * SEQ, QKV), BF),
            pltpu.VMEM((MB, SEQ, HALF), BF),
            pltpu.VMEM((MB, SEQ, HALF), BF),
            pltpu.VMEM((MB, SEQ, WIDTH), BF),
            pltpu.VMEM((8, WIDTH), F32),
            pltpu.VMEM((2, 8, HALF), F32),
            pltpu.VMEM((2, MB, 8, SEQ), F32),
            pltpu.VMEM((2, WIDTH), F32),
            pltpu.VMEM((MB, 2 * SEQ, HEAD), F32),
            pltpu.VMEM((MB, 2 * SEQ, HEAD), F32),
            pltpu.VMEM((MB, 2, SEQ, SEQ), F32),
            dma((12,)),
            dma((12,)),
            dma((10,)),
            dma((4, MB, 2)),
            dma((4, MB, 2)),
            dma((6, MB)),
            dma((6, MB)),
            dma((3, MB)),
            dma((3, MB)),
            dma((MB,)),
            dma((MB,)),
            dma((2, MB)),
            dma((2, MB)),
            dma((11, MB)),
            pltpu.SemaphoreType.REGULAR,
        ],
        compiler_params=pltpu.CompilerParams(
            collective_id=0, has_side_effects=True, vmem_limit_bytes=62 * 2**20
        ),
    )(*operands)


BAND = 192
SLICE = 48
LANES = (("z", 1024), ("y", 1024), ("z", 768), ("y", 768))


def grads_kernel(
    their_gate,
    their_up,
    their_down,
    n1_in,
    dqkv_in,
    att_in,
    da_in,
    gains_in,
    q_out,
    k_out,
    v_out,
    o_out,
    part_gate,
    part_up,
    part_down,
    gains_out,
    n1,
    dqkv,
    att,
    da,
    *rest,
):
    lane_refs, rest = [rest[i * 9 : i * 9 + 9] for i in range(len(LANES))], rest[9 * len(LANES) :]
    (
        small,
        small_recv,
        load_sem,
        send_sem,
        recv_sem,
        pair_send,
        pair_recv,
        small_send,
        small_recv_sem,
        out_sem,
    ) = rest
    f = lax.axis_index("fsdp")
    e = lax.axis_index("expert")
    y, x, z = e // 8, lax.rem(e // 4, 2), lax.rem(e, 4)
    other = 1 - f
    own_half = aligned(f * HALF, HALF, 128)
    other_half = aligned(other * HALF, HALF, 128)

    def along_y(d):
        return {"expert": lax.rem(y + d, 4) * 8 + x * 4 + z}

    def along_z(d):
        return {"expert": y * 8 + x * 4 + lax.rem(z + d, 4)}

    twin = {"expert": y * 8 + (1 - x) * 4 + z}
    partner = {"fsdp": other}

    barrier = pltpu.get_barrier_semaphore()
    neighbours = [along_y(d) for d in (1, 2, 3)] + [along_z(d) for d in (1, 2, 3)]
    neighbours += [twin, partner]
    for place in neighbours:
        pl.semaphore_signal(barrier, inc=1, device_id=place, device_id_type=MESH)

    loads = [
        (att_in, att),
        (da_in, da),
        (n1_in, n1),
        (dqkv_in, dqkv),
    ]
    loads = [pltpu.make_async_copy(a, b, load_sem.at[i]) for i, (a, b) in enumerate(loads)]
    for copy in loads:
        copy.start()

    def remote(src, dst, send, recv, place):
        return pltpu.make_async_remote_copy(
            src_ref=src,
            dst_ref=dst,
            send_sem=send,
            recv_sem=recv,
            device_id=place,
            device_id_type=MESH,
        )

    def wait_for(ref, sem):
        pltpu.make_async_copy(ref, ref, sem).wait()

    class Lane:
        def __init__(self, i):
            self.i = i
            self.v, self.far, self.merged, self.r1, self.s1, self.r2, self.s2, self.r3, self.g = (
                lane_refs[i]
            )
            axes = ((along_y, y), (along_z, z))
            (axis, at), (self.next, self.to) = axes if LANES[i][0] == "y" else axes[::-1]
            self.right, self.left = axis(1), axis(3)
            self.at = at
            half = LANES[i][1] // 2
            self.mine = aligned(x * half, half, 128)
            self.theirs = aligned((1 - x) * half, half, 128)
            self.place = aligned(at * BAND + self.to * SLICE, SLICE, 16)

        def rows(self, distance, part=None):
            start = lax.rem(self.at + distance, 4) * BAND
            if part is None:
                return aligned(start, BAND, 16)
            return aligned(start + part * (BAND // 2), BAND // 2, 16)

        def send(self, stage, src, dst, place):
            remote(
                src, dst, send_sem.at[self.i, stage], recv_sem.at[self.i, stage], place
            ).start()

        def arrived(self, stage, ref):
            wait_for(ref, recv_sem.at[self.i, stage])

        def spread(self):
            low = pl.ds(BAND // 2, BAND // 2)
            top = pl.ds(0, BAND // 2)
            self.send(0, self.v.at[self.rows(2, 0)], self.far.at[0], self.right)
            self.send(1, self.v.at[self.rows(2, 1)], self.far.at[1], self.left)
            self.send(2, self.v.at[self.rows(1, 1)], self.r1.at[0, low], self.right)
            self.send(3, self.v.at[self.rows(3, 0)], self.r1.at[1, top], self.left)

        def merge(self):
            low = pl.ds(BAND // 2, BAND // 2)
            top = pl.ds(0, BAND // 2)
            self.arrived(0, self.far.at[0])
            total = self.v[self.rows(1, 0)].astype(F32) + self.far[0].astype(F32)
            self.merged[0] = total.astype(BF)
            self.send(2, self.merged.at[0], self.r1.at[0, top], self.right)
            self.arrived(1, self.far.at[1])
            total = self.v[self.rows(3, 1)].astype(F32) + self.far[1].astype(F32)
            self.merged[1] = total.astype(BF)
            self.send(3, self.merged.at[1], self.r1.at[1, low], self.left)

        def join_one(self):
            self.arrived(2, self.r1.at[0])
            self.arrived(3, self.r1.at[1])
            total = self.v[self.rows(0)].astype(F32)
            total = total + self.r1[0].astype(F32) + self.r1[1].astype(F32)
            self.s1[...] = total.astype(BF)
            for d in (1, 2, 3):
                rows = aligned(lax.rem(self.to + d, 4) * SLICE, SLICE, 16)
                self.send(4, self.s1.at[rows], self.r2.at[self.to], self.next(d))

        def join_two(self):
            self.arrived(4, self.r2.at[pl.ds(0, 3)])
            total = self.s1[aligned(self.to * SLICE, SLICE, 16)].astype(F32)
            for d in (1, 2, 3):
                total = total + self.r2[lax.rem(self.to + d, 4)].astype(F32)
            self.s2[...] = total.astype(BF)
            self.send(5, self.s2.at[:, self.theirs], self.r3, twin)

        def join_three(self):
            self.arrived(5, self.r3)
            total = self.s2[:, self.mine].astype(F32) + self.r3[...].astype(F32)
            self.g[self.place, self.mine] = total.astype(BF)
            part = self.g.at[self.place, self.mine]
            self.send(6, part, part, twin)

        def gather_two(self):
            self.arrived(6, self.g.at[self.place, self.theirs])
            part = self.g.at[self.place]
            for d in (1, 2, 3):
                self.send(7, part, part, self.next(d))

        def gather_one(self):
            self.arrived(7, self.g.at[pl.ds(0, 3 * SLICE)])
            top, low = self.g.at[self.rows(0, 0)], self.g.at[self.rows(0, 1)]
            self.send(8, top, top, self.right)
            self.send(9, low, low, self.left)
            self.send(10, low, low, self.right)
            self.send(11, top, top, self.left)

        def pass_on(self):
            top, low = self.g.at[self.rows(3, 0)], self.g.at[self.rows(1, 1)]
            self.arrived(8, top)
            self.send(12, top, top, self.right)
            self.arrived(9, low)
            self.send(13, low, low, self.left)

        def finish(self):
            part = self.g.at[pl.ds(0, BAND // 2)]
            for stage in (10, 11, 12, 13):
                self.arrived(stage, part)

        def drain(self):
            half = self.v.at[pl.ds(0, BAND // 2)]
            band = self.v.at[pl.ds(0, BAND)]
            slices = self.v.at[pl.ds(0, 3 * SLICE)]
            sizes = [half, half, band, band, slices, self.s2.at[:, self.theirs]]
            sizes += [self.g.at[self.place, self.mine], slices] + [half] * 6
            for stage, ref in enumerate(sizes):
                wait_for(ref, send_sem.at[self.i, stage])

    out_one, query_one, out_two, query_two = lanes = [Lane(i) for i in range(len(LANES))]

    def over_micro(group, cols):
        block = jnp.concatenate([dqkv[m, group, :, cols] for m in range(MB)], axis=0)
        return dot_tn(n1[...], block).astype(BF)

    for copy in loads[:2]:
        copy.wait()
    for j in range(2):
        cols = pl.ds(j * 512, 512)
        out_one.v[:, cols] = dot_tn(att[...], da[:, cols]).astype(BF)
    pl.semaphore_wait(barrier, len(neighbours))
    out_one.spread()
    for copy in loads[2:4]:
        copy.wait()
    query_one.v[:, pl.ds(0, HALF)] = over_micro(0, pl.ds(0, HALF))
    query_one.v[:, pl.ds(HALF, 256)] = over_micro(1, pl.ds(0, 256))
    query_one.spread()
    small[...] = gains_in[...]
    small_pair = remote(
        small.at[:, other_half],
        small_recv.at[0],
        small_send.at[0],
        small_recv_sem.at[0],
        partner,
    )
    small_pair.start()
    out_two.v[:, pl.ds(0, 512)] = dot_tn(att[...], da[:, pl.ds(1024, 512)]).astype(BF)
    query_two.v[:, pl.ds(0, 512)] = over_micro(1, pl.ds(256, 512))
    for g in range(2):
        query_two.v[:, pl.ds(512 + g * HEAD, HEAD)] = over_micro(g, pl.ds(HALF, HEAD))
        out_two.v[:, pl.ds(512 + g * HEAD, HEAD)] = over_micro(g, pl.ds(HALF + HEAD, HEAD))

    pair = [
        remote(src, dst, pair_send.at[i], pair_recv.at[i], partner)
        for i, (src, dst) in enumerate(
            ((their_gate, part_gate), (their_up, part_up), (their_down, part_down))
        )
    ]
    pieces = [
        remote(src.at[rows], dst.at[rows], pair_send.at[n], pair_recv.at[n], partner)
        for n, src, dst, size in (
            (0, their_gate, part_gate, HALF // 4),
            (1, their_up, part_up, HALF // 4),
            (2, their_down, part_down, HIDDEN // 8),
        )
        for rows in [pl.ds(i * size, size) for i in range(4)]
    ]

    def send_pieces(start, stop):
        for copy in pieces[start:stop]:
            copy.start()

    def spread_small(i, axis):
        for d in (1, 2, 3):
            remote(
                small.at[:, pl.ds(0, HALF)],
                small_recv.at[1 + 3 * i + d - 1],
                small_send.at[1 + 3 * i + d - 1],
                small_recv_sem.at[1 + 3 * i + d - 1],
                axis(d),
            ).start()

    def join_small(i, axis):
        for d in (1, 2, 3):
            remote(
                small.at[:, pl.ds(0, HALF)],
                small_recv.at[1 + 3 * i + d - 1],
                small_send.at[1 + 3 * i + d - 1],
                small_recv_sem.at[1 + 3 * i + d - 1],
                axis(d),
            ).wait()
        total = small[:, pl.ds(0, HALF)]
        for d in (1, 2, 3):
            total = total + small_recv[1 + 3 * i + d - 1]
        small[:, pl.ds(0, HALF)] = total

    small_pair.wait()
    small[:, pl.ds(0, HALF)] = small[:, own_half] + small_recv[0]
    spread_small(0, along_y)

    out_two.spread()
    query_two.spread()
    send_pieces(0, 4)
    join_small(0, along_y)
    spread_small(1, along_z)
    for lane in lanes:
        lane.merge()
    for lane in lanes:
        lane.join_one()
    for lane in lanes:
        lane.join_two()
    join_small(1, along_z)
    small_twin = remote(
        small.at[:, pl.ds(0, HALF)],
        small_recv.at[7],
        small_send.at[7],
        small_recv_sem.at[7],
        twin,
    )
    small_twin.start()
    send_pieces(4, 5)
    for lane in lanes:
        lane.join_three()
    send_pieces(5, 12)
    for lane in lanes:
        lane.gather_two()
    for lane in lanes:
        lane.gather_one()
    for lane in lanes:
        lane.pass_on()
    small_twin.wait()
    gains_out[...] = small[:, pl.ds(0, HALF)] + small_recv[7]

    outs = []

    def out_copy(src, dst):
        copy = pltpu.make_async_copy(src, dst, out_sem.at[len(outs)])
        copy.start()
        outs.append(copy)

    out_one.finish()
    out_copy(out_one.g, o_out.at[:, pl.ds(0, 1024)])
    query_one.finish()
    out_copy(query_one.g, q_out.at[:, pl.ds(0, 1024)])
    out_two.finish()
    out_copy(out_two.g.at[:, pl.ds(0, 512)], o_out.at[:, pl.ds(1024, 512)])
    out_copy(out_two.g.at[:, pl.ds(512, 256)], v_out)
    query_two.finish()
    out_copy(query_two.g.at[:, pl.ds(0, 512)], q_out.at[:, pl.ds(1024, 512)])
    out_copy(query_two.g.at[:, pl.ds(512, 256)], k_out)

    for lane in lanes:
        lane.drain()
    for copy in pair:
        copy.wait()
    for copy in outs:
        copy.wait()


def reduce_grads(*operands):
    def out(*shape):
        return jax.ShapeDtypeStruct(shape, BF)

    vmem = pl.BlockSpec(memory_space=pltpu.VMEM)
    anywhere = pl.BlockSpec(memory_space=pl.ANY)
    dma = pltpu.SemaphoreType.DMA
    lanes = []
    for _, width in LANES:
        lanes += [
            pltpu.VMEM((HALF, width), BF),
            pltpu.VMEM((2, BAND // 2, width), BF),
            pltpu.VMEM((2, BAND // 2, width), BF),
            pltpu.VMEM((2, BAND, width), BF),
            pltpu.VMEM((BAND, width), BF),
            pltpu.VMEM((4, SLICE, width), BF),
            pltpu.VMEM((SLICE, width), BF),
            pltpu.VMEM((SLICE, width // 2), BF),
            pltpu.VMEM((HALF, width), BF),
        ]
    return pl.pallas_call(
        grads_kernel,
        name="grads",
        out_shape=(
            out(HALF, WIDTH),
            out(HALF, 256),
            out(HALF, 256),
            out(HALF, WIDTH),
            out(HALF, HIDDEN),
            out(HALF, HIDDEN),
            out(HIDDEN // 2, WIDTH),
            jax.ShapeDtypeStruct((8, HALF), F32),
        ),
        in_specs=[anywhere] * 7 + [vmem],
        out_specs=[anywhere] * 7 + [vmem],
        scratch_shapes=[
            pltpu.VMEM((MB * 2 * SEQ, HALF), BF),
            pltpu.VMEM((MB, 2, 2 * SEQ, QKV), BF),
            pltpu.VMEM((MB * 2 * SEQ, HALF), BF),
            pltpu.VMEM((MB * 2 * SEQ, WIDTH), BF),
        ]
        + lanes
        + [
            pltpu.VMEM((8, WIDTH), F32),
            pltpu.VMEM((8, 8, HALF), F32),
            dma((4,)),
            dma((len(LANES), 14)),
            dma((len(LANES), 14)),
            dma((3,)),
            dma((3,)),
            dma((8,)),
            dma((8,)),
            dma((9,)),
        ],
        compiler_params=pltpu.CompilerParams(
            collective_id=1, has_side_effects=True, vmem_limit_bytes=62 * 2**20
        ),
    )(*operands)


def finish_kernel(*refs):
    (q, k, v, o, own_g, own_u, own_d, part_g, part_u, part_d, acts, grads, gains), outs = (
        refs[:13],
        refs[13:],
    )
    for src, dst in zip((q, k, v, o), outs):
        dst[...] = src[...].astype(F32)
    for own, part, dst in zip((own_g, own_u, own_d), (part_g, part_u, part_d), outs[4:]):
        dst[...] = own[...].astype(F32) + part[...].astype(F32)
    outs[7][...] = acts[...]
    outs[8][...] = grads[...]
    outs[9][...] = gains[0:1]
    outs[10][...] = gains[1:2]


def finish(*blocks):
    steps = 4

    def spec(rows, cols):
        return pl.BlockSpec((rows // steps, cols), lambda i: (i, 0))

    def whole(rows, cols):
        return pl.BlockSpec((rows, cols), lambda i: (0, 0))

    gains = blocks[-1]
    split = blocks[:-1]
    results = split[:7] + split[10:]
    dtypes = [F32] * 7 + [BF] * 2
    return pl.pallas_call(
        finish_kernel,
        name="finish",
        grid=(steps,),
        out_shape=[jax.ShapeDtypeStruct(b.shape, t) for b, t in zip(results, dtypes)]
        + [jax.ShapeDtypeStruct((1, HALF), F32)] * 2,
        in_specs=[spec(*b.shape) for b in split] + [whole(*gains.shape)],
        out_specs=[spec(*b.shape) for b in results] + [whole(1, HALF)] * 2,
        compiler_params=pltpu.CompilerParams(vmem_limit_bytes=62 * 2**20),
    )(*blocks)


def local(
    inputs,
    cotangent,
    segments,
    expert_ids,
    gate_logits,
    w_query,
    key_projection,
    value_projection,
    w_out,
    gain_attn,
    gain_moe,
    w_gate,
    w_up,
    w_down,
):
    steps = np.arange(HEAD) % (HEAD // 2)
    frequency = (ROPE_BASE ** (-steps * 2.0 / HEAD)).astype(np.float32)[None]
    (
        acts,
        in_grads,
        gain_parts,
        own_gate,
        own_up,
        own_down,
        their_gate,
        their_up,
        their_down,
        n1,
        dqkv,
        att,
        da,
    ) = run_sections(
        inputs,
        cotangent,
        w_query[0],
        key_projection[0],
        value_projection[0],
        w_out[0],
        w_gate[0, 0],
        w_up[0, 0],
        w_down[0, 0],
        gain_attn,
        gain_moe,
        segments,
        jnp.swapaxes(expert_ids[0], 1, 2),
        jnp.swapaxes(gate_logits[0], 1, 2),
        jnp.asarray(frequency),
    )
    gq, gk, gv, go, part_gate, part_up, part_down, gains = reduce_grads(
        their_gate,
        their_up,
        their_down,
        n1.reshape(MB * 2 * SEQ, HALF),
        dqkv,
        att.reshape(MB * 2 * SEQ, HALF),
        da.reshape(MB * 2 * SEQ, WIDTH),
        gain_parts,
    )
    gq, gk, gv, go, grad_gate, grad_up, grad_down, acts, in_grads, gain_one, gain_two = finish(
        gq,
        gk,
        gv,
        go,
        own_gate,
        own_up,
        own_down,
        part_gate,
        part_up,
        part_down,
        acts.reshape(MB * SEQ, WIDTH),
        in_grads.reshape(MB * SEQ, WIDTH),
        gains,
    )
    return (
        acts.reshape(1, MB, SEQ, WIDTH),
        in_grads.reshape(1, MB, SEQ, WIDTH),
        gq[None],
        gk[None],
        gv[None],
        go[None],
        gain_one,
        gain_two,
        grad_gate[None, None],
        grad_up[None, None],
        grad_down[None, None],
    )


def solution(mesh):
    return jax.shard_map(
        local,
        mesh=mesh,
        in_specs=(
            P(None, ("fsdp", "expert"), None),
            P(None, ("fsdp", "expert"), None),
            P(None, ("fsdp", "expert")),
            P("section", None, ("fsdp", "expert"), None),
            P("section", None, ("fsdp", "expert"), None),
            P("section", "fsdp", None),
            P("section", "fsdp", None),
            P("section", "fsdp", None),
            P("section", "fsdp", None),
            P("section", "fsdp"),
            P("section", "fsdp"),
            P("section", "expert", "fsdp", None),
            P("section", "expert", "fsdp", None),
            P("section", "expert", "fsdp", None),
        ),
        out_specs=(
            P("section", None, ("fsdp", "expert"), None),
            P("section", None, ("fsdp", "expert"), None),
            P("section", "fsdp", None),
            P("section", "fsdp", None),
            P("section", "fsdp", None),
            P("section", "fsdp", None),
            P("section", "fsdp"),
            P("section", "fsdp"),
            P("section", "expert", "fsdp", None),
            P("section", "expert", "fsdp", None),
            P("section", "expert", "fsdp", None),
        ),
        check_vma=False,
    )
```

```python
import functools

import jax
import jax.numpy as jnp
import numpy as np
from jax import lax
from jax.experimental import pallas as pl
from jax.experimental.pallas import tpu as pltpu
from jax.sharding import PartitionSpec as P

MESH = pl.DeviceIdType.MESH
BF = jnp.bfloat16
F32 = jnp.float32

HEAD = 128
EPS = 1e-06
ROPE_BASE = 1000000.0
GELU_C = 0.7978845608
GELU_A = 0.044715

MB = 2
SEQ = 96
WIDTH = 1536
HALF = 768
EXPERTS = 32
PLANE = 16
SLOTS = 16
ROWS = EXPERTS * SLOTS
HIDDEN = 768
HEADS = 6
QKV = 1024


def dot(a, b):
    return jnp.dot(a, b, preferred_element_type=F32)


def dot_nt(a, b):
    return lax.dot_general(a, b, (((1,), (1,)), ((), ())), preferred_element_type=F32)


def dot_tn(a, b):
    return lax.dot_general(a, b, (((0,), (0,)), ((), ())), preferred_element_type=F32)


def aligned(start, size, unit):
    return pl.ds(pl.multiple_of(start, unit), size)


def inverse_rms(rows):
    return lax.rsqrt(jnp.mean(rows * rows, axis=-1, keepdims=True) + EPS)


def rms_back(rows, inverse, gain, grad):
    scaled = gain * grad
    return inverse * scaled - rows * (inverse * inverse * inverse) * jnp.mean(
        scaled * rows, axis=-1, keepdims=True
    )


def rotate(head, cos, sin):
    return head * cos + pltpu.roll(head, HEAD // 2, 1) * sin


(
    ENTER,
    PROJECT,
    ATTEND,
    NORM,
    TWIN,
    HIDE,
    GIVE,
    FAR,
    JOIN,
    GRAD,
    GRAD_TWIN,
    BACK_NEAR,
    BACK_FAR,
    FAR_BACK,
    MID,
    ATTEND_BACK,
    PROJECT_BACK,
    CLOSE,
    LOAD,
    IN_A,
    IN_B,
    IN_C,
    OUT_A,
    OUT_B,
    OUT_C,
    REST,
) = range(26)

FIRST_PLAN = (
    (ENTER, 0, 0),
    (ENTER, 1, 0),
    (PROJECT, 0, 0),
    (PROJECT, 1, 1),
    (ATTEND, 0, 1),
    (ATTEND, 1, 0),
    (NORM, 0, 1),
    (NORM, 1, 7),
    (TWIN, 0, 0),
    (TWIN, 1, 0),
    (HIDE, 0, 0),
    (HIDE, 1, 0),
    (GIVE, 0, 0),
    (GIVE, 1, 0),
    (FAR, 0, 0),
    (JOIN, 0, 0),
    (FAR, 1, 0),
    (JOIN, 1, 0),
    (GRAD, 0, 0),
    (GRAD_TWIN, 0, 0),
    (GRAD, 1, 0),
    (BACK_NEAR, 0, 0),
    (GRAD_TWIN, 1, 0),
    (BACK_FAR, 0, 0),
    (BACK_FAR, 1, 0),
    (BACK_NEAR, 1, 0),
    (FAR_BACK, 0, 0),
    (IN_A, 0, 0),
    (IN_B, 0, 0),
    (IN_C, 0, 0),
    (MID, 0, 0),
    (IN_A, 1, 0),
    (IN_B, 1, 0),
    (FAR_BACK, 1, 0),
    (ATTEND_BACK, 0, 0),
    (MID, 1, 0),
    (IN_C, 1, 0),
    (OUT_A, 0, 0),
    (PROJECT_BACK, 0, 0),
    (OUT_B, 0, 0),
    (ATTEND_BACK, 1, 0),
    (CLOSE, 0, 0),
    (OUT_C, 0, 0),
    (OUT_A, 1, 0),
    (PROJECT_BACK, 1, 0),
    (OUT_B, 1, 0),
    (OUT_C, 1, 0),
    (CLOSE, 1, 0),
)
SECOND_PLAN = (
    (GRAD, 0, 0),
    (GRAD, 1, 0),
    (LOAD, 0, 3),
    (ENTER, 0, 0),
    (PROJECT, 0, 1),
    (ENTER, 1, 0),
    (ATTEND, 0, 1),
    (PROJECT, 1, 0),
    (NORM, 0, 1),
    (ATTEND, 1, 1),
    (TWIN, 0, 0),
    (NORM, 1, 5),
    (TWIN, 1, 0),
    (GRAD_TWIN, 0, 0),
    (GRAD_TWIN, 1, 0),
    (HIDE, 0, 0),
    (HIDE, 1, 0),
    (BACK_FAR, 0, 0),
    (BACK_NEAR, 0, 0),
    (BACK_FAR, 1, 0),
    (BACK_NEAR, 1, 0),
    (GIVE, 0, 0),
    (GIVE, 1, 0),
    (FAR_BACK, 0, 0),
    (MID, 0, 0),
    (FAR_BACK, 1, 0),
    (ATTEND_BACK, 0, 0),
    (MID, 1, 0),
    (PROJECT_BACK, 0, 0),
    (ATTEND_BACK, 1, 0),
    (CLOSE, 0, 0),
    (PROJECT_BACK, 1, 0),
    (CLOSE, 1, 0),
    (IN_A, 0, 0),
    (IN_B, 0, 0),
    (IN_C, 0, 0),
    (IN_A, 1, 0),
    (IN_B, 1, 0),
    (IN_C, 1, 0),
    (OUT_A, 0, 0),
    (OUT_B, 0, 0),
    (OUT_C, 0, 0),
    (OUT_A, 1, 0),
    (OUT_B, 1, 0),
    (OUT_C, 1, 0),
    (FAR, 0, 0),
    (FAR, 1, 0),
    (JOIN, 0, 0),
    (JOIN, 1, 0),
)


def section_kernel(
    x_in,
    ct_in,
    wq_in,
    wk_in,
    wv_in,
    wo_in,
    wg_in,
    wu_in,
    wd_in,
    gain_one_in,
    gain_two_in,
    segments_in,
    ids_in,
    logits_in,
    freq_in,
    acts_out,
    ingrad_out,
    gains_out,
    own_gate_out,
    own_up_out,
    own_down_out,
    their_gate_out,
    their_up_out,
    their_down_out,
    n1_out,
    dqkv_out,
    att_out,
    da_out,
    wqkv,
    wo,
    wg,
    wu,
    wd,
    x_own,
    n1p,
    n1_send,
    pq_own,
    pq_send,
    pq_recv,
    qkvs,
    att,
    hid_one,
    part_own,
    part_send,
    part_recv,
    sel,
    cg_hi,
    cg_lo,
    n2pair,
    gpair,
    dsend,
    bsend,
    n2recv,
    yrecv,
    dyrecv,
    dn2recv,
    gs,
    us,
    hid,
    far_send,
    far_recv,
    acts_s,
    dh_s,
    da_pair,
    dqkv_all,
    dn1_send,
    dn1_recv,
    ingrad_s,
    gains_acc,
    side,
    meta,
    gains,
    cos_t,
    sin_t,
    mask_t,
    lw_sem,
    ws_sem,
    wr_sem,
    as_sem,
    ar_sem,
    ps_sem,
    pr_sem,
    ts_sem,
    tr_sem,
    xs_sem,
    xr_sem,
    gs_sem,
    gr_sem,
    out_sem,
    go_sem,
):
    sec = lax.axis_index("section")
    f = lax.axis_index("fsdp")
    e = lax.axis_index("expert")
    y, x, z = e // 8, lax.rem(e // 4, 2), lax.rem(e, 4)
    q = y * 4 + z
    away = 1 - x
    other = 1 - f
    own_rows = aligned(f * SEQ, SEQ, 16)
    own_half = aligned(f * HALF, HALF, 128)
    other_half = aligned(other * HALF, HALF, 128)
    partner = {"fsdp": other}
    twin_place = y * 8 + away * 4 + z
    twin = {"expert": twin_place}
    first, second = sec == 0, sec == 1

    def in_plane(d):
        at = lax.rem(q + d, PLANE)
        return at, {"expert": (at // 4) * 8 + x * 4 + lax.rem(at, 4)}

    barrier = pltpu.get_barrier_semaphore()

    @pl.loop(1, PLANE)
    def _(d):
        pl.semaphore_signal(barrier, inc=1, device_id=in_plane(d)[1], device_id_type=MESH)

    others = (
        twin,
        partner,
        {"section": 1 - sec},
        {"section": 1 - sec, "expert": twin_place},
    )
    for place in others:
        pl.semaphore_signal(barrier, inc=1, device_id=place, device_id_type=MESH)

    local = []
    for g in range(2):
        local += [
            (wq_in.at[:, pl.ds(g * HALF, HALF)], wqkv.at[:, pl.ds(g * QKV, HALF)]),
            (wk_in.at[:, pl.ds(g * HEAD, HEAD)], wqkv.at[:, pl.ds(g * QKV + HALF, HEAD)]),
            (wv_in.at[:, pl.ds(g * HEAD, HEAD)], wqkv.at[:, pl.ds(g * QKV + HALF + HEAD, HEAD)]),
        ]
    local += [
        (wo_in, wo),
        (wg_in, wg.at[own_half]),
        (wu_in, wu.at[own_half]),
        (wd_in, wd.at[aligned(f * (HIDDEN // 2), HIDDEN // 2, 16)]),
    ]
    local = [pltpu.make_async_copy(a, b, lw_sem.at[i]) for i, (a, b) in enumerate(local)]
    for copy in local:
        copy.start()
    x_local = pltpu.make_async_copy(x_in, x_own, lw_sem.at[10])
    ct_local = pltpu.make_async_copy(ct_in, gpair.at[:, x], lw_sem.at[11])
    pl.when(first)(x_local.start)
    pl.when(second)(ct_local.start)

    def remote(src, dst, send, recv, place):
        return pltpu.make_async_remote_copy(
            src_ref=src,
            dst_ref=dst,
            send_sem=send,
            recv_sem=recv,
            device_id=place,
            device_id_type=MESH,
        )

    def wait_for(ref, sem):
        pltpu.make_async_copy(ref, ref, sem).wait()

    def weight(src, dst, i):
        return remote(src, dst, ws_sem.at[i], wr_sem.at[i], partner)

    w_moe = [
        weight(wg_in, wg.at[own_half], 3),
        weight(wu_in, wu.at[own_half], 4),
        weight(wd_in, wd.at[aligned(f * (HIDDEN // 2), HIDDEN // 2, 16)], 5),
    ]

    w_pieces = [
        weight(src.at[aligned(i * size, size, 16)], dst.at[aligned(f * 4 * size + i * size, size, 16)], n)
        for n, src, dst, size in (
            (3, wg_in, wg, HALF // 4),
            (4, wu_in, wu, HALF // 4),
            (5, wd_in, wd, HIDDEN // 8),
        )
        for i in range(4)
    ]

    def ct_copy(m):
        return remote(ct_in.at[m], gpair.at[m, x], ws_sem.at[10 + m], gr_sem.at[x, m], twin)

    side[f, 0:1] = gain_one_in[...].astype(F32)
    side[f, 1:2] = gain_two_in[...].astype(F32)
    side[f, 2:4, :SEQ] = segments_in[...].astype(F32)
    for m in range(MB):
        meta[x, m, 0:4] = ids_in[m].astype(F32)
        meta[x, m, 4:8] = logits_in[m]
    row = lax.broadcasted_iota(jnp.int32, (SEQ, SEQ), 0)
    col = lax.broadcasted_iota(jnp.int32, (SEQ, SEQ), 1)
    unit = jnp.where(row == col, 1.0, 0.0).astype(BF)
    side_copy = weight(side.at[f], side.at[f], 8)
    meta_copy = remote(meta.at[x], meta.at[x], ws_sem.at[9], wr_sem.at[9], twin)
    gains_acc[...] = jnp.zeros_like(gains_acc)

    pl.semaphore_wait(barrier, PLANE - 1 + len(others))
    side_copy.start()
    meta_copy.start()

    @pl.when(first)
    def _():
        for copy in w_pieces[:2]:
            copy.start()

    meta_copy.wait_recv()
    earlier = jnp.where(row < col, 1.0, 0.0).astype(BF)

    @pl.loop(0, 2 * MB)
    def _(i):
        m, source = lax.rem(i, MB), i // MB
        rows = meta[source, m]
        ids, logits = rows[:4], rows[4:]
        raised = jnp.exp(logits - jnp.max(logits, axis=0, keepdims=True))
        gates = raised / jnp.sum(raised, axis=0, keepdims=True)
        place = lax.broadcasted_iota(jnp.int32, (PLANE, SEQ), 0)
        expert = ((place // 4) * 8 + x * 4 + lax.rem(place, 4)).astype(F32)
        named = jnp.zeros((PLANE, SEQ), F32)
        weights = jnp.zeros((PLANE, SEQ), F32)
        for k in range(4):
            hit = expert == ids[k : k + 1, :]
            named = jnp.where(hit, 1.0, named)
            weights = jnp.where(hit, gates[k : k + 1, :], weights)
        slot = dot(named.astype(BF), earlier)
        slot = jnp.where(named > 0.0, slot, -1.0)
        shape = (PLANE, SLOTS, SEQ)
        count = lax.broadcasted_iota(jnp.int32, shape, 1).astype(F32)
        chosen = jnp.where(jnp.broadcast_to(slot[:, None, :], shape) == count, 1.0, 0.0)
        scaled = chosen * jnp.broadcast_to(weights[:, None, :], shape)
        scaled = scaled.reshape(PLANE * SLOTS, SEQ)
        high = scaled.astype(BF)
        sel[m, source] = chosen.reshape(PLANE * SLOTS, SEQ).astype(BF)
        cg_hi[m, source] = high
        cg_lo[m, source] = (scaled - high.astype(F32)).astype(BF)

    side_copy.wait_recv()
    gains[:, pl.ds(0, HALF)] = side[0, 0:2]
    gains[:, pl.ds(HALF, HALF)] = side[1, 0:2]
    lane = lax.broadcasted_iota(jnp.int32, (SEQ, HEAD), 1)
    turn = jnp.where(lane < HEAD // 2, -1.0, 1.0)
    for m in range(MB):
        for s in range(2):
            across = jnp.broadcast_to(side[s, 2 + m : 3 + m, :SEQ], (SEQ, SEQ))
            down = dot_nt(unit, across.astype(BF))
            same = jnp.where(down == across, 1.0, 0.0)
            mask_t[m, s] = jnp.where(col <= row, same, 0.0)
            places = jnp.sum(jnp.where(col < row, same, 0.0), axis=1, keepdims=True)
            angles = places * freq_in[...]
            cos_t[m, pl.ds(s * SEQ, SEQ)] = jnp.cos(angles)
            sin_t[m, pl.ds(s * SEQ, SEQ)] = jnp.sin(angles) * turn

    def exchange_half(kind, m, src, dst, source):
        @pl.loop(1, PLANE)
        def _(d):
            at, place = in_plane(d)
            remote(
                src.at[m, at, source],
                dst.at[m, q, source],
                as_sem.at[kind, m, source],
                ar_sem.at[kind, m, source],
                place,
            ).start()

        dst[m, q, source] = src[m, q, source]

    def received(kind, m, dst, source):
        wait_for(dst.at[m, pl.ds(0, PLANE - 1), source], ar_sem.at[kind, m, source])

    def sent(kind, m, src, source):
        wait_for(src.at[m, pl.ds(0, PLANE - 1), source], as_sem.at[kind, m, source])

    def to_partner(kind, m, src, dst):
        return remote(src, dst, ps_sem.at[kind, m], pr_sem.at[kind, m], partner)

    def to_twin(kind, m, src, dst):
        return remote(src, dst, ts_sem.at[kind, m], tr_sem.at[kind, m], twin)

    def n2_copy(m):
        return to_twin(0, m, n2pair.at[m, x], n2pair.at[m, x])

    def far_copy(kind, m):
        return to_twin(kind, m, far_send.at[kind - 1, m], far_recv.at[kind - 1, m])

    def acts_copy(m):
        return remote(acts_s.at[m], x_own.at[m], xs_sem.at[m], xr_sem.at[m], {"section": 1})

    def n1_copy(m):
        return to_partner(4, m, n1_send.at[m], n1p.at[m, own_rows])

    def pq_copy(m):
        return to_partner(5, m, pq_send.at[m], pq_recv.at[m])

    def grad_copy(m, cross):
        place = {"section": 0, "expert": twin_place} if cross else {"section": 0}
        return remote(
            ingrad_s.at[m], gpair.at[m, x], gs_sem.at[cross, m], gr_sem.at[x, m], place
        )

    def out_copy(i, src, dst, m):
        return pltpu.make_async_copy(src, dst, out_sem.at[i, m])

    def flat(ref, m):
        return ref[m].reshape(ROWS, WIDTH)

    def spread(m, source, rows, dst, scale=None):
        @pl.loop(0, WIDTH // 512)
        def _(j):
            cols = aligned(j * 512, 512, 128)
            block = dot(sel[m, source], rows[m, source, :, cols])
            if scale is not None:
                block = block * scale
            dst[m, :, source, :, cols] = block.astype(BF).reshape(PLANE, SLOTS, 512)

    def load_step(m):
        pl.semaphore_wait(go_sem, 1)
        ct_copy(0).start()
        ct_copy(1).start()

    def heads_of(ref, m, rows):
        return jnp.concatenate(
            [ref[m, rows, pl.ds(h * HEAD, HEAD)] for h in range(HEADS)], axis=0
        )

    def softmax_of(m, s, queries, keys):
        scores = dot_nt(queries, keys) * HEAD ** (-0.5)
        allowed = jnp.concatenate([mask_t[m, s]] * HEADS, axis=0)
        scores = jnp.where(allowed > 0.0, scores, -1e30)
        raised = jnp.exp(scores - jnp.max(scores, axis=-1, keepdims=True))
        return raised / jnp.sum(raised, axis=-1, keepdims=True)

    def enter_step(m):
        pl.when(jnp.logical_and(first, m == 0))(x_local.wait)
        pl.when(second)(lambda: wait_for(x_own.at[m], xr_sem.at[m]))
        rows = x_own[m].astype(F32)
        scale = inverse_rms(rows)
        n1p[m, own_rows] = (x_own[m, :, own_half].astype(F32) * scale * gains[0:1, own_half]).astype(BF)
        n1_send[m] = (
            x_own[m, :, other_half].astype(F32) * scale * gains[0:1, other_half]
        ).astype(BF)
        n1_copy(m).start()

    def project_step(m):
        @pl.when(m == 0)
        def _():
            for copy in local[:6]:
                copy.wait()

        n1_copy(m).wait_recv()

        @pl.loop(0, QKV // 512)
        def _(j):
            cols = aligned(j * 512, 512, 128)
            from_w = aligned(other * QKV + j * 512, 512, 128)
            pq_send[m, :, cols] = dot(n1p[m], wqkv[:, from_w]).astype(BF)

        pq_copy(m).start()

        @pl.loop(0, QKV // 512)
        def _(j):
            cols = aligned(j * 512, 512, 128)
            from_w = aligned(f * QKV + j * 512, 512, 128)
            pq_own[m, :, cols] = dot(n1p[m], wqkv[:, from_w])

    def attend_step(m):
        pl.when(m == 0)(local[6].wait)
        pq_copy(m).wait_recv()
        cos, sin = cos_t[m], sin_t[m]
        for j in range(2 * HEADS - 4):
            cols = pl.ds(j * HEAD, HEAD)
            head = pq_own[m, :, cols] + pq_recv[m, :, cols].astype(F32)
            if j <= HEADS:
                head = rotate(head, cos, sin)
            qkvs[m, :, cols] = head.astype(BF)

        @pl.loop(0, 2)
        def _(i):
            s = jnp.where(i == 0, other, f)
            at = aligned(s * SEQ, SEQ, 16)
            queries = heads_of(qkvs, m, at)
            keys = qkvs[m, at, pl.ds(HALF, HEAD)]
            values = qkvs[m, at, pl.ds(HALF + HEAD, HEAD)]
            probs = softmax_of(m, s, queries, keys).astype(BF)
            mixed = dot(probs, values).astype(BF)
            for h in range(HEADS):
                att[m, at, pl.ds(h * HEAD, HEAD)] = mixed[h * SEQ : (h + 1) * SEQ]

            @pl.loop(0, WIDTH // 512)
            def _(j):
                cols = aligned(j * 512, 512, 128)
                block = dot(att[m, at], wo[:, cols])

                @pl.when(i == 0)
                def _():
                    part_send[m, :, cols] = block.astype(BF)

                @pl.when(i == 1)
                def _():
                    hid_one[m, :, cols] = block

            pl.when(i == 0)(to_partner(0, m, part_send.at[m], part_recv.at[m]).start)

    def norm_step(m):
        to_partner(0, m, part_send.at[m], part_recv.at[m]).wait_recv()
        rows = x_own[m].astype(F32) + (hid_one[m] + part_recv[m].astype(F32))
        hid_one[m] = rows
        n2pair[m, x] = (rows * inverse_rms(rows) * gains[1:2]).astype(BF)
        n2_copy(m).start()
        spread(m, x, n2pair, dsend)
        exchange_half(0, m, dsend, n2recv, x)

    def twin_step(m):
        n2_copy(m).wait_recv()
        spread(m, away, n2pair, dsend)
        exchange_half(0, m, dsend, n2recv, away)

    def hide_step(m):
        @pl.when(m == 0)
        def _():
            for copy in local[7:9]:
                copy.wait()
            for copy in w_moe[:2]:
                copy.wait_recv()

        for source in range(2):
            received(0, m, n2recv, source)

        @pl.loop(0, HIDDEN // 256)
        def _(j):
            cols = aligned(j * 256, 256, 128)
            rows = flat(n2recv, m)
            gate = dot(rows, wg[:, cols])
            up = dot(rows, wu[:, cols])
            bend = jnp.tanh(GELU_C * (gate + GELU_A * gate * gate * gate))
            shape = (PLANE, 2, SLOTS, 256)
            gs[m, :, :, :, cols] = gate.astype(BF).reshape(shape)
            us[m, :, :, :, cols] = up.astype(BF).reshape(shape)
            mixed = (0.5 * gate * (1.0 + bend) * up).astype(BF)
            hid[m, :, :, :, cols] = mixed.reshape(shape)


    def need_down():
        local[9].wait()
        w_moe[2].wait_recv()
        for copy in w_moe:
            copy.wait_send()

    def give_step(m):
        @pl.when(jnp.logical_and(first, m == 0))
        def _():
            need_down()
            pl.semaphore_signal(go_sem, inc=1, device_id={"section": 1}, device_id_type=MESH)

        @pl.loop(0, 2)
        def _(i):
            source = jnp.where(i == 0, away, x)
            sent(0, m, dsend, source)
            rows = hid[m, :, source].reshape(PLANE * SLOTS, HIDDEN)

            @pl.loop(0, WIDTH // 512)
            def _(j):
                cols = aligned(j * 512, 512, 128)
                block = dot(rows, wd[:, cols]).astype(BF)
                dsend[m, :, source, :, cols] = block.reshape(PLANE, SLOTS, 512)

            exchange_half(1, m, dsend, yrecv, source)

    def weighed(m, source, cols):
        block = yrecv[m, :, source, :, cols].reshape(PLANE * SLOTS, 512)
        return dot_tn(cg_hi[m, source], block) + dot_tn(cg_lo[m, source], block)

    def far_step(m):
        received(1, m, yrecv, away)

        @pl.loop(0, WIDTH // 512)
        def _(j):
            cols = aligned(j * 512, 512, 128)
            far_send[0, m, :, cols] = weighed(m, away, cols).astype(BF)

        far_copy(1, m).start()
        received(1, m, yrecv, x)

        @pl.loop(0, WIDTH // 512)
        def _(j):
            cols = aligned(j * 512, 512, 128)
            part_own[m, :, cols] = hid_one[m, :, cols] + weighed(m, x, cols)

    def join_step(m):
        far_copy(1, m).wait_recv()
        acts_s[m] = (part_own[m] + far_recv[0, m].astype(F32)).astype(BF)

        @pl.when(first)
        def _():
            acts_copy(m).start()

        out_copy(3, acts_s.at[m], acts_out.at[m], m).start()

    def dy_half(m, source):
        gate = cg_hi[m, source].astype(F32) + cg_lo[m, source].astype(F32)
        spread(m, source, gpair, bsend, jnp.sum(gate, axis=1, keepdims=True))
        exchange_half(2, m, bsend, dyrecv, source)

    def grad_step(m):
        @pl.when(first)
        def _():
            wait_for(gpair.at[m, x], gr_sem.at[x, m])

        @pl.when(jnp.logical_and(second, m == 0))
        def _():
            ct_local.wait()

        dy_half(m, x)

    def grad_twin_step(m):
        wait_for(gpair.at[m, away], gr_sem.at[away, m])
        dy_half(m, away)

    def back_step(source, m):
        pl.when(jnp.logical_and(second, jnp.logical_and(m == 0, source == away)))(need_down)
        received(2, m, dyrecv, source)

        @pl.loop(0, HIDDEN // 256)
        def _(j):
            cols = aligned(j * 256, 256, 128)
            shape = (PLANE, SLOTS, 256)
            dhid = dot_nt(dyrecv[m, :, source].reshape(PLANE * SLOTS, WIDTH), wd[cols, :])
            gate = gs[m, :, source, :, cols].reshape(PLANE * SLOTS, 256).astype(F32)
            up = us[m, :, source, :, cols].reshape(PLANE * SLOTS, 256).astype(F32)
            square = gate * gate
            bend = jnp.tanh(GELU_C * (gate + GELU_A * square * gate))
            half = 0.5 * (1.0 + bend)
            slope = half + 0.5 * gate * (1.0 - bend * bend) * (
                GELU_C * (1.0 + 3.0 * GELU_A * square)
            )
            gs[m, :, source, :, cols] = (dhid * up * slope).astype(BF).reshape(shape)
            us[m, :, source, :, cols] = (dhid * (gate * half)).astype(BF).reshape(shape)

        sent(2, m, bsend, source)

        @pl.loop(0, WIDTH // 512)
        def _(j):
            cols = aligned(j * 512, 512, 128)
            dgate = gs[m, :, source].reshape(PLANE * SLOTS, HIDDEN)
            dup = us[m, :, source].reshape(PLANE * SLOTS, HIDDEN)
            block = dot_nt(dgate, wg[cols, :]) + dot_nt(dup, wu[cols, :])
            bsend[m, :, source, :, cols] = block.astype(BF).reshape(PLANE, SLOTS, 512)

        exchange_half(3, m, bsend, dn2recv, source)

    def gathered(m, source, cols):
        return dot_tn(
            sel[m, source], dn2recv[m, :, source, :, cols].reshape(PLANE * SLOTS, 512)
        )

    def far_back_step(m):
        received(3, m, dn2recv, away)


        @pl.loop(0, WIDTH // 512)
        def _(j):
            cols = aligned(j * 512, 512, 128)
            far_send[1, m, :, cols] = gathered(m, away, cols).astype(BF)

        far_copy(2, m).start()
        received(3, m, dn2recv, x)

        @pl.when(jnp.logical_and(first, m == 1))
        def _():
            pl.semaphore_signal(go_sem, inc=1, device_id={"section": 1}, device_id_type=MESH)

        @pl.loop(0, WIDTH // 512)
        def _(j):
            cols = aligned(j * 512, 512, 128)
            dh_s[m, :, cols] = gathered(m, x, cols)

    def mid_step(m):
        far_copy(2, m).wait_recv()
        rows = hid_one[m]
        inverse = inverse_rms(rows)
        grad = dh_s[m] + far_recv[1, m].astype(F32)
        gains_acc[1:2] += jnp.sum(grad * rows * inverse, axis=0, keepdims=True)
        total = gpair[m, x].astype(F32) + rms_back(rows, inverse, gains[1:2], grad)
        dh_s[m] = total
        da_pair[m, own_rows] = total.astype(BF)
        da_copy(m).start()

    def da_copy(m):
        return to_partner(1, m, da_pair.at[m, own_rows], da_pair.at[m, own_rows])

    def dqkv_copy(m):
        return to_partner(3, m, dqkv_all.at[m, f], dqkv_all.at[m, f])

    def dn1_copy(m):
        return to_partner(2, m, dn1_send.at[m], dn1_recv.at[m])

    def attend_back_step(m):
        @pl.loop(0, 2)
        def _(i):
            s = jnp.where(i == 0, f, other)

            @pl.when(i == 1)
            def _():
                da_copy(m).wait_recv()
                out_copy(6, da_pair.at[m], da_out.at[m], m).start()

            at = aligned(s * SEQ, SEQ, 16)
            dmix = dot_nt(da_pair[m, at], wo[...]).astype(BF)
            dmix = jnp.concatenate(
                [dmix[:, h * HEAD : (h + 1) * HEAD] for h in range(HEADS)], axis=0
            )
            queries = heads_of(qkvs, m, at)
            keys = qkvs[m, at, pl.ds(HALF, HEAD)]
            values = qkvs[m, at, pl.ds(HALF + HEAD, HEAD)]
            probs = softmax_of(m, s, queries, keys)
            dprobs = dot_nt(dmix, values)
            dvalues = dot_tn(probs.astype(BF), dmix)
            dscores = probs * (dprobs - jnp.sum(dprobs * probs, axis=-1, keepdims=True))
            dscores = (dscores * HEAD ** (-0.5)).astype(BF)
            cos = cos_t[m, at]
            sin = -sin_t[m, at]
            dkeys = rotate(dot_tn(dscores, queries), cos, sin)
            dqueries = dot(dscores, keys)
            for h in range(HEADS):
                part = rotate(dqueries[h * SEQ : (h + 1) * SEQ], cos, sin)
                dqkv_all[m, f, at, pl.ds(h * HEAD, HEAD)] = part.astype(BF)
            dqkv_all[m, f, at, pl.ds(HALF, HEAD)] = dkeys.astype(BF)
            dqkv_all[m, f, at, pl.ds(HALF + HEAD, HEAD)] = dvalues.astype(BF)
            part = dqkv_all.at[m, f, at]
            to_partner(3, m, part, part).start()

    def project_back_step(m):
        dqkv_copy(m).wait_recv()

        @pl.loop(0, 2)
        def _(i):
            at = aligned(jnp.where(i == 0, other, f) * SEQ, SEQ, 16)

            @pl.loop(0, HALF // 256)
            def _(j):
                cols = aligned(j * 256, 256, 128)
                block = dot_nt(dqkv_all[m, 0, at], wqkv[cols, pl.ds(0, QKV)])
                block = block + dot_nt(dqkv_all[m, 1, at], wqkv[cols, pl.ds(QKV, QKV)])

                @pl.when(i == 0)
                def _():
                    dn1_send[m, :, cols] = block.astype(BF)

                @pl.when(i == 1)
                def _():
                    part_own[m, :, aligned(f * HALF + j * 256, 256, 128)] = block

            pl.when(i == 0)(dn1_copy(m).start)

    def close_step(m):
        dn1_copy(m).wait_recv()
        part_own[m, :, other_half] = dn1_recv[m].astype(F32)
        grad = part_own[m]
        rows = x_own[m].astype(F32)
        inverse = inverse_rms(rows)
        gains_acc[0:1] += jnp.sum(grad * rows * inverse, axis=0, keepdims=True)
        ingrad_s[m] = (dh_s[m] + rms_back(rows, inverse, gains[0:1], grad)).astype(BF)

        @pl.when(second)
        def _():
            for cross in (0, 1):
                grad_copy(m, cross).start()

        out_copy(7, ingrad_s.at[m], ingrad_out.at[m], m).start()
        out_copy(8, n1p.at[m], n1_out.at[m], m).start()
        out_copy(9, dqkv_all.at[m], dqkv_out.at[m], m).start()
        out_copy(10, att.at[m], att_out.at[m], m).start()

    half_rows = HALF
    quarter_rows = HIDDEN // 2

    def expert_out(i, m):
        src, own, their = (
            (wg, own_gate_out, their_gate_out),
            (wu, own_up_out, their_up_out),
            (wd, own_down_out, their_down_out),
        )[i]
        size = src.shape[0] // 2
        part = src.at[aligned(m * size, size, 16)]
        own = pltpu.make_async_copy(part, own, out_sem.at[i, m])
        their = pltpu.make_async_copy(part, their, out_sem.at[i, m])
        return own, their

    def start_out(i, m):
        own, their = expert_out(i, m)
        pl.when(m == f)(own.start)
        pl.when(m != f)(their.start)

    def grads_in_step(j, m):
        cols = aligned(m * half_rows + j * 256, 256, 128)
        rows = n2recv[:, :, :, :, cols].reshape(MB * ROWS, 256)
        wg[cols, :] = dot_tn(rows, gs[...].reshape(MB * ROWS, HIDDEN)).astype(BF)
        wu[cols, :] = dot_tn(rows, us[...].reshape(MB * ROWS, HIDDEN)).astype(BF)
        if j == 2:
            start_out(0, m)
            start_out(1, m)

    def grads_out_step(j, m):
        cols = aligned(m * quarter_rows, quarter_rows, 128)
        at = pl.ds(j * 512, 512)
        rows = dyrecv[:, :, :, :, at].reshape(MB * ROWS, 512)
        wd[cols, at] = dot_tn(hid[:, :, :, :, cols].reshape(MB * ROWS, quarter_rows), rows).astype(BF)
        if j == 2:
            start_out(2, m)

    steps = {
        IN_A: functools.partial(grads_in_step, 0),
        IN_B: functools.partial(grads_in_step, 1),
        IN_C: functools.partial(grads_in_step, 2),
        OUT_A: functools.partial(grads_out_step, 0),
        OUT_B: functools.partial(grads_out_step, 1),
        OUT_C: functools.partial(grads_out_step, 2),
        ENTER: enter_step,
        PROJECT: project_step,
        PROJECT_BACK: project_back_step,
        ATTEND: attend_step,
        NORM: norm_step,
        TWIN: twin_step,
        HIDE: hide_step,
        GIVE: give_step,
        FAR: far_step,
        JOIN: join_step,
        GRAD: grad_step,
        GRAD_TWIN: grad_twin_step,
        BACK_NEAR: functools.partial(back_step, x),
        BACK_FAR: functools.partial(back_step, away),
        FAR_BACK: far_back_step,
        MID: mid_step,
        ATTEND_BACK: attend_back_step,
        CLOSE: close_step,
        LOAD: load_step,
    }
    length = max(len(FIRST_PLAN), len(SECOND_PLAN))
    plans = [plan + ((REST, 0, 0),) * (length - len(plan)) for plan in (FIRST_PLAN, SECOND_PLAN)]

    @pl.loop(0, length)
    def _(i):
        code = jnp.int32(REST * MB)
        for at, ((step_a, m_a, _), (step_b, m_b, _)) in enumerate(zip(*plans)):
            here = jnp.where(first, step_a * MB + m_a, step_b * MB + m_b)
            code = jnp.where(i == at, here, code)
        m = lax.rem(code, MB)
        for step, work in steps.items():
            pl.when(code // MB == step)(functools.partial(work, m))
        for mine, plan, start in ((first, plans[0], 2), (second, plans[1], 0)):
            for at, (_, _, count) in enumerate(plan):
                if count:
                    part = w_pieces[start : start + count]

                    @pl.when(jnp.logical_and(mine, i == at))
                    def _():
                        for copy in part:
                            copy.start()

                start += count

    pl.when(second)(lambda: pl.semaphore_wait(go_sem, 1))

    gains_out[...] = gains_acc[...]

    @pl.loop(0, MB)
    def _(m):
        for source in range(2):
            sent(1, m, dsend, source)
            sent(3, m, bsend, source)
        to_partner(0, m, part_send.at[m], part_recv.at[m]).wait_send()
        da_copy(m).wait_send()
        dn1_copy(m).wait_send()
        dqkv_copy(m).wait_send()
        n1_copy(m).wait_send()
        pq_copy(m).wait_send()
        n2_copy(m).wait_send()
        far_copy(1, m).wait_send()
        far_copy(2, m).wait_send()

        @pl.when(first)
        def _():
            acts_copy(m).wait_send()

        @pl.when(second)
        def _():
            ct_copy(m).wait_send()
            for cross in (0, 1):
                grad_copy(m, cross).wait_send()

    side_copy.wait_send()
    meta_copy.wait_send()

    @pl.loop(0, MB)
    def _(m):
        pairs = (
            (3, acts_s.at[m], acts_out.at[m]),
            (6, da_pair.at[m], da_out.at[m]),
            (7, ingrad_s.at[m], ingrad_out.at[m]),
            (8, n1p.at[m], n1_out.at[m]),
            (9, dqkv_all.at[m], dqkv_out.at[m]),
            (10, att.at[m], att_out.at[m]),
        )
        for i, src, dst in pairs:
            out_copy(i, src, dst, m).wait()
        for i in range(3):
            expert_out(i, m)[0].wait()


def run_sections(*operands):
    def out(*shape, dtype=BF):
        return jax.ShapeDtypeStruct(shape, dtype)

    vmem = pl.BlockSpec(memory_space=pltpu.VMEM)
    anywhere = pl.BlockSpec(memory_space=pl.ANY)
    dma = pltpu.SemaphoreType.DMA
    blocks = (MB, PLANE, 2, SLOTS, WIDTH)
    return pl.pallas_call(
        section_kernel,
        name="sections",
        out_shape=(
            out(MB, SEQ, WIDTH),
            out(MB, SEQ, WIDTH),
            out(8, WIDTH, dtype=F32),
            out(HALF, HIDDEN),
            out(HALF, HIDDEN),
            out(HIDDEN // 2, WIDTH),
            out(HALF, HIDDEN),
            out(HALF, HIDDEN),
            out(HIDDEN // 2, WIDTH),
            out(MB, 2 * SEQ, HALF),
            out(MB, 2, 2 * SEQ, QKV),
            out(MB, 2 * SEQ, HALF),
            out(MB, 2 * SEQ, WIDTH),
        ),
        in_specs=[anywhere] * 9 + [vmem] * 6,
        out_specs=[anywhere] * 2 + [vmem] + [anywhere] * 10,
        scratch_shapes=[
            pltpu.VMEM((HALF, 2 * QKV), BF),
            pltpu.VMEM((HALF, WIDTH), BF),
            pltpu.VMEM((WIDTH, HIDDEN), BF),
            pltpu.VMEM((WIDTH, HIDDEN), BF),
            pltpu.VMEM((HIDDEN, WIDTH), BF),
            pltpu.VMEM((MB, SEQ, WIDTH), BF),
            pltpu.VMEM((MB, 2 * SEQ, HALF), BF),
            pltpu.VMEM((MB, SEQ, HALF), BF),
            pltpu.VMEM((MB, 2 * SEQ, QKV), F32),
            pltpu.VMEM((MB, 2 * SEQ, QKV), BF),
            pltpu.VMEM((MB, 2 * SEQ, QKV), BF),
            pltpu.VMEM((MB, 2 * SEQ, QKV), BF),
            pltpu.VMEM((MB, 2 * SEQ, HALF), BF),
            pltpu.VMEM((MB, SEQ, WIDTH), F32),
            pltpu.VMEM((MB, SEQ, WIDTH), F32),
            pltpu.VMEM((MB, SEQ, WIDTH), BF),
            pltpu.VMEM((MB, SEQ, WIDTH), BF),
            pltpu.VMEM((MB, 2, PLANE * SLOTS, SEQ), BF),
            pltpu.VMEM((MB, 2, PLANE * SLOTS, SEQ), BF),
            pltpu.VMEM((MB, 2, PLANE * SLOTS, SEQ), BF),
            pltpu.VMEM((MB, 2, SEQ, WIDTH), BF),
            pltpu.VMEM((MB, 2, SEQ, WIDTH), BF),
            pltpu.VMEM(blocks, BF),
            pltpu.VMEM(blocks, BF),
            pltpu.VMEM(blocks, BF),
            pltpu.VMEM(blocks, BF),
            pltpu.VMEM(blocks, BF),
            pltpu.VMEM(blocks, BF),
            pltpu.VMEM(blocks[:-1] + (HIDDEN,), BF),
            pltpu.VMEM(blocks[:-1] + (HIDDEN,), BF),
            pltpu.VMEM(blocks[:-1] + (HIDDEN,), BF),
            pltpu.VMEM((2, MB, SEQ, WIDTH), BF),
            pltpu.VMEM((2, MB, SEQ, WIDTH), BF),
            pltpu.VMEM((MB, SEQ, WIDTH), BF),
            pltpu.VMEM((MB, SEQ, WIDTH), F32),
            pltpu.VMEM((MB, 2 * SEQ, WIDTH), BF),
            pltpu.VMEM((MB, 2, 2 * SEQ, QKV), BF),
            pltpu.VMEM((MB, SEQ, HALF), BF),
            pltpu.VMEM((MB, SEQ, HALF), BF),
            pltpu.VMEM((MB, SEQ, WIDTH), BF),
            pltpu.VMEM((8, WIDTH), F32),
            pltpu.VMEM((2, 8, HALF), F32),
            pltpu.VMEM((2, MB, 8, SEQ), F32),
            pltpu.VMEM((2, WIDTH), F32),
            pltpu.VMEM((MB, 2 * SEQ, HEAD), F32),
            pltpu.VMEM((MB, 2 * SEQ, HEAD), F32),
            pltpu.VMEM((MB, 2, SEQ, SEQ), F32),
            dma((12,)),
            dma((12,)),
            dma((10,)),
            dma((4, MB, 2)),
            dma((4, MB, 2)),
            dma((6, MB)),
            dma((6, MB)),
            dma((3, MB)),
            dma((3, MB)),
            dma((MB,)),
            dma((MB,)),
            dma((2, MB)),
            dma((2, MB)),
            dma((11, MB)),
            pltpu.SemaphoreType.REGULAR,
        ],
        compiler_params=pltpu.CompilerParams(
            collective_id=0, has_side_effects=True, vmem_limit_bytes=62 * 2**20
        ),
    )(*operands)


BAND = 192
SLICE = 48
LANES = (("z", 1024), ("y", 1024), ("z", 768), ("y", 768))


def grads_kernel(
    their_gate,
    their_up,
    their_down,
    n1_in,
    dqkv_in,
    att_in,
    da_in,
    gains_in,
    q_out,
    k_out,
    v_out,
    o_out,
    part_gate,
    part_up,
    part_down,
    gains_out,
    n1,
    dqkv,
    att,
    da,
    *rest,
):
    lane_refs, rest = [rest[i * 9 : i * 9 + 9] for i in range(len(LANES))], rest[9 * len(LANES) :]
    (
        small,
        small_recv,
        load_sem,
        send_sem,
        recv_sem,
        pair_send,
        pair_recv,
        small_send,
        small_recv_sem,
        out_sem,
    ) = rest
    f = lax.axis_index("fsdp")
    e = lax.axis_index("expert")
    y, x, z = e // 8, lax.rem(e // 4, 2), lax.rem(e, 4)
    other = 1 - f
    own_half = aligned(f * HALF, HALF, 128)
    other_half = aligned(other * HALF, HALF, 128)

    def along_y(d):
        return {"expert": lax.rem(y + d, 4) * 8 + x * 4 + z}

    def along_z(d):
        return {"expert": y * 8 + x * 4 + lax.rem(z + d, 4)}

    twin = {"expert": y * 8 + (1 - x) * 4 + z}
    partner = {"fsdp": other}

    barrier = pltpu.get_barrier_semaphore()
    neighbours = [along_y(d) for d in (1, 2, 3)] + [along_z(d) for d in (1, 2, 3)]
    neighbours += [twin, partner]
    for place in neighbours:
        pl.semaphore_signal(barrier, inc=1, device_id=place, device_id_type=MESH)

    loads = [
        (att_in, att),
        (da_in, da),
        (n1_in, n1),
        (dqkv_in, dqkv),
    ]
    loads = [pltpu.make_async_copy(a, b, load_sem.at[i]) for i, (a, b) in enumerate(loads)]
    for copy in loads:
        copy.start()

    def remote(src, dst, send, recv, place):
        return pltpu.make_async_remote_copy(
            src_ref=src,
            dst_ref=dst,
            send_sem=send,
            recv_sem=recv,
            device_id=place,
            device_id_type=MESH,
        )

    def wait_for(ref, sem):
        pltpu.make_async_copy(ref, ref, sem).wait()

    class Lane:
        def __init__(self, i):
            self.i = i
            self.v, self.far, self.merged, self.r1, self.s1, self.r2, self.s2, self.r3, self.g = (
                lane_refs[i]
            )
            axes = ((along_y, y), (along_z, z))
            (axis, at), (self.next, self.to) = axes if LANES[i][0] == "y" else axes[::-1]
            self.right, self.left = axis(1), axis(3)
            self.at = at
            half = LANES[i][1] // 2
            self.mine = aligned(x * half, half, 128)
            self.theirs = aligned((1 - x) * half, half, 128)
            self.place = aligned(at * BAND + self.to * SLICE, SLICE, 16)

        def rows(self, distance, part=None):
            start = lax.rem(self.at + distance, 4) * BAND
            if part is None:
                return aligned(start, BAND, 16)
            return aligned(start + part * (BAND // 2), BAND // 2, 16)

        def send(self, stage, src, dst, place):
            remote(
                src, dst, send_sem.at[self.i, stage], recv_sem.at[self.i, stage], place
            ).start()

        def arrived(self, stage, ref):
            wait_for(ref, recv_sem.at[self.i, stage])

        def spread(self):
            low = pl.ds(BAND // 2, BAND // 2)
            top = pl.ds(0, BAND // 2)
            self.send(0, self.v.at[self.rows(2, 0)], self.far.at[0], self.right)
            self.send(1, self.v.at[self.rows(2, 1)], self.far.at[1], self.left)
            self.send(2, self.v.at[self.rows(1, 1)], self.r1.at[0, low], self.right)
            self.send(3, self.v.at[self.rows(3, 0)], self.r1.at[1, top], self.left)

        def merge(self):
            low = pl.ds(BAND // 2, BAND // 2)
            top = pl.ds(0, BAND // 2)
            self.arrived(0, self.far.at[0])
            total = self.v[self.rows(1, 0)].astype(F32) + self.far[0].astype(F32)
            self.merged[0] = total.astype(BF)
            self.send(2, self.merged.at[0], self.r1.at[0, top], self.right)
            self.arrived(1, self.far.at[1])
            total = self.v[self.rows(3, 1)].astype(F32) + self.far[1].astype(F32)
            self.merged[1] = total.astype(BF)
            self.send(3, self.merged.at[1], self.r1.at[1, low], self.left)

        def join_one(self):
            self.arrived(2, self.r1.at[0])
            self.arrived(3, self.r1.at[1])
            total = self.v[self.rows(0)].astype(F32)
            total = total + self.r1[0].astype(F32) + self.r1[1].astype(F32)
            self.s1[...] = total.astype(BF)
            for d in (1, 2, 3):
                rows = aligned(lax.rem(self.to + d, 4) * SLICE, SLICE, 16)
                self.send(4, self.s1.at[rows], self.r2.at[self.to], self.next(d))

        def join_two(self):
            self.arrived(4, self.r2.at[pl.ds(0, 3)])
            total = self.s1[aligned(self.to * SLICE, SLICE, 16)].astype(F32)
            for d in (1, 2, 3):
                total = total + self.r2[lax.rem(self.to + d, 4)].astype(F32)
            self.s2[...] = total.astype(BF)
            self.send(5, self.s2.at[:, self.theirs], self.r3, twin)

        def join_three(self):
            self.arrived(5, self.r3)
            total = self.s2[:, self.mine].astype(F32) + self.r3[...].astype(F32)
            self.g[self.place, self.mine] = total.astype(BF)
            part = self.g.at[self.place, self.mine]
            self.send(6, part, part, twin)

        def gather_two(self):
            self.arrived(6, self.g.at[self.place, self.theirs])
            part = self.g.at[self.place]
            for d in (1, 2, 3):
                self.send(7, part, part, self.next(d))

        def gather_one(self):
            self.arrived(7, self.g.at[pl.ds(0, 3 * SLICE)])
            top, low = self.g.at[self.rows(0, 0)], self.g.at[self.rows(0, 1)]
            self.send(8, top, top, self.right)
            self.send(9, low, low, self.left)
            self.send(10, low, low, self.right)
            self.send(11, top, top, self.left)

        def pass_on(self):
            top, low = self.g.at[self.rows(3, 0)], self.g.at[self.rows(1, 1)]
            self.arrived(8, top)
            self.send(12, top, top, self.right)
            self.arrived(9, low)
            self.send(13, low, low, self.left)

        def finish(self):
            part = self.g.at[pl.ds(0, BAND // 2)]
            for stage in (10, 11, 12, 13):
                self.arrived(stage, part)

        def drain(self):
            half = self.v.at[pl.ds(0, BAND // 2)]
            band = self.v.at[pl.ds(0, BAND)]
            slices = self.v.at[pl.ds(0, 3 * SLICE)]
            sizes = [half, half, band, band, slices, self.s2.at[:, self.theirs]]
            sizes += [self.g.at[self.place, self.mine], slices] + [half] * 6
            for stage, ref in enumerate(sizes):
                wait_for(ref, send_sem.at[self.i, stage])

    out_one, query_one, out_two, query_two = lanes = [Lane(i) for i in range(len(LANES))]

    def over_micro(group, cols):
        block = jnp.concatenate([dqkv[m, group, :, cols] for m in range(MB)], axis=0)
        return dot_tn(n1[...], block).astype(BF)

    for copy in loads[:2]:
        copy.wait()
    for j in range(2):
        cols = pl.ds(j * 512, 512)
        out_one.v[:, cols] = dot_tn(att[...], da[:, cols]).astype(BF)
    pl.semaphore_wait(barrier, len(neighbours))
    out_one.spread()
    for copy in loads[2:4]:
        copy.wait()
    query_one.v[:, pl.ds(0, HALF)] = over_micro(0, pl.ds(0, HALF))
    query_one.v[:, pl.ds(HALF, 256)] = over_micro(1, pl.ds(0, 256))
    query_one.spread()
    small[...] = gains_in[...]
    small_pair = remote(
        small.at[:, other_half],
        small_recv.at[0],
        small_send.at[0],
        small_recv_sem.at[0],
        partner,
    )
    small_pair.start()
    out_two.v[:, pl.ds(0, 512)] = dot_tn(att[...], da[:, pl.ds(1024, 512)]).astype(BF)
    query_two.v[:, pl.ds(0, 512)] = over_micro(1, pl.ds(256, 512))
    for g in range(2):
        query_two.v[:, pl.ds(512 + g * HEAD, HEAD)] = over_micro(g, pl.ds(HALF, HEAD))
        out_two.v[:, pl.ds(512 + g * HEAD, HEAD)] = over_micro(g, pl.ds(HALF + HEAD, HEAD))

    pair = [
        remote(src, dst, pair_send.at[i], pair_recv.at[i], partner)
        for i, (src, dst) in enumerate(
            ((their_gate, part_gate), (their_up, part_up), (their_down, part_down))
        )
    ]
    pieces = [
        remote(src.at[rows], dst.at[rows], pair_send.at[n], pair_recv.at[n], partner)
        for n, src, dst, size in (
            (0, their_gate, part_gate, HALF // 4),
            (1, their_up, part_up, HALF // 4),
            (2, their_down, part_down, HIDDEN // 8),
        )
        for rows in [pl.ds(i * size, size) for i in range(4)]
    ]

    def send_pieces(start, stop):
        for copy in pieces[start:stop]:
            copy.start()

    def spread_small(i, axis):
        for d in (1, 2, 3):
            remote(
                small.at[:, pl.ds(0, HALF)],
                small_recv.at[1 + 3 * i + d - 1],
                small_send.at[1 + 3 * i + d - 1],
                small_recv_sem.at[1 + 3 * i + d - 1],
                axis(d),
            ).start()

    def join_small(i, axis):
        for d in (1, 2, 3):
            remote(
                small.at[:, pl.ds(0, HALF)],
                small_recv.at[1 + 3 * i + d - 1],
                small_send.at[1 + 3 * i + d - 1],
                small_recv_sem.at[1 + 3 * i + d - 1],
                axis(d),
            ).wait()
        total = small[:, pl.ds(0, HALF)]
        for d in (1, 2, 3):
            total = total + small_recv[1 + 3 * i + d - 1]
        small[:, pl.ds(0, HALF)] = total

    small_pair.wait()
    small[:, pl.ds(0, HALF)] = small[:, own_half] + small_recv[0]
    spread_small(0, along_y)

    out_two.spread()
    query_two.spread()
    send_pieces(0, 4)
    join_small(0, along_y)
    spread_small(1, along_z)
    for lane in lanes:
        lane.merge()
    for lane in lanes:
        lane.join_one()
    for lane in lanes:
        lane.join_two()
    join_small(1, along_z)
    small_twin = remote(
        small.at[:, pl.ds(0, HALF)],
        small_recv.at[7],
        small_send.at[7],
        small_recv_sem.at[7],
        twin,
    )
    small_twin.start()
    send_pieces(4, 5)
    for lane in lanes:
        lane.join_three()
    send_pieces(5, 12)
    for lane in lanes:
        lane.gather_two()
    for lane in lanes:
        lane.gather_one()
    for lane in lanes:
        lane.pass_on()
    small_twin.wait()
    gains_out[...] = small[:, pl.ds(0, HALF)] + small_recv[7]

    outs = []

    def out_copy(src, dst):
        copy = pltpu.make_async_copy(src, dst, out_sem.at[len(outs)])
        copy.start()
        outs.append(copy)

    out_one.finish()
    out_copy(out_one.g, o_out.at[:, pl.ds(0, 1024)])
    query_one.finish()
    out_copy(query_one.g, q_out.at[:, pl.ds(0, 1024)])
    out_two.finish()
    out_copy(out_two.g.at[:, pl.ds(0, 512)], o_out.at[:, pl.ds(1024, 512)])
    out_copy(out_two.g.at[:, pl.ds(512, 256)], v_out)
    query_two.finish()
    out_copy(query_two.g.at[:, pl.ds(0, 512)], q_out.at[:, pl.ds(1024, 512)])
    out_copy(query_two.g.at[:, pl.ds(512, 256)], k_out)

    for lane in lanes:
        lane.drain()
    for copy in pair:
        copy.wait()
    for copy in outs:
        copy.wait()


def reduce_grads(*operands):
    def out(*shape):
        return jax.ShapeDtypeStruct(shape, BF)

    vmem = pl.BlockSpec(memory_space=pltpu.VMEM)
    anywhere = pl.BlockSpec(memory_space=pl.ANY)
    dma = pltpu.SemaphoreType.DMA
    lanes = []
    for _, width in LANES:
        lanes += [
            pltpu.VMEM((HALF, width), BF),
            pltpu.VMEM((2, BAND // 2, width), BF),
            pltpu.VMEM((2, BAND // 2, width), BF),
            pltpu.VMEM((2, BAND, width), BF),
            pltpu.VMEM((BAND, width), BF),
            pltpu.VMEM((4, SLICE, width), BF),
            pltpu.VMEM((SLICE, width), BF),
            pltpu.VMEM((SLICE, width // 2), BF),
            pltpu.VMEM((HALF, width), BF),
        ]
    return pl.pallas_call(
        grads_kernel,
        name="grads",
        out_shape=(
            out(HALF, WIDTH),
            out(HALF, 256),
            out(HALF, 256),
            out(HALF, WIDTH),
            out(HALF, HIDDEN),
            out(HALF, HIDDEN),
            out(HIDDEN // 2, WIDTH),
            jax.ShapeDtypeStruct((8, HALF), F32),
        ),
        in_specs=[anywhere] * 7 + [vmem],
        out_specs=[anywhere] * 7 + [vmem],
        scratch_shapes=[
            pltpu.VMEM((MB * 2 * SEQ, HALF), BF),
            pltpu.VMEM((MB, 2, 2 * SEQ, QKV), BF),
            pltpu.VMEM((MB * 2 * SEQ, HALF), BF),
            pltpu.VMEM((MB * 2 * SEQ, WIDTH), BF),
        ]
        + lanes
        + [
            pltpu.VMEM((8, WIDTH), F32),
            pltpu.VMEM((8, 8, HALF), F32),
            dma((4,)),
            dma((len(LANES), 14)),
            dma((len(LANES), 14)),
            dma((3,)),
            dma((3,)),
            dma((8,)),
            dma((8,)),
            dma((9,)),
        ],
        compiler_params=pltpu.CompilerParams(
            collective_id=1, has_side_effects=True, vmem_limit_bytes=62 * 2**20
        ),
    )(*operands)


def finish_kernel(*refs):
    (q, k, v, o, own_g, own_u, own_d, part_g, part_u, part_d, acts, grads, gains), outs = (
        refs[:13],
        refs[13:],
    )
    for src, dst in zip((q, k, v, o), outs):
        dst[...] = src[...].astype(F32)
    for own, part, dst in zip((own_g, own_u, own_d), (part_g, part_u, part_d), outs[4:]):
        dst[...] = own[...].astype(F32) + part[...].astype(F32)
    outs[7][...] = acts[...]
    outs[8][...] = grads[...]
    outs[9][...] = gains[0:1]
    outs[10][...] = gains[1:2]


def finish(*blocks):
    steps = 4

    def spec(rows, cols):
        return pl.BlockSpec((rows // steps, cols), lambda i: (i, 0))

    def whole(rows, cols):
        return pl.BlockSpec((rows, cols), lambda i: (0, 0))

    gains = blocks[-1]
    split = blocks[:-1]
    results = split[:7] + split[10:]
    dtypes = [F32] * 7 + [BF] * 2
    return pl.pallas_call(
        finish_kernel,
        name="finish",
        grid=(steps,),
        out_shape=[jax.ShapeDtypeStruct(b.shape, t) for b, t in zip(results, dtypes)]
        + [jax.ShapeDtypeStruct((1, HALF), F32)] * 2,
        in_specs=[spec(*b.shape) for b in split] + [whole(*gains.shape)],
        out_specs=[spec(*b.shape) for b in results] + [whole(1, HALF)] * 2,
        compiler_params=pltpu.CompilerParams(vmem_limit_bytes=62 * 2**20),
    )(*blocks)


def local(
    inputs,
    cotangent,
    segments,
    expert_ids,
    gate_logits,
    w_query,
    key_projection,
    value_projection,
    w_out,
    gain_attn,
    gain_moe,
    w_gate,
    w_up,
    w_down,
):
    steps = np.arange(HEAD) % (HEAD // 2)
    frequency = (ROPE_BASE ** (-steps * 2.0 / HEAD)).astype(np.float32)[None]
    (
        acts,
        in_grads,
        gain_parts,
        own_gate,
        own_up,
        own_down,
        their_gate,
        their_up,
        their_down,
        n1,
        dqkv,
        att,
        da,
    ) = run_sections(
        inputs,
        cotangent,
        w_query[0],
        key_projection[0],
        value_projection[0],
        w_out[0],
        w_gate[0, 0],
        w_up[0, 0],
        w_down[0, 0],
        gain_attn,
        gain_moe,
        segments,
        jnp.swapaxes(expert_ids[0], 1, 2),
        jnp.swapaxes(gate_logits[0], 1, 2),
        jnp.asarray(frequency),
    )
    gq, gk, gv, go, part_gate, part_up, part_down, gains = reduce_grads(
        their_gate,
        their_up,
        their_down,
        n1.reshape(MB * 2 * SEQ, HALF),
        dqkv,
        att.reshape(MB * 2 * SEQ, HALF),
        da.reshape(MB * 2 * SEQ, WIDTH),
        gain_parts,
    )
    gq, gk, gv, go, grad_gate, grad_up, grad_down, acts, in_grads, gain_one, gain_two = finish(
        gq,
        gk,
        gv,
        go,
        own_gate,
        own_up,
        own_down,
        part_gate,
        part_up,
        part_down,
        acts.reshape(MB * SEQ, WIDTH),
        in_grads.reshape(MB * SEQ, WIDTH),
        gains,
    )
    return (
        acts.reshape(1, MB, SEQ, WIDTH),
        in_grads.reshape(1, MB, SEQ, WIDTH),
        gq[None],
        gk[None],
        gv[None],
        go[None],
        gain_one,
        gain_two,
        grad_gate[None, None],
        grad_up[None, None],
        grad_down[None, None],
    )


def solution(mesh):
    return jax.shard_map(
        local,
        mesh=mesh,
        in_specs=(
            P(None, ("fsdp", "expert"), None),
            P(None, ("fsdp", "expert"), None),
            P(None, ("fsdp", "expert")),
            P("section", None, ("fsdp", "expert"), None),
            P("section", None, ("fsdp", "expert"), None),
            P("section", "fsdp", None),
            P("section", "fsdp", None),
            P("section", "fsdp", None),
            P("section", "fsdp", None),
            P("section", "fsdp"),
            P("section", "fsdp"),
            P("section", "expert", "fsdp", None),
            P("section", "expert", "fsdp", None),
            P("section", "expert", "fsdp", None),
        ),
        out_specs=(
            P("section", None, ("fsdp", "expert"), None),
            P("section", None, ("fsdp", "expert"), None),
            P("section", "fsdp", None),
            P("section", "fsdp", None),
            P("section", "fsdp", None),
            P("section", "fsdp", None),
            P("section", "fsdp"),
            P("section", "fsdp"),
            P("section", "expert", "fsdp", None),
            P("section", "expert", "fsdp", None),
            P("section", "expert", "fsdp", None),
        ),
        check_vma=False,
    )
```
